32 devices in a mesh: groups: 2 (over x), tensor: 8 (over z, y), bank: 2 (over core).
Axes of the slice: x: 2, y: 2, z: 4, core: 2. Of those that a mesh axis runs over, the one named last changes fastest.
Arguments:
- normed_hidden_input: bfloat16 [32, 8192], P(('groups', 'bank'), 'tensor'), parts along dimension 0, may hold values from -6 to 6
- beam_adapter_index: int32 [32], P(('groups', 'bank')), parts along dimension 0, may hold values from 0 to 31
- beam_cache_length: int32 [32], P(('groups', 'bank')), parts along dimension 0, may hold values from 128 to 2048
- query_weight: bfloat16 [8192, 8192], P('tensor'), may hold values from -0.0625 to 0.0625
- keyvalue_weight: bfloat16 [8192, 2048], P('tensor'), may hold values from -0.0625 to 0.0625
- output_weight: bfloat16 [8192, 8192], P('tensor'), may hold values from -1 to 1
- lowrank_down_factors: bfloat16 [32, 8192, 64], P('bank', 'tensor'), may hold values from -0.0625 to 0.0625
- lowrank_up_factors: bfloat16 [32, 64, 8192], P('bank', None, 'tensor'), may hold values from -0.75 to 0.75
- paged_key_cache: bfloat16 [32, 2048, 1024], P(('groups', 'bank'), 'tensor'), parts along dimension 0, may hold values from -190 to 190
- paged_value_cache: bfloat16 [32, 2048, 1024], P(('groups', 'bank'), 'tensor'), parts along dimension 0, may hold values from -6 to 6
Outputs:
- mixed_out: bfloat16 [32, 8192], P(('groups', 'bank'), 'tensor'), parts along dimension 0
The draws below stay inside these ranges and needn't reach their ends.
There are 2 independent parts, one for each index of `groups`. The reference program is written for one: setup_inputs(seed, part) draws one part's arguments, and reference() takes and returns one part's arrays. A program takes and returns all parts, laid end to end along the dimension named above; an argument that names none is the same for every part. Nothing has to cross between parts.
All inputs are finite; a program needn't handle non-finite values.
Results may differ from the reference program's by a relative error of at most 0.0071.
Values may be sent and summed in bfloat16 or wider, within the bound.
No kernel may reach another device: no remote copies, remote signals or barrier semaphores. Data moves between devices by JAX's collectives and lax.ppermute only.
A program may use at most 128 MiB of HBM per device.

```python
import math
import jax
import jax.numpy as jnp
import numpy as np

MODEL_DIM = 8192
HEAD_DIM = 128
KVH = 8
ADAPTER_RANK = 64
LEN = 2048
HEADS = 64
KVD = 1024
BEAMS = 16
ADAPTER_COUNT = 32


def draw_lengths(key):
    key = jax.random.fold_in(key, 5)
    key_lens, key_spot = jax.random.split(key)
    lengths = jax.random.randint(key_lens, (BEAMS,), LEN // 16, LEN + 1)
    long_beam = jax.random.randint(key_spot, (), 0, BEAMS)
    beam_index = jnp.arange(BEAMS)
    lengths = jnp.where(beam_index == long_beam, LEN, lengths)
    lengths = jnp.where(beam_index == (long_beam + 1) % BEAMS, LEN // 16, lengths)
    return lengths.astype(jnp.int32)


def draw_beam_cache_length(key, part):
    return draw_lengths(key)


def shifted_rows(key, base_values, lengths):
    key_first, key_gap, key_level, key_step = jax.random.split(key, 4)
    live_count = lengths[:, None]
    first_spot = jax.random.randint(key_first, (BEAMS, 1), 0, live_count)
    second_spot = (first_spot + 1 + jax.random.randint(key_gap, (BEAMS, 1), 0, live_count - 1)) % live_count
    level = jnp.exp(jax.random.uniform(key_level, (BEAMS, 1), jnp.float32, jnp.log(60.0), jnp.log(110.0)))
    second_level = level * jax.random.uniform(key_step, (BEAMS, 1), jnp.float32, 1.01, 1.03)
    spots = jnp.arange(LEN)[None, :]
    shift = jnp.where(spots == first_spot, level, 0.0) + jnp.where(spots == second_spot, second_level, 0.0)
    return base_values + shift[:, :, None]


def draw_paged_key_cache(key, part):
    lengths = draw_lengths(key)
    key = jax.random.fold_in(key, 3)
    key_base, key_shift = jax.random.split(key)
    shape_all = (BEAMS, LEN, KVH * HEAD_DIM)
    base_values = jax.random.truncated_normal(key_base, -6.0, 6.0, shape_all, jnp.float32)
    return shifted_rows(key_shift, base_values, lengths).astype(jnp.bfloat16)


def with_ends(result, rng, low, high):
    extent = result.shape
    spot = [jax.random.randint(jax.random.fold_in(rng, axis), (), 0, extent[axis]) for axis in range(len(extent))]
    result = result.at[tuple(spot)].set(low)
    longest = extent.index(max(extent))
    spot[longest] = (spot[longest] + 1) % extent[longest]
    return result.at[tuple(spot)].set(high)


def steps_of(stream_key, shape, cuts, low, high):
    gain = 1.0
    for axis_at, parts in cuts:
        draws = jax.random.uniform(jax.random.fold_in(jax.random.fold_in(stream_key, 6), axis_at), (parts,), jnp.float32, low / len(cuts), high / len(cuts))
        gain = gain * jnp.repeat(jnp.exp(draws), shape[axis_at] // parts).reshape((-1,) + (1,) * (len(shape) - 1 - axis_at))
    return gain


def cumulative_ranks(amount, slope):
    portions = [(1 << 20) // math.isqrt(grade ** slope) + 1 for grade in range(1, amount + 1)]
    width = 1 + sum(portions) // (1 << 30)
    return np.cumsum(np.array([max(1, weight // width) for weight in portions]))


def ranked_ids(rng, shape, number_of, slope):
    table = cumulative_ranks(number_of, slope)
    lot = jax.random.randint(jax.random.fold_in(rng, 1), shape, 0, int(table[number_of - 1]))
    standing = jnp.searchsorted(jnp.asarray(table, jnp.int32), lot, side="right")
    return jax.random.permutation(jax.random.fold_in(rng, 2), number_of)[standing].astype(jnp.int32)


def gaussian(stream_key, extent, deviation, most, pieces=(), kind=jnp.bfloat16):
    level = steps_of(stream_key, extent, pieces, -0.22, 0.18) if pieces else 1.0
    values = jax.random.normal(stream_key, extent, jnp.float32) * deviation * level
    return jnp.minimum(jnp.maximum(values, -most), most).astype(kind)


def setup_inputs(seed: int = 0, part: int = 0) -> dict:
    streams_of = jax.random.split(jax.random.key(seed), 11)
    part_keys = jax.random.split(jax.random.fold_in(streams_of[10], part), 11)
    normed_hidden_input = gaussian(part_keys[0], (BEAMS, MODEL_DIM), 1.0, 6.0, ((0, 2), (1, 8)))
    beam_adapter_index = with_ends(ranked_ids(part_keys[1], (BEAMS,), ADAPTER_COUNT, 2), jax.random.fold_in(part_keys[1], 3), 0, ADAPTER_COUNT - 1).astype(jnp.int32)
    beam_cache_length = draw_beam_cache_length(jax.random.fold_in(jax.random.fold_in(streams_of[10], part), 71), part)
    query_weight = gaussian(streams_of[3], (MODEL_DIM, MODEL_DIM), MODEL_DIM ** -0.5, 0.0625, ((0, 8),))
    keyvalue_weight = gaussian(streams_of[4], (MODEL_DIM, 2 * KVD), MODEL_DIM ** -0.5, 0.0625, ((0, 8),))
    output_weight = gaussian(streams_of[5], (MODEL_DIM, MODEL_DIM), (MODEL_DIM // 256) ** -0.5, 1.0, ((0, 8),))
    lowrank_down_factors = gaussian(streams_of[6], (ADAPTER_COUNT, MODEL_DIM, ADAPTER_RANK), MODEL_DIM ** -0.5, 0.0625, ((0, 2), (1, 8)))
    lowrank_up_factors = gaussian(streams_of[7], (ADAPTER_COUNT, ADAPTER_RANK, MODEL_DIM), ADAPTER_RANK ** -0.5, 0.75, ((0, 2), (2, 8)))
    paged_key_cache = draw_paged_key_cache(jax.random.fold_in(jax.random.fold_in(streams_of[10], part), 71), part)
    paged_value_cache = gaussian(part_keys[9], (BEAMS, LEN, KVD), 1.0, 6.0, ((0, 2), (1, 8)))
    return dict(normed_hidden_input=normed_hidden_input, beam_adapter_index=beam_adapter_index, beam_cache_length=beam_cache_length, query_weight=query_weight, keyvalue_weight=keyvalue_weight, output_weight=output_weight, lowrank_down_factors=lowrank_down_factors, lowrank_up_factors=lowrank_up_factors, paged_key_cache=paged_key_cache, paged_value_cache=paged_value_cache)


def apply_rotary(values, positions, head_size):
    row_count, col_count = values.shape
    half_size = head_size // 2
    frequency = jnp.power(500000.0, -2.0 * jnp.arange(half_size, dtype=jnp.float32) / head_size)
    angles = positions.astype(jnp.float32)[:, None] * frequency[None, :]
    cosine_table = jnp.cos(angles)[:, None, :]
    sine_table = jnp.sin(angles)[:, None, :]
    shaped = values.reshape(row_count, col_count // head_size, 2, half_size)
    first_half = shaped[:, :, 0]
    second_half = shaped[:, :, 1]
    rotated = jnp.stack([first_half * cosine_table - second_half * sine_table, second_half * cosine_table + first_half * sine_table], axis=2)
    return rotated.reshape(row_count, col_count)


def reference(normed_hidden_input, beam_adapter_index, beam_cache_length, query_weight, keyvalue_weight, output_weight, lowrank_down_factors, lowrank_up_factors, paged_key_cache, paged_value_cache):
    query_plain = jnp.dot(normed_hidden_input, query_weight, preferred_element_type=jnp.float32)
    keyval = jnp.dot(normed_hidden_input, keyvalue_weight, preferred_element_type=jnp.float32)
    chosen_down_factor = lowrank_down_factors[beam_adapter_index].astype(jnp.float32)
    inner_total = jnp.einsum('ci,cim->cm', normed_hidden_input.astype(jnp.float32), chosen_down_factor).astype(jnp.bfloat16)
    chosen_up_factor = lowrank_up_factors[beam_adapter_index].astype(jnp.float32)
    lowrank_delta = jnp.einsum('mc,mct->mt', inner_total.astype(jnp.float32), chosen_up_factor)
    kv_width = KVH * HEAD_DIM
    group_size = HEADS // KVH
    query_rotated = apply_rotary(query_plain + lowrank_delta, beam_cache_length, HEAD_DIM).astype(jnp.bfloat16)
    key_new = apply_rotary(keyval[:, :kv_width], beam_cache_length, HEAD_DIM).astype(jnp.bfloat16)
    value_new = keyval[:, kv_width:].astype(jnp.bfloat16)
    query_heads = query_rotated.reshape(BEAMS, KVH, group_size, HEAD_DIM).astype(jnp.float32)
    key_block = paged_key_cache.reshape(BEAMS, LEN, KVH, HEAD_DIM).astype(jnp.float32)
    value_block = paged_value_cache.reshape(BEAMS, LEN, KVH, HEAD_DIM).astype(jnp.float32)
    score_scale = 1.0 / (HEAD_DIM ** 0.5)
    scores = jnp.einsum('bkgh,bpkh->bkgp', query_heads, key_block) * score_scale
    live_mask = (jnp.arange(LEN)[None, :] < beam_cache_length[:, None])[:, None, None, :]
    scores = jnp.where(live_mask, scores, -1e30)
    score_new = jnp.einsum('bkgh,bkh->bkg', query_heads, key_new.reshape(BEAMS, KVH, HEAD_DIM).astype(jnp.float32)) * score_scale
    peak_score = jnp.maximum(jnp.max(scores, axis=-1), score_new)
    weights = jnp.where(live_mask, jnp.exp(scores - peak_score[..., None]), 0.0)
    new_weight = jnp.exp(score_new - peak_score)
    weight_total = jnp.sum(weights, axis=-1) + new_weight
    weighted = jnp.einsum('bkgp,bpkh->bkgh', weights.astype(jnp.bfloat16).astype(jnp.float32), value_block)
    weighted = weighted + new_weight.astype(jnp.bfloat16).astype(jnp.float32)[..., None] * value_new.reshape(BEAMS, KVH, HEAD_DIM).astype(jnp.float32)[:, :, None, :]
    attended = (weighted / weight_total[..., None]).reshape(BEAMS, MODEL_DIM).astype(jnp.bfloat16)
    mixed_out = normed_hidden_input.astype(jnp.float32) + jnp.dot(attended, output_weight, preferred_element_type=jnp.float32)
    return mixed_out.astype(jnp.bfloat16)
```

```python
import functools

import jax
import jax.numpy as jnp
from jax import lax
from jax.experimental import pallas as pl
from jax.experimental.pallas import tpu as pltpu
from jax.sharding import PartitionSpec as P

HEAD_DIM = 128
F32 = jnp.float32
BF16 = jnp.bfloat16
LINK = jnp.float32
VMEM_LIMIT = 40 * 1024 * 1024


def whole():
    return pl.BlockSpec(memory_space=pltpu.VMEM)


def iota(shape, axis):
    return lax.broadcasted_iota(jnp.int32, shape, axis)


def params():
    return pltpu.CompilerParams(
        vmem_limit_bytes=VMEM_LIMIT, dimension_semantics=("arbitrary",)
    )


def project_kernel(place, x_ref, wq_ref, wk_ref, wv_ref, *outs):
    step = pl.program_id(0)
    x = x_ref[...]
    width = wq_ref.shape[1]
    q = jnp.dot(x, wq_ref[...], preferred_element_type=F32).astype(LINK)
    k = jnp.dot(x, wk_ref[...], preferred_element_type=F32).astype(LINK)
    v = jnp.dot(x, wv_ref[...], preferred_element_type=F32).astype(LINK)
    for slot, out in enumerate(outs):

        @pl.when(step == slot)
        def _(out=out):
            out[:, :width] = q
            out[:, width : width + HEAD_DIM] = k
            out[:, width + HEAD_DIM :] = v


def project(place, x, wq, wkv, ranks):
    rows, depth = x.shape
    width = wq.shape[1] // ranks
    kv_heads = wkv.shape[1] // 2 // HEAD_DIM
    return pl.pallas_call(
        project_kernel,
        grid_spec=pltpu.PrefetchScalarGridSpec(
            num_scalar_prefetch=1,
            grid=(ranks,),
            in_specs=[
                pl.BlockSpec((rows, depth), lambda s, p: (0, 0)),
                pl.BlockSpec((depth, width), lambda s, p: (0, s ^ p[0])),
                pl.BlockSpec((depth, HEAD_DIM), lambda s, p: (0, s ^ p[0])),
                pl.BlockSpec((depth, HEAD_DIM), lambda s, p: (0, kv_heads + (s ^ p[0]))),
            ],
            out_specs=[pl.BlockSpec((rows, width + 2 * HEAD_DIM), lambda s, p: (0, 0))] * ranks,
        ),
        out_shape=[jax.ShapeDtypeStruct((rows, width + 2 * HEAD_DIM), LINK)] * ranks,
        compiler_params=params(),
        cost_estimate=pl.CostEstimate(
            flops=2 * rows * depth * (wq.shape[1] + wkv.shape[1]),
            bytes_accessed=2 * (wq.size + wkv.size),
            transcendentals=0,
        ),
        name="project",
    )(place, x, wq, wkv, wkv)


def adapter_column(index_ref, rows):
    row = iota((rows, HEAD_DIM), 0)
    column = jnp.zeros((rows, HEAD_DIM), jnp.int32)
    for r in range(rows):
        column = jnp.where(row == r, index_ref[r], column)
    return column


def down_kernel(index_ref, bank_ref, x_ref, other_ref, down_ref, out_ref):
    rows = 2 * x_ref.shape[0]
    rank = down_ref.shape[1]
    count = down_ref.shape[0]
    x = jnp.concatenate([x_ref[...].astype(F32), other_ref[...].astype(F32)], axis=0)
    flat = down_ref[...].reshape(count * rank, down_ref.shape[2])
    every = lax.dot_general(
        x.astype(BF16), flat, (((1,), (1,)), ((), ())), preferred_element_type=F32
    )
    column = adapter_column(index_ref, rows) - bank_ref[0] * count
    lane = iota((rows, HEAD_DIM), 1)
    per = HEAD_DIM // rank
    total = jnp.zeros((rows, HEAD_DIM), F32)
    for j in range(count // per):
        part = every[:, j * HEAD_DIM : (j + 1) * HEAD_DIM]
        total += jnp.where(lane // rank + j * per == column, part, 0.0)
    out_ref[...] = total


def down(index, bank, x, other, factors):
    rows = 2 * x.shape[0]
    smem = pl.BlockSpec(memory_space=pltpu.SMEM)
    return pl.pallas_call(
        down_kernel,
        in_specs=[smem, smem, whole(), whole(), whole()],
        out_specs=whole(),
        out_shape=jax.ShapeDtypeStruct((rows, HEAD_DIM), F32),
        compiler_params=pltpu.CompilerParams(vmem_limit_bytes=VMEM_LIMIT),
        cost_estimate=pl.CostEstimate(
            flops=2 * rows * factors.size, bytes_accessed=2 * factors.size, transcendentals=0
        ),
        name="down",
    )(index, bank, x, other, factors)


def up_kernel(index_ref, bank_ref, *refs):
    *parts, up_ref, own_ref, other_ref = refs
    rows = parts[0].shape[0]
    count, rank, width = up_ref.shape
    total = parts[0][...]
    for part in parts[1:]:
        total += part[...]
    total = total.astype(BF16).astype(F32)
    column = adapter_column(index_ref, rows) - bank_ref[0] * count
    lane = iota((rows, HEAD_DIM), 1)
    per = HEAD_DIM // rank
    spread = jnp.concatenate(
        [
            jnp.where(lane // rank + j * per == column, total, 0.0)
            for j in range(count // per)
        ],
        axis=1,
    ).astype(BF16)
    delta = jnp.dot(
        spread, up_ref[...].reshape(count * rank, width), preferred_element_type=F32
    )
    own_ref[...] = delta[: rows // 2]
    other_ref[...] = delta[rows // 2 :]


def up(index, bank, parts, factors):
    rows = parts[0].shape[0]
    width = factors.shape[2]
    smem = pl.BlockSpec(memory_space=pltpu.SMEM)
    return pl.pallas_call(
        up_kernel,
        in_specs=[smem, smem] + [whole()] * (len(parts) + 1),
        out_specs=[whole()] * 2,
        out_shape=[jax.ShapeDtypeStruct((rows // 2, width), F32)] * 2,
        compiler_params=pltpu.CompilerParams(vmem_limit_bytes=VMEM_LIMIT),
        cost_estimate=pl.CostEstimate(
            flops=2 * rows * factors.size, bytes_accessed=2 * factors.size, transcendentals=0
        ),
        name="up",
    )(index, bank, *parts, factors)


def rotate(v, cosine, sine):
    return v * cosine + pltpu.roll(v, HEAD_DIM // 2, 1) * sine


def rotate_kernel(*refs):
    *parts, own_ref, other_ref, cos_ref, sin_ref, q_ref, k_ref, v_ref, rows_ref = refs
    total = parts[0][...].astype(F32)
    for part in parts[1:]:
        total += part[...].astype(F32)
    width = own_ref.shape[1]
    query = total[:, :width] + (own_ref[...] + other_ref[...])
    cosine, sine = cos_ref[...], sin_ref[...]
    for g in range(width // HEAD_DIM):
        rows_ref[:, g, :] = rotate(query[:, g * HEAD_DIM : (g + 1) * HEAD_DIM], cosine, sine)
    q_ref[...] = rows_ref[...].reshape(q_ref.shape).astype(BF16)
    k_ref[...] = (
        rotate(total[:, width : width + HEAD_DIM], cosine, sine).astype(BF16).astype(F32)
    )
    v_ref[...] = total[:, width + HEAD_DIM :].astype(BF16).astype(F32)


def rotated(parts, own, other, cosine, sine):
    rows, width = own.shape
    heads = width // HEAD_DIM
    small = jax.ShapeDtypeStruct((rows, HEAD_DIM), F32)
    return pl.pallas_call(
        rotate_kernel,
        in_specs=[whole()] * (len(parts) + 4),
        out_specs=[whole()] * 3,
        out_shape=[jax.ShapeDtypeStruct((rows * heads, HEAD_DIM), BF16), small, small],
        scratch_shapes=[pltpu.VMEM((rows, heads, HEAD_DIM), F32)],
        compiler_params=pltpu.CompilerParams(vmem_limit_bytes=VMEM_LIMIT),
        name="rotate",
    )(*parts, own, other, cosine, sine)


def attend_kernel(ranks, place, length, *refs):
    queries = refs[:ranks]
    k_ref, v_ref = refs[ranks : ranks + 2]
    outs = refs[ranks + 2 : 2 * ranks + 2]
    q_rows, o_rows, stats = refs[2 * ranks + 2 :]
    beam = pl.program_id(0)
    beams = pl.num_programs(0)
    rank = place[0]
    group = q_rows.shape[1] // stats.shape[0]
    heads = ranks * group
    positions = k_ref.shape[1]

    @pl.when(beam == 0)
    def _():
        for s, query in enumerate(queries):
            q_rows[s] = query[...].astype(F32)

    first = pl.multiple_of(beam * group, group)
    q = q_rows[:, pl.ds(first, group), :].reshape(heads, HEAD_DIM)
    key_head = (iota((heads, HEAD_DIM), 0) // group) ^ rank
    wide = jnp.concatenate(
        [jnp.where(key_head == c, q, 0.0) for c in range(ranks)], axis=1
    ).astype(BF16)
    scores = lax.dot_general(
        wide, k_ref[0], (((1,), (1,)), ((), ())), preferred_element_type=F32
    ) * (1.0 / HEAD_DIM**0.5)
    live = rank * positions + iota((heads, positions), 1) < length[beam]
    scores = jnp.where(live, scores, -1e30)
    peak = jnp.max(scores, axis=1, keepdims=True)
    weights = jnp.where(live, jnp.exp(scores - peak), 0.0)
    total = jnp.sum(weights, axis=1, keepdims=True)
    product = jnp.dot(weights.astype(BF16), v_ref[0], preferred_element_type=F32)
    own = jnp.zeros((heads, HEAD_DIM), F32)
    for c in range(ranks):
        own = jnp.where(key_head == c, product[:, c * HEAD_DIM : (c + 1) * HEAD_DIM], own)
    o_rows[:, pl.ds(first, group), :] = own.reshape(ranks, group, HEAD_DIM)
    row, lane = iota((heads, HEAD_DIM), 0), iota((heads, HEAD_DIM), 1)
    spread = jnp.where(row == lane, peak, 0.0) + jnp.where(row + heads == lane, total, 0.0)
    stats[pl.ds(beam, 1), :] = jnp.sum(spread, axis=0, keepdims=True)

    @pl.when(beam == beams - 1)
    def _():
        high = stats[...].astype(BF16).astype(F32)
        rest = stats[...] - high
        middle = rest.astype(BF16).astype(F32)
        low = rest - middle
        tail = jnp.concatenate([high, middle, low, jnp.zeros_like(low)], axis=0)
        for s, out in enumerate(outs):
            out[...] = jnp.concatenate([o_rows[s], tail], axis=0).astype(BF16)


def attend(place, length, queries, keys, values):
    ranks = len(queries)
    beams, positions, width = keys.shape
    rows = queries[0].shape[0]
    out_rows = rows + 4 * beams
    return pl.pallas_call(
        functools.partial(attend_kernel, ranks),
        grid_spec=pltpu.PrefetchScalarGridSpec(
            num_scalar_prefetch=2,
            grid=(beams,),
            in_specs=[pl.BlockSpec((rows, HEAD_DIM), lambda i, p, n: (0, 0))] * ranks
            + [pl.BlockSpec((1, positions, width), lambda i, p, n: (i, 0, 0))] * 2,
            out_specs=[pl.BlockSpec((out_rows, HEAD_DIM), lambda i, p, n: (0, 0))] * ranks,
            scratch_shapes=[
                pltpu.VMEM((ranks, rows, HEAD_DIM), F32),
                pltpu.VMEM((ranks, rows, HEAD_DIM), F32),
                pltpu.VMEM((beams, HEAD_DIM), F32),
            ],
        ),
        out_shape=[jax.ShapeDtypeStruct((out_rows, HEAD_DIM), BF16)] * ranks,
        compiler_params=params(),
        cost_estimate=pl.CostEstimate(
            flops=4 * rows * ranks * positions * width,
            bytes_accessed=4 * keys.size,
            transcendentals=rows * ranks * positions,
        ),
        name="attend",
    )(place, length, *queries, keys, values)


def output_kernel(ranks, place, *refs):
    parts = refs[:ranks]
    q_ref, k_ref, v_ref, w_ref = refs[ranks : ranks + 4]
    outs = refs[ranks + 4 : 2 * ranks + 4]
    joined, attended = refs[2 * ranks + 4 :]
    step = pl.program_id(0)
    beams, group, _ = joined.shape
    rows = beams * group

    def by_row(v):
        return jnp.broadcast_to(v[:, None, :], (beams, group, HEAD_DIM)).reshape(rows, HEAD_DIM)

    @pl.when(step == 0)
    def _():
        row, lane = iota((rows, HEAD_DIM), 0), iota((rows, HEAD_DIM), 1)
        heads = ranks * group
        score = jnp.sum(
            q_ref[...].astype(F32) * by_row(k_ref[...]), axis=1, keepdims=True
        ) * (1.0 / HEAD_DIM**0.5)
        peaks, totals, weighted = [], [], []
        top = score
        for s, part in enumerate(parts):
            block = part[...].astype(F32)
            tail = (
                block[rows : rows + beams]
                + block[rows + beams : rows + 2 * beams]
                + block[rows + 2 * beams : rows + 3 * beams]
            )
            tail = by_row(tail)
            head = s * group + row % group
            peak = jnp.sum(jnp.where(lane == head, tail, 0.0), axis=1, keepdims=True)
            total = jnp.sum(jnp.where(lane == heads + head, tail, 0.0), axis=1, keepdims=True)
            top = jnp.maximum(top, peak)
            peaks.append(peak)
            totals.append(total)
            weighted.append(block[:rows])
        new = jnp.exp(score - top)
        everything = new
        result = new.astype(BF16).astype(F32) * by_row(v_ref[...])
        for peak, total, block in zip(peaks, totals, weighted):
            factor = jnp.exp(peak - top)
            everything += total * factor
            result += block * factor
        joined[...] = (result / everything).reshape(joined.shape)
        for g in range(group):
            attended[:, g * HEAD_DIM : (g + 1) * HEAD_DIM] = joined[:, g, :].astype(BF16)

    mixed = jnp.dot(attended[...], w_ref[...], preferred_element_type=F32).astype(BF16)
    for slot, out in enumerate(outs):

        @pl.when(step == slot)
        def _(out=out):
            out[...] = mixed


def output(place, parts, query, key_new, value_new, weight):
    ranks = len(parts)
    beams = key_new.shape[0]
    depth = weight.shape[0]
    width = weight.shape[1] // ranks
    group = depth // HEAD_DIM
    once = lambda a: pl.BlockSpec(a.shape, lambda s, p: (0, 0))
    return pl.pallas_call(
        functools.partial(output_kernel, ranks),
        grid_spec=pltpu.PrefetchScalarGridSpec(
            num_scalar_prefetch=1,
            grid=(ranks,),
            in_specs=[once(a) for a in (*parts, query, key_new, value_new)]
            + [pl.BlockSpec((depth, width), lambda s, p: (0, s ^ p[0]))],
            out_specs=[pl.BlockSpec((beams, width), lambda s, p: (0, 0))] * ranks,
            scratch_shapes=[
                pltpu.VMEM((beams, group, HEAD_DIM), F32),
                pltpu.VMEM((beams, depth), BF16),
            ],
        ),
        out_shape=[jax.ShapeDtypeStruct((beams, width), BF16)] * ranks,
        compiler_params=params(),
        cost_estimate=pl.CostEstimate(
            flops=2 * beams * weight.size, bytes_accessed=2 * weight.size, transcendentals=0
        ),
        name="output",
    )(place, *parts, query, key_new, value_new, weight)


def residual_kernel(x_ref, *refs):
    *parts, out_ref = refs
    total = parts[0][...].astype(F32)
    for part in parts[1:]:
        total += part[...].astype(F32)
    out_ref[...] = (x_ref[...].astype(F32) + total).astype(BF16)


def residual(x, parts):
    return pl.pallas_call(
        residual_kernel,
        in_specs=[whole()] * (len(parts) + 1),
        out_specs=whole(),
        out_shape=jax.ShapeDtypeStruct(x.shape, BF16),
        name="residual",
    )(x, *parts)


def traded(blocks, ranks):
    return [blocks[0]] + [
        lax.ppermute(blocks[s], "tensor", [(i, i ^ s) for i in range(ranks)])
        for s in range(1, ranks)
    ]


def matched_body(
    normed_hidden_input,
    beam_adapter_index,
    beam_cache_length,
    query_weight,
    keyvalue_weight,
    output_weight,
    lowrank_down_factors,
    lowrank_up_factors,
    paged_key_cache,
    paged_value_cache,
):
    x = normed_hidden_input
    ranks = lax.axis_size("tensor")
    place = lax.axis_index("tensor").astype(jnp.int32).reshape(1)
    bank = lax.axis_index("bank").astype(jnp.int32).reshape(1)
    swap = [(0, 1), (1, 0)]
    x_other = lax.ppermute(x, "bank", swap)
    index = jnp.concatenate([beam_adapter_index, lax.ppermute(beam_adapter_index, "bank", swap)])
    half = HEAD_DIM // 2
    frequency = jnp.power(500000.0, -2.0 * jnp.arange(half, dtype=F32) / HEAD_DIM)
    angles = beam_cache_length.astype(F32)[:, None] * frequency[None, :]
    cosine = jnp.tile(jnp.cos(angles), (1, 2))
    sine = jnp.sin(angles)
    sine = jnp.concatenate([-sine, sine], axis=1)

    parts = traded(project(place, x, query_weight, keyvalue_weight, ranks), ranks)
    inner = down(index, bank, x, x_other, lowrank_down_factors.swapaxes(1, 2))
    delta_own, delta_sent = up(index, bank, traded([inner] * ranks, ranks), lowrank_up_factors)
    delta_other = lax.ppermute(delta_sent, "bank", swap)
    query, key_new, value_new = rotated(parts, delta_own, delta_other, cosine, sine)
    partial = attend(
        place,
        beam_cache_length,
        traded([query] * ranks, ranks),
        paged_key_cache,
        paged_value_cache,
    )
    mixed = output(place, traded(partial, ranks), query, key_new, value_new, output_weight)
    return residual(x, traded(mixed, ranks))


def joined(x, axis, combine):
    everything = jax.tree.map(lambda part: lax.all_gather(part, axis), x)
    leading = jax.tree.map(lambda part: part[0], everything)

    def turn(k, so_far):
        return combine(so_far, jax.tree.map(lambda part: part[k], everything))

    return lax.fori_loop(1, lax.axis_size(axis), turn, leading)


def apply_rotary(values, positions, head_size):
    row_count, col_count = values.shape
    half_size = head_size // 2
    frequency = jnp.power(500000.0, -2.0 * jnp.arange(half_size, dtype=jnp.float32) / head_size)
    angles = positions.astype(jnp.float32)[:, None] * frequency[None, :]
    cosine_table = jnp.cos(angles)[:, None, :]
    sine_table = jnp.sin(angles)[:, None, :]
    shaped = values.reshape(row_count, col_count // head_size, 2, half_size)
    first_half = shaped[:, :, 0]
    second_half = shaped[:, :, 1]
    rotated = jnp.stack(
        [
            first_half * cosine_table - second_half * sine_table,
            second_half * cosine_table + first_half * sine_table,
        ],
        axis=2,
    )
    return rotated.reshape(row_count, col_count)


def combine_parts(first_part, second_part):
    peak_one, total_one, weighted_one = first_part
    peak_two, total_two, weighted_two = second_part
    peak_both = jnp.maximum(peak_one, peak_two)
    factor_one = jnp.exp(peak_one - peak_both)
    factor_two = jnp.exp(peak_two - peak_both)
    return (
        peak_both,
        total_one * factor_one + total_two * factor_two,
        weighted_one * factor_one[..., None] + weighted_two * factor_two[..., None],
    )


def finish_heads(peak_score, weight_total, weighted, score_new, value_rows):
    peak_final = jnp.maximum(peak_score, score_new)
    old_factor = jnp.exp(peak_score - peak_final)
    new_weight = jnp.exp(score_new - peak_final)
    weight_total = weight_total * old_factor + new_weight
    weighted = (
        weighted * old_factor[..., None]
        + new_weight.astype(jnp.bfloat16).astype(jnp.float32)[..., None] * value_rows
    )
    return weighted / weight_total[..., None]


def body(
    normed_hidden_input,
    beam_adapter_index,
    beam_cache_length,
    query_weight,
    keyvalue_weight,
    output_weight,
    lowrank_down_factors,
    lowrank_up_factors,
    paged_key_cache,
    paged_value_cache,
):
    beam_rows, width_part = normed_hidden_input.shape
    model_width = query_weight.shape[1]
    kv_width = keyvalue_weight.shape[1] // 2
    head_count = model_width // HEAD_DIM
    kv_heads = kv_width // HEAD_DIM
    group_size = head_count // kv_heads
    tensor_index = lax.axis_index("tensor")
    query_part = jnp.dot(normed_hidden_input, query_weight, preferred_element_type=jnp.float32)
    keyval_part = jnp.dot(normed_hidden_input, keyvalue_weight, preferred_element_type=jnp.float32)
    down_all, up_all = (
        lax.all_gather(lowrank_down_factors, "bank", axis=0, tiled=True),
        lax.all_gather(lowrank_up_factors, "bank", axis=0, tiled=True),
    )
    inner_part = jnp.einsum(
        "ci,cim->cm",
        normed_hidden_input,
        down_all[beam_adapter_index],
        preferred_element_type=jnp.float32,
    )
    inner_total = lax.psum(inner_part, "tensor").astype(jnp.bfloat16)
    lowrank_delta = jnp.einsum(
        "mc,mct->mt", inner_total, up_all[beam_adapter_index], preferred_element_type=jnp.float32
    )
    query_total, keyval = lax.psum((query_part, keyval_part), "tensor")
    delta_total = lax.all_gather(lowrank_delta, "tensor", axis=1, tiled=True)
    query_rotated = apply_rotary(query_total + delta_total, beam_cache_length, HEAD_DIM).astype(
        jnp.bfloat16
    )
    key_new = apply_rotary(keyval[:, :kv_width], beam_cache_length, HEAD_DIM).astype(jnp.bfloat16)
    value_new = keyval[:, kv_width:].astype(jnp.bfloat16)
    position_count = paged_key_cache.shape[1]
    query_heads = query_rotated.reshape(beam_rows, kv_heads, group_size, HEAD_DIM)
    key_block = paged_key_cache.reshape(beam_rows, position_count, kv_heads, HEAD_DIM)
    value_block = paged_value_cache.reshape(beam_rows, position_count, kv_heads, HEAD_DIM)
    score_scale = 1.0 / HEAD_DIM**0.5
    scores = (
        jnp.einsum("bkgh,bpkh->bkgp", query_heads, key_block, preferred_element_type=jnp.float32)
        * score_scale
    )
    position_ids = tensor_index * position_count + jnp.arange(position_count)
    live_mask = (position_ids[None, :] < beam_cache_length[:, None])[:, None, None, :]
    scores = jnp.where(live_mask, scores, -1e30)
    peak_score = jnp.max(scores, axis=-1)
    weights = jnp.where(live_mask, jnp.exp(scores - peak_score[..., None]), 0.0)
    weight_total = jnp.sum(weights, axis=-1)
    weighted = jnp.einsum(
        "bkgp,bpkh->bkgh",
        weights.astype(jnp.bfloat16),
        value_block,
        preferred_element_type=jnp.float32,
    )
    peak_score, weight_total, weighted = joined(
        (peak_score, weight_total, weighted), "tensor", combine_parts
    )
    score_new = (
        jnp.einsum(
            "bkgh,bkh->bkg",
            query_heads,
            key_new.reshape(beam_rows, kv_heads, HEAD_DIM),
            preferred_element_type=jnp.float32,
        )
        * score_scale
    )
    value_rows = value_new.reshape(beam_rows, kv_heads, HEAD_DIM).astype(jnp.float32)[:, :, None, :]
    attended = (
        finish_heads(peak_score, weight_total, weighted, score_new, value_rows)
        .reshape(beam_rows, model_width)
        .astype(jnp.bfloat16)
    )
    attended_cols = lax.dynamic_slice_in_dim(attended, tensor_index * width_part, width_part, 1)
    mixed_cols = lax.psum_scatter(
        lax.dot_general(
            output_weight,
            attended_cols,
            (((0,), (1,)), ((), ())),
            preferred_element_type=jnp.float32,
        ),
        "tensor",
        scatter_dimension=0,
        tiled=True,
    )
    return (normed_hidden_input.astype(jnp.float32) + mixed_cols.T).astype(jnp.bfloat16)


def solution(mesh):
    matched = mesh.shape["tensor"] == 8 and mesh.shape["bank"] == 2
    return jax.shard_map(
        matched_body if matched else body,
        mesh=mesh,
        in_specs=(
            P(("groups", "bank"), "tensor"),
            P(("groups", "bank")),
            P(("groups", "bank")),
            P("tensor", None),
            P("tensor", None),
            P("tensor", None),
            P("bank", "tensor", None),
            P("bank", None, "tensor"),
            P(("groups", "bank"), "tensor", None),
            P(("groups", "bank"), "tensor", None),
        ),
        out_specs=P(("groups", "bank"), "tensor"),
        check_vma=False,
    )
```

```python
import functools

import jax
import jax.numpy as jnp
from jax import lax
from jax.experimental import pallas as pl
from jax.experimental.pallas import tpu as pltpu
from jax.sharding import PartitionSpec as P

HEAD_DIM = 128
F32 = jnp.float32
BF16 = jnp.bfloat16
CHUNKS = 4
VMEM_LIMIT = 40 * 1024 * 1024


def whole():
    return pl.BlockSpec(memory_space=pltpu.VMEM)


def iota(shape, axis):
    return lax.broadcasted_iota(jnp.int32, shape, axis)


def params():
    return pltpu.CompilerParams(
        vmem_limit_bytes=VMEM_LIMIT, dimension_semantics=("arbitrary",)
    )


def chunked(weight, width, index):
    depth = weight.shape[0] // CHUNKS
    return [
        pl.BlockSpec((depth, width), lambda *a, c=c: (c, index(*a))) for c in range(CHUNKS)
    ]


def chunk_product(x, refs):
    depth = refs[0].shape[0]
    total = None
    for c, ref in enumerate(refs):
        part = jnp.dot(
            x[:, c * depth : (c + 1) * depth], ref[...], preferred_element_type=F32
        )
        total = part if total is None else total + part
    return total


def project_kernel(x_ref, *refs):
    *weights, out = refs
    x = x_ref[...]
    width = weights[0].shape[1]
    out[0, :, :width] = chunk_product(x, weights[:CHUNKS])
    out[0, :, width : width + HEAD_DIM] = chunk_product(x, weights[CHUNKS : 2 * CHUNKS])
    out[0, :, width + HEAD_DIM :] = chunk_product(x, weights[2 * CHUNKS :])


def project(x, wq, wkv, ranks):
    rows, depth = x.shape
    width = wq.shape[1] // ranks
    kv_heads = wkv.shape[1] // 2 // HEAD_DIM
    out = (ranks, rows, width + 2 * HEAD_DIM)
    return pl.pallas_call(
        project_kernel,
        grid=(ranks,),
        in_specs=[pl.BlockSpec((rows, depth), lambda s: (0, 0))]
        + chunked(wq, width, lambda s: s)
        + chunked(wkv, HEAD_DIM, lambda s: s)
        + chunked(wkv, HEAD_DIM, lambda s: kv_heads + s),
        out_specs=pl.BlockSpec((1,) + out[1:], lambda s: (s, 0, 0)),
        out_shape=jax.ShapeDtypeStruct(out, F32),
        compiler_params=params(),
        cost_estimate=pl.CostEstimate(
            flops=2 * rows * depth * (wq.shape[1] + wkv.shape[1]),
            bytes_accessed=2 * (wq.size + wkv.size),
            transcendentals=0,
        ),
        name="project",
    )(x, *[wq] * CHUNKS, *[wkv] * (2 * CHUNKS))


def adapter_column(index_ref, rows):
    row = iota((rows, HEAD_DIM), 0)
    column = jnp.zeros((rows, HEAD_DIM), jnp.int32)
    for r in range(rows):
        column = jnp.where(row == r, index_ref[r], column)
    return column


def down_kernel(index_ref, bank_ref, x_ref, other_ref, down_ref, out_ref):
    rows = 2 * x_ref.shape[0]
    rank = down_ref.shape[1]
    count = down_ref.shape[0]
    x = jnp.concatenate([x_ref[...].astype(F32), other_ref[...].astype(F32)], axis=0)
    flat = down_ref[...].reshape(count * rank, down_ref.shape[2])
    every = lax.dot_general(
        x.astype(BF16), flat, (((1,), (1,)), ((), ())), preferred_element_type=F32
    )
    column = adapter_column(index_ref, rows) - bank_ref[0] * count
    lane = iota((rows, HEAD_DIM), 1)
    per = HEAD_DIM // rank
    total = jnp.zeros((rows, HEAD_DIM), F32)
    for j in range(count // per):
        part = every[:, j * HEAD_DIM : (j + 1) * HEAD_DIM]
        total += jnp.where(lane // rank + j * per == column, part, 0.0)
    for slot in range(out_ref.shape[0]):
        out_ref[slot] = total


def down(index, bank, x, other, factors, ranks):
    rows = 2 * x.shape[0]
    smem = pl.BlockSpec(memory_space=pltpu.SMEM)
    return pl.pallas_call(
        down_kernel,
        in_specs=[smem, smem, whole(), whole(), whole()],
        out_specs=whole(),
        out_shape=jax.ShapeDtypeStruct((ranks, rows, HEAD_DIM), F32),
        compiler_params=pltpu.CompilerParams(vmem_limit_bytes=VMEM_LIMIT),
        cost_estimate=pl.CostEstimate(
            flops=2 * rows * factors.size, bytes_accessed=2 * factors.size, transcendentals=0
        ),
        name="down",
    )(index, bank, x, other, factors)


def up_kernel(index_ref, bank_ref, parts_ref, up_ref, own_ref, other_ref):
    rows = parts_ref.shape[1]
    count, rank, width = up_ref.shape
    total = jnp.sum(parts_ref[...], axis=0).astype(BF16).astype(F32)
    column = adapter_column(index_ref, rows) - bank_ref[0] * count
    lane = iota((rows, HEAD_DIM), 1)
    per = HEAD_DIM // rank
    spread = jnp.concatenate(
        [
            jnp.where(lane // rank + j * per == column, total, 0.0)
            for j in range(count // per)
        ],
        axis=1,
    ).astype(BF16)
    delta = jnp.dot(
        spread, up_ref[...].reshape(count * rank, width), preferred_element_type=F32
    )
    own_ref[...] = delta[: rows // 2]
    other_ref[...] = delta[rows // 2 :]


def up(index, bank, parts, factors):
    rows = parts.shape[1]
    width = factors.shape[2]
    smem = pl.BlockSpec(memory_space=pltpu.SMEM)
    return pl.pallas_call(
        up_kernel,
        in_specs=[smem, smem, whole(), whole()],
        out_specs=[whole()] * 2,
        out_shape=[jax.ShapeDtypeStruct((rows // 2, width), F32)] * 2,
        compiler_params=pltpu.CompilerParams(vmem_limit_bytes=VMEM_LIMIT),
        cost_estimate=pl.CostEstimate(
            flops=2 * rows * factors.size, bytes_accessed=2 * factors.size, transcendentals=0
        ),
        name="up",
    )(index, bank, parts, factors)


def rotate(v, cosine, sine):
    return v * cosine + pltpu.roll(v, HEAD_DIM // 2, 1) * sine


def rotate_kernel(
    parts_ref, own_ref, other_ref, cos_ref, sin_ref, q_ref, k_ref, v_ref, rows_ref
):
    total = jnp.sum(parts_ref[...], axis=0)
    width = own_ref.shape[1]
    query = total[:, :width] + (own_ref[...] + other_ref[...])
    cosine, sine = cos_ref[...], sin_ref[...]
    for g in range(width // HEAD_DIM):
        rows_ref[:, g, :] = rotate(query[:, g * HEAD_DIM : (g + 1) * HEAD_DIM], cosine, sine)
    rows = rows_ref[...].reshape(q_ref.shape[1:]).astype(BF16)
    for slot in range(q_ref.shape[0]):
        q_ref[slot] = rows
    k_ref[...] = (
        rotate(total[:, width : width + HEAD_DIM], cosine, sine).astype(BF16).astype(F32)
    )
    v_ref[...] = total[:, width + HEAD_DIM :].astype(BF16).astype(F32)


def rotated(parts, own, other, cosine, sine):
    rows, width = own.shape
    heads = width // HEAD_DIM
    small = jax.ShapeDtypeStruct((rows, HEAD_DIM), F32)
    return pl.pallas_call(
        rotate_kernel,
        in_specs=[whole()] * 5,
        out_specs=[whole()] * 3,
        out_shape=[
            jax.ShapeDtypeStruct((parts.shape[0], rows * heads, HEAD_DIM), BF16),
            small,
            small,
        ],
        scratch_shapes=[pltpu.VMEM((rows, heads, HEAD_DIM), F32)],
        compiler_params=pltpu.CompilerParams(vmem_limit_bytes=VMEM_LIMIT),
        name="rotate",
    )(parts, own, other, cosine, sine)


def attend_kernel(place, length, q_ref, k_ref, v_ref, out_ref, q_rows, o_rows, stats):
    beam = pl.program_id(0)
    beams = pl.num_programs(0)
    ranks = q_ref.shape[0]
    group = q_rows.shape[1] // stats.shape[0]
    heads = ranks * group
    positions = k_ref.shape[1]

    @pl.when(beam == 0)
    def _():
        q_rows[...] = q_ref[...].astype(F32)

    first = pl.multiple_of(beam * group, group)
    q = q_rows[:, pl.ds(first, group), :].reshape(heads, HEAD_DIM)
    key_head = iota((heads, HEAD_DIM), 0) // group
    wide = jnp.concatenate(
        [jnp.where(key_head == c, q, 0.0) for c in range(ranks)], axis=1
    ).astype(BF16)
    scores = lax.dot_general(
        wide, k_ref[0], (((1,), (1,)), ((), ())), preferred_element_type=F32
    ) * (1.0 / HEAD_DIM**0.5)
    live = place[0] * positions + iota((heads, positions), 1) < length[beam]
    scores = jnp.where(live, scores, -1e30)
    peak = jnp.max(scores, axis=1, keepdims=True)
    weights = jnp.where(live, jnp.exp(scores - peak), 0.0)
    total = jnp.sum(weights, axis=1, keepdims=True)
    product = jnp.dot(weights.astype(BF16), v_ref[0], preferred_element_type=F32)
    for c in range(ranks):
        o_rows[c, pl.ds(first, group), :] = product[
            c * group : (c + 1) * group, c * HEAD_DIM : (c + 1) * HEAD_DIM
        ]
    row, lane = iota((heads, HEAD_DIM), 0), iota((heads, HEAD_DIM), 1)
    spread = jnp.where(row == lane, peak, 0.0) + jnp.where(row + heads == lane, total, 0.0)
    stats[pl.ds(beam, 1), :] = jnp.sum(spread, axis=0, keepdims=True)

    @pl.when(beam == beams - 1)
    def _():
        high = stats[...].astype(BF16).astype(F32)
        rest = stats[...] - high
        middle = rest.astype(BF16).astype(F32)
        low = rest - middle
        tail = jnp.concatenate([high, middle, low, jnp.zeros_like(low)], axis=0)
        for c in range(ranks):
            out_ref[c] = jnp.concatenate([o_rows[c], tail], axis=0).astype(BF16)


def attend(place, length, queries, keys, values):
    ranks, rows, _ = queries.shape
    beams, positions, width = keys.shape
    out = (ranks, rows + 4 * beams, HEAD_DIM)
    return pl.pallas_call(
        attend_kernel,
        grid_spec=pltpu.PrefetchScalarGridSpec(
            num_scalar_prefetch=2,
            grid=(beams,),
            in_specs=[pl.BlockSpec(queries.shape, lambda i, p, n: (0, 0, 0))]
            + [pl.BlockSpec((1, positions, width), lambda i, p, n: (i, 0, 0))] * 2,
            out_specs=pl.BlockSpec(out, lambda i, p, n: (0, 0, 0)),
            scratch_shapes=[
                pltpu.VMEM((ranks, rows, HEAD_DIM), F32),
                pltpu.VMEM((ranks, rows, HEAD_DIM), F32),
                pltpu.VMEM((beams, HEAD_DIM), F32),
            ],
        ),
        out_shape=jax.ShapeDtypeStruct(out, BF16),
        compiler_params=params(),
        cost_estimate=pl.CostEstimate(
            flops=4 * rows * ranks * positions * width,
            bytes_accessed=4 * keys.size,
            transcendentals=rows * ranks * positions,
        ),
        name="attend",
    )(place, length, queries, keys, values)


def output_kernel(place, parts_ref, q_ref, k_ref, v_ref, *refs):
    *weights, out, joined, attended = refs
    ranks = parts_ref.shape[0]
    beams, group, _ = joined.shape
    rows = beams * group

    def by_row(v):
        return jnp.broadcast_to(v[:, None, :], (beams, group, HEAD_DIM)).reshape(rows, HEAD_DIM)

    @pl.when(pl.program_id(0) == 0)
    def _():
        head = place[0] * group + iota((rows, HEAD_DIM), 0) % group
        lane = iota((rows, HEAD_DIM), 1)
        score = jnp.sum(
            q_ref[0].astype(F32) * by_row(k_ref[...]), axis=1, keepdims=True
        ) * (1.0 / HEAD_DIM**0.5)
        peaks, totals, weighted = [], [], []
        top = score
        for s in range(ranks):
            block = parts_ref[s].astype(F32)
            tail = by_row(
                block[rows : rows + beams]
                + block[rows + beams : rows + 2 * beams]
                + block[rows + 2 * beams : rows + 3 * beams]
            )
            peak = jnp.sum(jnp.where(lane == head, tail, 0.0), axis=1, keepdims=True)
            total = jnp.sum(
                jnp.where(lane == ranks * group + head, tail, 0.0), axis=1, keepdims=True
            )
            top = jnp.maximum(top, peak)
            peaks.append(peak)
            totals.append(total)
            weighted.append(block[:rows])
        new = jnp.exp(score - top)
        everything = new
        result = new.astype(BF16).astype(F32) * by_row(v_ref[...])
        for peak, total, block in zip(peaks, totals, weighted):
            factor = jnp.exp(peak - top)
            everything += total * factor
            result += block * factor
        joined[...] = (result / everything).reshape(joined.shape)
        for g in range(group):
            attended[:, g * HEAD_DIM : (g + 1) * HEAD_DIM] = joined[:, g, :].astype(BF16)

    out[0] = chunk_product(attended[...], weights).astype(BF16)


def output(place, parts, query, key_new, value_new, weight):
    ranks = parts.shape[0]
    beams = key_new.shape[0]
    depth = weight.shape[0]
    width = weight.shape[1] // ranks
    group = depth // HEAD_DIM
    return pl.pallas_call(
        output_kernel,
        grid_spec=pltpu.PrefetchScalarGridSpec(
            num_scalar_prefetch=1,
            grid=(ranks,),
            in_specs=[
                pl.BlockSpec(parts.shape, lambda s, p: (0, 0, 0)),
                pl.BlockSpec((1,) + query.shape[1:], lambda s, p: (0, 0, 0)),
                pl.BlockSpec(key_new.shape, lambda s, p: (0, 0)),
                pl.BlockSpec(value_new.shape, lambda s, p: (0, 0)),
            ]
            + chunked(weight, width, lambda s, p: s),
            out_specs=pl.BlockSpec((1, beams, width), lambda s, p: (s, 0, 0)),
            scratch_shapes=[
                pltpu.VMEM((beams, group, HEAD_DIM), F32),
                pltpu.VMEM((beams, depth), BF16),
            ],
        ),
        out_shape=jax.ShapeDtypeStruct((ranks, beams, width), BF16),
        compiler_params=params(),
        cost_estimate=pl.CostEstimate(
            flops=2 * beams * weight.size, bytes_accessed=2 * weight.size, transcendentals=0
        ),
        name="output",
    )(place, parts, query, key_new, value_new, *[weight] * CHUNKS)


def residual_kernel(x_ref, parts_ref, out_ref):
    total = jnp.sum(parts_ref[...].astype(F32), axis=0)
    out_ref[...] = (x_ref[...].astype(F32) + total).astype(BF16)


def residual(x, parts):
    return pl.pallas_call(
        residual_kernel,
        in_specs=[whole()] * 2,
        out_specs=whole(),
        out_shape=jax.ShapeDtypeStruct(x.shape, BF16),
        name="residual",
    )(x, parts)


def traded(blocks):
    return lax.all_to_all(blocks, "tensor", 0, 0, tiled=True)


def matched_body(
    normed_hidden_input,
    beam_adapter_index,
    beam_cache_length,
    query_weight,
    keyvalue_weight,
    output_weight,
    lowrank_down_factors,
    lowrank_up_factors,
    paged_key_cache,
    paged_value_cache,
):
    x = normed_hidden_input
    ranks = lax.axis_size("tensor")
    place = lax.axis_index("tensor").astype(jnp.int32).reshape(1)
    bank = lax.axis_index("bank").astype(jnp.int32).reshape(1)
    swap = [(0, 1), (1, 0)]
    x_other = lax.ppermute(x, "bank", swap)
    index = jnp.concatenate([beam_adapter_index, lax.ppermute(beam_adapter_index, "bank", swap)])
    half = HEAD_DIM // 2
    frequency = jnp.power(500000.0, -2.0 * jnp.arange(half, dtype=F32) / HEAD_DIM)
    angles = beam_cache_length.astype(F32)[:, None] * frequency[None, :]
    cosine = jnp.tile(jnp.cos(angles), (1, 2))
    sine = jnp.sin(angles)
    sine = jnp.concatenate([-sine, sine], axis=1)

    parts = traded(project(x, query_weight, keyvalue_weight, ranks))
    inner = down(index, bank, x, x_other, lowrank_down_factors.swapaxes(1, 2), ranks)
    delta_own, delta_sent = up(index, bank, traded(inner), lowrank_up_factors)
    delta_other = lax.ppermute(delta_sent, "bank", swap)
    query, key_new, value_new = rotated(parts, delta_own, delta_other, cosine, sine)
    partial = attend(place, beam_cache_length, traded(query), paged_key_cache, paged_value_cache)
    mixed = output(place, traded(partial), query, key_new, value_new, output_weight)
    return residual(x, traded(mixed))


def joined(x, axis, combine):
    everything = jax.tree.map(lambda part: lax.all_gather(part, axis), x)
    leading = jax.tree.map(lambda part: part[0], everything)

    def turn(k, so_far):
        return combine(so_far, jax.tree.map(lambda part: part[k], everything))

    return lax.fori_loop(1, lax.axis_size(axis), turn, leading)


def apply_rotary(values, positions, head_size):
    row_count, col_count = values.shape
    half_size = head_size // 2
    frequency = jnp.power(500000.0, -2.0 * jnp.arange(half_size, dtype=jnp.float32) / head_size)
    angles = positions.astype(jnp.float32)[:, None] * frequency[None, :]
    cosine_table = jnp.cos(angles)[:, None, :]
    sine_table = jnp.sin(angles)[:, None, :]
    shaped = values.reshape(row_count, col_count // head_size, 2, half_size)
    first_half = shaped[:, :, 0]
    second_half = shaped[:, :, 1]
    rotated = jnp.stack(
        [
            first_half * cosine_table - second_half * sine_table,
            second_half * cosine_table + first_half * sine_table,
        ],
        axis=2,
    )
    return rotated.reshape(row_count, col_count)


def combine_parts(first_part, second_part):
    peak_one, total_one, weighted_one = first_part
    peak_two, total_two, weighted_two = second_part
    peak_both = jnp.maximum(peak_one, peak_two)
    factor_one = jnp.exp(peak_one - peak_both)
    factor_two = jnp.exp(peak_two - peak_both)
    return (
        peak_both,
        total_one * factor_one + total_two * factor_two,
        weighted_one * factor_one[..., None] + weighted_two * factor_two[..., None],
    )


def finish_heads(peak_score, weight_total, weighted, score_new, value_rows):
    peak_final = jnp.maximum(peak_score, score_new)
    old_factor = jnp.exp(peak_score - peak_final)
    new_weight = jnp.exp(score_new - peak_final)
    weight_total = weight_total * old_factor + new_weight
    weighted = (
        weighted * old_factor[..., None]
        + new_weight.astype(jnp.bfloat16).astype(jnp.float32)[..., None] * value_rows
    )
    return weighted / weight_total[..., None]


def body(
    normed_hidden_input,
    beam_adapter_index,
    beam_cache_length,
    query_weight,
    keyvalue_weight,
    output_weight,
    lowrank_down_factors,
    lowrank_up_factors,
    paged_key_cache,
    paged_value_cache,
):
    beam_rows, width_part = normed_hidden_input.shape
    model_width = query_weight.shape[1]
    kv_width = keyvalue_weight.shape[1] // 2
    head_count = model_width // HEAD_DIM
    kv_heads = kv_width // HEAD_DIM
    group_size = head_count // kv_heads
    tensor_index = lax.axis_index("tensor")
    query_part = jnp.dot(normed_hidden_input, query_weight, preferred_element_type=jnp.float32)
    keyval_part = jnp.dot(normed_hidden_input, keyvalue_weight, preferred_element_type=jnp.float32)
    down_all, up_all = (
        lax.all_gather(lowrank_down_factors, "bank", axis=0, tiled=True),
        lax.all_gather(lowrank_up_factors, "bank", axis=0, tiled=True),
    )
    inner_part = jnp.einsum(
        "ci,cim->cm",
        normed_hidden_input,
        down_all[beam_adapter_index],
        preferred_element_type=jnp.float32,
    )
    inner_total = lax.psum(inner_part, "tensor").astype(jnp.bfloat16)
    lowrank_delta = jnp.einsum(
        "mc,mct->mt", inner_total, up_all[beam_adapter_index], preferred_element_type=jnp.float32
    )
    query_total, keyval = lax.psum((query_part, keyval_part), "tensor")
    delta_total = lax.all_gather(lowrank_delta, "tensor", axis=1, tiled=True)
    query_rotated = apply_rotary(query_total + delta_total, beam_cache_length, HEAD_DIM).astype(
        jnp.bfloat16
    )
    key_new = apply_rotary(keyval[:, :kv_width], beam_cache_length, HEAD_DIM).astype(jnp.bfloat16)
    value_new = keyval[:, kv_width:].astype(jnp.bfloat16)
    position_count = paged_key_cache.shape[1]
    query_heads = query_rotated.reshape(beam_rows, kv_heads, group_size, HEAD_DIM)
    key_block = paged_key_cache.reshape(beam_rows, position_count, kv_heads, HEAD_DIM)
    value_block = paged_value_cache.reshape(beam_rows, position_count, kv_heads, HEAD_DIM)
    score_scale = 1.0 / HEAD_DIM**0.5
    scores = (
        jnp.einsum("bkgh,bpkh->bkgp", query_heads, key_block, preferred_element_type=jnp.float32)
        * score_scale
    )
    position_ids = tensor_index * position_count + jnp.arange(position_count)
    live_mask = (position_ids[None, :] < beam_cache_length[:, None])[:, None, None, :]
    scores = jnp.where(live_mask, scores, -1e30)
    peak_score = jnp.max(scores, axis=-1)
    weights = jnp.where(live_mask, jnp.exp(scores - peak_score[..., None]), 0.0)
    weight_total = jnp.sum(weights, axis=-1)
    weighted = jnp.einsum(
        "bkgp,bpkh->bkgh",
        weights.astype(jnp.bfloat16),
        value_block,
        preferred_element_type=jnp.float32,
    )
    peak_score, weight_total, weighted = joined(
        (peak_score, weight_total, weighted), "tensor", combine_parts
    )
    score_new = (
        jnp.einsum(
            "bkgh,bkh->bkg",
            query_heads,
            key_new.reshape(beam_rows, kv_heads, HEAD_DIM),
            preferred_element_type=jnp.float32,
        )
        * score_scale
    )
    value_rows = value_new.reshape(beam_rows, kv_heads, HEAD_DIM).astype(jnp.float32)[:, :, None, :]
    attended = (
        finish_heads(peak_score, weight_total, weighted, score_new, value_rows)
        .reshape(beam_rows, model_width)
        .astype(jnp.bfloat16)
    )
    attended_cols = lax.dynamic_slice_in_dim(attended, tensor_index * width_part, width_part, 1)
    mixed_cols = lax.psum_scatter(
        lax.dot_general(
            output_weight,
            attended_cols,
            (((0,), (1,)), ((), ())),
            preferred_element_type=jnp.float32,
        ),
        "tensor",
        scatter_dimension=0,
        tiled=True,
    )
    return (normed_hidden_input.astype(jnp.float32) + mixed_cols.T).astype(jnp.bfloat16)


def solution(mesh):
    matched = mesh.shape["tensor"] == 8 and mesh.shape["bank"] == 2
    return jax.shard_map(
        matched_body if matched else body,
        mesh=mesh,
        in_specs=(
            P(("groups", "bank"), "tensor"),
            P(("groups", "bank")),
            P(("groups", "bank")),
            P("tensor", None),
            P("tensor", None),
            P("tensor", None),
            P("bank", "tensor", None),
            P("bank", None, "tensor"),
            P(("groups", "bank"), "tensor", None),
            P(("groups", "bank"), "tensor", None),
        ),
        out_specs=P(("groups", "bank"), "tensor"),
        check_vma=False,
    )
```

```python
import jax
import jax.numpy as jnp
from jax import lax
from jax.experimental import pallas as pl
from jax.experimental.pallas import tpu as pltpu
from jax.sharding import PartitionSpec as P

HEAD_DIM = 128
F32 = jnp.float32
BF16 = jnp.bfloat16
CHUNKS = 4
VMEM_LIMIT = 40 * 1024 * 1024


def whole():
    return pl.BlockSpec(memory_space=pltpu.VMEM)


def scalar():
    return pl.BlockSpec(memory_space=pltpu.SMEM)


def in_hbm(array):
    return pltpu.with_memory_space_constraint(array, pltpu.HBM)


def shape(*dims, dtype=F32):
    return jax.ShapeDtypeStruct(dims, dtype)


def iota(dims, axis):
    return lax.broadcasted_iota(jnp.int32, dims, axis)


def params(**more):
    return pltpu.CompilerParams(vmem_limit_bytes=VMEM_LIMIT, **more)


def both_banks(own_ref, other_ref, rows_ref):
    rows = jnp.concatenate([own_ref[...].astype(F32), other_ref[...].astype(F32)], axis=0)
    rows_ref[...] = rows.astype(BF16)


def chunked(weight, width, index):
    depth = weight.shape[0] // CHUNKS
    return [
        pl.BlockSpec((depth, width), lambda *a, c=c: (c, index(*a))) for c in range(CHUNKS)
    ]


def chunk_product(x, refs):
    depth = refs[0].shape[0]
    total = None
    for c, ref in enumerate(refs):
        part = jnp.dot(
            x[:, c * depth : (c + 1) * depth], ref[...], preferred_element_type=F32
        )
        total = part if total is None else total + part
    return total


def adapter_column(refs, bank, count):
    rows = len(refs) * refs[0].shape[0]
    row = iota((rows, HEAD_DIM), 0)
    column = jnp.zeros((rows, HEAD_DIM), jnp.int32)
    for r in range(rows):
        ref = refs[r // refs[0].shape[0]]
        column = jnp.where(row == r, ref[r % ref.shape[0]], column)
    return column - bank * count


def project_kernel(first, place, bank, *refs):
    if first:
        (own_index, other_index, x_ref, other_ref), refs = refs[:4], refs[4:]
        *weights, kv_ref, down_ref, out, inner, rows = refs
    else:
        (x_ref, other_ref), refs = refs[:2], refs[2:]
        *weights, kv_ref, inner, out, rows = refs
    width = weights[0].shape[1]

    @pl.when(pl.program_id(0) == 0)
    def _():
        both_banks(x_ref, other_ref, rows)
        if first:
            count, rank, depth = down_ref.shape
            every = lax.dot_general(
                rows[...],
                down_ref[...].reshape(count * rank, depth),
                (((1,), (1,)), ((), ())),
                preferred_element_type=F32,
            )
            column = adapter_column((own_index, other_index), bank[0], count)
            lane = iota(column.shape, 1)
            per = HEAD_DIM // rank
            total = jnp.zeros(column.shape, F32)
            for j in range(count // per):
                part = every[:, j * HEAD_DIM : (j + 1) * HEAD_DIM]
                total += jnp.where(lane // rank + j * per == column, part, 0.0)
            inner[...] = total

    x = rows[...]
    out[0, :, :width] = chunk_product(x, weights)
    out[0, :, width : width + HEAD_DIM] = jnp.dot(x, kv_ref[...], preferred_element_type=F32)
    out[0, :, width + HEAD_DIM :] = inner[...]


def project(place, bank, x, other, wq, wkv, ranks, down=None, index=None, inner=None):
    rows, depth = x.shape
    first = inner is None
    width = wq.shape[1] // ranks // 2
    out = (ranks // 2, 2 * rows, width + 2 * HEAD_DIM)
    rank_of = lambda s, p: (2 * s + (1 if first else 0)) ^ p[0]
    same = lambda a: pl.BlockSpec(a.shape, lambda s, p, b: (0,) * a.ndim)
    out_specs = [pl.BlockSpec((1,) + out[1:], lambda s, p, b: (s, 0, 0))]
    out_shape = [shape(*out)]
    small = jax.ShapeDtypeStruct((2 * rows, HEAD_DIM), F32)
    if first:
        out_specs.append(same(small))
        out_shape.append(small)
    return pl.pallas_call(
        lambda *refs: project_kernel(first, *refs),
        grid_spec=pltpu.PrefetchScalarGridSpec(
            num_scalar_prefetch=2,
            grid=(ranks // 2,),
            in_specs=([scalar(), scalar()] if first else [])
            + [same(x), same(other)]
            + chunked(wq, width, lambda s, p, b: 2 * rank_of(s, p) + b[0])
            + [pl.BlockSpec((depth, HEAD_DIM), lambda s, p, b: (0, rank_of(s, p) + ranks * b[0]))]
            + ([same(down)] if first else [same(inner)]),
            out_specs=out_specs,
            scratch_shapes=[pltpu.VMEM((2 * rows, depth), BF16)],
        ),
        out_shape=out_shape,
        compiler_params=params(dimension_semantics=("arbitrary",)),
        cost_estimate=pl.CostEstimate(
            flops=rows * depth * (wq.shape[1] + wkv.shape[1]),
            bytes_accessed=(wq.size + wkv.size) // 2,
            transcendentals=0,
        ),
        name="project_sent" if first else "project_kept",
    )(
        place,
        bank,
        *(index if first else ()),
        x,
        other,
        *[wq] * CHUNKS,
        wkv,
        down if first else inner,
    )


def halve_kernel(kept_ref, came_ref, sent_out, kept_out):
    for i in range(kept_out.shape[0]):
        for out, j in ((kept_out, 2 * i), (sent_out, 2 * i + 1)):
            out[i] = (kept_ref[j].astype(F32) + came_ref[j].astype(F32)).astype(out.dtype)


def halve(kept, came):
    half = jax.ShapeDtypeStruct((kept.shape[0] // 2,) + kept.shape[1:], kept.dtype)
    return pl.pallas_call(
        halve_kernel,
        in_specs=[whole()] * 2,
        out_specs=[whole()] * 2,
        out_shape=[half, half],
        compiler_params=params(),
        name="halve",
    )(kept, came)


def correct_kernel(bank, own_index, other_index, kept_ref, came_ref, up_ref, own_out, other_out):
    total = kept_ref[0] + came_ref[0]
    count, rank, width = up_ref.shape
    half = width // 2
    inner = total[:, half + HEAD_DIM :].astype(BF16).astype(F32)
    column = adapter_column((own_index, other_index), bank[0], count)
    lane = iota(column.shape, 1)
    per = HEAD_DIM // rank
    spread = jnp.concatenate(
        [
            jnp.where(lane // rank + j * per == column, inner, 0.0)
            for j in range(count // per)
        ],
        axis=1,
    ).astype(BF16)
    delta = jnp.dot(
        spread, up_ref[...].reshape(count * rank, width), preferred_element_type=F32
    )
    rows = own_out.shape[0]
    for side in range(2):
        columns = slice(side * half, (side + 1) * half)
        part = delta[:, columns] + jnp.where(bank[0] == side, total[:, :half], 0.0)
        own_out[:, columns] = part[:rows]
        other_out[:, columns] = part[rows:]
    own_out[:, width:] = total[:rows, half : half + HEAD_DIM]
    other_out[:, width:] = total[rows:, half : half + HEAD_DIM]


def correct(bank, index, kept, came, up):
    rows = kept.shape[1]
    out = shape(rows // 2, up.shape[2] + HEAD_DIM)
    return pl.pallas_call(
        correct_kernel,
        in_specs=[scalar()] * 3 + [whole()] * 3,
        out_specs=[whole()] * 2,
        out_shape=[out, out],
        compiler_params=params(),
        cost_estimate=pl.CostEstimate(
            flops=2 * rows * up.size, bytes_accessed=2 * up.size, transcendentals=0
        ),
        name="correct",
    )(bank, *index, kept, came, up)


def rotate(v, cosine, sine):
    return v * cosine + pltpu.roll(v, HEAD_DIM // 2, 1) * sine


def rotate_kernel(bank, own_ref, came_ref, cos_ref, sin_ref, q_ref, k_ref, v_ref, rows_ref):
    width = own_ref.shape[1] - HEAD_DIM
    cosine, sine = cos_ref[...], sin_ref[...]
    for g in range(width // HEAD_DIM):
        columns = slice(g * HEAD_DIM, (g + 1) * HEAD_DIM)
        rows_ref[:, g, :] = rotate(own_ref[:, columns] + came_ref[:, columns], cosine, sine)
    q_ref[0] = rows_ref[...].reshape(q_ref.shape[1:]).astype(BF16)
    own, came = own_ref[:, width:], came_ref[:, width:]
    key = jnp.where(bank[0] == 0, own, came)
    value = jnp.where(bank[0] == 0, came, own)
    k_ref[...] = rotate(key, cosine, sine).astype(BF16).astype(F32)
    v_ref[...] = value.astype(BF16).astype(F32)


def rotated(bank, own, came, cosine, sine):
    rows = own.shape[0]
    heads = own.shape[1] // HEAD_DIM - 1
    return pl.pallas_call(
        rotate_kernel,
        in_specs=[scalar()] + [whole()] * 4,
        out_specs=[whole()] * 3,
        out_shape=[
            shape(1, rows * heads, HEAD_DIM, dtype=BF16),
            shape(rows, HEAD_DIM),
            shape(rows, HEAD_DIM),
        ],
        scratch_shapes=[pltpu.VMEM((rows, heads, HEAD_DIM), F32)],
        compiler_params=params(),
        name="rotate",
    )(bank, own, came, cosine, sine)


def join_kernel(first_ref, second_ref, out_ref):
    half = first_ref.shape[0]
    out_ref[:half] = first_ref[...]
    out_ref[half:] = second_ref[...]


def join(first, second):
    return pl.pallas_call(
        join_kernel,
        in_specs=[whole()] * 2,
        out_specs=whole(),
        out_shape=shape(2 * first.shape[0], *first.shape[1:], dtype=first.dtype),
        compiler_params=params(),
        name="join",
    )(first, second)


def gathered_slots(ranks):
    slots, bit = [0], ranks // 2
    while bit:
        slots += [slot ^ bit for slot in slots]
        bit //= 2
    return slots


def attend_kernel(place, length, near_ref, far_ref, k_ref, v_ref, out_ref, q_rows, o_rows, stats):
    beam = pl.program_id(0)
    beams = pl.num_programs(0)
    ranks = 2 * near_ref.shape[0]
    group = q_rows.shape[1] // stats.shape[0]
    heads = ranks * group
    positions = k_ref.shape[1]

    @pl.when(beam == 0)
    def _():
        q_rows[: ranks // 2] = near_ref[...].astype(F32)
        q_rows[ranks // 2 :] = far_ref[...].astype(F32)

    first = pl.multiple_of(beam * group, group)
    q = q_rows[:, pl.ds(first, group), :].reshape(heads, HEAD_DIM)
    head_of = [place[0] ^ slot for slot in gathered_slots(ranks)]
    row = iota((heads, HEAD_DIM), 0)
    key_head = jnp.zeros((heads, HEAD_DIM), jnp.int32)
    for i, head in enumerate(head_of):
        key_head = jnp.where(row // group == i, head, key_head)
    wide = jnp.concatenate(
        [jnp.where(key_head == c, q, 0.0) for c in range(ranks)], axis=1
    ).astype(BF16)
    scores = lax.dot_general(
        wide, k_ref[0], (((1,), (1,)), ((), ())), preferred_element_type=F32
    ) * (1.0 / HEAD_DIM**0.5)
    live = place[0] * positions + iota((heads, positions), 1) < length[beam]
    scores = jnp.where(live, scores, -1e30)
    peak = jnp.max(scores, axis=1, keepdims=True)
    weights = jnp.where(live, jnp.exp(scores - peak), 0.0)
    total = jnp.sum(weights, axis=1, keepdims=True)
    product = jnp.dot(weights.astype(BF16), v_ref[0], preferred_element_type=F32)
    own = jnp.zeros((heads, HEAD_DIM), F32)
    for c in range(ranks):
        own = jnp.where(key_head == c, product[:, c * HEAD_DIM : (c + 1) * HEAD_DIM], own)
    for i, head in enumerate(head_of):
        o_rows[head, pl.ds(first, group), :] = own[i * group : (i + 1) * group]
    lane = iota((heads, HEAD_DIM), 1)
    head = key_head * group + row % group
    spread = jnp.where(head == lane, peak, 0.0) + jnp.where(head + heads == lane, total, 0.0)
    stats[pl.ds(beam, 1), :] = jnp.sum(spread, axis=0, keepdims=True)

    @pl.when(beam == beams - 1)
    def _():
        high = stats[...].astype(BF16).astype(F32)
        rest = stats[...] - high
        middle = rest.astype(BF16).astype(F32)
        low = rest - middle
        tail = jnp.concatenate([high, middle, low, jnp.zeros_like(low)], axis=0)
        for c in range(ranks):
            out_ref[c] = jnp.concatenate([o_rows[c], tail], axis=0).astype(BF16)


def attend(place, length, near, far, keys, values):
    ranks, rows = 2 * near.shape[0], near.shape[1]
    beams, positions, width = keys.shape
    out = (ranks, rows + 4 * beams, HEAD_DIM)
    return pl.pallas_call(
        attend_kernel,
        grid_spec=pltpu.PrefetchScalarGridSpec(
            num_scalar_prefetch=2,
            grid=(beams,),
            in_specs=[pl.BlockSpec(near.shape, lambda i, p, n: (0, 0, 0))] * 2
            + [pl.BlockSpec((1, positions, width), lambda i, p, n: (i, 0, 0))] * 2,
            out_specs=pl.BlockSpec(out, lambda i, p, n: (0, 0, 0)),
            scratch_shapes=[
                pltpu.VMEM((ranks, rows, HEAD_DIM), F32),
                pltpu.VMEM((ranks, rows, HEAD_DIM), F32),
                pltpu.VMEM((beams, HEAD_DIM), F32),
            ],
        ),
        out_shape=jax.ShapeDtypeStruct(out, BF16),
        compiler_params=params(dimension_semantics=("arbitrary",)),
        cost_estimate=pl.CostEstimate(
            flops=4 * rows * ranks * positions * width,
            bytes_accessed=4 * keys.size,
            transcendentals=rows * ranks * positions,
        ),
        name="attend",
    )(place, length, near, far, keys, values)


def combine_kernel(place, parts_ref, q_ref, k_ref, v_ref, out_ref, joined):
    ranks = parts_ref.shape[0]
    beams, group, _ = joined.shape
    rows = beams * group

    def by_row(v):
        return jnp.broadcast_to(v[:, None, :], (beams, group, HEAD_DIM)).reshape(rows, HEAD_DIM)

    head = place[0] * group + iota((rows, HEAD_DIM), 0) % group
    lane = iota((rows, HEAD_DIM), 1)
    score = jnp.sum(q_ref[0].astype(F32) * by_row(k_ref[...]), axis=1, keepdims=True) * (
        1.0 / HEAD_DIM**0.5
    )
    peaks, totals, weighted = [], [], []
    top = score
    for s in range(ranks):
        block = parts_ref[s].astype(F32)
        tail = by_row(
            block[rows : rows + beams]
            + block[rows + beams : rows + 2 * beams]
            + block[rows + 2 * beams : rows + 3 * beams]
        )
        peak = jnp.sum(jnp.where(lane == head, tail, 0.0), axis=1, keepdims=True)
        total = jnp.sum(
            jnp.where(lane == ranks * group + head, tail, 0.0), axis=1, keepdims=True
        )
        top = jnp.maximum(top, peak)
        peaks.append(peak)
        totals.append(total)
        weighted.append(block[:rows])
    new = jnp.exp(score - top)
    everything = new
    result = new.astype(BF16).astype(F32) * by_row(v_ref[...])
    for peak, total, block in zip(peaks, totals, weighted):
        factor = jnp.exp(peak - top)
        everything += total * factor
        result += block * factor
    joined[...] = (result / everything).reshape(joined.shape)
    for g in range(group):
        out_ref[:, g * HEAD_DIM : (g + 1) * HEAD_DIM] = joined[:, g, :].astype(BF16)


def combine(place, parts, query, key_new, value_new):
    beams = key_new.shape[0]
    group = query.shape[1] // beams
    return pl.pallas_call(
        combine_kernel,
        in_specs=[scalar()] + [whole()] * 4,
        out_specs=whole(),
        out_shape=shape(beams, group * HEAD_DIM, dtype=BF16),
        scratch_shapes=[pltpu.VMEM((beams, group, HEAD_DIM), F32)],
        compiler_params=params(),
        name="combine",
    )(place, parts, query, key_new, value_new)


def output_kernel(place, bank, own_ref, other_ref, *refs):
    *weights, out, rows = refs

    @pl.when(pl.program_id(0) == 0)
    def _():
        both_banks(own_ref, other_ref, rows)

    out[0] = chunk_product(rows[...], weights).astype(BF16)


def output(place, bank, own, other, weight, ranks, parity):
    beams, depth = own.shape
    width = weight.shape[1] // ranks // 2
    out = (ranks // 2, 2 * beams, width)
    column = lambda s, p, b: 2 * ((2 * s + parity) ^ p[0]) + b[0]
    return pl.pallas_call(
        output_kernel,
        grid_spec=pltpu.PrefetchScalarGridSpec(
            num_scalar_prefetch=2,
            grid=(ranks // 2,),
            in_specs=[pl.BlockSpec(own.shape, lambda s, p, b: (0, 0))] * 2
            + chunked(weight, width, column),
            out_specs=pl.BlockSpec((1,) + out[1:], lambda s, p, b: (s, 0, 0)),
            scratch_shapes=[pltpu.VMEM((2 * beams, depth), BF16)],
        ),
        out_shape=shape(*out, dtype=BF16),
        compiler_params=params(dimension_semantics=("arbitrary",)),
        cost_estimate=pl.CostEstimate(
            flops=beams * weight.size, bytes_accessed=weight.size // 2, transcendentals=0
        ),
        name="output_sent" if parity else "output_kept",
    )(place, bank, own, other, *[weight] * CHUNKS)


def part_kernel(kept_ref, came_ref, own_out, other_out):
    total = kept_ref[0].astype(F32) + came_ref[0].astype(F32)
    rows = own_out.shape[0]
    own_out[...] = total[:rows]
    other_out[...] = total[rows:].astype(BF16)


def part(kept, came):
    _, rows, width = kept.shape
    return pl.pallas_call(
        part_kernel,
        in_specs=[whole()] * 2,
        out_specs=[whole()] * 2,
        out_shape=[shape(rows // 2, width), shape(rows // 2, width, dtype=BF16)],
        compiler_params=params(),
        name="part",
    )(kept, came)


def residual_kernel(bank, x_ref, own_ref, came_ref, out_ref):
    half = own_ref.shape[1]
    own, came = own_ref[...], came_ref[...].astype(F32)
    for side in range(2):
        columns = slice(side * half, (side + 1) * half)
        total = jnp.where(bank[0] == side, own, came)
        out_ref[:, columns] = (x_ref[:, columns].astype(F32) + total).astype(BF16)


def residual(bank, x, own, came):
    return pl.pallas_call(
        residual_kernel,
        in_specs=[scalar()] + [whole()] * 3,
        out_specs=whole(),
        out_shape=jax.ShapeDtypeStruct(x.shape, BF16),
        compiler_params=params(),
        name="residual",
    )(bank, x, own, came)


def swapped(x):
    return lax.ppermute(x, "bank", [(0, 1), (1, 0)])


def hop(x, bit):
    ranks = lax.axis_size("tensor")
    return lax.ppermute(x, "tensor", [(i, i ^ bit) for i in range(ranks)])


def matched_body(
    normed_hidden_input,
    beam_adapter_index,
    beam_cache_length,
    query_weight,
    keyvalue_weight,
    output_weight,
    lowrank_down_factors,
    lowrank_up_factors,
    paged_key_cache,
    paged_value_cache,
):
    x = normed_hidden_input
    ranks = lax.axis_size("tensor")
    place = lax.axis_index("tensor").astype(jnp.int32).reshape(1)
    bank = lax.axis_index("bank").astype(jnp.int32).reshape(1)
    index = (beam_adapter_index, swapped(beam_adapter_index))
    x_other = swapped(x)
    half = HEAD_DIM // 2
    frequency = jnp.power(500000.0, -2.0 * jnp.arange(half, dtype=F32) / HEAD_DIM)
    angles = beam_cache_length.astype(F32)[:, None] * frequency[None, :]
    cosine = jnp.tile(jnp.cos(angles), (1, 2))
    sine = jnp.sin(angles)
    sine = jnp.concatenate([-sine, sine], axis=1)

    weights = in_hbm(query_weight), in_hbm(keyvalue_weight)
    sent, inner = project(
        place,
        bank,
        x,
        x_other,
        *weights,
        ranks,
        down=in_hbm(lowrank_down_factors.swapaxes(1, 2)),
        index=index,
    )
    came = hop(sent, 1)
    (kept,) = project(place, bank, x, x_other, *weights, ranks, inner=inner)
    sent, kept = halve(kept, came)
    sent, kept = halve(kept, hop(sent, 2))
    own, other = correct(bank, index, kept, hop(sent, 4), lowrank_up_factors)
    query, key_new, value_new = rotated(bank, own, swapped(other), cosine, sine)

    near = join(query, hop(query, 4))
    near = join(near, hop(near, 2))
    partial = attend(
        place,
        beam_cache_length,
        near,
        hop(near, 1),
        in_hbm(paged_key_cache),
        in_hbm(paged_value_cache),
    )
    parts = lax.all_to_all(partial, "tensor", 0, 0, tiled=True)
    attended = combine(place, parts, query, key_new, value_new)
    attended_other = swapped(attended)

    weight = in_hbm(output_weight)
    came = hop(output(place, bank, attended, attended_other, weight, ranks, 1), 1)
    kept = output(place, bank, attended, attended_other, weight, ranks, 0)
    sent, kept = halve(kept, came)
    sent, kept = halve(kept, hop(sent, 2))
    own, other = part(kept, hop(sent, 4))
    return residual(bank, x, own, swapped(other))


def joined(x, axis, combine):
    everything = jax.tree.map(lambda part: lax.all_gather(part, axis), x)
    leading = jax.tree.map(lambda part: part[0], everything)

    def turn(k, so_far):
        return combine(so_far, jax.tree.map(lambda part: part[k], everything))

    return lax.fori_loop(1, lax.axis_size(axis), turn, leading)


def apply_rotary(values, positions, head_size):
    row_count, col_count = values.shape
    half_size = head_size // 2
    frequency = jnp.power(500000.0, -2.0 * jnp.arange(half_size, dtype=jnp.float32) / head_size)
    angles = positions.astype(jnp.float32)[:, None] * frequency[None, :]
    cosine_table = jnp.cos(angles)[:, None, :]
    sine_table = jnp.sin(angles)[:, None, :]
    shaped = values.reshape(row_count, col_count // head_size, 2, half_size)
    first_half = shaped[:, :, 0]
    second_half = shaped[:, :, 1]
    rotated = jnp.stack(
        [
            first_half * cosine_table - second_half * sine_table,
            second_half * cosine_table + first_half * sine_table,
        ],
        axis=2,
    )
    return rotated.reshape(row_count, col_count)


def combine_parts(first_part, second_part):
    peak_one, total_one, weighted_one = first_part
    peak_two, total_two, weighted_two = second_part
    peak_both = jnp.maximum(peak_one, peak_two)
    factor_one = jnp.exp(peak_one - peak_both)
    factor_two = jnp.exp(peak_two - peak_both)
    return (
        peak_both,
        total_one * factor_one + total_two * factor_two,
        weighted_one * factor_one[..., None] + weighted_two * factor_two[..., None],
    )


def finish_heads(peak_score, weight_total, weighted, score_new, value_rows):
    peak_final = jnp.maximum(peak_score, score_new)
    old_factor = jnp.exp(peak_score - peak_final)
    new_weight = jnp.exp(score_new - peak_final)
    weight_total = weight_total * old_factor + new_weight
    weighted = (
        weighted * old_factor[..., None]
        + new_weight.astype(jnp.bfloat16).astype(jnp.float32)[..., None] * value_rows
    )
    return weighted / weight_total[..., None]


def body(
    normed_hidden_input,
    beam_adapter_index,
    beam_cache_length,
    query_weight,
    keyvalue_weight,
    output_weight,
    lowrank_down_factors,
    lowrank_up_factors,
    paged_key_cache,
    paged_value_cache,
):
    beam_rows, width_part = normed_hidden_input.shape
    model_width = query_weight.shape[1]
    kv_width = keyvalue_weight.shape[1] // 2
    head_count = model_width // HEAD_DIM
    kv_heads = kv_width // HEAD_DIM
    group_size = head_count // kv_heads
    tensor_index = lax.axis_index("tensor")
    query_part = jnp.dot(normed_hidden_input, query_weight, preferred_element_type=jnp.float32)
    keyval_part = jnp.dot(normed_hidden_input, keyvalue_weight, preferred_element_type=jnp.float32)
    down_all, up_all = (
        lax.all_gather(lowrank_down_factors, "bank", axis=0, tiled=True),
        lax.all_gather(lowrank_up_factors, "bank", axis=0, tiled=True),
    )
    inner_part = jnp.einsum(
        "ci,cim->cm",
        normed_hidden_input,
        down_all[beam_adapter_index],
        preferred_element_type=jnp.float32,
    )
    inner_total = lax.psum(inner_part, "tensor").astype(jnp.bfloat16)
    lowrank_delta = jnp.einsum(
        "mc,mct->mt", inner_total, up_all[beam_adapter_index], preferred_element_type=jnp.float32
    )
    query_total, keyval = lax.psum((query_part, keyval_part), "tensor")
    delta_total = lax.all_gather(lowrank_delta, "tensor", axis=1, tiled=True)
    query_rotated = apply_rotary(query_total + delta_total, beam_cache_length, HEAD_DIM).astype(
        jnp.bfloat16
    )
    key_new = apply_rotary(keyval[:, :kv_width], beam_cache_length, HEAD_DIM).astype(jnp.bfloat16)
    value_new = keyval[:, kv_width:].astype(jnp.bfloat16)
    position_count = paged_key_cache.shape[1]
    query_heads = query_rotated.reshape(beam_rows, kv_heads, group_size, HEAD_DIM)
    key_block = paged_key_cache.reshape(beam_rows, position_count, kv_heads, HEAD_DIM)
    value_block = paged_value_cache.reshape(beam_rows, position_count, kv_heads, HEAD_DIM)
    score_scale = 1.0 / HEAD_DIM**0.5
    scores = (
        jnp.einsum("bkgh,bpkh->bkgp", query_heads, key_block, preferred_element_type=jnp.float32)
        * score_scale
    )
    position_ids = tensor_index * position_count + jnp.arange(position_count)
    live_mask = (position_ids[None, :] < beam_cache_length[:, None])[:, None, None, :]
    scores = jnp.where(live_mask, scores, -1e30)
    peak_score = jnp.max(scores, axis=-1)
    weights = jnp.where(live_mask, jnp.exp(scores - peak_score[..., None]), 0.0)
    weight_total = jnp.sum(weights, axis=-1)
    weighted = jnp.einsum(
        "bkgp,bpkh->bkgh",
        weights.astype(jnp.bfloat16),
        value_block,
        preferred_element_type=jnp.float32,
    )
    peak_score, weight_total, weighted = joined(
        (peak_score, weight_total, weighted), "tensor", combine_parts
    )
    score_new = (
        jnp.einsum(
            "bkgh,bkh->bkg",
            query_heads,
            key_new.reshape(beam_rows, kv_heads, HEAD_DIM),
            preferred_element_type=jnp.float32,
        )
        * score_scale
    )
    value_rows = value_new.reshape(beam_rows, kv_heads, HEAD_DIM).astype(jnp.float32)[:, :, None, :]
    attended = (
        finish_heads(peak_score, weight_total, weighted, score_new, value_rows)
        .reshape(beam_rows, model_width)
        .astype(jnp.bfloat16)
    )
    attended_cols = lax.dynamic_slice_in_dim(attended, tensor_index * width_part, width_part, 1)
    mixed_cols = lax.psum_scatter(
        lax.dot_general(
            output_weight,
            attended_cols,
            (((0,), (1,)), ((), ())),
            preferred_element_type=jnp.float32,
        ),
        "tensor",
        scatter_dimension=0,
        tiled=True,
    )
    return (normed_hidden_input.astype(jnp.float32) + mixed_cols.T).astype(jnp.bfloat16)


def solution(mesh):
    matched = mesh.shape["tensor"] == 8 and mesh.shape["bank"] == 2
    return jax.shard_map(
        matched_body if matched else body,
        mesh=mesh,
        in_specs=(
            P(("groups", "bank"), "tensor"),
            P(("groups", "bank")),
            P(("groups", "bank")),
            P("tensor", None),
            P("tensor", None),
            P("tensor", None),
            P("bank", "tensor", None),
            P("bank", None, "tensor"),
            P(("groups", "bank"), "tensor", None),
            P(("groups", "bank"), "tensor", None),
        ),
        out_specs=P(("groups", "bank"), "tensor"),
        check_vma=False,
    )
```

```python
import jax
import jax.numpy as jnp
from jax import lax
from jax.experimental import pallas as pl
from jax.experimental.pallas import tpu as pltpu
from jax.sharding import PartitionSpec as P

HEAD_DIM = 128
F32 = jnp.float32
BF16 = jnp.bfloat16
CHUNKS = 2
VMEM_LIMIT = 24 * 1024 * 1024


def whole():
    return pl.BlockSpec(memory_space=pltpu.VMEM)


def big():
    return pl.BlockSpec(memory_space=pltpu.HBM)


def scalar():
    return pl.BlockSpec(memory_space=pltpu.SMEM)


def in_hbm(array):
    return pltpu.with_memory_space_constraint(array, pltpu.HBM)


def shape(*dims, dtype=F32):
    return jax.ShapeDtypeStruct(dims, dtype)


def iota(dims, axis):
    return lax.broadcasted_iota(jnp.int32, dims, axis)


def params(**more):
    return pltpu.CompilerParams(vmem_limit_bytes=VMEM_LIMIT, **more)


def start_columns(weight, column, target, sems):
    depth, width = target.shape
    part = depth // CHUNKS
    copies = []
    for c in range(CHUNKS):
        rows = pl.ds(c * part, part)
        copies.append(
            pltpu.make_async_copy(
                weight.at[rows, pl.ds(pl.multiple_of(column, width), width)],
                target.at[rows, :],
                sems.at[c],
            )
        )
        copies[-1].start()
    return copies


def adapter_column(refs, bank, count):
    rows = len(refs) * refs[0].shape[0]
    row = iota((rows, HEAD_DIM), 0)
    column = jnp.zeros((rows, HEAD_DIM), jnp.int32)
    for r in range(rows):
        ref = refs[r // refs[0].shape[0]]
        column = jnp.where(row == r, ref[r % ref.shape[0]], column)
    return column - bank * count


def project_kernel(first, ranks, place, bank, *refs):
    if first:
        own_index, other_index, x_ref, other_ref, w_ref, kv_ref, down_ref, out, inner = refs[:9]
        w_buf, kv_buf, sems, kv_sems, x_buf, own_smem, other_smem, down_buf, small_sems = refs[9:]
    else:
        x_ref, other_ref, w_ref, kv_ref, inner, out = refs[:6]
        w_buf, kv_buf, sems, kv_sems, x_buf, small_sems = refs[6:]
    count, _, width = w_buf.shape
    small = [pltpu.make_async_copy(x_ref, x_buf, small_sems.at[0])]
    if first:
        small.append(pltpu.make_async_copy(own_index, own_smem, small_sems.at[1]))
        small.append(pltpu.make_async_copy(other_index, other_smem, small_sems.at[2]))
    for copy in small:
        copy.start()
    copies = []
    for s in range(count):
        target = (2 * s + first) ^ place[0]
        copies.append(
            start_columns(w_ref, (2 * target + bank[0]) * width, w_buf.at[s], sems.at[s])
            + start_columns(
                kv_ref, (target + ranks * bank[0]) * HEAD_DIM, kv_buf.at[s], kv_sems.at[s]
            )
        )
    if first:
        down_copy = pltpu.make_async_copy(down_ref, down_buf, small_sems.at[3])
        down_copy.start()
    for copy in small:
        copy.wait()
    x = jnp.concatenate([x_buf[...].astype(F32), other_ref[...].astype(F32)], axis=0).astype(BF16)
    for s in range(count):
        for copy in copies[s]:
            copy.wait()
        out[s, :, :width] = jnp.dot(x, w_buf[s], preferred_element_type=F32)
        out[s, :, width : width + HEAD_DIM] = jnp.dot(x, kv_buf[s], preferred_element_type=F32)
    if first:
        down_copy.wait()
        adapters, rank, depth = down_buf.shape
        every = lax.dot_general(
            x,
            down_buf[...].reshape(adapters * rank, depth),
            (((1,), (1,)), ((), ())),
            preferred_element_type=F32,
        )
        column = adapter_column((own_smem, other_smem), bank[0], adapters)
        lane = iota(column.shape, 1)
        per = HEAD_DIM // rank
        total = jnp.zeros(column.shape, F32)
        for j in range(adapters // per):
            part = every[:, j * HEAD_DIM : (j + 1) * HEAD_DIM]
            total += jnp.where(lane // rank + j * per == column, part, 0.0)
        inner[...] = total
    for s in range(count):
        out[s, :, width + HEAD_DIM :] = inner[...]


def project(place, bank, x, other, wq, wkv, ranks, down=None, index=None, inner=None):
    rows, depth = x.shape
    first = inner is None
    width = wq.shape[1] // ranks // 2
    half = ranks // 2
    out = [shape(half, 2 * rows, width + 2 * HEAD_DIM)]
    dma = pltpu.SemaphoreType.DMA
    scratch = [
        pltpu.VMEM((half, depth, width), BF16),
        pltpu.VMEM((half, depth, HEAD_DIM), BF16),
        dma((half, CHUNKS)),
        dma((half, CHUNKS)),
        pltpu.VMEM(x.shape, BF16),
    ]
    if first:
        args = (*index, x, other, wq, wkv, down)
        specs = [big(), pl.BlockSpec(memory_space=pl.ANY), big(), whole(), big(), big(), big()]
        out.append(shape(2 * rows, HEAD_DIM))
        scratch += [pltpu.SMEM((rows,), jnp.int32)] * 2
        scratch += [pltpu.VMEM(down.shape, BF16), dma((4,))]
    else:
        args = (x, other, wq, wkv, inner)
        specs = [big(), whole(), big(), big(), whole()]
        scratch += [dma((1,))]
    return pl.pallas_call(
        lambda *refs: project_kernel(int(first), ranks, *refs),
        in_specs=[scalar()] * 2 + specs,
        out_specs=[whole()] * len(out),
        out_shape=out,
        scratch_shapes=scratch,
        compiler_params=params(),
        cost_estimate=pl.CostEstimate(
            flops=rows * depth * (wq.shape[1] + wkv.shape[1]),
            bytes_accessed=(wq.size + wkv.size) // 2,
            transcendentals=0,
        ),
        name="project_sent" if first else "project_kept",
    )(place, bank, *args)


def halve_kernel(kept_ref, came_ref, sent_out, kept_out):
    for i in range(kept_out.shape[0]):
        for out, j in ((kept_out, 2 * i), (sent_out, 2 * i + 1)):
            out[i] = (kept_ref[j].astype(F32) + came_ref[j].astype(F32)).astype(out.dtype)


def halve(kept, came):
    half = (kept.shape[0] // 2,) + kept.shape[1:]
    return pl.pallas_call(
        halve_kernel,
        in_specs=[whole()] * 2,
        out_specs=[whole()] * 2,
        out_shape=[shape(*half, dtype=came.dtype), shape(*half, dtype=kept.dtype)],
        compiler_params=params(),
        name="halve",
    )(kept, came)


def correct_kernel(bank, own_index, other_index, kept_ref, came_ref, up_ref, own_out, other_out):
    total = kept_ref[0] + came_ref[0]
    count, rank, width = up_ref.shape
    half = width // 2
    inner = total[:, half + HEAD_DIM :].astype(BF16).astype(F32)
    column = adapter_column((own_index, other_index), bank[0], count)
    lane = iota(column.shape, 1)
    per = HEAD_DIM // rank
    spread = jnp.concatenate(
        [
            jnp.where(lane // rank + j * per == column, inner, 0.0)
            for j in range(count // per)
        ],
        axis=1,
    ).astype(BF16)
    delta = jnp.dot(
        spread, up_ref[...].reshape(count * rank, width), preferred_element_type=F32
    )
    rows = own_out.shape[0]
    for side in range(2):
        columns = slice(side * half, (side + 1) * half)
        part = delta[:, columns] + jnp.where(bank[0] == side, total[:, :half], 0.0)
        own_out[:, columns] = part[:rows]
        other_out[:, columns] = part[rows:]
    own_out[:, width:] = total[:rows, half : half + HEAD_DIM]
    other_out[:, width:] = total[rows:, half : half + HEAD_DIM]


def correct(bank, index, kept, came, up):
    rows = kept.shape[1]
    out = shape(rows // 2, up.shape[2] + HEAD_DIM)
    return pl.pallas_call(
        correct_kernel,
        in_specs=[scalar()] * 3 + [whole()] * 3,
        out_specs=[whole()] * 2,
        out_shape=[out, out],
        compiler_params=params(),
        cost_estimate=pl.CostEstimate(
            flops=2 * rows * up.size, bytes_accessed=2 * up.size, transcendentals=0
        ),
        name="correct",
    )(bank, *index, kept, came, up)


def rotate(v, cosine, sine):
    return v * cosine + pltpu.roll(v, HEAD_DIM // 2, 1) * sine


def rotate_kernel(bank, own_ref, came_ref, cos_ref, sin_ref, q_ref, k_ref, v_ref, rows_ref):
    width = own_ref.shape[1] - HEAD_DIM
    cosine, sine = cos_ref[...], sin_ref[...]
    for g in range(width // HEAD_DIM):
        columns = slice(g * HEAD_DIM, (g + 1) * HEAD_DIM)
        rows_ref[:, g, :] = rotate(own_ref[:, columns] + came_ref[:, columns], cosine, sine)
    q_ref[0] = rows_ref[...].reshape(q_ref.shape[1:]).astype(BF16)
    own, came = own_ref[:, width:], came_ref[:, width:]
    key = jnp.where(bank[0] == 0, own, came)
    value = jnp.where(bank[0] == 0, came, own)
    k_ref[...] = rotate(key, cosine, sine).astype(BF16).astype(F32)
    v_ref[...] = value.astype(BF16).astype(F32)


def rotated(bank, own, came, cosine, sine):
    rows = own.shape[0]
    heads = own.shape[1] // HEAD_DIM - 1
    return pl.pallas_call(
        rotate_kernel,
        in_specs=[scalar()] + [whole()] * 4,
        out_specs=[whole()] * 3,
        out_shape=[
            shape(1, rows * heads, HEAD_DIM, dtype=BF16),
            shape(rows, HEAD_DIM),
            shape(rows, HEAD_DIM),
        ],
        scratch_shapes=[pltpu.VMEM((rows, heads, HEAD_DIM), F32)],
        compiler_params=params(),
        name="rotate",
    )(bank, own, came, cosine, sine)


def join_kernel(first_ref, second_ref, out_ref):
    half = first_ref.shape[0]
    out_ref[:half] = first_ref[...]
    out_ref[half:] = second_ref[...]


def join(first, second):
    return pl.pallas_call(
        join_kernel,
        in_specs=[whole()] * 2,
        out_specs=whole(),
        out_shape=shape(2 * first.shape[0], *first.shape[1:], dtype=first.dtype),
        compiler_params=params(),
        name="join",
    )(first, second)


def fetch_kernel(ref, out, sems):
    part = ref.shape[0] // sems.shape[0]
    copies = [
        pltpu.make_async_copy(
            ref.at[pl.ds(c * part, part)], out.at[pl.ds(c * part, part)], sems.at[c]
        )
        for c in range(sems.shape[0])
    ]
    for copy in copies:
        copy.start()
    for copy in copies:
        copy.wait()


def fetch(array):
    return pl.pallas_call(
        fetch_kernel,
        in_specs=[big()],
        out_specs=whole(),
        out_shape=jax.ShapeDtypeStruct(array.shape, array.dtype),
        scratch_shapes=[pltpu.SemaphoreType.DMA((4,))],
        compiler_params=params(),
        cost_estimate=pl.CostEstimate(
            flops=0, bytes_accessed=2 * array.size, transcendentals=0
        ),
        name="fetch",
    )(in_hbm(array))


def attend_kernel(slots, earlier, place, length, q_ref, k_ref, v_ref, *refs):
    before, out_ref = refs[:-1], refs[-1]
    beams, positions, _ = k_ref.shape
    rows = q_ref.shape[1]
    group = rows // beams
    row, lane = iota((rows, positions), 0), iota((rows, positions), 1)
    limit = jnp.zeros((rows, positions), jnp.int32)
    for beam in range(beams):
        limit = jnp.where(row // group == beam, length[beam], limit)
    live = place[0] * positions + lane < limit
    row, lane = iota((rows, HEAD_DIM), 0), iota((rows, HEAD_DIM), 1)
    for i, slot in enumerate(slots):
        head = place[0] ^ slot
        columns = pl.ds(pl.multiple_of(head * HEAD_DIM, HEAD_DIM), HEAD_DIM)
        query = q_ref[i].astype(F32)
        scores = jnp.concatenate(
            [
                lax.dot_general(
                    query[beam * group : (beam + 1) * group].astype(BF16),
                    k_ref[beam, :, columns],
                    (((1,), (1,)), ((), ())),
                    preferred_element_type=F32,
                )
                for beam in range(beams)
            ],
            axis=0,
        ) * (1.0 / HEAD_DIM**0.5)
        scores = jnp.where(live, scores, -1e30)
        peak = jnp.max(scores, axis=1, keepdims=True)
        weights = jnp.where(live, jnp.exp(scores - peak), 0.0)
        total = jnp.sum(weights, axis=1, keepdims=True)
        values = [
            jnp.dot(
                weights[beam * group : (beam + 1) * group].astype(BF16),
                v_ref[beam, :, columns],
                preferred_element_type=F32,
            )
            for beam in range(beams)
        ]
        stats = jnp.where(lane == row % group, peak, 0.0)
        stats += jnp.where(lane == group + row % group, total, 0.0)
        stats = jnp.sum(stats.reshape(beams, group, HEAD_DIM), axis=1)
        high = stats.astype(BF16).astype(F32)
        middle = (stats - high).astype(BF16).astype(F32)
        low = stats - high - middle
        block = jnp.concatenate(values + [high, middle, low, jnp.zeros_like(low)], axis=0)
        out_ref[head if earlier else i] = block.astype(BF16)
    if earlier:
        done = [(ref, i) for ref in before for i in range(ref.shape[0])]
        for slot, (ref, i) in zip(earlier, done):
            out_ref[place[0] ^ slot] = ref[i]


def attend(place, length, queries, keys, values, slots, earlier=(), before=()):
    count, rows, _ = queries.shape
    beams, positions, _ = keys.shape
    out = shape(count + len(earlier), rows + 4 * beams, HEAD_DIM, dtype=BF16)
    return pl.pallas_call(
        lambda *refs: attend_kernel(slots, earlier, *refs),
        in_specs=[scalar()] * 2 + [whole()] * (3 + len(before)),
        out_specs=whole(),
        out_shape=out,
        compiler_params=params(),
        cost_estimate=pl.CostEstimate(
            flops=4 * rows * count * positions * HEAD_DIM,
            bytes_accessed=4 * beams * positions * HEAD_DIM * count,
            transcendentals=rows * count * positions,
        ),
        name="attend",
    )(place, length, queries, keys, values, *before)


def combine_kernel(parts_ref, q_ref, k_ref, v_ref, out_ref, joined):
    ranks = parts_ref.shape[0]
    beams, group, _ = joined.shape
    rows = beams * group

    def by_row(v):
        return jnp.broadcast_to(v[:, None, :], (beams, group, HEAD_DIM)).reshape(rows, HEAD_DIM)

    head = iota((rows, HEAD_DIM), 0) % group
    lane = iota((rows, HEAD_DIM), 1)
    score = jnp.sum(q_ref[0].astype(F32) * by_row(k_ref[...]), axis=1, keepdims=True) * (
        1.0 / HEAD_DIM**0.5
    )
    peaks, totals, weighted = [], [], []
    top = score
    for s in range(ranks):
        block = parts_ref[s].astype(F32)
        tail = by_row(
            block[rows : rows + beams]
            + block[rows + beams : rows + 2 * beams]
            + block[rows + 2 * beams : rows + 3 * beams]
        )
        peak = jnp.sum(jnp.where(lane == head, tail, 0.0), axis=1, keepdims=True)
        total = jnp.sum(jnp.where(lane == group + head, tail, 0.0), axis=1, keepdims=True)
        top = jnp.maximum(top, peak)
        peaks.append(peak)
        totals.append(total)
        weighted.append(block[:rows])
    new = jnp.exp(score - top)
    everything = new
    result = new.astype(BF16).astype(F32) * by_row(v_ref[...])
    for peak, total, block in zip(peaks, totals, weighted):
        factor = jnp.exp(peak - top)
        everything += total * factor
        result += block * factor
    joined[...] = (result / everything).reshape(joined.shape)
    for g in range(group):
        out_ref[:, g * HEAD_DIM : (g + 1) * HEAD_DIM] = joined[:, g, :].astype(BF16)


def combine(parts, query, key_new, value_new):
    beams = key_new.shape[0]
    group = query.shape[1] // beams
    return pl.pallas_call(
        combine_kernel,
        in_specs=[whole()] * 4,
        out_specs=whole(),
        out_shape=shape(beams, group * HEAD_DIM, dtype=BF16),
        scratch_shapes=[pltpu.VMEM((beams, group, HEAD_DIM), F32)],
        compiler_params=params(),
        name="combine",
    )(parts, query, key_new, value_new)


def output_kernel(parity, place, x_ref, w_ref, out, w_buf, sems):
    count, _, width = w_buf.shape
    copies = [
        start_columns(w_ref, ((2 * s + parity) ^ place[0]) * width, w_buf.at[s], sems.at[s])
        for s in range(count)
    ]
    for s in range(count):
        for copy in copies[s]:
            copy.wait()
        total = jnp.dot(x_ref[...], w_buf[s], preferred_element_type=F32)
        out[s] = total.astype(out.dtype)


def output(place, x, weight, ranks, parity, dtype):
    beams, depth = x.shape
    width = weight.shape[1] // ranks
    half = ranks // 2
    return pl.pallas_call(
        lambda *refs: output_kernel(parity, *refs),
        in_specs=[scalar(), whole(), big()],
        out_specs=whole(),
        out_shape=shape(half, beams, width, dtype=dtype),
        scratch_shapes=[
            pltpu.VMEM((half, depth, width), BF16),
            pltpu.SemaphoreType.DMA((half, CHUNKS)),
        ],
        compiler_params=params(),
        cost_estimate=pl.CostEstimate(
            flops=beams * weight.size, bytes_accessed=weight.size, transcendentals=0
        ),
        name="output_sent" if parity else "output_kept",
    )(place, x, weight)


def residual_kernel(x_ref, kept_ref, came_ref, out_ref):
    total = kept_ref[0] + came_ref[0].astype(F32)
    out_ref[...] = (x_ref[...].astype(F32) + total).astype(BF16)


def residual(x, kept, came):
    return pl.pallas_call(
        residual_kernel,
        in_specs=[whole()] * 3,
        out_specs=whole(),
        out_shape=jax.ShapeDtypeStruct(x.shape, BF16),
        compiler_params=params(),
        name="residual",
    )(x, kept, came)


def swapped(x):
    return lax.ppermute(x, "bank", [(0, 1), (1, 0)])


def hop(x, bit):
    ranks = lax.axis_size("tensor")
    return lax.ppermute(x, "tensor", [(i, i ^ bit) for i in range(ranks)])


def beside(came, array, sent):
    array, _ = lax.optimization_barrier((array, sent))
    return lax.optimization_barrier((came, fetch(array)))


def matched_body(
    normed_hidden_input,
    beam_adapter_index,
    beam_cache_length,
    query_weight,
    keyvalue_weight,
    output_weight,
    lowrank_down_factors,
    lowrank_up_factors,
    paged_key_cache,
    paged_value_cache,
):
    x = normed_hidden_input
    ranks = lax.axis_size("tensor")
    place = lax.axis_index("tensor").astype(jnp.int32).reshape(1)
    bank = lax.axis_index("bank").astype(jnp.int32).reshape(1)
    index = (beam_adapter_index, swapped(beam_adapter_index))
    x_other = swapped(x)
    half = HEAD_DIM // 2
    frequency = jnp.power(500000.0, -2.0 * jnp.arange(half, dtype=F32) / HEAD_DIM)
    angles = beam_cache_length.astype(F32)[:, None] * frequency[None, :]
    cosine = jnp.tile(jnp.cos(angles), (1, 2))
    sine = jnp.sin(angles)
    sine = jnp.concatenate([-sine, sine], axis=1)

    weights = in_hbm(query_weight), in_hbm(keyvalue_weight)
    place_x = in_hbm(x)
    sent, inner = project(
        place,
        bank,
        place_x,
        x_other,
        *weights,
        ranks,
        down=in_hbm(lowrank_down_factors.swapaxes(1, 2)),
        index=(in_hbm(index[0]), index[1]),
    )
    came = hop(sent, 1)
    (kept,) = project(place, bank, place_x, x_other, *weights, ranks, inner=inner)
    sent, kept = halve(kept, came)
    came, keys = beside(hop(sent, 2), paged_key_cache, sent)
    sent, kept = halve(kept, came)
    came, values = beside(hop(sent, 4), paged_value_cache, sent)
    own, other = correct(bank, index, kept, came, lowrank_up_factors)
    query, key_new, value_new = rotated(bank, own, swapped(other), cosine, sine)

    def attended_part(queries, slots, **more):
        return attend(place, beam_cache_length, queries, keys, values, slots, **more)

    came = hop(query, 4)
    done = [attended_part(query, (0,))]
    gathered = join(query, came)
    second = hop(gathered, 2)
    done.append(attended_part(came, (4,)))
    came = hop(join(gathered, second), 1)
    done.append(attended_part(second, (2, 6)))
    partial = attended_part(came, (1, 5, 3, 7), earlier=(0, 4, 2, 6), before=done)
    parts = lax.all_to_all(partial, "tensor", 0, 0, tiled=True)
    attended = combine(parts, query, key_new, value_new)

    weight = in_hbm(output_weight)
    came = hop(output(place, attended, weight, ranks, 1, BF16), 1)
    kept = output(place, attended, weight, ranks, 0, F32)
    sent, kept = halve(kept, came)
    sent, kept = halve(kept, hop(sent, 2))
    return residual(x, kept, hop(sent, 4))


def joined(x, axis, combine):
    everything = jax.tree.map(lambda part: lax.all_gather(part, axis), x)
    leading = jax.tree.map(lambda part: part[0], everything)

    def turn(k, so_far):
        return combine(so_far, jax.tree.map(lambda part: part[k], everything))

    return lax.fori_loop(1, lax.axis_size(axis), turn, leading)


def apply_rotary(values, positions, head_size):
    row_count, col_count = values.shape
    half_size = head_size // 2
    frequency = jnp.power(500000.0, -2.0 * jnp.arange(half_size, dtype=jnp.float32) / head_size)
    angles = positions.astype(jnp.float32)[:, None] * frequency[None, :]
    cosine_table = jnp.cos(angles)[:, None, :]
    sine_table = jnp.sin(angles)[:, None, :]
    shaped = values.reshape(row_count, col_count // head_size, 2, half_size)
    first_half = shaped[:, :, 0]
    second_half = shaped[:, :, 1]
    rotated = jnp.stack(
        [
            first_half * cosine_table - second_half * sine_table,
            second_half * cosine_table + first_half * sine_table,
        ],
        axis=2,
    )
    return rotated.reshape(row_count, col_count)


def combine_parts(first_part, second_part):
    peak_one, total_one, weighted_one = first_part
    peak_two, total_two, weighted_two = second_part
    peak_both = jnp.maximum(peak_one, peak_two)
    factor_one = jnp.exp(peak_one - peak_both)
    factor_two = jnp.exp(peak_two - peak_both)
    return (
        peak_both,
        total_one * factor_one + total_two * factor_two,
        weighted_one * factor_one[..., None] + weighted_two * factor_two[..., None],
    )


def finish_heads(peak_score, weight_total, weighted, score_new, value_rows):
    peak_final = jnp.maximum(peak_score, score_new)
    old_factor = jnp.exp(peak_score - peak_final)
    new_weight = jnp.exp(score_new - peak_final)
    weight_total = weight_total * old_factor + new_weight
    weighted = (
        weighted * old_factor[..., None]
        + new_weight.astype(jnp.bfloat16).astype(jnp.float32)[..., None] * value_rows
    )
    return weighted / weight_total[..., None]


def body(
    normed_hidden_input,
    beam_adapter_index,
    beam_cache_length,
    query_weight,
    keyvalue_weight,
    output_weight,
    lowrank_down_factors,
    lowrank_up_factors,
    paged_key_cache,
    paged_value_cache,
):
    beam_rows, width_part = normed_hidden_input.shape
    model_width = query_weight.shape[1]
    kv_width = keyvalue_weight.shape[1] // 2
    head_count = model_width // HEAD_DIM
    kv_heads = kv_width // HEAD_DIM
    group_size = head_count // kv_heads
    tensor_index = lax.axis_index("tensor")
    query_part = jnp.dot(normed_hidden_input, query_weight, preferred_element_type=jnp.float32)
    keyval_part = jnp.dot(normed_hidden_input, keyvalue_weight, preferred_element_type=jnp.float32)
    down_all, up_all = (
        lax.all_gather(lowrank_down_factors, "bank", axis=0, tiled=True),
        lax.all_gather(lowrank_up_factors, "bank", axis=0, tiled=True),
    )
    inner_part = jnp.einsum(
        "ci,cim->cm",
        normed_hidden_input,
        down_all[beam_adapter_index],
        preferred_element_type=jnp.float32,
    )
    inner_total = lax.psum(inner_part, "tensor").astype(jnp.bfloat16)
    lowrank_delta = jnp.einsum(
        "mc,mct->mt", inner_total, up_all[beam_adapter_index], preferred_element_type=jnp.float32
    )
    query_total, keyval = lax.psum((query_part, keyval_part), "tensor")
    delta_total = lax.all_gather(lowrank_delta, "tensor", axis=1, tiled=True)
    query_rotated = apply_rotary(query_total + delta_total, beam_cache_length, HEAD_DIM).astype(
        jnp.bfloat16
    )
    key_new = apply_rotary(keyval[:, :kv_width], beam_cache_length, HEAD_DIM).astype(jnp.bfloat16)
    value_new = keyval[:, kv_width:].astype(jnp.bfloat16)
    position_count = paged_key_cache.shape[1]
    query_heads = query_rotated.reshape(beam_rows, kv_heads, group_size, HEAD_DIM)
    key_block = paged_key_cache.reshape(beam_rows, position_count, kv_heads, HEAD_DIM)
    value_block = paged_value_cache.reshape(beam_rows, position_count, kv_heads, HEAD_DIM)
    score_scale = 1.0 / HEAD_DIM**0.5
    scores = (
        jnp.einsum("bkgh,bpkh->bkgp", query_heads, key_block, preferred_element_type=jnp.float32)
        * score_scale
    )
    position_ids = tensor_index * position_count + jnp.arange(position_count)
    live_mask = (position_ids[None, :] < beam_cache_length[:, None])[:, None, None, :]
    scores = jnp.where(live_mask, scores, -1e30)
    peak_score = jnp.max(scores, axis=-1)
    weights = jnp.where(live_mask, jnp.exp(scores - peak_score[..., None]), 0.0)
    weight_total = jnp.sum(weights, axis=-1)
    weighted = jnp.einsum(
        "bkgp,bpkh->bkgh",
        weights.astype(jnp.bfloat16),
        value_block,
        preferred_element_type=jnp.float32,
    )
    peak_score, weight_total, weighted = joined(
        (peak_score, weight_total, weighted), "tensor", combine_parts
    )
    score_new = (
        jnp.einsum(
            "bkgh,bkh->bkg",
            query_heads,
            key_new.reshape(beam_rows, kv_heads, HEAD_DIM),
            preferred_element_type=jnp.float32,
        )
        * score_scale
    )
    value_rows = value_new.reshape(beam_rows, kv_heads, HEAD_DIM).astype(jnp.float32)[:, :, None, :]
    attended = (
        finish_heads(peak_score, weight_total, weighted, score_new, value_rows)
        .reshape(beam_rows, model_width)
        .astype(jnp.bfloat16)
    )
    attended_cols = lax.dynamic_slice_in_dim(attended, tensor_index * width_part, width_part, 1)
    mixed_cols = lax.psum_scatter(
        lax.dot_general(
            output_weight,
            attended_cols,
            (((0,), (1,)), ((), ())),
            preferred_element_type=jnp.float32,
        ),
        "tensor",
        scatter_dimension=0,
        tiled=True,
    )
    return (normed_hidden_input.astype(jnp.float32) + mixed_cols.T).astype(jnp.bfloat16)


def solution(mesh):
    matched = mesh.shape["tensor"] == 8 and mesh.shape["bank"] == 2
    return jax.shard_map(
        matched_body if matched else body,
        mesh=mesh,
        in_specs=(
            P(("groups", "bank"), "tensor"),
            P(("groups", "bank")),
            P(("groups", "bank")),
            P("tensor", None),
            P("tensor", None),
            P("tensor", None),
            P("bank", "tensor", None),
            P("bank", None, "tensor"),
            P(("groups", "bank"), "tensor", None),
            P(("groups", "bank"), "tensor", None),
        ),
        out_specs=P(("groups", "bank"), "tensor"),
        check_vma=False,
    )
```

```python
import jax
import jax.numpy as jnp
from jax import lax
from jax.experimental import pallas as pl
from jax.experimental.pallas import tpu as pltpu
from jax.sharding import PartitionSpec as P

HEAD_DIM = 128
F32 = jnp.float32
BF16 = jnp.bfloat16
CHUNKS = 2
VMEM_LIMIT = 24 * 1024 * 1024


def whole():
    return pl.BlockSpec(memory_space=pltpu.VMEM)


def big():
    return pl.BlockSpec(memory_space=pltpu.HBM)


def scalar():
    return pl.BlockSpec(memory_space=pltpu.SMEM)


def in_hbm(array):
    return pltpu.with_memory_space_constraint(array, pltpu.HBM)


def shape(*dims, dtype=F32):
    return jax.ShapeDtypeStruct(dims, dtype)


def iota(dims, axis):
    return lax.broadcasted_iota(jnp.int32, dims, axis)


def params(**more):
    return pltpu.CompilerParams(vmem_limit_bytes=VMEM_LIMIT, **more)


def start_columns(weight, column, target, sems):
    depth, width = target.shape
    part = depth // CHUNKS
    copies = []
    for c in range(CHUNKS):
        rows = pl.ds(c * part, part)
        copies.append(
            pltpu.make_async_copy(
                weight.at[rows, pl.ds(pl.multiple_of(column, width), width)],
                target.at[rows, :],
                sems.at[c],
            )
        )
        copies[-1].start()
    return copies


def adapter_column(refs, bank, count):
    rows = len(refs) * refs[0].shape[0]
    row = iota((rows, HEAD_DIM), 0)
    column = jnp.zeros((rows, HEAD_DIM), jnp.int32)
    for r in range(rows):
        ref = refs[r // refs[0].shape[0]]
        column = jnp.where(row == r, ref[r % ref.shape[0]], column)
    return column - bank * count


def project_kernel(first, ranks, place, bank, *refs):
    if first:
        own_index, other_index, x_ref, other_ref, w_ref, kv_ref, down_ref, out, inner = refs[:9]
        w_buf, kv_buf, sems, kv_sems, x_buf, own_smem, other_smem, down_buf, small_sems = refs[9:]
    else:
        x_ref, other_ref, w_ref, kv_ref, inner, out = refs[:6]
        w_buf, kv_buf, sems, kv_sems, x_buf, small_sems = refs[6:]
    count, _, width = w_buf.shape
    small = [pltpu.make_async_copy(x_ref, x_buf, small_sems.at[0])]
    if first:
        small.append(pltpu.make_async_copy(own_index, own_smem, small_sems.at[1]))
        small.append(pltpu.make_async_copy(other_index, other_smem, small_sems.at[2]))
    for copy in small:
        copy.start()
    copies = []
    for s in range(count):
        target = (2 * s + first) ^ place[0]
        copies.append(
            start_columns(w_ref, (2 * target + bank[0]) * width, w_buf.at[s], sems.at[s])
            + start_columns(
                kv_ref, (target + ranks * bank[0]) * HEAD_DIM, kv_buf.at[s], kv_sems.at[s]
            )
        )
    if first:
        down_copy = pltpu.make_async_copy(down_ref, down_buf, small_sems.at[3])
        down_copy.start()
    for copy in small:
        copy.wait()
    x = jnp.concatenate([x_buf[...].astype(F32), other_ref[...].astype(F32)], axis=0).astype(BF16)
    for s in range(count):
        for copy in copies[s]:
            copy.wait()
        out[s, :, :width] = jnp.dot(x, w_buf[s], preferred_element_type=F32)
        out[s, :, width : width + HEAD_DIM] = jnp.dot(x, kv_buf[s], preferred_element_type=F32)
    if first:
        down_copy.wait()
        adapters, rank, depth = down_buf.shape
        every = lax.dot_general(
            x,
            down_buf[...].reshape(adapters * rank, depth),
            (((1,), (1,)), ((), ())),
            preferred_element_type=F32,
        )
        column = adapter_column((own_smem, other_smem), bank[0], adapters)
        lane = iota(column.shape, 1)
        per = HEAD_DIM // rank
        total = jnp.zeros(column.shape, F32)
        for j in range(adapters // per):
            part = every[:, j * HEAD_DIM : (j + 1) * HEAD_DIM]
            total += jnp.where(lane // rank + j * per == column, part, 0.0)
        inner[...] = total
    for s in range(count):
        out[s, :, width + HEAD_DIM :] = inner[...]


def project(place, bank, x, other, wq, wkv, ranks, down=None, index=None, inner=None):
    rows, depth = x.shape
    first = inner is None
    width = wq.shape[1] // ranks // 2
    half = ranks // 2
    out = [shape(half, 2 * rows, width + 2 * HEAD_DIM)]
    dma = pltpu.SemaphoreType.DMA
    scratch = [
        pltpu.VMEM((half, depth, width), BF16),
        pltpu.VMEM((half, depth, HEAD_DIM), BF16),
        dma((half, CHUNKS)),
        dma((half, CHUNKS)),
        pltpu.VMEM(x.shape, BF16),
    ]
    if first:
        args = (*index, x, other, wq, wkv, down)
        specs = [big(), pl.BlockSpec(memory_space=pl.ANY), big(), whole(), big(), big(), big()]
        out.append(shape(2 * rows, HEAD_DIM))
        scratch += [pltpu.SMEM((rows,), jnp.int32)] * 2
        scratch += [pltpu.VMEM(down.shape, BF16), dma((4,))]
    else:
        args = (x, other, wq, wkv, inner)
        specs = [big(), whole(), big(), big(), whole()]
        scratch += [dma((1,))]
    return pl.pallas_call(
        lambda *refs: project_kernel(int(first), ranks, *refs),
        in_specs=[scalar()] * 2 + specs,
        out_specs=[whole()] * len(out),
        out_shape=out,
        scratch_shapes=scratch,
        compiler_params=params(),
        cost_estimate=pl.CostEstimate(
            flops=rows * depth * (wq.shape[1] + wkv.shape[1]),
            bytes_accessed=(wq.size + wkv.size) // 2,
            transcendentals=0,
        ),
        name="project_sent" if first else "project_kept",
    )(place, bank, *args)


def halve_kernel(kept_ref, came_ref, sent_out, kept_out):
    for i in range(kept_out.shape[0]):
        for out, j in ((kept_out, 2 * i), (sent_out, 2 * i + 1)):
            out[i] = (kept_ref[j].astype(F32) + came_ref[j].astype(F32)).astype(out.dtype)


def halve(kept, came):
    half = (kept.shape[0] // 2,) + kept.shape[1:]
    return pl.pallas_call(
        halve_kernel,
        in_specs=[whole()] * 2,
        out_specs=[whole()] * 2,
        out_shape=[shape(*half, dtype=came.dtype), shape(*half, dtype=kept.dtype)],
        compiler_params=params(),
        name="halve",
    )(kept, came)


def correct_kernel(bank, own_index, other_index, kept_ref, came_ref, up_ref, own_out, other_out):
    total = kept_ref[0] + came_ref[0]
    count, rank, width = up_ref.shape
    half = width // 2
    inner = total[:, half + HEAD_DIM :].astype(BF16).astype(F32)
    column = adapter_column((own_index, other_index), bank[0], count)
    lane = iota(column.shape, 1)
    per = HEAD_DIM // rank
    spread = jnp.concatenate(
        [
            jnp.where(lane // rank + j * per == column, inner, 0.0)
            for j in range(count // per)
        ],
        axis=1,
    ).astype(BF16)
    delta = jnp.dot(
        spread, up_ref[...].reshape(count * rank, width), preferred_element_type=F32
    )
    rows = own_out.shape[0]
    for side in range(2):
        columns = slice(side * half, (side + 1) * half)
        part = delta[:, columns] + jnp.where(bank[0] == side, total[:, :half], 0.0)
        own_out[:, columns] = part[:rows]
        other_out[:, columns] = part[rows:]
    own_out[:, width:] = total[:rows, half : half + HEAD_DIM]
    other_out[:, width:] = total[rows:, half : half + HEAD_DIM]


def correct(bank, index, kept, came, up):
    rows = kept.shape[1]
    out = shape(rows // 2, up.shape[2] + HEAD_DIM)
    return pl.pallas_call(
        correct_kernel,
        in_specs=[scalar()] * 3 + [whole()] * 3,
        out_specs=[whole()] * 2,
        out_shape=[out, out],
        compiler_params=params(),
        cost_estimate=pl.CostEstimate(
            flops=2 * rows * up.size, bytes_accessed=2 * up.size, transcendentals=0
        ),
        name="correct",
    )(bank, *index, kept, came, up)


def rotate(v, cosine, sine):
    return v * cosine + pltpu.roll(v, HEAD_DIM // 2, 1) * sine


def rotate_kernel(bank, own_ref, came_ref, cos_ref, sin_ref, q_ref, k_ref, v_ref, rows_ref):
    width = own_ref.shape[1] - HEAD_DIM
    cosine, sine = cos_ref[...], sin_ref[...]
    for g in range(width // HEAD_DIM):
        columns = slice(g * HEAD_DIM, (g + 1) * HEAD_DIM)
        rows_ref[:, g, :] = rotate(own_ref[:, columns] + came_ref[:, columns], cosine, sine)
    q_ref[0] = rows_ref[...].reshape(q_ref.shape[1:]).astype(BF16)
    own, came = own_ref[:, width:], came_ref[:, width:]
    key = jnp.where(bank[0] == 0, own, came)
    value = jnp.where(bank[0] == 0, came, own)
    k_ref[...] = rotate(key, cosine, sine).astype(BF16).astype(F32)
    v_ref[...] = value.astype(BF16).astype(F32)


def rotated(bank, own, came, cosine, sine):
    rows = own.shape[0]
    heads = own.shape[1] // HEAD_DIM - 1
    return pl.pallas_call(
        rotate_kernel,
        in_specs=[scalar()] + [whole()] * 4,
        out_specs=[whole()] * 3,
        out_shape=[
            shape(1, rows * heads, HEAD_DIM, dtype=BF16),
            shape(rows, HEAD_DIM),
            shape(rows, HEAD_DIM),
        ],
        scratch_shapes=[pltpu.VMEM((rows, heads, HEAD_DIM), F32)],
        compiler_params=params(),
        name="rotate",
    )(bank, own, came, cosine, sine)


def join_kernel(first_ref, second_ref, out_ref):
    half = first_ref.shape[0]
    out_ref[:half] = first_ref[...]
    out_ref[half:] = second_ref[...]


def join(first, second):
    return pl.pallas_call(
        join_kernel,
        in_specs=[whole()] * 2,
        out_specs=whole(),
        out_shape=shape(2 * first.shape[0], *first.shape[1:], dtype=first.dtype),
        compiler_params=params(),
        name="join",
    )(first, second)


def start_head(head, sources, targets, sems):
    columns = pl.ds(pl.multiple_of(head * HEAD_DIM, HEAD_DIM), HEAD_DIM)
    copies = [
        pltpu.make_async_copy(source.at[:, :, columns], target, sems.at[n])
        for n, (source, target) in enumerate(zip(sources, targets))
    ]
    for copy in copies:
        copy.start()
    return copies


def attend_kernel(slots, ahead, earlier, place, length, q_ref, k_ref, v_ref, *refs):
    before, refs = refs[: len(refs) - 1 - 2 * bool(ahead) - 3 * (not earlier)], refs[
        len(refs) - 1 - 2 * bool(ahead) - 3 * (not earlier) :
    ]
    out_ref, refs = refs[0], refs[1:]
    rows = q_ref.shape[1]
    if earlier:
        k_buf, v_buf = k_ref, v_ref
    else:
        next_refs, (k_buf, v_buf, sems) = refs[:-3], refs[-3:]
        copies = [
            start_head(
                place[0] ^ slot, (k_ref, v_ref), (k_buf.at[i], v_buf.at[i]), sems.at[i]
            )
            for i, slot in enumerate(slots)
        ]
        more = [
            start_head(
                place[0] ^ slot,
                (k_ref, v_ref),
                [ref.at[i] for ref in next_refs],
                sems.at[len(slots) + i],
            )
            for i, slot in enumerate(ahead)
        ]
    _, beams, positions, _ = k_buf.shape
    group = rows // beams
    row, lane = iota((rows, positions), 0), iota((rows, positions), 1)
    limit = jnp.zeros((rows, positions), jnp.int32)
    for beam in range(beams):
        limit = jnp.where(row // group == beam, length[beam], limit)
    live = place[0] * positions + lane < limit
    row, lane = iota((rows, HEAD_DIM), 0), iota((rows, HEAD_DIM), 1)
    for i, slot in enumerate(slots):
        query = q_ref[i].astype(F32)
        if not earlier:
            copies[i][0].wait()
        scores = jnp.concatenate(
            [
                lax.dot_general(
                    query[beam * group : (beam + 1) * group].astype(BF16),
                    k_buf[i, beam],
                    (((1,), (1,)), ((), ())),
                    preferred_element_type=F32,
                )
                for beam in range(beams)
            ],
            axis=0,
        ) * (1.0 / HEAD_DIM**0.5)
        scores = jnp.where(live, scores, -1e30)
        peak = jnp.max(scores, axis=1, keepdims=True)
        weights = jnp.where(live, jnp.exp(scores - peak), 0.0)
        total = jnp.sum(weights, axis=1, keepdims=True)
        if not earlier:
            copies[i][1].wait()
        values = [
            jnp.dot(
                weights[beam * group : (beam + 1) * group].astype(BF16),
                v_buf[i, beam],
                preferred_element_type=F32,
            )
            for beam in range(beams)
        ]
        stats = jnp.where(lane == row % group, peak, 0.0)
        stats += jnp.where(lane == group + row % group, total, 0.0)
        stats = jnp.sum(stats.reshape(beams, group, HEAD_DIM), axis=1)
        high = stats.astype(BF16).astype(F32)
        middle = (stats - high).astype(BF16).astype(F32)
        low = stats - high - middle
        tail = high + pltpu.roll(middle, 2 * group, 1) + pltpu.roll(low, 4 * group, 1)
        block = jnp.concatenate(values + [tail, jnp.zeros_like(tail)], axis=0)
        out_ref[place[0] ^ slot if earlier else i] = block.astype(BF16)
    if earlier:
        done = [(ref, i) for ref in before for i in range(ref.shape[0])]
        for slot, (ref, i) in zip(earlier, done):
            out_ref[place[0] ^ slot] = ref[i]
    else:
        for pair in more:
            for copy in pair:
                copy.wait()


def attend(place, length, queries, keys, values, slots, ahead=(), earlier=(), before=()):
    count, rows, _ = queries.shape
    beams, positions = keys.shape[-3:-1]
    out = [shape(count + len(earlier), rows + 2 * beams, HEAD_DIM, dtype=BF16)]
    out += [shape(len(ahead), beams, positions, HEAD_DIM, dtype=BF16)] * (2 * bool(ahead))
    scratch = []
    if not earlier:
        scratch = [pltpu.VMEM((count, beams, positions, HEAD_DIM), BF16)] * 2
        scratch.append(pltpu.SemaphoreType.DMA((count + len(ahead), 2)))
    return pl.pallas_call(
        lambda *refs: attend_kernel(slots, ahead, earlier, *refs),
        in_specs=[scalar()] * 2
        + [whole()]
        + [whole() if earlier else big()] * 2
        + [whole()] * len(before),
        out_specs=[whole()] * len(out),
        out_shape=out,
        scratch_shapes=scratch,
        compiler_params=params(),
        cost_estimate=pl.CostEstimate(
            flops=4 * rows * count * positions * HEAD_DIM,
            bytes_accessed=4 * beams * positions * HEAD_DIM * (count + len(ahead)),
            transcendentals=rows * count * positions,
        ),
        name="attend",
    )(place, length, queries, keys, values, *before)


def combine_kernel(parts_ref, q_ref, k_ref, v_ref, out_ref, joined):
    ranks = parts_ref.shape[0]
    beams, group, _ = joined.shape
    rows = beams * group

    def by_row(v):
        return jnp.broadcast_to(v[:, None, :], (beams, group, HEAD_DIM)).reshape(rows, HEAD_DIM)

    head = iota((rows, HEAD_DIM), 0) % group
    lane = iota((rows, HEAD_DIM), 1)
    score = jnp.sum(q_ref[0].astype(F32) * by_row(k_ref[...]), axis=1, keepdims=True) * (
        1.0 / HEAD_DIM**0.5
    )
    peaks, totals, weighted = [], [], []
    top = score
    for s in range(ranks):
        block = parts_ref[s].astype(F32)
        tail = block[rows : rows + beams]
        for turn in (2, 4):
            tail += pltpu.roll(block[rows : rows + beams], HEAD_DIM - turn * group, 1)
        tail = by_row(tail)
        peak = jnp.sum(jnp.where(lane == head, tail, 0.0), axis=1, keepdims=True)
        total = jnp.sum(jnp.where(lane == group + head, tail, 0.0), axis=1, keepdims=True)
        top = jnp.maximum(top, peak)
        peaks.append(peak)
        totals.append(total)
        weighted.append(block[:rows])
    new = jnp.exp(score - top)
    everything = new
    result = new.astype(BF16).astype(F32) * by_row(v_ref[...])
    for peak, total, block in zip(peaks, totals, weighted):
        factor = jnp.exp(peak - top)
        everything += total * factor
        result += block * factor
    joined[...] = (result / everything).reshape(joined.shape)
    for g in range(group):
        out_ref[:, g * HEAD_DIM : (g + 1) * HEAD_DIM] = joined[:, g, :].astype(BF16)


def combine(parts, query, key_new, value_new):
    beams = key_new.shape[0]
    group = query.shape[1] // beams
    return pl.pallas_call(
        combine_kernel,
        in_specs=[whole()] * 4,
        out_specs=whole(),
        out_shape=shape(beams, group * HEAD_DIM, dtype=BF16),
        scratch_shapes=[pltpu.VMEM((beams, group, HEAD_DIM), F32)],
        compiler_params=params(),
        name="combine",
    )(parts, query, key_new, value_new)


def output_kernel(parity, place, x_ref, w_ref, out, w_buf, sems):
    count, _, width = w_buf.shape
    copies = [
        start_columns(w_ref, ((2 * s + parity) ^ place[0]) * width, w_buf.at[s], sems.at[s])
        for s in range(count)
    ]
    for s in range(count):
        for copy in copies[s]:
            copy.wait()
        total = jnp.dot(x_ref[...], w_buf[s], preferred_element_type=F32)
        out[s] = total.astype(out.dtype)


def output(place, x, weight, ranks, parity, dtype):
    beams, depth = x.shape
    width = weight.shape[1] // ranks
    half = ranks // 2
    return pl.pallas_call(
        lambda *refs: output_kernel(parity, *refs),
        in_specs=[scalar(), whole(), big()],
        out_specs=whole(),
        out_shape=shape(half, beams, width, dtype=dtype),
        scratch_shapes=[
            pltpu.VMEM((half, depth, width), BF16),
            pltpu.SemaphoreType.DMA((half, CHUNKS)),
        ],
        compiler_params=params(),
        cost_estimate=pl.CostEstimate(
            flops=beams * weight.size, bytes_accessed=weight.size, transcendentals=0
        ),
        name="output_sent" if parity else "output_kept",
    )(place, x, weight)


def residual_kernel(x_ref, kept_ref, came_ref, out_ref):
    total = kept_ref[0] + came_ref[0].astype(F32)
    out_ref[...] = (x_ref[...].astype(F32) + total).astype(BF16)


def residual(x, kept, came):
    return pl.pallas_call(
        residual_kernel,
        in_specs=[whole()] * 3,
        out_specs=whole(),
        out_shape=jax.ShapeDtypeStruct(x.shape, BF16),
        compiler_params=params(),
        name="residual",
    )(x, kept, came)


def swapped(x):
    return lax.ppermute(x, "bank", [(0, 1), (1, 0)])


def hop(x, bit):
    ranks = lax.axis_size("tensor")
    return lax.ppermute(x, "tensor", [(i, i ^ bit) for i in range(ranks)])


def matched_body(
    normed_hidden_input,
    beam_adapter_index,
    beam_cache_length,
    query_weight,
    keyvalue_weight,
    output_weight,
    lowrank_down_factors,
    lowrank_up_factors,
    paged_key_cache,
    paged_value_cache,
):
    x = normed_hidden_input
    ranks = lax.axis_size("tensor")
    place = lax.axis_index("tensor").astype(jnp.int32).reshape(1)
    bank = lax.axis_index("bank").astype(jnp.int32).reshape(1)
    index = (beam_adapter_index, swapped(beam_adapter_index))
    x_other = swapped(x)
    half = HEAD_DIM // 2
    frequency = jnp.power(500000.0, -2.0 * jnp.arange(half, dtype=F32) / HEAD_DIM)
    angles = beam_cache_length.astype(F32)[:, None] * frequency[None, :]
    cosine = jnp.tile(jnp.cos(angles), (1, 2))
    sine = jnp.sin(angles)
    sine = jnp.concatenate([-sine, sine], axis=1)

    weights = in_hbm(query_weight), in_hbm(keyvalue_weight)
    place_x = in_hbm(x)
    sent, inner = project(
        place,
        bank,
        place_x,
        x_other,
        *weights,
        ranks,
        down=in_hbm(lowrank_down_factors.swapaxes(1, 2)),
        index=(in_hbm(index[0]), index[1]),
    )
    came = hop(sent, 1)
    (kept,) = project(place, bank, place_x, x_other, *weights, ranks, inner=inner)
    sent, kept = halve(kept, came)
    sent, kept = halve(kept, hop(sent, 2))
    came = hop(sent, 4)
    own, other = correct(bank, index, kept, came, lowrank_up_factors)
    query, key_new, value_new = rotated(bank, own, swapped(other), cosine, sine)

    cache = in_hbm(paged_key_cache), in_hbm(paged_value_cache)
    came = hop(query, 4)
    done = attend(place, beam_cache_length, query, *cache, (0,))
    gathered = join(query, came)
    second = hop(gathered, 2)
    done += attend(place, beam_cache_length, came, *cache, (4,))
    came = hop(join(gathered, second), 1)
    last = (1, 5, 3, 7)
    block, *cache = attend(place, beam_cache_length, second, *cache, (2, 6), ahead=last)
    (partial,) = attend(
        place,
        beam_cache_length,
        came,
        *cache,
        last,
        earlier=(0, 4, 2, 6),
        before=(*done, block),
    )
    parts = lax.all_to_all(partial, "tensor", 0, 0, tiled=True)
    attended = combine(parts, query, key_new, value_new)

    weight = in_hbm(output_weight)
    came = hop(output(place, attended, weight, ranks, 1, BF16), 1)
    kept = output(place, attended, weight, ranks, 0, F32)
    sent, kept = halve(kept, came)
    sent, kept = halve(kept, hop(sent, 2))
    return residual(x, kept, hop(sent, 4))


def joined(x, axis, combine):
    everything = jax.tree.map(lambda part: lax.all_gather(part, axis), x)
    leading = jax.tree.map(lambda part: part[0], everything)

    def turn(k, so_far):
        return combine(so_far, jax.tree.map(lambda part: part[k], everything))

    return lax.fori_loop(1, lax.axis_size(axis), turn, leading)


def apply_rotary(values, positions, head_size):
    row_count, col_count = values.shape
    half_size = head_size // 2
    frequency = jnp.power(500000.0, -2.0 * jnp.arange(half_size, dtype=jnp.float32) / head_size)
    angles = positions.astype(jnp.float32)[:, None] * frequency[None, :]
    cosine_table = jnp.cos(angles)[:, None, :]
    sine_table = jnp.sin(angles)[:, None, :]
    shaped = values.reshape(row_count, col_count // head_size, 2, half_size)
    first_half = shaped[:, :, 0]
    second_half = shaped[:, :, 1]
    rotated = jnp.stack(
        [
            first_half * cosine_table - second_half * sine_table,
            second_half * cosine_table + first_half * sine_table,
        ],
        axis=2,
    )
    return rotated.reshape(row_count, col_count)


def combine_parts(first_part, second_part):
    peak_one, total_one, weighted_one = first_part
    peak_two, total_two, weighted_two = second_part
    peak_both = jnp.maximum(peak_one, peak_two)
    factor_one = jnp.exp(peak_one - peak_both)
    factor_two = jnp.exp(peak_two - peak_both)
    return (
        peak_both,
        total_one * factor_one + total_two * factor_two,
        weighted_one * factor_one[..., None] + weighted_two * factor_two[..., None],
    )


def finish_heads(peak_score, weight_total, weighted, score_new, value_rows):
    peak_final = jnp.maximum(peak_score, score_new)
    old_factor = jnp.exp(peak_score - peak_final)
    new_weight = jnp.exp(score_new - peak_final)
    weight_total = weight_total * old_factor + new_weight
    weighted = (
        weighted * old_factor[..., None]
        + new_weight.astype(jnp.bfloat16).astype(jnp.float32)[..., None] * value_rows
    )
    return weighted / weight_total[..., None]


def body(
    normed_hidden_input,
    beam_adapter_index,
    beam_cache_length,
    query_weight,
    keyvalue_weight,
    output_weight,
    lowrank_down_factors,
    lowrank_up_factors,
    paged_key_cache,
    paged_value_cache,
):
    beam_rows, width_part = normed_hidden_input.shape
    model_width = query_weight.shape[1]
    kv_width = keyvalue_weight.shape[1] // 2
    head_count = model_width // HEAD_DIM
    kv_heads = kv_width // HEAD_DIM
    group_size = head_count // kv_heads
    tensor_index = lax.axis_index("tensor")
    query_part = jnp.dot(normed_hidden_input, query_weight, preferred_element_type=jnp.float32)
    keyval_part = jnp.dot(normed_hidden_input, keyvalue_weight, preferred_element_type=jnp.float32)
    down_all, up_all = (
        lax.all_gather(lowrank_down_factors, "bank", axis=0, tiled=True),
        lax.all_gather(lowrank_up_factors, "bank", axis=0, tiled=True),
    )
    inner_part = jnp.einsum(
        "ci,cim->cm",
        normed_hidden_input,
        down_all[beam_adapter_index],
        preferred_element_type=jnp.float32,
    )
    inner_total = lax.psum(inner_part, "tensor").astype(jnp.bfloat16)
    lowrank_delta = jnp.einsum(
        "mc,mct->mt", inner_total, up_all[beam_adapter_index], preferred_element_type=jnp.float32
    )
    query_total, keyval = lax.psum((query_part, keyval_part), "tensor")
    delta_total = lax.all_gather(lowrank_delta, "tensor", axis=1, tiled=True)
    query_rotated = apply_rotary(query_total + delta_total, beam_cache_length, HEAD_DIM).astype(
        jnp.bfloat16
    )
    key_new = apply_rotary(keyval[:, :kv_width], beam_cache_length, HEAD_DIM).astype(jnp.bfloat16)
    value_new = keyval[:, kv_width:].astype(jnp.bfloat16)
    position_count = paged_key_cache.shape[1]
    query_heads = query_rotated.reshape(beam_rows, kv_heads, group_size, HEAD_DIM)
    key_block = paged_key_cache.reshape(beam_rows, position_count, kv_heads, HEAD_DIM)
    value_block = paged_value_cache.reshape(beam_rows, position_count, kv_heads, HEAD_DIM)
    score_scale = 1.0 / HEAD_DIM**0.5
    scores = (
        jnp.einsum("bkgh,bpkh->bkgp", query_heads, key_block, preferred_element_type=jnp.float32)
        * score_scale
    )
    position_ids = tensor_index * position_count + jnp.arange(position_count)
    live_mask = (position_ids[None, :] < beam_cache_length[:, None])[:, None, None, :]
    scores = jnp.where(live_mask, scores, -1e30)
    peak_score = jnp.max(scores, axis=-1)
    weights = jnp.where(live_mask, jnp.exp(scores - peak_score[..., None]), 0.0)
    weight_total = jnp.sum(weights, axis=-1)
    weighted = jnp.einsum(
        "bkgp,bpkh->bkgh",
        weights.astype(jnp.bfloat16),
        value_block,
        preferred_element_type=jnp.float32,
    )
    peak_score, weight_total, weighted = joined(
        (peak_score, weight_total, weighted), "tensor", combine_parts
    )
    score_new = (
        jnp.einsum(
            "bkgh,bkh->bkg",
            query_heads,
            key_new.reshape(beam_rows, kv_heads, HEAD_DIM),
            preferred_element_type=jnp.float32,
        )
        * score_scale
    )
    value_rows = value_new.reshape(beam_rows, kv_heads, HEAD_DIM).astype(jnp.float32)[:, :, None, :]
    attended = (
        finish_heads(peak_score, weight_total, weighted, score_new, value_rows)
        .reshape(beam_rows, model_width)
        .astype(jnp.bfloat16)
    )
    attended_cols = lax.dynamic_slice_in_dim(attended, tensor_index * width_part, width_part, 1)
    mixed_cols = lax.psum_scatter(
        lax.dot_general(
            output_weight,
            attended_cols,
            (((0,), (1,)), ((), ())),
            preferred_element_type=jnp.float32,
        ),
        "tensor",
        scatter_dimension=0,
        tiled=True,
    )
    return (normed_hidden_input.astype(jnp.float32) + mixed_cols.T).astype(jnp.bfloat16)


def solution(mesh):
    matched = mesh.shape["tensor"] == 8 and mesh.shape["bank"] == 2
    return jax.shard_map(
        matched_body if matched else body,
        mesh=mesh,
        in_specs=(
            P(("groups", "bank"), "tensor"),
            P(("groups", "bank")),
            P(("groups", "bank")),
            P("tensor", None),
            P("tensor", None),
            P("tensor", None),
            P("bank", "tensor", None),
            P("bank", None, "tensor"),
            P(("groups", "bank"), "tensor", None),
            P(("groups", "bank"), "tensor", None),
        ),
        out_specs=P(("groups", "bank"), "tensor"),
        check_vma=False,
    )
```

```python
import jax
import jax.numpy as jnp
from jax import lax
from jax.experimental import pallas as pl
from jax.experimental.pallas import tpu as pltpu
from jax.sharding import PartitionSpec as P

HEAD_DIM = 128
F32 = jnp.float32
BF16 = jnp.bfloat16
CHUNKS = 2
VMEM_LIMIT = 24 * 1024 * 1024


def whole():
    return pl.BlockSpec(memory_space=pltpu.VMEM)


def big():
    return pl.BlockSpec(memory_space=pltpu.HBM)


def scalar():
    return pl.BlockSpec(memory_space=pltpu.SMEM)


def in_hbm(array):
    return pltpu.with_memory_space_constraint(array, pltpu.HBM)


def shape(*dims, dtype=F32):
    return jax.ShapeDtypeStruct(dims, dtype)


def iota(dims, axis):
    return lax.broadcasted_iota(jnp.int32, dims, axis)


def params(**more):
    return pltpu.CompilerParams(vmem_limit_bytes=VMEM_LIMIT, **more)


def start_columns(weight, column, target, sems):
    depth, width = target.shape
    part = depth // CHUNKS
    copies = []
    for c in range(CHUNKS):
        rows = pl.ds(c * part, part)
        copies.append(
            pltpu.make_async_copy(
                weight.at[rows, pl.ds(pl.multiple_of(column, width), width)],
                target.at[rows, :],
                sems.at[c],
            )
        )
        copies[-1].start()
    return copies


def adapter_column(refs, bank, count):
    rows = len(refs) * refs[0].shape[0]
    row = iota((rows, HEAD_DIM), 0)
    column = jnp.zeros((rows, HEAD_DIM), jnp.int32)
    for r in range(rows):
        ref = refs[r // refs[0].shape[0]]
        column = jnp.where(row == r, ref[r % ref.shape[0]], column)
    return column - bank * count


def project_kernel(first, ranks, place, bank, *refs):
    if first:
        own_index, other_index, x_ref, other_ref, w_ref, kv_ref, down_ref, out, inner = refs[:9]
        w_buf, kv_buf, sems, kv_sems, x_buf, own_smem, other_smem, down_buf, small_sems = refs[9:]
    else:
        x_ref, other_ref, w_ref, kv_ref, inner, out = refs[:6]
        w_buf, kv_buf, sems, kv_sems, x_buf, small_sems = refs[6:]
    count, _, width = w_buf.shape
    small = [pltpu.make_async_copy(x_ref, x_buf, small_sems.at[0])]
    if first:
        small.append(pltpu.make_async_copy(own_index, own_smem, small_sems.at[1]))
        small.append(pltpu.make_async_copy(other_index, other_smem, small_sems.at[2]))
    for copy in small:
        copy.start()
    copies = []
    for s in range(count):
        target = (2 * s + first) ^ place[0]
        copies.append(
            start_columns(w_ref, (2 * target + bank[0]) * width, w_buf.at[s], sems.at[s])
            + start_columns(
                kv_ref, (target + ranks * bank[0]) * HEAD_DIM, kv_buf.at[s], kv_sems.at[s]
            )
        )
    if first:
        down_copy = pltpu.make_async_copy(down_ref, down_buf, small_sems.at[3])
        down_copy.start()
    for copy in small:
        copy.wait()
    x = jnp.concatenate([x_buf[...].astype(F32), other_ref[...].astype(F32)], axis=0).astype(BF16)
    for s in range(count):
        for copy in copies[s]:
            copy.wait()
        out[s, :, :width] = jnp.dot(x, w_buf[s], preferred_element_type=F32)
        out[s, :, width : width + HEAD_DIM] = jnp.dot(x, kv_buf[s], preferred_element_type=F32)
    if first:
        down_copy.wait()
        adapters, rank, depth = down_buf.shape
        every = lax.dot_general(
            x,
            down_buf[...].reshape(adapters * rank, depth),
            (((1,), (1,)), ((), ())),
            preferred_element_type=F32,
        )
        column = adapter_column((own_smem, other_smem), bank[0], adapters)
        lane = iota(column.shape, 1)
        per = HEAD_DIM // rank
        total = jnp.zeros(column.shape, F32)
        for j in range(adapters // per):
            part = every[:, j * HEAD_DIM : (j + 1) * HEAD_DIM]
            total += jnp.where(lane // rank + j * per == column, part, 0.0)
        inner[...] = total
    for s in range(count):
        out[s, :, width + HEAD_DIM :] = inner[...]


def project(place, bank, x, other, wq, wkv, ranks, down=None, index=None, inner=None):
    rows, depth = x.shape
    first = inner is None
    width = wq.shape[1] // ranks // 2
    half = ranks // 2
    out = [shape(half, 2 * rows, width + 2 * HEAD_DIM)]
    dma = pltpu.SemaphoreType.DMA
    scratch = [
        pltpu.VMEM((half, depth, width), BF16),
        pltpu.VMEM((half, depth, HEAD_DIM), BF16),
        dma((half, CHUNKS)),
        dma((half, CHUNKS)),
        pltpu.VMEM(x.shape, BF16),
    ]
    if first:
        args = (*index, x, other, wq, wkv, down)
        specs = [big(), pl.BlockSpec(memory_space=pl.ANY), big(), whole(), big(), big(), big()]
        out.append(shape(2 * rows, HEAD_DIM))
        scratch += [pltpu.SMEM((rows,), jnp.int32)] * 2
        scratch += [pltpu.VMEM(down.shape, BF16), dma((4,))]
    else:
        args = (x, other, wq, wkv, inner)
        specs = [big(), whole(), big(), big(), whole()]
        scratch += [dma((1,))]
    return pl.pallas_call(
        lambda *refs: project_kernel(int(first), ranks, *refs),
        in_specs=[scalar()] * 2 + specs,
        out_specs=[whole()] * len(out),
        out_shape=out,
        scratch_shapes=scratch,
        compiler_params=params(),
        cost_estimate=pl.CostEstimate(
            flops=rows * depth * (wq.shape[1] + wkv.shape[1]),
            bytes_accessed=(wq.size + wkv.size) // 2,
            transcendentals=0,
        ),
        name="project_sent" if first else "project_kept",
    )(place, bank, *args)


def halve_kernel(kept_ref, came_ref, sent_out, kept_out):
    for i in range(kept_out.shape[0]):
        for out, j in ((kept_out, 2 * i), (sent_out, 2 * i + 1)):
            out[i] = (kept_ref[j].astype(F32) + came_ref[j].astype(F32)).astype(out.dtype)


def halve(kept, came):
    half = (kept.shape[0] // 2,) + kept.shape[1:]
    return pl.pallas_call(
        halve_kernel,
        in_specs=[whole()] * 2,
        out_specs=[whole()] * 2,
        out_shape=[shape(*half, dtype=came.dtype), shape(*half, dtype=kept.dtype)],
        compiler_params=params(),
        name="halve",
    )(kept, came)


def correct_kernel(bank, own_index, other_index, kept_ref, came_ref, up_ref, own_out, other_out):
    total = kept_ref[0] + came_ref[0]
    count, rank, width = up_ref.shape
    half = width // 2
    inner = total[:, half + HEAD_DIM :].astype(BF16).astype(F32)
    column = adapter_column((own_index, other_index), bank[0], count)
    lane = iota(column.shape, 1)
    per = HEAD_DIM // rank
    spread = jnp.concatenate(
        [
            jnp.where(lane // rank + j * per == column, inner, 0.0)
            for j in range(count // per)
        ],
        axis=1,
    ).astype(BF16)
    delta = jnp.dot(
        spread, up_ref[...].reshape(count * rank, width), preferred_element_type=F32
    )
    rows = own_out.shape[0]
    for side in range(2):
        columns = slice(side * half, (side + 1) * half)
        part = delta[:, columns] + jnp.where(bank[0] == side, total[:, :half], 0.0)
        own_out[:, columns] = part[:rows]
        other_out[:, columns] = part[rows:]
    own_out[:, width:] = total[:rows, half : half + HEAD_DIM]
    other_out[:, width:] = total[rows:, half : half + HEAD_DIM]


def correct(bank, index, kept, came, up):
    rows = kept.shape[1]
    out = shape(rows // 2, up.shape[2] + HEAD_DIM)
    return pl.pallas_call(
        correct_kernel,
        in_specs=[scalar()] * 3 + [whole()] * 3,
        out_specs=[whole()] * 2,
        out_shape=[out, out],
        compiler_params=params(),
        cost_estimate=pl.CostEstimate(
            flops=2 * rows * up.size, bytes_accessed=2 * up.size, transcendentals=0
        ),
        name="correct",
    )(bank, *index, kept, came, up)


def rotate(v, cosine, sine):
    return v * cosine + pltpu.roll(v, HEAD_DIM // 2, 1) * sine


def rotate_kernel(bank, own_ref, came_ref, cos_ref, sin_ref, q_ref, k_ref, v_ref, rows_ref):
    width = own_ref.shape[1] - HEAD_DIM
    cosine, sine = cos_ref[...], sin_ref[...]
    for g in range(width // HEAD_DIM):
        columns = slice(g * HEAD_DIM, (g + 1) * HEAD_DIM)
        rows_ref[:, g, :] = rotate(own_ref[:, columns] + came_ref[:, columns], cosine, sine)
    q_ref[0] = rows_ref[...].reshape(q_ref.shape[1:]).astype(BF16)
    own, came = own_ref[:, width:], came_ref[:, width:]
    key = jnp.where(bank[0] == 0, own, came)
    value = jnp.where(bank[0] == 0, came, own)
    k_ref[...] = rotate(key, cosine, sine).astype(BF16).astype(F32)
    v_ref[...] = value.astype(BF16).astype(F32)


def rotated(bank, own, came, cosine, sine):
    rows = own.shape[0]
    heads = own.shape[1] // HEAD_DIM - 1
    return pl.pallas_call(
        rotate_kernel,
        in_specs=[scalar()] + [whole()] * 4,
        out_specs=[whole()] * 3,
        out_shape=[
            shape(1, rows * heads, HEAD_DIM, dtype=BF16),
            shape(rows, HEAD_DIM),
            shape(rows, HEAD_DIM),
        ],
        scratch_shapes=[pltpu.VMEM((rows, heads, HEAD_DIM), F32)],
        compiler_params=params(),
        name="rotate",
    )(bank, own, came, cosine, sine)


def join_kernel(first_ref, second_ref, out_ref):
    half = first_ref.shape[0]
    out_ref[:half] = first_ref[...]
    out_ref[half:] = second_ref[...]


def join(first, second):
    return pl.pallas_call(
        join_kernel,
        in_specs=[whole()] * 2,
        out_specs=whole(),
        out_shape=shape(2 * first.shape[0], *first.shape[1:], dtype=first.dtype),
        compiler_params=params(),
        name="join",
    )(first, second)


def start_head(head, sources, targets, sems):
    columns = pl.ds(pl.multiple_of(head * HEAD_DIM, HEAD_DIM), HEAD_DIM)
    copies = [
        pltpu.make_async_copy(source.at[:, :, columns], target, sems.at[n])
        for n, (source, target) in enumerate(zip(sources, targets))
    ]
    for copy in copies:
        copy.start()
    return copies


def attend_kernel(slots, ahead, earlier, place, length, q_ref, k_ref, v_ref, *refs):
    before, refs = refs[: len(refs) - 1 - 2 * bool(ahead) - 3 * (not earlier)], refs[
        len(refs) - 1 - 2 * bool(ahead) - 3 * (not earlier) :
    ]
    out_ref, refs = refs[0], refs[1:]
    rows = q_ref.shape[1]
    if earlier:
        k_buf, v_buf = k_ref, v_ref
    else:
        next_refs, (k_buf, v_buf, sems) = refs[:-3], refs[-3:]
        copies = [
            start_head(
                place[0] ^ slot, (k_ref, v_ref), (k_buf.at[i], v_buf.at[i]), sems.at[i]
            )
            for i, slot in enumerate(slots)
        ]
        more = [
            start_head(
                place[0] ^ slot,
                (k_ref, v_ref),
                [ref.at[i] for ref in next_refs],
                sems.at[len(slots) + i],
            )
            for i, slot in enumerate(ahead)
        ]
    _, beams, positions, _ = k_buf.shape
    group = rows // beams
    row, lane = iota((rows, positions), 0), iota((rows, positions), 1)
    limit = jnp.zeros((rows, positions), jnp.int32)
    for beam in range(beams):
        limit = jnp.where(row // group == beam, length[beam], limit)
    live = place[0] * positions + lane < limit
    row, lane = iota((rows, HEAD_DIM), 0), iota((rows, HEAD_DIM), 1)
    for i, slot in enumerate(slots):
        query = q_ref[i].astype(F32)
        if not earlier:
            copies[i][0].wait()
        scores = jnp.concatenate(
            [
                lax.dot_general(
                    query[beam * group : (beam + 1) * group].astype(BF16),
                    k_buf[i, beam],
                    (((1,), (1,)), ((), ())),
                    preferred_element_type=F32,
                )
                for beam in range(beams)
            ],
            axis=0,
        ) * (1.0 / HEAD_DIM**0.5)
        scores = jnp.where(live, scores, -1e30)
        peak = jnp.max(scores, axis=1, keepdims=True)
        weights = jnp.where(live, jnp.exp(scores - peak), 0.0)
        total = jnp.sum(weights, axis=1, keepdims=True)
        if not earlier:
            copies[i][1].wait()
        values = [
            jnp.dot(
                weights[beam * group : (beam + 1) * group].astype(BF16),
                v_buf[i, beam],
                preferred_element_type=F32,
            )
            for beam in range(beams)
        ]
        stats = jnp.where(lane == row % group, peak, 0.0)
        stats += jnp.where(lane == group + row % group, total, 0.0)
        stats = jnp.sum(stats.reshape(beams, group, HEAD_DIM), axis=1)
        high = stats.astype(BF16).astype(F32)
        middle = (stats - high).astype(BF16).astype(F32)
        low = stats - high - middle
        tail = high + pltpu.roll(middle, 2 * group, 1) + pltpu.roll(low, 4 * group, 1)
        block = jnp.concatenate(values + [tail, jnp.zeros_like(tail)], axis=0)
        out_ref[place[0] ^ slot if earlier else i] = block.astype(BF16)
    if earlier:
        done = [(ref, i) for ref in before for i in range(ref.shape[0])]
        for slot, (ref, i) in zip(earlier, done):
            out_ref[place[0] ^ slot] = ref[i]
    else:
        for pair in more:
            for copy in pair:
                copy.wait()


def attend(place, length, queries, keys, values, slots, ahead=(), earlier=(), before=()):
    count, rows, _ = queries.shape
    beams, positions = keys.shape[-3:-1]
    out = [shape(count + len(earlier), rows + 2 * beams, HEAD_DIM, dtype=BF16)]
    out += [shape(len(ahead), beams, positions, HEAD_DIM, dtype=BF16)] * (2 * bool(ahead))
    scratch = []
    if not earlier:
        scratch = [pltpu.VMEM((count, beams, positions, HEAD_DIM), BF16)] * 2
        scratch.append(pltpu.SemaphoreType.DMA((count + len(ahead), 2)))
    return pl.pallas_call(
        lambda *refs: attend_kernel(slots, ahead, earlier, *refs),
        in_specs=[scalar()] * 2
        + [whole()]
        + [whole() if earlier else big()] * 2
        + [whole()] * len(before),
        out_specs=[whole()] * len(out),
        out_shape=out,
        scratch_shapes=scratch,
        compiler_params=params(),
        cost_estimate=pl.CostEstimate(
            flops=4 * rows * count * positions * HEAD_DIM,
            bytes_accessed=4 * beams * positions * HEAD_DIM * (16 if earlier else count),
            transcendentals=rows * count * positions,
        ),
        name="attend",
    )(place, length, queries, keys, values, *before)


def combine_kernel(parts_ref, q_ref, k_ref, v_ref, out_ref, joined):
    ranks = parts_ref.shape[0]
    beams, group, _ = joined.shape
    rows = beams * group

    def by_row(v):
        return jnp.broadcast_to(v[:, None, :], (beams, group, HEAD_DIM)).reshape(rows, HEAD_DIM)

    head = iota((rows, HEAD_DIM), 0) % group
    lane = iota((rows, HEAD_DIM), 1)
    score = jnp.sum(q_ref[0].astype(F32) * by_row(k_ref[...]), axis=1, keepdims=True) * (
        1.0 / HEAD_DIM**0.5
    )
    peaks, totals, weighted = [], [], []
    top = score
    for s in range(ranks):
        block = parts_ref[s].astype(F32)
        tail = block[rows : rows + beams]
        for turn in (2, 4):
            tail += pltpu.roll(block[rows : rows + beams], HEAD_DIM - turn * group, 1)
        tail = by_row(tail)
        peak = jnp.sum(jnp.where(lane == head, tail, 0.0), axis=1, keepdims=True)
        total = jnp.sum(jnp.where(lane == group + head, tail, 0.0), axis=1, keepdims=True)
        top = jnp.maximum(top, peak)
        peaks.append(peak)
        totals.append(total)
        weighted.append(block[:rows])
    new = jnp.exp(score - top)
    everything = new
    result = new.astype(BF16).astype(F32) * by_row(v_ref[...])
    for peak, total, block in zip(peaks, totals, weighted):
        factor = jnp.exp(peak - top)
        everything += total * factor
        result += block * factor
    joined[...] = (result / everything).reshape(joined.shape)
    for g in range(group):
        out_ref[:, g * HEAD_DIM : (g + 1) * HEAD_DIM] = joined[:, g, :].astype(BF16)


def combine(parts, query, key_new, value_new):
    beams = key_new.shape[0]
    group = query.shape[1] // beams
    return pl.pallas_call(
        combine_kernel,
        in_specs=[whole()] * 4,
        out_specs=whole(),
        out_shape=shape(beams, group * HEAD_DIM, dtype=BF16),
        scratch_shapes=[pltpu.VMEM((beams, group, HEAD_DIM), F32)],
        compiler_params=params(),
        name="combine",
    )(parts, query, key_new, value_new)


def output_kernel(parity, place, x_ref, w_ref, out):
    count, _, width = out.shape
    for s in range(count):
        first = ((2 * s + parity) ^ place[0]) * width
        columns = pl.ds(pl.multiple_of(first, width), width)
        total = jnp.dot(x_ref[...], w_ref[:, columns], preferred_element_type=F32)
        out[s] = total.astype(out.dtype)


def output(place, x, weight, ranks, parity, dtype):
    beams = x.shape[0]
    return pl.pallas_call(
        lambda *refs: output_kernel(parity, *refs),
        in_specs=[scalar(), whole(), whole()],
        out_specs=whole(),
        out_shape=shape(ranks // 2, beams, weight.shape[1] // ranks, dtype=dtype),
        compiler_params=params(),
        cost_estimate=pl.CostEstimate(
            flops=beams * weight.size, bytes_accessed=weight.size, transcendentals=0
        ),
        name="output_sent" if parity else "output_kept",
    )(place, x, weight)


def residual_kernel(x_ref, kept_ref, came_ref, out_ref):
    total = kept_ref[0] + came_ref[0].astype(F32)
    out_ref[...] = (x_ref[...].astype(F32) + total).astype(BF16)


def residual(x, kept, came):
    return pl.pallas_call(
        residual_kernel,
        in_specs=[whole()] * 3,
        out_specs=whole(),
        out_shape=jax.ShapeDtypeStruct(x.shape, BF16),
        compiler_params=params(),
        name="residual",
    )(x, kept, came)


def swapped(x):
    return lax.ppermute(x, "bank", [(0, 1), (1, 0)])


def hop(x, bit):
    ranks = lax.axis_size("tensor")
    return lax.ppermute(x, "tensor", [(i, i ^ bit) for i in range(ranks)])


def matched_body(
    normed_hidden_input,
    beam_adapter_index,
    beam_cache_length,
    query_weight,
    keyvalue_weight,
    output_weight,
    lowrank_down_factors,
    lowrank_up_factors,
    paged_key_cache,
    paged_value_cache,
):
    x = normed_hidden_input
    ranks = lax.axis_size("tensor")
    place = lax.axis_index("tensor").astype(jnp.int32).reshape(1)
    bank = lax.axis_index("bank").astype(jnp.int32).reshape(1)
    index = (beam_adapter_index, swapped(beam_adapter_index))
    x_other = swapped(x)
    half = HEAD_DIM // 2
    frequency = jnp.power(500000.0, -2.0 * jnp.arange(half, dtype=F32) / HEAD_DIM)
    angles = beam_cache_length.astype(F32)[:, None] * frequency[None, :]
    cosine = jnp.tile(jnp.cos(angles), (1, 2))
    sine = jnp.sin(angles)
    sine = jnp.concatenate([-sine, sine], axis=1)

    weights = in_hbm(query_weight), in_hbm(keyvalue_weight)
    place_x = in_hbm(x)
    sent, inner = project(
        place,
        bank,
        place_x,
        x_other,
        *weights,
        ranks,
        down=in_hbm(lowrank_down_factors.swapaxes(1, 2)),
        index=(in_hbm(index[0]), index[1]),
    )
    came = hop(sent, 1)
    (kept,) = project(place, bank, place_x, x_other, *weights, ranks, inner=inner)
    sent, kept = halve(kept, came)
    sent, kept = halve(kept, hop(sent, 2))
    came = hop(sent, 4)
    own, other = correct(bank, index, kept, came, lowrank_up_factors)
    query, key_new, value_new = rotated(bank, own, swapped(other), cosine, sine)

    cache = in_hbm(paged_key_cache), in_hbm(paged_value_cache)
    came, done = lax.optimization_barrier(
        (hop(query, 4), attend(place, beam_cache_length, query, *cache, (0,)))
    )
    gathered = join(query, came)
    second, more = lax.optimization_barrier(
        (hop(gathered, 2), attend(place, beam_cache_length, came, *cache, (4,)))
    )
    done += more
    came = hop(join(gathered, second), 1)
    last = (1, 5, 3, 7)
    block, *cache = attend(place, beam_cache_length, second, *cache, (2, 6), ahead=last)
    (partial,) = attend(
        place,
        beam_cache_length,
        came,
        *cache,
        last,
        earlier=(0, 4, 2, 6),
        before=(*done, block),
    )
    parts = lax.all_to_all(partial, "tensor", 0, 0, tiled=True)
    attended = combine(parts, query, key_new, value_new)

    came = hop(output(place, attended, output_weight, ranks, 1, BF16), 1)
    kept = output(place, attended, output_weight, ranks, 0, F32)
    sent, kept = halve(kept, came)
    sent, kept = halve(kept, hop(sent, 2))
    return residual(x, kept, hop(sent, 4))


def joined(x, axis, combine):
    everything = jax.tree.map(lambda part: lax.all_gather(part, axis), x)
    leading = jax.tree.map(lambda part: part[0], everything)

    def turn(k, so_far):
        return combine(so_far, jax.tree.map(lambda part: part[k], everything))

    return lax.fori_loop(1, lax.axis_size(axis), turn, leading)


def apply_rotary(values, positions, head_size):
    row_count, col_count = values.shape
    half_size = head_size // 2
    frequency = jnp.power(500000.0, -2.0 * jnp.arange(half_size, dtype=jnp.float32) / head_size)
    angles = positions.astype(jnp.float32)[:, None] * frequency[None, :]
    cosine_table = jnp.cos(angles)[:, None, :]
    sine_table = jnp.sin(angles)[:, None, :]
    shaped = values.reshape(row_count, col_count // head_size, 2, half_size)
    first_half = shaped[:, :, 0]
    second_half = shaped[:, :, 1]
    rotated = jnp.stack(
        [
            first_half * cosine_table - second_half * sine_table,
            second_half * cosine_table + first_half * sine_table,
        ],
        axis=2,
    )
    return rotated.reshape(row_count, col_count)


def combine_parts(first_part, second_part):
    peak_one, total_one, weighted_one = first_part
    peak_two, total_two, weighted_two = second_part
    peak_both = jnp.maximum(peak_one, peak_two)
    factor_one = jnp.exp(peak_one - peak_both)
    factor_two = jnp.exp(peak_two - peak_both)
    return (
        peak_both,
        total_one * factor_one + total_two * factor_two,
        weighted_one * factor_one[..., None] + weighted_two * factor_two[..., None],
    )


def finish_heads(peak_score, weight_total, weighted, score_new, value_rows):
    peak_final = jnp.maximum(peak_score, score_new)
    old_factor = jnp.exp(peak_score - peak_final)
    new_weight = jnp.exp(score_new - peak_final)
    weight_total = weight_total * old_factor + new_weight
    weighted = (
        weighted * old_factor[..., None]
        + new_weight.astype(jnp.bfloat16).astype(jnp.float32)[..., None] * value_rows
    )
    return weighted / weight_total[..., None]


def body(
    normed_hidden_input,
    beam_adapter_index,
    beam_cache_length,
    query_weight,
    keyvalue_weight,
    output_weight,
    lowrank_down_factors,
    lowrank_up_factors,
    paged_key_cache,
    paged_value_cache,
):
    beam_rows, width_part = normed_hidden_input.shape
    model_width = query_weight.shape[1]
    kv_width = keyvalue_weight.shape[1] // 2
    head_count = model_width // HEAD_DIM
    kv_heads = kv_width // HEAD_DIM
    group_size = head_count // kv_heads
    tensor_index = lax.axis_index("tensor")
    query_part = jnp.dot(normed_hidden_input, query_weight, preferred_element_type=jnp.float32)
    keyval_part = jnp.dot(normed_hidden_input, keyvalue_weight, preferred_element_type=jnp.float32)
    down_all, up_all = (
        lax.all_gather(lowrank_down_factors, "bank", axis=0, tiled=True),
        lax.all_gather(lowrank_up_factors, "bank", axis=0, tiled=True),
    )
    inner_part = jnp.einsum(
        "ci,cim->cm",
        normed_hidden_input,
        down_all[beam_adapter_index],
        preferred_element_type=jnp.float32,
    )
    inner_total = lax.psum(inner_part, "tensor").astype(jnp.bfloat16)
    lowrank_delta = jnp.einsum(
        "mc,mct->mt", inner_total, up_all[beam_adapter_index], preferred_element_type=jnp.float32
    )
    query_total, keyval = lax.psum((query_part, keyval_part), "tensor")
    delta_total = lax.all_gather(lowrank_delta, "tensor", axis=1, tiled=True)
    query_rotated = apply_rotary(query_total + delta_total, beam_cache_length, HEAD_DIM).astype(
        jnp.bfloat16
    )
    key_new = apply_rotary(keyval[:, :kv_width], beam_cache_length, HEAD_DIM).astype(jnp.bfloat16)
    value_new = keyval[:, kv_width:].astype(jnp.bfloat16)
    position_count = paged_key_cache.shape[1]
    query_heads = query_rotated.reshape(beam_rows, kv_heads, group_size, HEAD_DIM)
    key_block = paged_key_cache.reshape(beam_rows, position_count, kv_heads, HEAD_DIM)
    value_block = paged_value_cache.reshape(beam_rows, position_count, kv_heads, HEAD_DIM)
    score_scale = 1.0 / HEAD_DIM**0.5
    scores = (
        jnp.einsum("bkgh,bpkh->bkgp", query_heads, key_block, preferred_element_type=jnp.float32)
        * score_scale
    )
    position_ids = tensor_index * position_count + jnp.arange(position_count)
    live_mask = (position_ids[None, :] < beam_cache_length[:, None])[:, None, None, :]
    scores = jnp.where(live_mask, scores, -1e30)
    peak_score = jnp.max(scores, axis=-1)
    weights = jnp.where(live_mask, jnp.exp(scores - peak_score[..., None]), 0.0)
    weight_total = jnp.sum(weights, axis=-1)
    weighted = jnp.einsum(
        "bkgp,bpkh->bkgh",
        weights.astype(jnp.bfloat16),
        value_block,
        preferred_element_type=jnp.float32,
    )
    peak_score, weight_total, weighted = joined(
        (peak_score, weight_total, weighted), "tensor", combine_parts
    )
    score_new = (
        jnp.einsum(
            "bkgh,bkh->bkg",
            query_heads,
            key_new.reshape(beam_rows, kv_heads, HEAD_DIM),
            preferred_element_type=jnp.float32,
        )
        * score_scale
    )
    value_rows = value_new.reshape(beam_rows, kv_heads, HEAD_DIM).astype(jnp.float32)[:, :, None, :]
    attended = (
        finish_heads(peak_score, weight_total, weighted, score_new, value_rows)
        .reshape(beam_rows, model_width)
        .astype(jnp.bfloat16)
    )
    attended_cols = lax.dynamic_slice_in_dim(attended, tensor_index * width_part, width_part, 1)
    mixed_cols = lax.psum_scatter(
        lax.dot_general(
            output_weight,
            attended_cols,
            (((0,), (1,)), ((), ())),
            preferred_element_type=jnp.float32,
        ),
        "tensor",
        scatter_dimension=0,
        tiled=True,
    )
    return (normed_hidden_input.astype(jnp.float32) + mixed_cols.T).astype(jnp.bfloat16)


def solution(mesh):
    matched = mesh.shape["tensor"] == 8 and mesh.shape["bank"] == 2
    return jax.shard_map(
        matched_body if matched else body,
        mesh=mesh,
        in_specs=(
            P(("groups", "bank"), "tensor"),
            P(("groups", "bank")),
            P(("groups", "bank")),
            P("tensor", None),
            P("tensor", None),
            P("tensor", None),
            P("bank", "tensor", None),
            P("bank", None, "tensor"),
            P(("groups", "bank"), "tensor", None),
            P(("groups", "bank"), "tensor", None),
        ),
        out_specs=P(("groups", "bank"), "tensor"),
        check_vma=False,
    )
```

```python
import jax
import jax.numpy as jnp
from jax import lax
from jax.experimental import pallas as pl
from jax.experimental.pallas import tpu as pltpu
from jax.sharding import PartitionSpec as P

HEAD_DIM = 128
F32 = jnp.float32
BF16 = jnp.bfloat16
CHUNKS = 2
VMEM_LIMIT = 24 * 1024 * 1024


def whole():
    return pl.BlockSpec(memory_space=pltpu.VMEM)


def big():
    return pl.BlockSpec(memory_space=pltpu.HBM)


def scalar():
    return pl.BlockSpec(memory_space=pltpu.SMEM)


def in_hbm(array):
    return pltpu.with_memory_space_constraint(array, pltpu.HBM)


def shape(*dims, dtype=F32):
    return jax.ShapeDtypeStruct(dims, dtype)


def iota(dims, axis):
    return lax.broadcasted_iota(jnp.int32, dims, axis)


def params(**more):
    return pltpu.CompilerParams(vmem_limit_bytes=VMEM_LIMIT, **more)


def start_columns(weight, column, target, sems):
    depth, width = target.shape
    part = depth // CHUNKS
    copies = []
    for c in range(CHUNKS):
        rows = pl.ds(c * part, part)
        copies.append(
            pltpu.make_async_copy(
                weight.at[rows, pl.ds(pl.multiple_of(column, width), width)],
                target.at[rows, :],
                sems.at[c],
            )
        )
        copies[-1].start()
    return copies


def adapter_column(refs, bank, count):
    rows = len(refs) * refs[0].shape[0]
    row = iota((rows, HEAD_DIM), 0)
    column = jnp.zeros((rows, HEAD_DIM), jnp.int32)
    for r in range(rows):
        ref = refs[r // refs[0].shape[0]]
        column = jnp.where(row == r, ref[r % ref.shape[0]], column)
    return column - bank * count


def start_slots(parity, ranks, place, bank, w_ref, kv_ref, w_buf, kv_buf, sems, kv_sems):
    count, _, width = w_buf.shape
    copies = []
    for s in range(count):
        target = (2 * s + parity) ^ place[0]
        copies.append(
            start_columns(w_ref, (2 * target + bank[0]) * width, w_buf.at[s], sems.at[s])
            + start_columns(
                kv_ref, (target + ranks * bank[0]) * HEAD_DIM, kv_buf.at[s], kv_sems.at[s]
            )
        )
    return copies


def fetch_kernel(ranks, place, bank, w_ref, kv_ref, down_ref, w_buf, kv_buf, down_buf, *sems):
    copies = start_slots(1, ranks, place, bank, w_ref, kv_ref, w_buf, kv_buf, *sems[:2])
    down_copy = pltpu.make_async_copy(down_ref, down_buf, sems[2])
    down_copy.start()
    for slot in copies:
        for copy in slot:
            copy.wait()
    down_copy.wait()


def slot_buffers(wq, ranks):
    depth, half = wq.shape[0], ranks // 2
    return [
        shape(half, depth, wq.shape[1] // ranks // 2, dtype=BF16),
        shape(half, depth, HEAD_DIM, dtype=BF16),
    ]


def fetch(place, bank, wq, wkv, down, ranks):
    dma = pltpu.SemaphoreType.DMA
    out = slot_buffers(wq, ranks) + [jax.ShapeDtypeStruct(down.shape, BF16)]
    return pl.pallas_call(
        lambda *refs: fetch_kernel(ranks, *refs),
        in_specs=[scalar()] * 2 + [big()] * 3,
        out_specs=[whole()] * 3,
        out_shape=out,
        scratch_shapes=[dma((ranks // 2, CHUNKS)), dma((ranks // 2, CHUNKS)), dma(())],
        compiler_params=params(),
        cost_estimate=pl.CostEstimate(
            flops=0,
            bytes_accessed=wq.size // 2 + wkv.size // 2 + 2 * down.size,
            transcendentals=0,
        ),
        name="fetch",
    )(place, bank, wq, wkv, down)


def beam_rows(x_ref, other_ref):
    rows = [x_ref[...].astype(F32), other_ref[...].astype(F32)]
    return jnp.concatenate(rows, axis=0).astype(BF16)


def project_sent_kernel(
    bank, own_ref, came_ref, x_ref, other_ref, w_buf, kv_buf, down_buf, out, inner, column_out
):
    count, _, width = w_buf.shape
    x = beam_rows(x_ref, other_ref)
    for s in range(count):
        out[s, :, :width] = jnp.dot(x, w_buf[s], preferred_element_type=F32)
        out[s, :, width : width + HEAD_DIM] = jnp.dot(x, kv_buf[s], preferred_element_type=F32)
    adapters, rank, depth = down_buf.shape
    every = lax.dot_general(
        x,
        down_buf[...].reshape(adapters * rank, depth),
        (((1,), (1,)), ((), ())),
        preferred_element_type=F32,
    )
    column = adapter_column((own_ref, came_ref), bank[0], adapters)
    column_out[...] = column
    lane = iota(column.shape, 1)
    per = HEAD_DIM // rank
    total = jnp.zeros(column.shape, F32)
    for j in range(adapters // per):
        part = every[:, j * HEAD_DIM : (j + 1) * HEAD_DIM]
        total += jnp.where(lane // rank + j * per == column, part, 0.0)
    inner[...] = total
    for s in range(count):
        out[s, :, width + HEAD_DIM :] = total


def project_sent(bank, index, x, other, weights):
    half, _, width = weights[0].shape
    rows = 2 * x.shape[0]
    return pl.pallas_call(
        project_sent_kernel,
        in_specs=[scalar()] * 3 + [whole()] * 5,
        out_specs=[whole()] * 3,
        out_shape=[
            shape(half, rows, width + 2 * HEAD_DIM),
            shape(rows, HEAD_DIM),
            shape(rows, HEAD_DIM, dtype=jnp.int32),
        ],
        compiler_params=params(),
        cost_estimate=pl.CostEstimate(
            flops=2 * rows * sum(w.size for w in weights),
            bytes_accessed=2 * sum(w.size for w in weights),
            transcendentals=0,
        ),
        name="project_sent",
    )(bank, *index, x, other, *weights)


def project_kept_kernel(
    ranks, place, bank, length, x_ref, other_ref, w_ref, kv_ref, inner, out, live, *scratch
):
    w_buf, kv_buf = scratch[:2]
    copies = start_slots(0, ranks, place, bank, w_ref, kv_ref, *scratch)
    count, _, width = w_buf.shape
    beams = x_ref.shape[0]
    row = iota(live.shape, 0)
    limit = jnp.zeros(live.shape, jnp.int32)
    for beam in range(beams):
        limit = jnp.where(row // (live.shape[0] // beams) == beam, length[beam], limit)
    live[...] = limit
    x = beam_rows(x_ref, other_ref)
    for s in range(count):
        for copy in copies[s]:
            copy.wait()
        out[s, :, :width] = jnp.dot(x, w_buf[s], preferred_element_type=F32)
        out[s, :, width : width + HEAD_DIM] = jnp.dot(x, kv_buf[s], preferred_element_type=F32)
        out[s, :, width + HEAD_DIM :] = inner[...]


def project_kept(place, bank, length, x, other, wq, wkv, inner, ranks):
    beams, depth = x.shape
    rows = 2 * beams
    buffers = slot_buffers(wq, ranks)
    half, _, width = buffers[0].shape
    dma = pltpu.SemaphoreType.DMA
    return pl.pallas_call(
        lambda *refs: project_kept_kernel(ranks, *refs),
        in_specs=[scalar()] * 3 + [whole()] * 2 + [big()] * 2 + [whole()],
        out_specs=[whole()] * 2,
        out_shape=[
            shape(half, rows, width + 2 * HEAD_DIM),
            shape(beams * wq.shape[1] // ranks // HEAD_DIM, HEAD_DIM, dtype=jnp.int32),
        ],
        scratch_shapes=[pltpu.VMEM(b.shape, BF16) for b in buffers]
        + [dma((half, CHUNKS)), dma((half, CHUNKS))],
        compiler_params=params(),
        cost_estimate=pl.CostEstimate(
            flops=rows * depth * (wq.shape[1] + wkv.shape[1]) // 2,
            bytes_accessed=wq.size + wkv.size,
            transcendentals=0,
        ),
        name="project_kept",
    )(place, bank, length, x, other, wq, wkv, inner)


def correct_kernel(bank, column_ref, kept_ref, came_ref, up_ref, own_out, other_out):
    total = kept_ref[0] + came_ref[0]
    count, rank, width = up_ref.shape
    half = width // 2
    inner = total[:, half + HEAD_DIM :].astype(BF16).astype(F32)
    column = column_ref[...]
    lane = iota(column.shape, 1)
    per = HEAD_DIM // rank
    spread = jnp.concatenate(
        [
            jnp.where(lane // rank + j * per == column, inner, 0.0)
            for j in range(count // per)
        ],
        axis=1,
    ).astype(BF16)
    delta = jnp.dot(
        spread, up_ref[...].reshape(count * rank, width), preferred_element_type=F32
    )
    rows = own_out.shape[0]
    for side in range(2):
        columns = slice(side * half, (side + 1) * half)
        part = delta[:, columns] + jnp.where(bank[0] == side, total[:, :half], 0.0)
        own_out[:, columns] = part[:rows]
        other_out[:, columns] = part[rows:]
    own_out[:, width:] = total[:rows, half : half + HEAD_DIM]
    other_out[:, width:] = total[rows:, half : half + HEAD_DIM]


def correct(bank, column, kept, came, up):
    rows = kept.shape[1]
    out = shape(rows // 2, up.shape[2] + HEAD_DIM)
    return pl.pallas_call(
        correct_kernel,
        in_specs=[scalar()] + [whole()] * 4,
        out_specs=[whole()] * 2,
        out_shape=[out, out],
        compiler_params=params(),
        cost_estimate=pl.CostEstimate(
            flops=2 * rows * up.size, bytes_accessed=2 * up.size, transcendentals=0
        ),
        name="correct",
    )(bank, column, kept, came, up)


def halve_kernel(kept_ref, came_ref, sent_out, kept_out):
    for i in range(kept_out.shape[0]):
        kept_out[i] = kept_ref[2 * i] + came_ref[2 * i]
        sent_out[i] = kept_ref[2 * i + 1] + came_ref[2 * i + 1]


def halve(kept, came):
    half = jax.ShapeDtypeStruct((kept.shape[0] // 2,) + kept.shape[1:], kept.dtype)
    return pl.pallas_call(
        halve_kernel,
        in_specs=[whole()] * 2,
        out_specs=[whole()] * 2,
        out_shape=[half, half],
        compiler_params=params(),
        name="halve",
    )(kept, came)


def rotate(v, cosine, sine):
    return v * cosine + pltpu.roll(v, HEAD_DIM // 2, 1) * sine


def rotate_kernel(bank, own_ref, came_ref, cos_ref, sin_ref, q_ref, k_ref, v_ref, rows_ref):
    width = own_ref.shape[1] - HEAD_DIM
    cosine, sine = cos_ref[...], sin_ref[...]
    for g in range(width // HEAD_DIM):
        columns = slice(g * HEAD_DIM, (g + 1) * HEAD_DIM)
        rows_ref[:, g, :] = rotate(own_ref[:, columns] + came_ref[:, columns], cosine, sine)
    q_ref[0] = rows_ref[...].reshape(q_ref.shape[1:]).astype(BF16)
    own, came = own_ref[:, width:], came_ref[:, width:]
    key = jnp.where(bank[0] == 0, own, came)
    value = jnp.where(bank[0] == 0, came, own)
    k_ref[...] = rotate(key, cosine, sine).astype(BF16).astype(F32)
    v_ref[...] = value.astype(BF16).astype(F32)


def rotated(bank, own, came, cosine, sine):
    rows = own.shape[0]
    heads = own.shape[1] // HEAD_DIM - 1
    return pl.pallas_call(
        rotate_kernel,
        in_specs=[scalar()] + [whole()] * 4,
        out_specs=[whole()] * 3,
        out_shape=[
            shape(1, rows * heads, HEAD_DIM, dtype=BF16),
            shape(rows, HEAD_DIM),
            shape(rows, HEAD_DIM),
        ],
        scratch_shapes=[pltpu.VMEM((rows, heads, HEAD_DIM), F32)],
        compiler_params=params(),
        name="rotate",
    )(bank, own, came, cosine, sine)


def join_kernel(first_ref, second_ref, out_ref):
    half = first_ref.shape[0]
    out_ref[:half] = first_ref[...]
    out_ref[half:] = second_ref[...]


def join(first, second):
    return pl.pallas_call(
        join_kernel,
        in_specs=[whole()] * 2,
        out_specs=whole(),
        out_shape=shape(2 * first.shape[0], *first.shape[1:], dtype=first.dtype),
        compiler_params=params(),
        name="join",
    )(first, second)


def attend_kernel(slots, earlier, place, length_ref, q_ref, k_ref, v_ref, *refs):
    before, out_ref = refs[:-1], refs[-1]
    beams, positions, _ = k_ref.shape
    rows = q_ref.shape[1]
    group = rows // beams
    row, lane = iota((rows, HEAD_DIM), 0), iota((rows, HEAD_DIM), 1)
    left = length_ref[...] - place[0] * positions
    live = jnp.concatenate(
        [lane + first < left for first in range(0, positions, HEAD_DIM)], axis=1
    )
    for i, slot in enumerate(slots):
        head = place[0] ^ slot
        columns = pl.ds(pl.multiple_of(head * HEAD_DIM, HEAD_DIM), HEAD_DIM)
        query = q_ref[i].astype(F32)
        scores = jnp.concatenate(
            [
                lax.dot_general(
                    query[beam * group : (beam + 1) * group].astype(BF16),
                    k_ref[beam, :, columns],
                    (((1,), (1,)), ((), ())),
                    preferred_element_type=F32,
                )
                for beam in range(beams)
            ],
            axis=0,
        ) * (1.0 / HEAD_DIM**0.5)
        scores = jnp.where(live, scores, -1e30)
        peak = jnp.max(scores, axis=1, keepdims=True)
        weights = jnp.where(live, jnp.exp(scores - peak), 0.0)
        total = jnp.sum(weights, axis=1, keepdims=True)
        values = [
            jnp.dot(
                weights[beam * group : (beam + 1) * group].astype(BF16),
                v_ref[beam, :, columns],
                preferred_element_type=F32,
            )
            for beam in range(beams)
        ]
        stats = jnp.where(lane == row % group, peak, 0.0)
        stats += jnp.where(lane == group + row % group, total, 0.0)
        stats = jnp.sum(stats.reshape(beams, group, HEAD_DIM), axis=1)
        high = stats.astype(BF16).astype(F32)
        middle = (stats - high).astype(BF16).astype(F32)
        low = stats - high - middle
        tail = high + pltpu.roll(middle, 2 * group, 1) + pltpu.roll(low, 4 * group, 1)
        block = jnp.concatenate(values + [tail, jnp.zeros_like(tail)], axis=0)
        out_ref[head if earlier else i] = block.astype(BF16)
    if earlier:
        done = [(ref, i) for ref in before for i in range(ref.shape[0])]
        for slot, (ref, i) in zip(earlier, done):
            out_ref[place[0] ^ slot] = ref[i]


def attend(place, length, queries, keys, values, slots, earlier=(), before=()):
    count, rows, _ = queries.shape
    beams, positions, _ = keys.shape
    return pl.pallas_call(
        lambda *refs: attend_kernel(slots, earlier, *refs),
        in_specs=[scalar()] + [whole()] * (4 + len(before)),
        out_specs=whole(),
        out_shape=shape(count + len(earlier), rows + 2 * beams, HEAD_DIM, dtype=BF16),
        compiler_params=params(),
        cost_estimate=pl.CostEstimate(
            flops=4 * rows * count * positions * HEAD_DIM,
            bytes_accessed=4 * beams * positions * HEAD_DIM * (16 if earlier else count),
            transcendentals=rows * count * positions,
        ),
        name="attend",
    )(place, length, queries, keys, values, *before)


def combine_kernel(parts_ref, q_ref, k_ref, v_ref, out_ref, joined):
    ranks = parts_ref.shape[0]
    beams, group, _ = joined.shape
    rows = beams * group

    def by_row(v):
        return jnp.broadcast_to(v[:, None, :], (beams, group, HEAD_DIM)).reshape(rows, HEAD_DIM)

    head = iota((rows, HEAD_DIM), 0) % group
    lane = iota((rows, HEAD_DIM), 1)
    score = jnp.sum(q_ref[0].astype(F32) * by_row(k_ref[...]), axis=1, keepdims=True) * (
        1.0 / HEAD_DIM**0.5
    )
    peaks, totals, weighted = [], [], []
    top = score
    for s in range(ranks):
        block = parts_ref[s].astype(F32)
        tail = block[rows : rows + beams]
        for turn in (2, 4):
            tail += pltpu.roll(block[rows : rows + beams], HEAD_DIM - turn * group, 1)
        tail = by_row(tail)
        peak = jnp.sum(jnp.where(lane == head, tail, 0.0), axis=1, keepdims=True)
        total = jnp.sum(jnp.where(lane == group + head, tail, 0.0), axis=1, keepdims=True)
        top = jnp.maximum(top, peak)
        peaks.append(peak)
        totals.append(total)
        weighted.append(block[:rows])
    new = jnp.exp(score - top)
    everything = new
    result = new.astype(BF16).astype(F32) * by_row(v_ref[...])
    for peak, total, block in zip(peaks, totals, weighted):
        factor = jnp.exp(peak - top)
        everything += total * factor
        result += block * factor
    joined[...] = (result / everything).reshape(joined.shape)
    for g in range(group):
        out_ref[:, g * HEAD_DIM : (g + 1) * HEAD_DIM] = joined[:, g, :].astype(BF16)


def combine(parts, query, key_new, value_new):
    beams = key_new.shape[0]
    group = query.shape[1] // beams
    return pl.pallas_call(
        combine_kernel,
        in_specs=[whole()] * 4,
        out_specs=whole(),
        out_shape=shape(beams, group * HEAD_DIM, dtype=BF16),
        scratch_shapes=[pltpu.VMEM((beams, group, HEAD_DIM), F32)],
        compiler_params=params(),
        name="combine",
    )(parts, query, key_new, value_new)


def output_kernel(x_ref, w_ref, out):
    count, _, width = out.shape
    for s in range(count):
        columns = slice(s * width, (s + 1) * width)
        total = jnp.dot(x_ref[...], w_ref[:, columns], preferred_element_type=F32)
        out[s] = total.astype(BF16)


def output(x, weight, ranks):
    beams = x.shape[0]
    return pl.pallas_call(
        output_kernel,
        in_specs=[whole()] * 2,
        out_specs=whole(),
        out_shape=shape(ranks, beams, weight.shape[1] // ranks, dtype=BF16),
        compiler_params=params(),
        cost_estimate=pl.CostEstimate(
            flops=2 * beams * weight.size, bytes_accessed=2 * weight.size, transcendentals=0
        ),
        name="output",
    )(x, weight)


def residual_kernel(x_ref, parts_ref, out_ref):
    total = jnp.sum(parts_ref[...].astype(F32), axis=0)
    out_ref[...] = (x_ref[...].astype(F32) + total).astype(BF16)


def residual(x, parts):
    return pl.pallas_call(
        residual_kernel,
        in_specs=[whole()] * 2,
        out_specs=whole(),
        out_shape=jax.ShapeDtypeStruct(x.shape, BF16),
        compiler_params=params(),
        name="residual",
    )(x, parts)


def swapped(x):
    return lax.ppermute(x, "bank", [(0, 1), (1, 0)])


def traded(blocks):
    return lax.all_to_all(blocks, "tensor", 0, 0, tiled=True)


def hop(x, bit):
    ranks = lax.axis_size("tensor")
    return lax.ppermute(x, "tensor", [(i, i ^ bit) for i in range(ranks)])


def matched_body(
    normed_hidden_input,
    beam_adapter_index,
    beam_cache_length,
    query_weight,
    keyvalue_weight,
    output_weight,
    lowrank_down_factors,
    lowrank_up_factors,
    paged_key_cache,
    paged_value_cache,
):
    x = normed_hidden_input
    ranks = lax.axis_size("tensor")
    place = lax.axis_index("tensor").astype(jnp.int32).reshape(1)
    bank = lax.axis_index("bank").astype(jnp.int32).reshape(1)
    index = (beam_adapter_index, swapped(beam_adapter_index))
    x_other = swapped(x)
    half = HEAD_DIM // 2
    frequency = jnp.power(500000.0, -2.0 * jnp.arange(half, dtype=F32) / HEAD_DIM)
    angles = beam_cache_length.astype(F32)[:, None] * frequency[None, :]
    cosine = jnp.tile(jnp.cos(angles), (1, 2))
    sine = jnp.sin(angles)
    sine = jnp.concatenate([-sine, sine], axis=1)

    weights = in_hbm(query_weight), in_hbm(keyvalue_weight)
    down = in_hbm(lowrank_down_factors.swapaxes(1, 2))
    odd = fetch(place, bank, *weights, down, ranks)
    sent, inner, column = project_sent(bank, index, x, x_other, odd)
    came = hop(sent, 1)
    kept, length = project_kept(
        place, bank, beam_cache_length, x, x_other, *weights, inner, ranks
    )
    sent, kept = halve(kept, came)
    sent, kept = halve(kept, hop(sent, 2))
    own, other = correct(bank, column, kept, hop(sent, 4), lowrank_up_factors)
    query, key_new, value_new = rotated(bank, own, swapped(other), cosine, sine)

    def attended_part(queries, slots, **more):
        cache = paged_key_cache, paged_value_cache
        return attend(place, length, queries, *cache, slots, **more)

    came, done = lax.optimization_barrier((hop(query, 4), attended_part(query, (0,))))
    gathered = join(query, came)
    second, more = lax.optimization_barrier((hop(gathered, 2), attended_part(came, (4,))))
    came = hop(join(gathered, second), 1)
    done = done, more, attended_part(second, (2, 6))
    partial = attended_part(came, (1, 5, 3, 7), earlier=(0, 4, 2, 6), before=done)
    attended = combine(traded(partial), query, key_new, value_new)
    return residual(x, traded(output(attended, output_weight, ranks)))


def joined(x, axis, combine):
    everything = jax.tree.map(lambda part: lax.all_gather(part, axis), x)
    leading = jax.tree.map(lambda part: part[0], everything)

    def turn(k, so_far):
        return combine(so_far, jax.tree.map(lambda part: part[k], everything))

    return lax.fori_loop(1, lax.axis_size(axis), turn, leading)


def apply_rotary(values, positions, head_size):
    row_count, col_count = values.shape
    half_size = head_size // 2
    frequency = jnp.power(500000.0, -2.0 * jnp.arange(half_size, dtype=jnp.float32) / head_size)
    angles = positions.astype(jnp.float32)[:, None] * frequency[None, :]
    cosine_table = jnp.cos(angles)[:, None, :]
    sine_table = jnp.sin(angles)[:, None, :]
    shaped = values.reshape(row_count, col_count // head_size, 2, half_size)
    first_half = shaped[:, :, 0]
    second_half = shaped[:, :, 1]
    rotated = jnp.stack(
        [
            first_half * cosine_table - second_half * sine_table,
            second_half * cosine_table + first_half * sine_table,
        ],
        axis=2,
    )
    return rotated.reshape(row_count, col_count)


def combine_parts(first_part, second_part):
    peak_one, total_one, weighted_one = first_part
    peak_two, total_two, weighted_two = second_part
    peak_both = jnp.maximum(peak_one, peak_two)
    factor_one = jnp.exp(peak_one - peak_both)
    factor_two = jnp.exp(peak_two - peak_both)
    return (
        peak_both,
        total_one * factor_one + total_two * factor_two,
        weighted_one * factor_one[..., None] + weighted_two * factor_two[..., None],
    )


def finish_heads(peak_score, weight_total, weighted, score_new, value_rows):
    peak_final = jnp.maximum(peak_score, score_new)
    old_factor = jnp.exp(peak_score - peak_final)
    new_weight = jnp.exp(score_new - peak_final)
    weight_total = weight_total * old_factor + new_weight
    weighted = (
        weighted * old_factor[..., None]
        + new_weight.astype(jnp.bfloat16).astype(jnp.float32)[..., None] * value_rows
    )
    return weighted / weight_total[..., None]


def body(
    normed_hidden_input,
    beam_adapter_index,
    beam_cache_length,
    query_weight,
    keyvalue_weight,
    output_weight,
    lowrank_down_factors,
    lowrank_up_factors,
    paged_key_cache,
    paged_value_cache,
):
    beam_rows, width_part = normed_hidden_input.shape
    model_width = query_weight.shape[1]
    kv_width = keyvalue_weight.shape[1] // 2
    head_count = model_width // HEAD_DIM
    kv_heads = kv_width // HEAD_DIM
    group_size = head_count // kv_heads
    tensor_index = lax.axis_index("tensor")
    query_part = jnp.dot(normed_hidden_input, query_weight, preferred_element_type=jnp.float32)
    keyval_part = jnp.dot(normed_hidden_input, keyvalue_weight, preferred_element_type=jnp.float32)
    down_all, up_all = (
        lax.all_gather(lowrank_down_factors, "bank", axis=0, tiled=True),
        lax.all_gather(lowrank_up_factors, "bank", axis=0, tiled=True),
    )
    inner_part = jnp.einsum(
        "ci,cim->cm",
        normed_hidden_input,
        down_all[beam_adapter_index],
        preferred_element_type=jnp.float32,
    )
    inner_total = lax.psum(inner_part, "tensor").astype(jnp.bfloat16)
    lowrank_delta = jnp.einsum(
        "mc,mct->mt", inner_total, up_all[beam_adapter_index], preferred_element_type=jnp.float32
    )
    query_total, keyval = lax.psum((query_part, keyval_part), "tensor")
    delta_total = lax.all_gather(lowrank_delta, "tensor", axis=1, tiled=True)
    query_rotated = apply_rotary(query_total + delta_total, beam_cache_length, HEAD_DIM).astype(
        jnp.bfloat16
    )
    key_new = apply_rotary(keyval[:, :kv_width], beam_cache_length, HEAD_DIM).astype(jnp.bfloat16)
    value_new = keyval[:, kv_width:].astype(jnp.bfloat16)
    position_count = paged_key_cache.shape[1]
    query_heads = query_rotated.reshape(beam_rows, kv_heads, group_size, HEAD_DIM)
    key_block = paged_key_cache.reshape(beam_rows, position_count, kv_heads, HEAD_DIM)
    value_block = paged_value_cache.reshape(beam_rows, position_count, kv_heads, HEAD_DIM)
    score_scale = 1.0 / HEAD_DIM**0.5
    scores = (
        jnp.einsum("bkgh,bpkh->bkgp", query_heads, key_block, preferred_element_type=jnp.float32)
        * score_scale
    )
    position_ids = tensor_index * position_count + jnp.arange(position_count)
    live_mask = (position_ids[None, :] < beam_cache_length[:, None])[:, None, None, :]
    scores = jnp.where(live_mask, scores, -1e30)
    peak_score = jnp.max(scores, axis=-1)
    weights = jnp.where(live_mask, jnp.exp(scores - peak_score[..., None]), 0.0)
    weight_total = jnp.sum(weights, axis=-1)
    weighted = jnp.einsum(
        "bkgp,bpkh->bkgh",
        weights.astype(jnp.bfloat16),
        value_block,
        preferred_element_type=jnp.float32,
    )
    peak_score, weight_total, weighted = joined(
        (peak_score, weight_total, weighted), "tensor", combine_parts
    )
    score_new = (
        jnp.einsum(
            "bkgh,bkh->bkg",
            query_heads,
            key_new.reshape(beam_rows, kv_heads, HEAD_DIM),
            preferred_element_type=jnp.float32,
        )
        * score_scale
    )
    value_rows = value_new.reshape(beam_rows, kv_heads, HEAD_DIM).astype(jnp.float32)[:, :, None, :]
    attended = (
        finish_heads(peak_score, weight_total, weighted, score_new, value_rows)
        .reshape(beam_rows, model_width)
        .astype(jnp.bfloat16)
    )
    attended_cols = lax.dynamic_slice_in_dim(attended, tensor_index * width_part, width_part, 1)
    mixed_cols = lax.psum_scatter(
        lax.dot_general(
            output_weight,
            attended_cols,
            (((0,), (1,)), ((), ())),
            preferred_element_type=jnp.float32,
        ),
        "tensor",
        scatter_dimension=0,
        tiled=True,
    )
    return (normed_hidden_input.astype(jnp.float32) + mixed_cols.T).astype(jnp.bfloat16)


def solution(mesh):
    matched = mesh.shape["tensor"] == 8 and mesh.shape["bank"] == 2
    return jax.shard_map(
        matched_body if matched else body,
        mesh=mesh,
        in_specs=(
            P(("groups", "bank"), "tensor"),
            P(("groups", "bank")),
            P(("groups", "bank")),
            P("tensor", None),
            P("tensor", None),
            P("tensor", None),
            P("bank", "tensor", None),
            P("bank", None, "tensor"),
            P(("groups", "bank"), "tensor", None),
            P(("groups", "bank"), "tensor", None),
        ),
        out_specs=P(("groups", "bank"), "tensor"),
        check_vma=False,
    )
```

```python
import jax
import jax.numpy as jnp
from jax import lax
from jax.experimental import pallas as pl
from jax.experimental.pallas import tpu as pltpu
from jax.sharding import PartitionSpec as P

HEAD_DIM = 128
F32 = jnp.float32
BF16 = jnp.bfloat16
CHUNKS = 2
MIB = 1024 * 1024


def whole():
    return pl.BlockSpec(memory_space=pltpu.VMEM)


def big():
    return pl.BlockSpec(memory_space=pltpu.HBM)


def scalar():
    return pl.BlockSpec(memory_space=pltpu.SMEM)


def in_hbm(array):
    return pltpu.with_memory_space_constraint(array, pltpu.HBM)


def shape(*dims, dtype=F32):
    return jax.ShapeDtypeStruct(dims, dtype)


def iota(dims, axis):
    return lax.broadcasted_iota(jnp.int32, dims, axis)


def params(mib=4):
    return pltpu.CompilerParams(vmem_limit_bytes=mib * MIB)


def start_columns(weight, column, target, sems):
    depth, width = target.shape
    part = depth // CHUNKS
    copies = []
    for c in range(CHUNKS):
        rows = pl.ds(c * part, part)
        copies.append(
            pltpu.make_async_copy(
                weight.at[rows, pl.ds(pl.multiple_of(column, width), width)],
                target.at[rows, :],
                sems.at[c],
            )
        )
        copies[-1].start()
    return copies


def adapter_column(refs, bank, count):
    rows = len(refs) * refs[0].shape[0]
    row = iota((rows, HEAD_DIM), 0)
    column = jnp.zeros((rows, HEAD_DIM), jnp.int32)
    for r in range(rows):
        ref = refs[r // refs[0].shape[0]]
        column = jnp.where(row == r, ref[r % ref.shape[0]], column)
    return column - bank * count


def start_slots(parity, first, ranks, place, bank, w_ref, kv_ref, w_buf, kv_buf, sems, kv_sems):
    count, _, width = w_buf.shape
    copies = []
    for s in range(count):
        target = (2 * (first + s) + parity) ^ place[0]
        copies.append(
            start_columns(w_ref, (2 * target + bank[0]) * width, w_buf.at[s], sems.at[s])
            + start_columns(
                kv_ref, (target + ranks * bank[0]) * HEAD_DIM, kv_buf.at[s], kv_sems.at[s]
            )
        )
    return copies


def wait_all(copies):
    for slot in copies:
        for copy in slot:
            copy.wait()


def fetch_kernel(ranks, place, bank, w_ref, kv_ref, down_ref, w_buf, kv_buf, down_buf, *sems):
    down_copy = pltpu.make_async_copy(down_ref, down_buf, sems[2])
    down_copy.start()
    wait_all(start_slots(1, 0, ranks, place, bank, w_ref, kv_ref, w_buf, kv_buf, *sems[:2]))
    down_copy.wait()


def slot_buffers(wq, ranks, count):
    depth = wq.shape[0]
    return [
        shape(count, depth, wq.shape[1] // ranks // 2, dtype=BF16),
        shape(count, depth, HEAD_DIM, dtype=BF16),
    ]


def slot_sems(count):
    return [pltpu.SemaphoreType.DMA((count, CHUNKS))] * 2


def fetch(place, bank, wq, wkv, down, ranks):
    out = slot_buffers(wq, ranks, 1) + [jax.ShapeDtypeStruct(down.shape, BF16)]
    return pl.pallas_call(
        lambda *refs: fetch_kernel(ranks, *refs),
        in_specs=[scalar()] * 2 + [big()] * 3,
        out_specs=[whole()] * 3,
        out_shape=out,
        scratch_shapes=slot_sems(1) + [pltpu.SemaphoreType.DMA(())],
        compiler_params=params(),
        cost_estimate=pl.CostEstimate(
            flops=0, bytes_accessed=2 * sum(o.size for o in out), transcendentals=0
        ),
        name="fetch",
    )(place, bank, wq, wkv, down)


def beam_rows(x_ref, other_ref):
    rows = [x_ref[...].astype(F32), other_ref[...].astype(F32)]
    return jnp.concatenate(rows, axis=0).astype(BF16)


def project_slot(x, w, kv, out):
    width = w.shape[1]
    out[:, :width] = jnp.dot(x, w[...], preferred_element_type=F32)
    out[:, width : width + HEAD_DIM] = jnp.dot(x, kv[...], preferred_element_type=F32)


def project_sent_kernel(ranks, place, bank, own_ref, came_ref, *refs):
    x_ref, other_ref, w_ref, kv_ref, w_first, kv_first, down_buf, out, inner, column_out = refs[:10]
    w_buf, kv_buf = refs[10:12]
    copies = start_slots(1, 1, ranks, place, bank, w_ref, kv_ref, *refs[10:])
    width = w_first.shape[2]
    x = beam_rows(x_ref, other_ref)
    adapters, rank, depth = down_buf.shape
    every = lax.dot_general(
        x,
        down_buf[...].reshape(adapters * rank, depth),
        (((1,), (1,)), ((), ())),
        preferred_element_type=F32,
    )
    column = adapter_column((own_ref, came_ref), bank[0], adapters)
    column_out[...] = column
    lane = iota(column.shape, 1)
    per = HEAD_DIM // rank
    total = jnp.zeros(column.shape, F32)
    for j in range(adapters // per):
        part = every[:, j * HEAD_DIM : (j + 1) * HEAD_DIM]
        total += jnp.where(lane // rank + j * per == column, part, 0.0)
    inner[...] = total
    for s in range(out.shape[0]):
        out[s, :, width + HEAD_DIM :] = total
    project_slot(x, w_first.at[0], kv_first.at[0], out.at[0])
    for s, slot in enumerate(copies):
        wait_all([slot])
        project_slot(x, w_buf.at[s], kv_buf.at[s], out.at[s + 1])


def project_sent(place, bank, index, x, other, wq, wkv, ahead, ranks):
    rows, half = 2 * x.shape[0], ranks // 2
    buffers = slot_buffers(wq, ranks, half - 1)
    return pl.pallas_call(
        lambda *refs: project_sent_kernel(ranks, *refs),
        in_specs=[scalar()] * 4 + [whole()] * 2 + [big()] * 2 + [whole()] * 3,
        out_specs=[whole()] * 3,
        out_shape=[
            shape(half, rows, wq.shape[1] // ranks // 2 + 2 * HEAD_DIM),
            shape(rows, HEAD_DIM),
            shape(rows, HEAD_DIM, dtype=jnp.int32),
        ],
        scratch_shapes=[pltpu.VMEM(b.shape, BF16) for b in buffers] + slot_sems(half - 1),
        compiler_params=params(8),
        cost_estimate=pl.CostEstimate(
            flops=rows * (wq.size + wkv.size) // 2,
            bytes_accessed=(wq.size + wkv.size) // 2,
            transcendentals=0,
        ),
        name="project_sent",
    )(place, bank, *index, x, other, wq, wkv, *ahead)


def project_kept_kernel(
    ranks, place, bank, length, x_ref, other_ref, w_ref, kv_ref, inner, out, live, *scratch
):
    w_buf, kv_buf = scratch[:2]
    copies = start_slots(0, 0, ranks, place, bank, w_ref, kv_ref, *scratch)
    width = w_buf.shape[2]
    beams = x_ref.shape[0]
    row = iota(live.shape, 0)
    limit = jnp.zeros(live.shape, jnp.int32)
    for beam in range(beams):
        limit = jnp.where(row // (live.shape[0] // beams) == beam, length[beam], limit)
    live[...] = limit
    x = beam_rows(x_ref, other_ref)
    for s, slot in enumerate(copies):
        wait_all([slot])
        project_slot(x, w_buf.at[s], kv_buf.at[s], out.at[s])
        out[s, :, width + HEAD_DIM :] = inner[...]


def project_kept(place, bank, length, x, other, wq, wkv, inner, ranks):
    beams, depth = x.shape
    rows = 2 * beams
    half = ranks // 2
    buffers = slot_buffers(wq, ranks, half)
    return pl.pallas_call(
        lambda *refs: project_kept_kernel(ranks, *refs),
        in_specs=[scalar()] * 3 + [whole()] * 2 + [big()] * 2 + [whole()],
        out_specs=[whole()] * 2,
        out_shape=[
            shape(half, rows, buffers[0].shape[2] + 2 * HEAD_DIM),
            shape(beams * wq.shape[1] // ranks // HEAD_DIM, HEAD_DIM, dtype=jnp.int32),
        ],
        scratch_shapes=[pltpu.VMEM(b.shape, BF16) for b in buffers] + slot_sems(half),
        compiler_params=params(8),
        cost_estimate=pl.CostEstimate(
            flops=rows * depth * (wq.shape[1] + wkv.shape[1]) // 2,
            bytes_accessed=wq.size + wkv.size,
            transcendentals=0,
        ),
        name="project_kept",
    )(place, bank, length, x, other, wq, wkv, inner)


def correct_kernel(bank, column_ref, kept_ref, came_ref, up_ref, own_out, other_out):
    total = kept_ref[0] + came_ref[0]
    count, rank, width = up_ref.shape
    half = width // 2
    inner = total[:, half + HEAD_DIM :].astype(BF16).astype(F32)
    column = column_ref[...]
    lane = iota(column.shape, 1)
    per = HEAD_DIM // rank
    spread = jnp.concatenate(
        [
            jnp.where(lane // rank + j * per == column, inner, 0.0)
            for j in range(count // per)
        ],
        axis=1,
    ).astype(BF16)
    delta = jnp.dot(
        spread, up_ref[...].reshape(count * rank, width), preferred_element_type=F32
    )
    rows = own_out.shape[0]
    for side in range(2):
        columns = slice(side * half, (side + 1) * half)
        part = delta[:, columns] + jnp.where(bank[0] == side, total[:, :half], 0.0)
        own_out[:, columns] = part[:rows]
        other_out[:, columns] = part[rows:]
    own_out[:, width:] = total[:rows, half : half + HEAD_DIM]
    other_out[:, width:] = total[rows:, half : half + HEAD_DIM]


def correct(bank, column, kept, came, up):
    rows = kept.shape[1]
    out = shape(rows // 2, up.shape[2] + HEAD_DIM)
    return pl.pallas_call(
        correct_kernel,
        in_specs=[scalar()] + [whole()] * 4,
        out_specs=[whole()] * 2,
        out_shape=[out, out],
        compiler_params=params(),
        cost_estimate=pl.CostEstimate(
            flops=2 * rows * up.size, bytes_accessed=2 * up.size, transcendentals=0
        ),
        name="correct",
    )(bank, column, kept, came, up)


def halve_kernel(kept_ref, came_ref, sent_out, kept_out):
    for i in range(kept_out.shape[0]):
        kept_out[i] = kept_ref[2 * i] + came_ref[2 * i]
        sent_out[i] = kept_ref[2 * i + 1] + came_ref[2 * i + 1]


def halve(kept, came):
    half = jax.ShapeDtypeStruct((kept.shape[0] // 2,) + kept.shape[1:], kept.dtype)
    return pl.pallas_call(
        halve_kernel,
        in_specs=[whole()] * 2,
        out_specs=[whole()] * 2,
        out_shape=[half, half],
        compiler_params=params(),
        name="halve",
    )(kept, came)


def rotate(v, cosine, sine):
    return v * cosine + pltpu.roll(v, HEAD_DIM // 2, 1) * sine


def rotate_kernel(bank, own_ref, came_ref, cos_ref, sin_ref, q_ref, k_ref, v_ref, rows_ref):
    width = own_ref.shape[1] - HEAD_DIM
    cosine, sine = cos_ref[...], sin_ref[...]
    for g in range(width // HEAD_DIM):
        columns = slice(g * HEAD_DIM, (g + 1) * HEAD_DIM)
        rows_ref[:, g, :] = rotate(own_ref[:, columns] + came_ref[:, columns], cosine, sine)
    q_ref[0] = rows_ref[...].reshape(q_ref.shape[1:]).astype(BF16)
    own, came = own_ref[:, width:], came_ref[:, width:]
    key = jnp.where(bank[0] == 0, own, came)
    value = jnp.where(bank[0] == 0, came, own)
    k_ref[...] = rotate(key, cosine, sine).astype(BF16).astype(F32)
    v_ref[...] = value.astype(BF16).astype(F32)


def rotated(bank, own, came, cosine, sine):
    rows = own.shape[0]
    heads = own.shape[1] // HEAD_DIM - 1
    return pl.pallas_call(
        rotate_kernel,
        in_specs=[scalar()] + [whole()] * 4,
        out_specs=[whole()] * 3,
        out_shape=[
            shape(1, rows * heads, HEAD_DIM, dtype=BF16),
            shape(rows, HEAD_DIM),
            shape(rows, HEAD_DIM),
        ],
        scratch_shapes=[pltpu.VMEM((rows, heads, HEAD_DIM), F32)],
        compiler_params=params(),
        name="rotate",
    )(bank, own, came, cosine, sine)


def join_kernel(first_ref, second_ref, out_ref):
    half = first_ref.shape[0]
    out_ref[:half] = first_ref[...]
    out_ref[half:] = second_ref[...]


def join(first, second):
    return pl.pallas_call(
        join_kernel,
        in_specs=[whole()] * 2,
        out_specs=whole(),
        out_shape=shape(2 * first.shape[0], *first.shape[1:], dtype=first.dtype),
        compiler_params=params(),
        name="join",
    )(first, second)


def attend_kernel(slots, earlier, place, length_ref, q_ref, k_ref, v_ref, *refs):
    before, out_ref = refs[:-1], refs[-1]
    beams, positions, _ = k_ref.shape
    rows = q_ref.shape[1]
    group = rows // beams
    row, lane = iota((rows, HEAD_DIM), 0), iota((rows, HEAD_DIM), 1)
    left = length_ref[...] - place[0] * positions
    live = jnp.concatenate(
        [lane + first < left for first in range(0, positions, HEAD_DIM)], axis=1
    )
    for i, slot in enumerate(slots):
        head = place[0] ^ slot
        columns = pl.ds(pl.multiple_of(head * HEAD_DIM, HEAD_DIM), HEAD_DIM)
        query = q_ref[i].astype(F32)
        scores = jnp.concatenate(
            [
                lax.dot_general(
                    query[beam * group : (beam + 1) * group].astype(BF16),
                    k_ref[beam, :, columns],
                    (((1,), (1,)), ((), ())),
                    preferred_element_type=F32,
                )
                for beam in range(beams)
            ],
            axis=0,
        ) * (1.0 / HEAD_DIM**0.5)
        scores = jnp.where(live, scores, -1e30)
        peak = jnp.max(scores, axis=1, keepdims=True)
        weights = jnp.where(live, jnp.exp(scores - peak), 0.0)
        total = jnp.sum(weights, axis=1, keepdims=True)
        values = [
            jnp.dot(
                weights[beam * group : (beam + 1) * group].astype(BF16),
                v_ref[beam, :, columns],
                preferred_element_type=F32,
            )
            for beam in range(beams)
        ]
        stats = jnp.where(lane == row % group, peak, 0.0)
        stats += jnp.where(lane == group + row % group, total, 0.0)
        stats = jnp.sum(stats.reshape(beams, group, HEAD_DIM), axis=1)
        high = stats.astype(BF16).astype(F32)
        middle = (stats - high).astype(BF16).astype(F32)
        low = stats - high - middle
        tail = high + pltpu.roll(middle, 2 * group, 1) + pltpu.roll(low, 4 * group, 1)
        block = jnp.concatenate(values + [tail, jnp.zeros_like(tail)], axis=0)
        out_ref[head if earlier else i] = block.astype(BF16)
    if earlier:
        done = [(ref, i) for ref in before for i in range(ref.shape[0])]
        for slot, (ref, i) in zip(earlier, done):
            out_ref[place[0] ^ slot] = ref[i]


def attend(place, length, queries, keys, values, slots, earlier=(), before=()):
    count, rows, _ = queries.shape
    beams, positions, _ = keys.shape
    return pl.pallas_call(
        lambda *refs: attend_kernel(slots, earlier, *refs),
        in_specs=[scalar()] + [whole()] * (4 + len(before)),
        out_specs=whole(),
        out_shape=shape(count + len(earlier), rows + 2 * beams, HEAD_DIM, dtype=BF16),
        compiler_params=params(),
        cost_estimate=pl.CostEstimate(
            flops=4 * rows * count * positions * HEAD_DIM,
            bytes_accessed=4 * beams * positions * HEAD_DIM * (16 if earlier else count),
            transcendentals=rows * count * positions,
        ),
        name="attend",
    )(place, length, queries, keys, values, *before)


def combine_kernel(parts_ref, q_ref, k_ref, v_ref, out_ref, joined):
    ranks = parts_ref.shape[0]
    beams, group, _ = joined.shape
    rows = beams * group

    def by_row(v):
        return jnp.broadcast_to(v[:, None, :], (beams, group, HEAD_DIM)).reshape(rows, HEAD_DIM)

    head = iota((rows, HEAD_DIM), 0) % group
    lane = iota((rows, HEAD_DIM), 1)
    score = jnp.sum(q_ref[0].astype(F32) * by_row(k_ref[...]), axis=1, keepdims=True) * (
        1.0 / HEAD_DIM**0.5
    )
    peaks, totals, weighted = [], [], []
    top = score
    for s in range(ranks):
        block = parts_ref[s].astype(F32)
        tail = block[rows : rows + beams]
        for turn in (2, 4):
            tail += pltpu.roll(block[rows : rows + beams], HEAD_DIM - turn * group, 1)
        tail = by_row(tail)
        peak = jnp.sum(jnp.where(lane == head, tail, 0.0), axis=1, keepdims=True)
        total = jnp.sum(jnp.where(lane == group + head, tail, 0.0), axis=1, keepdims=True)
        top = jnp.maximum(top, peak)
        peaks.append(peak)
        totals.append(total)
        weighted.append(block[:rows])
    new = jnp.exp(score - top)
    everything = new
    result = new.astype(BF16).astype(F32) * by_row(v_ref[...])
    for peak, total, block in zip(peaks, totals, weighted):
        factor = jnp.exp(peak - top)
        everything += total * factor
        result += block * factor
    joined[...] = (result / everything).reshape(joined.shape)
    for g in range(group):
        out_ref[:, g * HEAD_DIM : (g + 1) * HEAD_DIM] = joined[:, g, :].astype(BF16)


def combine(parts, query, key_new, value_new):
    beams = key_new.shape[0]
    group = query.shape[1] // beams
    return pl.pallas_call(
        combine_kernel,
        in_specs=[whole()] * 4,
        out_specs=whole(),
        out_shape=shape(beams, group * HEAD_DIM, dtype=BF16),
        scratch_shapes=[pltpu.VMEM((beams, group, HEAD_DIM), F32)],
        compiler_params=params(),
        name="combine",
    )(parts, query, key_new, value_new)


def output_kernel(x_ref, w_ref, out):
    count, _, width = out.shape
    for s in range(count):
        columns = slice(s * width, (s + 1) * width)
        total = jnp.dot(x_ref[...], w_ref[:, columns], preferred_element_type=F32)
        out[s] = total.astype(BF16)


def output(x, weight, ranks):
    beams = x.shape[0]
    return pl.pallas_call(
        output_kernel,
        in_specs=[whole()] * 2,
        out_specs=whole(),
        out_shape=shape(ranks, beams, weight.shape[1] // ranks, dtype=BF16),
        compiler_params=params(),
        cost_estimate=pl.CostEstimate(
            flops=2 * beams * weight.size, bytes_accessed=2 * weight.size, transcendentals=0
        ),
        name="output",
    )(x, weight)


def residual_kernel(x_ref, parts_ref, out_ref):
    total = jnp.sum(parts_ref[...].astype(F32), axis=0)
    out_ref[...] = (x_ref[...].astype(F32) + total).astype(BF16)


def residual(x, parts):
    return pl.pallas_call(
        residual_kernel,
        in_specs=[whole()] * 2,
        out_specs=whole(),
        out_shape=jax.ShapeDtypeStruct(x.shape, BF16),
        compiler_params=params(),
        name="residual",
    )(x, parts)


def swapped(x):
    return lax.ppermute(x, "bank", [(0, 1), (1, 0)])


def traded(blocks):
    return lax.all_to_all(blocks, "tensor", 0, 0, tiled=True)


def hop(x, bit):
    ranks = lax.axis_size("tensor")
    return lax.ppermute(x, "tensor", [(i, i ^ bit) for i in range(ranks)])


def matched_body(
    normed_hidden_input,
    beam_adapter_index,
    beam_cache_length,
    query_weight,
    keyvalue_weight,
    output_weight,
    lowrank_down_factors,
    lowrank_up_factors,
    paged_key_cache,
    paged_value_cache,
):
    x = normed_hidden_input
    ranks = lax.axis_size("tensor")
    place = lax.axis_index("tensor").astype(jnp.int32).reshape(1)
    bank = lax.axis_index("bank").astype(jnp.int32).reshape(1)
    index = (beam_adapter_index, swapped(beam_adapter_index))
    x_other = swapped(x)
    lane = jnp.arange(HEAD_DIM, dtype=jnp.int32)
    half = HEAD_DIM // 2
    frequency = jnp.power(500000.0, -2.0 * (lane % half).astype(F32) / HEAD_DIM)
    angles = beam_cache_length.astype(F32)[:, None] * frequency[None, :]
    cosine = jnp.cos(angles)
    sine = jnp.where(lane < half, -1.0, 1.0) * jnp.sin(angles)
    weights = in_hbm(query_weight), in_hbm(keyvalue_weight)
    down = in_hbm(lowrank_down_factors.swapaxes(1, 2))
    ahead = fetch(place, bank, *weights, down, ranks)
    sent, inner, column = project_sent(
        place, bank, index, x, x_other, *weights, ahead, ranks
    )
    came = hop(sent, 1)
    kept, length = project_kept(
        place, bank, beam_cache_length, x, x_other, *weights, inner, ranks
    )
    sent, kept = halve(kept, came)
    sent, kept = halve(kept, hop(sent, 2))
    own, other = correct(bank, column, kept, hop(sent, 4), lowrank_up_factors)
    query, key_new, value_new = rotated(bank, own, swapped(other), cosine, sine)

    def attended_part(queries, slots, **more):
        cache = paged_key_cache, paged_value_cache
        return attend(place, length, queries, *cache, slots, **more)

    came, done = lax.optimization_barrier((hop(query, 4), attended_part(query, (0,))))
    gathered = join(query, came)
    second, more = lax.optimization_barrier((hop(gathered, 2), attended_part(came, (4,))))
    came = hop(join(gathered, second), 1)
    done = done, more, attended_part(second, (2, 6))
    partial = attended_part(came, (1, 5, 3, 7), earlier=(0, 4, 2, 6), before=done)
    attended = combine(traded(partial), query, key_new, value_new)
    return residual(x, traded(output(attended, output_weight, ranks)))


def joined(x, axis, combine):
    everything = jax.tree.map(lambda part: lax.all_gather(part, axis), x)
    leading = jax.tree.map(lambda part: part[0], everything)

    def turn(k, so_far):
        return combine(so_far, jax.tree.map(lambda part: part[k], everything))

    return lax.fori_loop(1, lax.axis_size(axis), turn, leading)


def apply_rotary(values, positions, head_size):
    row_count, col_count = values.shape
    half_size = head_size // 2
    frequency = jnp.power(500000.0, -2.0 * jnp.arange(half_size, dtype=jnp.float32) / head_size)
    angles = positions.astype(jnp.float32)[:, None] * frequency[None, :]
    cosine_table = jnp.cos(angles)[:, None, :]
    sine_table = jnp.sin(angles)[:, None, :]
    shaped = values.reshape(row_count, col_count // head_size, 2, half_size)
    first_half = shaped[:, :, 0]
    second_half = shaped[:, :, 1]
    rotated = jnp.stack(
        [
            first_half * cosine_table - second_half * sine_table,
            second_half * cosine_table + first_half * sine_table,
        ],
        axis=2,
    )
    return rotated.reshape(row_count, col_count)


def combine_parts(first_part, second_part):
    peak_one, total_one, weighted_one = first_part
    peak_two, total_two, weighted_two = second_part
    peak_both = jnp.maximum(peak_one, peak_two)
    factor_one = jnp.exp(peak_one - peak_both)
    factor_two = jnp.exp(peak_two - peak_both)
    return (
        peak_both,
        total_one * factor_one + total_two * factor_two,
        weighted_one * factor_one[..., None] + weighted_two * factor_two[..., None],
    )


def finish_heads(peak_score, weight_total, weighted, score_new, value_rows):
    peak_final = jnp.maximum(peak_score, score_new)
    old_factor = jnp.exp(peak_score - peak_final)
    new_weight = jnp.exp(score_new - peak_final)
    weight_total = weight_total * old_factor + new_weight
    weighted = (
        weighted * old_factor[..., None]
        + new_weight.astype(jnp.bfloat16).astype(jnp.float32)[..., None] * value_rows
    )
    return weighted / weight_total[..., None]


def body(
    normed_hidden_input,
    beam_adapter_index,
    beam_cache_length,
    query_weight,
    keyvalue_weight,
    output_weight,
    lowrank_down_factors,
    lowrank_up_factors,
    paged_key_cache,
    paged_value_cache,
):
    beam_rows, width_part = normed_hidden_input.shape
    model_width = query_weight.shape[1]
    kv_width = keyvalue_weight.shape[1] // 2
    head_count = model_width // HEAD_DIM
    kv_heads = kv_width // HEAD_DIM
    group_size = head_count // kv_heads
    tensor_index = lax.axis_index("tensor")
    query_part = jnp.dot(normed_hidden_input, query_weight, preferred_element_type=jnp.float32)
    keyval_part = jnp.dot(normed_hidden_input, keyvalue_weight, preferred_element_type=jnp.float32)
    down_all, up_all = (
        lax.all_gather(lowrank_down_factors, "bank", axis=0, tiled=True),
        lax.all_gather(lowrank_up_factors, "bank", axis=0, tiled=True),
    )
    inner_part = jnp.einsum(
        "ci,cim->cm",
        normed_hidden_input,
        down_all[beam_adapter_index],
        preferred_element_type=jnp.float32,
    )
    inner_total = lax.psum(inner_part, "tensor").astype(jnp.bfloat16)
    lowrank_delta = jnp.einsum(
        "mc,mct->mt", inner_total, up_all[beam_adapter_index], preferred_element_type=jnp.float32
    )
    query_total, keyval = lax.psum((query_part, keyval_part), "tensor")
    delta_total = lax.all_gather(lowrank_delta, "tensor", axis=1, tiled=True)
    query_rotated = apply_rotary(query_total + delta_total, beam_cache_length, HEAD_DIM).astype(
        jnp.bfloat16
    )
    key_new = apply_rotary(keyval[:, :kv_width], beam_cache_length, HEAD_DIM).astype(jnp.bfloat16)
    value_new = keyval[:, kv_width:].astype(jnp.bfloat16)
    position_count = paged_key_cache.shape[1]
    query_heads = query_rotated.reshape(beam_rows, kv_heads, group_size, HEAD_DIM)
    key_block = paged_key_cache.reshape(beam_rows, position_count, kv_heads, HEAD_DIM)
    value_block = paged_value_cache.reshape(beam_rows, position_count, kv_heads, HEAD_DIM)
    score_scale = 1.0 / HEAD_DIM**0.5
    scores = (
        jnp.einsum("bkgh,bpkh->bkgp", query_heads, key_block, preferred_element_type=jnp.float32)
        * score_scale
    )
    position_ids = tensor_index * position_count + jnp.arange(position_count)
    live_mask = (position_ids[None, :] < beam_cache_length[:, None])[:, None, None, :]
    scores = jnp.where(live_mask, scores, -1e30)
    peak_score = jnp.max(scores, axis=-1)
    weights = jnp.where(live_mask, jnp.exp(scores - peak_score[..., None]), 0.0)
    weight_total = jnp.sum(weights, axis=-1)
    weighted = jnp.einsum(
        "bkgp,bpkh->bkgh",
        weights.astype(jnp.bfloat16),
        value_block,
        preferred_element_type=jnp.float32,
    )
    peak_score, weight_total, weighted = joined(
        (peak_score, weight_total, weighted), "tensor", combine_parts
    )
    score_new = (
        jnp.einsum(
            "bkgh,bkh->bkg",
            query_heads,
            key_new.reshape(beam_rows, kv_heads, HEAD_DIM),
            preferred_element_type=jnp.float32,
        )
        * score_scale
    )
    value_rows = value_new.reshape(beam_rows, kv_heads, HEAD_DIM).astype(jnp.float32)[:, :, None, :]
    attended = (
        finish_heads(peak_score, weight_total, weighted, score_new, value_rows)
        .reshape(beam_rows, model_width)
        .astype(jnp.bfloat16)
    )
    attended_cols = lax.dynamic_slice_in_dim(attended, tensor_index * width_part, width_part, 1)
    mixed_cols = lax.psum_scatter(
        lax.dot_general(
            output_weight,
            attended_cols,
            (((0,), (1,)), ((), ())),
            preferred_element_type=jnp.float32,
        ),
        "tensor",
        scatter_dimension=0,
        tiled=True,
    )
    return (normed_hidden_input.astype(jnp.float32) + mixed_cols.T).astype(jnp.bfloat16)


def solution(mesh):
    matched = mesh.shape["tensor"] == 8 and mesh.shape["bank"] == 2
    return jax.shard_map(
        matched_body if matched else body,
        mesh=mesh,
        in_specs=(
            P(("groups", "bank"), "tensor"),
            P(("groups", "bank")),
            P(("groups", "bank")),
            P("tensor", None),
            P("tensor", None),
            P("tensor", None),
            P("bank", "tensor", None),
            P("bank", None, "tensor"),
            P(("groups", "bank"), "tensor", None),
            P(("groups", "bank"), "tensor", None),
        ),
        out_specs=P(("groups", "bank"), "tensor"),
        check_vma=False,
    )
```

```python
import jax
import jax.numpy as jnp
from jax import lax
from jax.experimental import pallas as pl
from jax.experimental.pallas import tpu as pltpu
from jax.sharding import PartitionSpec as P

HEAD_DIM = 128
F32 = jnp.float32
BF16 = jnp.bfloat16
CHUNKS = 2
MIB = 1024 * 1024


def whole():
    return pl.BlockSpec(memory_space=pltpu.VMEM)


def big():
    return pl.BlockSpec(memory_space=pltpu.HBM)


def scalar():
    return pl.BlockSpec(memory_space=pltpu.SMEM)


def in_hbm(array):
    return pltpu.with_memory_space_constraint(array, pltpu.HBM)


def shape(*dims, dtype=F32):
    return jax.ShapeDtypeStruct(dims, dtype)


def iota(dims, axis):
    return lax.broadcasted_iota(jnp.int32, dims, axis)


def params(mib=4):
    return pltpu.CompilerParams(vmem_limit_bytes=mib * MIB)


def exchanged(slot):
    return slot & ~3 | (slot & 1) << 1 | slot >> 1 & 1


def rank_of(place, bank, slot):
    return place ^ (slot + bank * (exchanged(slot) - slot))


def start_columns(weight, column, target, sems):
    depth, width = target.shape
    part = depth // CHUNKS
    copies = []
    for c in range(CHUNKS):
        rows = pl.ds(c * part, part)
        copies.append(
            pltpu.make_async_copy(
                weight.at[rows, pl.ds(pl.multiple_of(column, width), width)],
                target.at[rows, :],
                sems.at[c],
            )
        )
        copies[-1].start()
    return copies


def adapter_column(refs, bank, count):
    rows = len(refs) * refs[0].shape[0]
    row = iota((rows, HEAD_DIM), 0)
    column = jnp.zeros((rows, HEAD_DIM), jnp.int32)
    for r in range(rows):
        ref = refs[r // refs[0].shape[0]]
        column = jnp.where(row == r, ref[r % ref.shape[0]], column)
    return column - bank * count


def start_slots(parity, ranks, place, bank, w_ref, kv_ref, w_buf, kv_buf, sems, kv_sems):
    count, _, width = w_buf.shape
    copies = []
    for s in range(count):
        target = rank_of(place[0], bank[0], 2 * s + parity)
        copies.append(
            start_columns(w_ref, (2 * target + bank[0]) * width, w_buf.at[s], sems.at[s])
            + start_columns(
                kv_ref, (target + ranks * bank[0]) * HEAD_DIM, kv_buf.at[s], kv_sems.at[s]
            )
        )
    return copies


def wait_all(copies):
    for slot in copies:
        for copy in slot:
            copy.wait()


def fetch_kernel(ranks, place, bank, w_ref, kv_ref, down_ref, w_buf, kv_buf, down_buf, *sems):
    down_copy = pltpu.make_async_copy(down_ref, down_buf, sems[2])
    down_copy.start()
    wait_all(start_slots(1, ranks, place, bank, w_ref, kv_ref, w_buf, kv_buf, *sems[:2]))
    down_copy.wait()


def slot_buffers(wq, ranks):
    count, depth = ranks // 2, wq.shape[0]
    return [
        shape(count, depth, wq.shape[1] // ranks // 2, dtype=BF16),
        shape(count, depth, HEAD_DIM, dtype=BF16),
    ]


def slot_sems(count):
    return [pltpu.SemaphoreType.DMA((count, CHUNKS))] * 2


def fetch(place, bank, wq, wkv, down, ranks):
    out = slot_buffers(wq, ranks) + [jax.ShapeDtypeStruct(down.shape, BF16)]
    return pl.pallas_call(
        lambda *refs: fetch_kernel(ranks, *refs),
        in_specs=[scalar()] * 2 + [big()] * 3,
        out_specs=[whole()] * 3,
        out_shape=out,
        scratch_shapes=slot_sems(ranks // 2) + [pltpu.SemaphoreType.DMA(())],
        compiler_params=params(),
        cost_estimate=pl.CostEstimate(
            flops=0, bytes_accessed=2 * sum(o.size for o in out), transcendentals=0
        ),
        name="fetch",
    )(place, bank, wq, wkv, down)


def beam_rows(x_ref, other_ref):
    rows = [x_ref[...].astype(F32), other_ref[...].astype(F32)]
    return jnp.concatenate(rows, axis=0).astype(BF16)


def project_slot(x, w, kv, out):
    width = w.shape[1]
    out[:, :width] = jnp.dot(x, w[...], preferred_element_type=F32)
    out[:, width : width + HEAD_DIM] = jnp.dot(x, kv[...], preferred_element_type=F32)


def project_sent_kernel(
    bank, own_ref, came_ref, x_ref, other_ref, w_buf, kv_buf, down_buf, *refs
):
    out, inner, column_out, *index, sems = refs
    copies = [
        pltpu.make_async_copy(ref, held, sems.at[n])
        for n, (ref, held) in enumerate(zip((own_ref, came_ref), index))
    ]
    for copy in copies:
        copy.start()
    width = w_buf.shape[2]
    x = beam_rows(x_ref, other_ref)
    for s in range(out.shape[0]):
        project_slot(x, w_buf.at[s], kv_buf.at[s], out.at[s])
    adapters, rank, depth = down_buf.shape
    every = lax.dot_general(
        x,
        down_buf[...].reshape(adapters * rank, depth),
        (((1,), (1,)), ((), ())),
        preferred_element_type=F32,
    )
    for copy in copies:
        copy.wait()
    column = adapter_column(index, bank[0], adapters)
    column_out[...] = column
    lane = iota(column.shape, 1)
    per = HEAD_DIM // rank
    total = jnp.zeros(column.shape, F32)
    for j in range(adapters // per):
        part = every[:, j * HEAD_DIM : (j + 1) * HEAD_DIM]
        total += jnp.where(lane // rank + j * per == column, part, 0.0)
    inner[...] = total
    for s in range(out.shape[0]):
        out[s, :, width + HEAD_DIM :] = total


def project_sent(bank, index, x, other, weights):
    half, _, width = weights[0].shape
    rows = 2 * x.shape[0]
    return pl.pallas_call(
        project_sent_kernel,
        in_specs=[scalar(), big(), pl.BlockSpec(memory_space=pl.ANY)] + [whole()] * 5,
        out_specs=[whole()] * 3,
        out_shape=[
            shape(half, rows, width + 2 * HEAD_DIM),
            shape(rows, HEAD_DIM),
            shape(rows, HEAD_DIM, dtype=jnp.int32),
        ],
        scratch_shapes=[pltpu.SMEM(index[0].shape, jnp.int32)] * 2
        + [pltpu.SemaphoreType.DMA((2,))],
        compiler_params=params(),
        cost_estimate=pl.CostEstimate(
            flops=2 * rows * sum(w.size for w in weights),
            bytes_accessed=2 * sum(w.size for w in weights),
            transcendentals=0,
        ),
        name="project_sent",
    )(bank, in_hbm(index[0]), index[1], x, other, *weights)


def project_kept_kernel(
    ranks, place, bank, length, x_ref, other_ref, w_ref, kv_ref, inner, out, live, *scratch
):
    w_buf, kv_buf = scratch[:2]
    copies = start_slots(0, ranks, place, bank, w_ref, kv_ref, *scratch)
    width = w_buf.shape[2]
    beams = x_ref.shape[0]
    row = iota(live.shape, 0)
    limit = jnp.zeros(live.shape, jnp.int32)
    for beam in range(beams):
        limit = jnp.where(row // (live.shape[0] // beams) == beam, length[beam], limit)
    live[...] = limit
    x = beam_rows(x_ref, other_ref)
    for s, slot in enumerate(copies):
        wait_all([slot])
        project_slot(x, w_buf.at[s], kv_buf.at[s], out.at[s])
        out[s, :, width + HEAD_DIM :] = inner[...]


def project_kept(place, bank, length, x, other, wq, wkv, inner, ranks):
    beams, depth = x.shape
    rows = 2 * beams
    half = ranks // 2
    buffers = slot_buffers(wq, ranks)
    return pl.pallas_call(
        lambda *refs: project_kept_kernel(ranks, *refs),
        in_specs=[scalar()] * 3 + [whole()] * 2 + [big()] * 2 + [whole()],
        out_specs=[whole()] * 2,
        out_shape=[
            shape(half, rows, buffers[0].shape[2] + 2 * HEAD_DIM),
            shape(beams * wq.shape[1] // ranks // HEAD_DIM, HEAD_DIM, dtype=jnp.int32),
        ],
        scratch_shapes=[pltpu.VMEM(b.shape, BF16) for b in buffers] + slot_sems(half),
        compiler_params=params(8),
        cost_estimate=pl.CostEstimate(
            flops=rows * depth * (wq.shape[1] + wkv.shape[1]) // 2,
            bytes_accessed=wq.size + wkv.size,
            transcendentals=0,
        ),
        name="project_kept",
    )(place, bank, length, x, other, wq, wkv, inner)


def correct_kernel(bank, column_ref, kept_ref, came_ref, up_ref, own_out, other_out):
    total = kept_ref[0] + came_ref[0]
    count, rank, width = up_ref.shape
    half = width // 2
    inner = total[:, half + HEAD_DIM :].astype(BF16).astype(F32)
    column = column_ref[...]
    lane = iota(column.shape, 1)
    per = HEAD_DIM // rank
    spread = jnp.concatenate(
        [
            jnp.where(lane // rank + j * per == column, inner, 0.0)
            for j in range(count // per)
        ],
        axis=1,
    ).astype(BF16)
    delta = jnp.dot(
        spread, up_ref[...].reshape(count * rank, width), preferred_element_type=F32
    )
    rows = own_out.shape[0]
    for side in range(2):
        columns = slice(side * half, (side + 1) * half)
        part = delta[:, columns] + jnp.where(bank[0] == side, total[:, :half], 0.0)
        own_out[:, columns] = part[:rows]
        other_out[:, columns] = part[rows:]
    own_out[:, width:] = total[:rows, half : half + HEAD_DIM]
    other_out[:, width:] = total[rows:, half : half + HEAD_DIM]


def correct(bank, column, kept, came, up):
    rows = kept.shape[1]
    out = shape(rows // 2, up.shape[2] + HEAD_DIM)
    return pl.pallas_call(
        correct_kernel,
        in_specs=[scalar()] + [whole()] * 4,
        out_specs=[whole()] * 2,
        out_shape=[out, out],
        compiler_params=params(),
        cost_estimate=pl.CostEstimate(
            flops=2 * rows * up.size, bytes_accessed=2 * up.size, transcendentals=0
        ),
        name="correct",
    )(bank, column, kept, came, up)


def halve_kernel(kept_ref, came_ref, sent_out, kept_out):
    for i in range(kept_out.shape[0]):
        kept_out[i] = kept_ref[2 * i] + came_ref[2 * i]
        sent_out[i] = kept_ref[2 * i + 1] + came_ref[2 * i + 1]


def halve(kept, came):
    half = jax.ShapeDtypeStruct((kept.shape[0] // 2,) + kept.shape[1:], kept.dtype)
    return pl.pallas_call(
        halve_kernel,
        in_specs=[whole()] * 2,
        out_specs=[whole()] * 2,
        out_shape=[half, half],
        compiler_params=params(),
        name="halve",
    )(kept, came)


def rotate(v, cosine, sine):
    return v * cosine + pltpu.roll(v, HEAD_DIM // 2, 1) * sine


def rotate_kernel(bank, own_ref, came_ref, cos_ref, sin_ref, q_ref, k_ref, v_ref, rows_ref):
    width = own_ref.shape[1] - HEAD_DIM
    cosine, sine = cos_ref[...], sin_ref[...]
    for g in range(width // HEAD_DIM):
        columns = slice(g * HEAD_DIM, (g + 1) * HEAD_DIM)
        rows_ref[:, g, :] = rotate(own_ref[:, columns] + came_ref[:, columns], cosine, sine)
    q_ref[0] = rows_ref[...].reshape(q_ref.shape[1:]).astype(BF16)
    own, came = own_ref[:, width:], came_ref[:, width:]
    key = jnp.where(bank[0] == 0, own, came)
    value = jnp.where(bank[0] == 0, came, own)
    k_ref[...] = rotate(key, cosine, sine).astype(BF16).astype(F32)
    v_ref[...] = value.astype(BF16).astype(F32)


def rotated(bank, own, came, cosine, sine):
    rows = own.shape[0]
    heads = own.shape[1] // HEAD_DIM - 1
    return pl.pallas_call(
        rotate_kernel,
        in_specs=[scalar()] + [whole()] * 4,
        out_specs=[whole()] * 3,
        out_shape=[
            shape(1, rows * heads, HEAD_DIM, dtype=BF16),
            shape(rows, HEAD_DIM),
            shape(rows, HEAD_DIM),
        ],
        scratch_shapes=[pltpu.VMEM((rows, heads, HEAD_DIM), F32)],
        compiler_params=params(),
        name="rotate",
    )(bank, own, came, cosine, sine)


def join_kernel(first_ref, second_ref, out_ref):
    half = first_ref.shape[0]
    out_ref[:half] = first_ref[...]
    out_ref[half:] = second_ref[...]


def join(first, second):
    return pl.pallas_call(
        join_kernel,
        in_specs=[whole()] * 2,
        out_specs=whole(),
        out_shape=shape(2 * first.shape[0], *first.shape[1:], dtype=first.dtype),
        compiler_params=params(),
        name="join",
    )(first, second)


def attend_kernel(slots, earlier, place, bank, length_ref, q_ref, k_ref, v_ref, *refs):
    before, out_ref = refs[:-1], refs[-1]
    beams, positions, _ = k_ref.shape
    rows = q_ref.shape[1]
    group = rows // beams
    row, lane = iota((rows, HEAD_DIM), 0), iota((rows, HEAD_DIM), 1)
    left = length_ref[...] - place[0] * positions
    live = jnp.concatenate(
        [lane + first < left for first in range(0, positions, HEAD_DIM)], axis=1
    )
    for i, slot in enumerate(slots):
        head = rank_of(place[0], bank[0], slot)
        columns = pl.ds(pl.multiple_of(head * HEAD_DIM, HEAD_DIM), HEAD_DIM)
        query = q_ref[i].astype(F32)
        scores = jnp.concatenate(
            [
                lax.dot_general(
                    query[beam * group : (beam + 1) * group].astype(BF16),
                    k_ref[beam, :, columns],
                    (((1,), (1,)), ((), ())),
                    preferred_element_type=F32,
                )
                for beam in range(beams)
            ],
            axis=0,
        ) * (1.0 / HEAD_DIM**0.5)
        scores = jnp.where(live, scores, -1e30)
        peak = jnp.max(scores, axis=1, keepdims=True)
        weights = jnp.where(live, jnp.exp(scores - peak), 0.0)
        total = jnp.sum(weights, axis=1, keepdims=True)
        values = [
            jnp.dot(
                weights[beam * group : (beam + 1) * group].astype(BF16),
                v_ref[beam, :, columns],
                preferred_element_type=F32,
            )
            for beam in range(beams)
        ]
        stats = jnp.where(lane == row % group, peak, 0.0)
        stats += jnp.where(lane == group + row % group, total, 0.0)
        stats = jnp.sum(stats.reshape(beams, group, HEAD_DIM), axis=1)
        high = stats.astype(BF16).astype(F32)
        middle = (stats - high).astype(BF16).astype(F32)
        low = stats - high - middle
        tail = high + pltpu.roll(middle, 2 * group, 1) + pltpu.roll(low, 4 * group, 1)
        block = jnp.concatenate(values + [tail, jnp.zeros_like(tail)], axis=0)
        out_ref[head if earlier else i] = block.astype(BF16)
    if earlier:
        done = [(ref, i) for ref in before for i in range(ref.shape[0])]
        for slot, (ref, i) in zip(earlier, done):
            out_ref[rank_of(place[0], bank[0], slot)] = ref[i]


def attend(place, bank, length, queries, keys, values, slots, earlier=(), before=()):
    count, rows, _ = queries.shape
    beams, positions, _ = keys.shape
    return pl.pallas_call(
        lambda *refs: attend_kernel(slots, earlier, *refs),
        in_specs=[scalar()] * 2 + [whole()] * (4 + len(before)),
        out_specs=whole(),
        out_shape=shape(count + len(earlier), rows + 2 * beams, HEAD_DIM, dtype=BF16),
        compiler_params=params(),
        cost_estimate=pl.CostEstimate(
            flops=4 * rows * count * positions * HEAD_DIM,
            bytes_accessed=4 * beams * positions * HEAD_DIM * (16 if earlier else count),
            transcendentals=rows * count * positions,
        ),
        name="attend",
    )(place, bank, length, queries, keys, values, *before)


def combine_kernel(parts_ref, q_ref, k_ref, v_ref, out_ref, joined):
    ranks = parts_ref.shape[0]
    beams, group, _ = joined.shape
    rows = beams * group

    def by_row(v):
        return jnp.broadcast_to(v[:, None, :], (beams, group, HEAD_DIM)).reshape(rows, HEAD_DIM)

    head = iota((rows, HEAD_DIM), 0) % group
    lane = iota((rows, HEAD_DIM), 1)
    score = jnp.sum(q_ref[0].astype(F32) * by_row(k_ref[...]), axis=1, keepdims=True) * (
        1.0 / HEAD_DIM**0.5
    )
    peaks, totals, weighted = [], [], []
    top = score
    for s in range(ranks):
        block = parts_ref[s].astype(F32)
        tail = block[rows : rows + beams]
        for turn in (2, 4):
            tail += pltpu.roll(block[rows : rows + beams], HEAD_DIM - turn * group, 1)
        tail = by_row(tail)
        peak = jnp.sum(jnp.where(lane == head, tail, 0.0), axis=1, keepdims=True)
        total = jnp.sum(jnp.where(lane == group + head, tail, 0.0), axis=1, keepdims=True)
        top = jnp.maximum(top, peak)
        peaks.append(peak)
        totals.append(total)
        weighted.append(block[:rows])
    new = jnp.exp(score - top)
    everything = new
    result = new.astype(BF16).astype(F32) * by_row(v_ref[...])
    for peak, total, block in zip(peaks, totals, weighted):
        factor = jnp.exp(peak - top)
        everything += total * factor
        result += block * factor
    joined[...] = (result / everything).reshape(joined.shape)
    for g in range(group):
        out_ref[:, g * HEAD_DIM : (g + 1) * HEAD_DIM] = joined[:, g, :].astype(BF16)


def combine(parts, query, key_new, value_new):
    beams = key_new.shape[0]
    group = query.shape[1] // beams
    return pl.pallas_call(
        combine_kernel,
        in_specs=[whole()] * 4,
        out_specs=whole(),
        out_shape=shape(beams, group * HEAD_DIM, dtype=BF16),
        scratch_shapes=[pltpu.VMEM((beams, group, HEAD_DIM), F32)],
        compiler_params=params(),
        name="combine",
    )(parts, query, key_new, value_new)


def output_kernel(x_ref, w_ref, out):
    count, _, width = out.shape
    for s in range(count):
        columns = slice(s * width, (s + 1) * width)
        total = jnp.dot(x_ref[...], w_ref[:, columns], preferred_element_type=F32)
        out[s] = total.astype(BF16)


def output(x, weight, ranks):
    beams = x.shape[0]
    return pl.pallas_call(
        output_kernel,
        in_specs=[whole()] * 2,
        out_specs=whole(),
        out_shape=shape(ranks, beams, weight.shape[1] // ranks, dtype=BF16),
        compiler_params=params(),
        cost_estimate=pl.CostEstimate(
            flops=2 * beams * weight.size, bytes_accessed=2 * weight.size, transcendentals=0
        ),
        name="output",
    )(x, weight)


def residual_kernel(x_ref, parts_ref, out_ref):
    total = jnp.sum(parts_ref[...].astype(F32), axis=0)
    out_ref[...] = (x_ref[...].astype(F32) + total).astype(BF16)


def residual(x, parts):
    return pl.pallas_call(
        residual_kernel,
        in_specs=[whole()] * 2,
        out_specs=whole(),
        out_shape=jax.ShapeDtypeStruct(x.shape, BF16),
        compiler_params=params(),
        name="residual",
    )(x, parts)


def swapped(x):
    return lax.ppermute(x, "bank", [(0, 1), (1, 0)])


def traded(blocks):
    return lax.all_to_all(blocks, "tensor", 0, 0, tiled=True)


def hop(x, bit):
    pairs = []
    for rank in range(lax.axis_size("tensor")):
        for bank in range(2):
            pairs.append((2 * rank + bank, 2 * rank_of(rank, bank, bit) + bank))
    return lax.ppermute(x, ("tensor", "bank"), pairs)


def matched_body(
    normed_hidden_input,
    beam_adapter_index,
    beam_cache_length,
    query_weight,
    keyvalue_weight,
    output_weight,
    lowrank_down_factors,
    lowrank_up_factors,
    paged_key_cache,
    paged_value_cache,
):
    x = normed_hidden_input
    ranks = lax.axis_size("tensor")
    place = lax.axis_index("tensor").astype(jnp.int32).reshape(1)
    bank = lax.axis_index("bank").astype(jnp.int32).reshape(1)
    index = (beam_adapter_index, swapped(beam_adapter_index))
    x_other = swapped(x)
    lane = jnp.arange(HEAD_DIM, dtype=jnp.int32)
    half = HEAD_DIM // 2
    frequency = jnp.power(500000.0, -2.0 * (lane % half).astype(F32) / HEAD_DIM)
    angles = beam_cache_length.astype(F32)[:, None] * frequency[None, :]
    cosine = jnp.cos(angles)
    sine = jnp.where(lane < half, -1.0, 1.0) * jnp.sin(angles)
    weights = in_hbm(query_weight), in_hbm(keyvalue_weight)
    down = in_hbm(lowrank_down_factors.swapaxes(1, 2))
    ahead = fetch(place, bank, *weights, down, ranks)
    sent, inner, column = project_sent(bank, index, x, x_other, ahead)
    came = hop(sent, 1)
    kept, length = project_kept(
        place, bank, beam_cache_length, x, x_other, *weights, inner, ranks
    )
    sent, kept = halve(kept, came)
    sent, kept = halve(kept, hop(sent, 2))
    own, other = correct(bank, column, kept, hop(sent, 4), lowrank_up_factors)
    query, key_new, value_new = rotated(bank, own, swapped(other), cosine, sine)

    def attended_part(queries, slots, **more):
        cache = paged_key_cache, paged_value_cache
        return attend(place, bank, length, queries, *cache, slots, **more)

    came, done = lax.optimization_barrier((hop(query, 4), attended_part(query, (0,))))
    gathered = join(query, came)
    second, more = lax.optimization_barrier((hop(gathered, 2), attended_part(came, (4,))))
    came = hop(join(gathered, second), 1)
    done = done, more, attended_part(second, (2, 6))
    partial = attended_part(came, (1, 5, 3, 7), earlier=(0, 4, 2, 6), before=done)
    attended = combine(traded(partial), query, key_new, value_new)
    return residual(x, traded(output(attended, output_weight, ranks)))


def joined(x, axis, combine):
    everything = jax.tree.map(lambda part: lax.all_gather(part, axis), x)
    leading = jax.tree.map(lambda part: part[0], everything)

    def turn(k, so_far):
        return combine(so_far, jax.tree.map(lambda part: part[k], everything))

    return lax.fori_loop(1, lax.axis_size(axis), turn, leading)


def apply_rotary(values, positions, head_size):
    row_count, col_count = values.shape
    half_size = head_size // 2
    frequency = jnp.power(500000.0, -2.0 * jnp.arange(half_size, dtype=jnp.float32) / head_size)
    angles = positions.astype(jnp.float32)[:, None] * frequency[None, :]
    cosine_table = jnp.cos(angles)[:, None, :]
    sine_table = jnp.sin(angles)[:, None, :]
    shaped = values.reshape(row_count, col_count // head_size, 2, half_size)
    first_half = shaped[:, :, 0]
    second_half = shaped[:, :, 1]
    rotated = jnp.stack(
        [
            first_half * cosine_table - second_half * sine_table,
            second_half * cosine_table + first_half * sine_table,
        ],
        axis=2,
    )
    return rotated.reshape(row_count, col_count)


def combine_parts(first_part, second_part):
    peak_one, total_one, weighted_one = first_part
    peak_two, total_two, weighted_two = second_part
    peak_both = jnp.maximum(peak_one, peak_two)
    factor_one = jnp.exp(peak_one - peak_both)
    factor_two = jnp.exp(peak_two - peak_both)
    return (
        peak_both,
        total_one * factor_one + total_two * factor_two,
        weighted_one * factor_one[..., None] + weighted_two * factor_two[..., None],
    )


def finish_heads(peak_score, weight_total, weighted, score_new, value_rows):
    peak_final = jnp.maximum(peak_score, score_new)
    old_factor = jnp.exp(peak_score - peak_final)
    new_weight = jnp.exp(score_new - peak_final)
    weight_total = weight_total * old_factor + new_weight
    weighted = (
        weighted * old_factor[..., None]
        + new_weight.astype(jnp.bfloat16).astype(jnp.float32)[..., None] * value_rows
    )
    return weighted / weight_total[..., None]


def body(
    normed_hidden_input,
    beam_adapter_index,
    beam_cache_length,
    query_weight,
    keyvalue_weight,
    output_weight,
    lowrank_down_factors,
    lowrank_up_factors,
    paged_key_cache,
    paged_value_cache,
):
    beam_rows, width_part = normed_hidden_input.shape
    model_width = query_weight.shape[1]
    kv_width = keyvalue_weight.shape[1] // 2
    head_count = model_width // HEAD_DIM
    kv_heads = kv_width // HEAD_DIM
    group_size = head_count // kv_heads
    tensor_index = lax.axis_index("tensor")
    query_part = jnp.dot(normed_hidden_input, query_weight, preferred_element_type=jnp.float32)
    keyval_part = jnp.dot(normed_hidden_input, keyvalue_weight, preferred_element_type=jnp.float32)
    down_all, up_all = (
        lax.all_gather(lowrank_down_factors, "bank", axis=0, tiled=True),
        lax.all_gather(lowrank_up_factors, "bank", axis=0, tiled=True),
    )
    inner_part = jnp.einsum(
        "ci,cim->cm",
        normed_hidden_input,
        down_all[beam_adapter_index],
        preferred_element_type=jnp.float32,
    )
    inner_total = lax.psum(inner_part, "tensor").astype(jnp.bfloat16)
    lowrank_delta = jnp.einsum(
        "mc,mct->mt", inner_total, up_all[beam_adapter_index], preferred_element_type=jnp.float32
    )
    query_total, keyval = lax.psum((query_part, keyval_part), "tensor")
    delta_total = lax.all_gather(lowrank_delta, "tensor", axis=1, tiled=True)
    query_rotated = apply_rotary(query_total + delta_total, beam_cache_length, HEAD_DIM).astype(
        jnp.bfloat16
    )
    key_new = apply_rotary(keyval[:, :kv_width], beam_cache_length, HEAD_DIM).astype(jnp.bfloat16)
    value_new = keyval[:, kv_width:].astype(jnp.bfloat16)
    position_count = paged_key_cache.shape[1]
    query_heads = query_rotated.reshape(beam_rows, kv_heads, group_size, HEAD_DIM)
    key_block = paged_key_cache.reshape(beam_rows, position_count, kv_heads, HEAD_DIM)
    value_block = paged_value_cache.reshape(beam_rows, position_count, kv_heads, HEAD_DIM)
    score_scale = 1.0 / HEAD_DIM**0.5
    scores = (
        jnp.einsum("bkgh,bpkh->bkgp", query_heads, key_block, preferred_element_type=jnp.float32)
        * score_scale
    )
    position_ids = tensor_index * position_count + jnp.arange(position_count)
    live_mask = (position_ids[None, :] < beam_cache_length[:, None])[:, None, None, :]
    scores = jnp.where(live_mask, scores, -1e30)
    peak_score = jnp.max(scores, axis=-1)
    weights = jnp.where(live_mask, jnp.exp(scores - peak_score[..., None]), 0.0)
    weight_total = jnp.sum(weights, axis=-1)
    weighted = jnp.einsum(
        "bkgp,bpkh->bkgh",
        weights.astype(jnp.bfloat16),
        value_block,
        preferred_element_type=jnp.float32,
    )
    peak_score, weight_total, weighted = joined(
        (peak_score, weight_total, weighted), "tensor", combine_parts
    )
    score_new = (
        jnp.einsum(
            "bkgh,bkh->bkg",
            query_heads,
            key_new.reshape(beam_rows, kv_heads, HEAD_DIM),
            preferred_element_type=jnp.float32,
        )
        * score_scale
    )
    value_rows = value_new.reshape(beam_rows, kv_heads, HEAD_DIM).astype(jnp.float32)[:, :, None, :]
    attended = (
        finish_heads(peak_score, weight_total, weighted, score_new, value_rows)
        .reshape(beam_rows, model_width)
        .astype(jnp.bfloat16)
    )
    attended_cols = lax.dynamic_slice_in_dim(attended, tensor_index * width_part, width_part, 1)
    mixed_cols = lax.psum_scatter(
        lax.dot_general(
            output_weight,
            attended_cols,
            (((0,), (1,)), ((), ())),
            preferred_element_type=jnp.float32,
        ),
        "tensor",
        scatter_dimension=0,
        tiled=True,
    )
    return (normed_hidden_input.astype(jnp.float32) + mixed_cols.T).astype(jnp.bfloat16)


def solution(mesh):
    matched = mesh.shape["tensor"] == 8 and mesh.shape["bank"] == 2
    return jax.shard_map(
        matched_body if matched else body,
        mesh=mesh,
        in_specs=(
            P(("groups", "bank"), "tensor"),
            P(("groups", "bank")),
            P(("groups", "bank")),
            P("tensor", None),
            P("tensor", None),
            P("tensor", None),
            P("bank", "tensor", None),
            P("bank", None, "tensor"),
            P(("groups", "bank"), "tensor", None),
            P(("groups", "bank"), "tensor", None),
        ),
        out_specs=P(("groups", "bank"), "tensor"),
        check_vma=False,
    )
```

```python
import jax
import jax.numpy as jnp
from jax import lax
from jax.experimental import pallas as pl
from jax.experimental.pallas import tpu as pltpu
from jax.sharding import PartitionSpec as P

HEAD_DIM = 128
F32 = jnp.float32
BF16 = jnp.bfloat16
CHUNKS = 2
MIB = 1024 * 1024


def whole():
    return pl.BlockSpec(memory_space=pltpu.VMEM)


def big():
    return pl.BlockSpec(memory_space=pltpu.HBM)


def scalar():
    return pl.BlockSpec(memory_space=pltpu.SMEM)


def in_hbm(array):
    return pltpu.with_memory_space_constraint(array, pltpu.HBM)


def shape(*dims, dtype=F32):
    return jax.ShapeDtypeStruct(dims, dtype)


def iota(dims, axis):
    return lax.broadcasted_iota(jnp.int32, dims, axis)


def params(mib=4):
    return pltpu.CompilerParams(vmem_limit_bytes=mib * MIB)


def exchanged(slot):
    return slot & ~3 | (slot & 1) << 1 | slot >> 1 & 1


def rank_of(place, bank, slot):
    return place ^ (slot + bank * (exchanged(slot) - slot))


def start_columns(weight, column, target, sems):
    depth, width = target.shape
    part = depth // CHUNKS
    copies = []
    for c in range(CHUNKS):
        rows = pl.ds(c * part, part)
        copies.append(
            pltpu.make_async_copy(
                weight.at[rows, pl.ds(pl.multiple_of(column, width), width)],
                target.at[rows, :],
                sems.at[c],
            )
        )
        copies[-1].start()
    return copies


def adapter_column(refs, bank, count):
    rows = len(refs) * refs[0].shape[0]
    row = iota((rows, HEAD_DIM), 0)
    column = jnp.zeros((rows, HEAD_DIM), jnp.int32)
    for r in range(rows):
        ref = refs[r // refs[0].shape[0]]
        column = jnp.where(row == r, ref[r % ref.shape[0]], column)
    return column - bank * count


def start_slots(parity, ranks, place, bank, w_ref, kv_ref, w_buf, kv_buf, sems, kv_sems):
    count, _, width = w_buf.shape
    copies = []
    for s in range(count):
        target = rank_of(place[0], bank[0], 2 * s + parity)
        copies.append(
            start_columns(w_ref, (2 * target + bank[0]) * width, w_buf.at[s], sems.at[s])
            + start_columns(
                kv_ref, (target + ranks * bank[0]) * HEAD_DIM, kv_buf.at[s], kv_sems.at[s]
            )
        )
    return copies


def wait_all(copies):
    for slot in copies:
        for copy in slot:
            copy.wait()


def fetch_kernel(ranks, place, bank, w_ref, kv_ref, down_ref, w_buf, kv_buf, down_buf, *sems):
    down_copy = pltpu.make_async_copy(down_ref, down_buf, sems[2])
    down_copy.start()
    wait_all(start_slots(1, ranks, place, bank, w_ref, kv_ref, w_buf, kv_buf, *sems[:2]))
    down_copy.wait()


def slot_buffers(wq, ranks):
    count, depth = ranks // 2, wq.shape[0]
    return [
        shape(count, depth, wq.shape[1] // ranks // 2, dtype=BF16),
        shape(count, depth, HEAD_DIM, dtype=BF16),
    ]


def slot_sems(count):
    return [pltpu.SemaphoreType.DMA((count, CHUNKS))] * 2


def fetch(place, bank, wq, wkv, down, ranks):
    out = slot_buffers(wq, ranks) + [jax.ShapeDtypeStruct(down.shape, BF16)]
    return pl.pallas_call(
        lambda *refs: fetch_kernel(ranks, *refs),
        in_specs=[scalar()] * 2 + [big()] * 3,
        out_specs=[whole()] * 3,
        out_shape=out,
        scratch_shapes=slot_sems(ranks // 2) + [pltpu.SemaphoreType.DMA(())],
        compiler_params=params(),
        cost_estimate=pl.CostEstimate(
            flops=0, bytes_accessed=2 * sum(o.size for o in out), transcendentals=0
        ),
        name="fetch",
    )(place, bank, wq, wkv, down)


def beam_rows(x_ref, other_ref):
    rows = [x_ref[...].astype(F32), other_ref[...].astype(F32)]
    return jnp.concatenate(rows, axis=0).astype(BF16)


def project_slot(x, w, kv, out):
    width = w.shape[1]
    out[:, :width] = jnp.dot(x, w[...], preferred_element_type=F32)
    out[:, width : width + HEAD_DIM] = jnp.dot(x, kv[...], preferred_element_type=F32)


def project_sent_kernel(
    bank, own_ref, came_ref, x_ref, other_ref, w_buf, kv_buf, down_buf, *refs
):
    out, inner, column_out, *index, sems = refs
    copies = [
        pltpu.make_async_copy(ref, held, sems.at[n])
        for n, (ref, held) in enumerate(zip((own_ref, came_ref), index))
    ]
    for copy in copies:
        copy.start()
    width = w_buf.shape[2]
    x = beam_rows(x_ref, other_ref)
    for s in range(out.shape[0]):
        project_slot(x, w_buf.at[s], kv_buf.at[s], out.at[s])
    adapters, rank, depth = down_buf.shape
    every = lax.dot_general(
        x,
        down_buf[...].reshape(adapters * rank, depth),
        (((1,), (1,)), ((), ())),
        preferred_element_type=F32,
    )
    for copy in copies:
        copy.wait()
    column = adapter_column(index, bank[0], adapters)
    column_out[...] = column
    lane = iota(column.shape, 1)
    per = HEAD_DIM // rank
    total = jnp.zeros(column.shape, F32)
    for j in range(adapters // per):
        part = every[:, j * HEAD_DIM : (j + 1) * HEAD_DIM]
        total += jnp.where(lane // rank + j * per == column, part, 0.0)
    inner[...] = total
    for s in range(out.shape[0]):
        out[s, :, width + HEAD_DIM :] = total


def project_sent(bank, index, x, other, weights):
    half, _, width = weights[0].shape
    rows = 2 * x.shape[0]
    return pl.pallas_call(
        project_sent_kernel,
        in_specs=[scalar(), big(), pl.BlockSpec(memory_space=pl.ANY)] + [whole()] * 5,
        out_specs=[whole()] * 3,
        out_shape=[
            shape(half, rows, width + 2 * HEAD_DIM),
            shape(rows, HEAD_DIM),
            shape(rows, HEAD_DIM, dtype=jnp.int32),
        ],
        scratch_shapes=[pltpu.SMEM(index[0].shape, jnp.int32)] * 2
        + [pltpu.SemaphoreType.DMA((2,))],
        compiler_params=params(),
        cost_estimate=pl.CostEstimate(
            flops=2 * rows * sum(w.size for w in weights),
            bytes_accessed=2 * sum(w.size for w in weights),
            transcendentals=0,
        ),
        name="project_sent",
    )(bank, in_hbm(index[0]), index[1], x, other, *weights)


def project_kept_kernel(
    ranks, place, bank, length, x_ref, other_ref, w_ref, kv_ref, inner, out, live, *scratch
):
    w_buf, kv_buf = scratch[:2]
    copies = start_slots(0, ranks, place, bank, w_ref, kv_ref, *scratch)
    width = w_buf.shape[2]
    beams = x_ref.shape[0]
    row = iota(live.shape, 0)
    limit = jnp.zeros(live.shape, jnp.int32)
    for beam in range(beams):
        limit = jnp.where(row // (live.shape[0] // beams) == beam, length[beam], limit)
    live[...] = limit
    x = beam_rows(x_ref, other_ref)
    for s, slot in enumerate(copies):
        wait_all([slot])
        project_slot(x, w_buf.at[s], kv_buf.at[s], out.at[s])
        out[s, :, width + HEAD_DIM :] = inner[...]


def project_kept(place, bank, length, x, other, wq, wkv, inner, ranks):
    beams, depth = x.shape
    rows = 2 * beams
    half = ranks // 2
    buffers = slot_buffers(wq, ranks)
    return pl.pallas_call(
        lambda *refs: project_kept_kernel(ranks, *refs),
        in_specs=[scalar()] * 3 + [whole()] * 2 + [big()] * 2 + [whole()],
        out_specs=[whole()] * 2,
        out_shape=[
            shape(half, rows, buffers[0].shape[2] + 2 * HEAD_DIM),
            shape(beams * wq.shape[1] // ranks // HEAD_DIM, HEAD_DIM, dtype=jnp.int32),
        ],
        scratch_shapes=[pltpu.VMEM(b.shape, BF16) for b in buffers] + slot_sems(half),
        compiler_params=params(8),
        cost_estimate=pl.CostEstimate(
            flops=rows * depth * (wq.shape[1] + wkv.shape[1]) // 2,
            bytes_accessed=wq.size + wkv.size,
            transcendentals=0,
        ),
        name="project_kept",
    )(place, bank, length, x, other, wq, wkv, inner)


def correct_kernel(bank, column_ref, up_ref, *refs):
    *parts, own_out, other_out = refs
    total = parts[0][...]
    for part in parts[1:]:
        total += part[...]
    count, rank, width = up_ref.shape
    half = width // 2
    inner = total[:, half + HEAD_DIM :].astype(BF16).astype(F32)
    column = column_ref[...]
    lane = iota(column.shape, 1)
    per = HEAD_DIM // rank
    spread = jnp.concatenate(
        [
            jnp.where(lane // rank + j * per == column, inner, 0.0)
            for j in range(count // per)
        ],
        axis=1,
    ).astype(BF16)
    delta = jnp.dot(
        spread, up_ref[...].reshape(count * rank, width), preferred_element_type=F32
    )
    rows = own_out.shape[0]
    for side in range(2):
        columns = slice(side * half, (side + 1) * half)
        part = delta[:, columns] + jnp.where(bank[0] == side, total[:, :half], 0.0)
        own_out[:, columns] = part[:rows]
        other_out[:, columns] = part[rows:]
    own_out[:, width:] = total[:rows, half : half + HEAD_DIM]
    other_out[:, width:] = total[rows:, half : half + HEAD_DIM]


def correct(bank, column, up, parts):
    rows = parts[0].shape[0]
    out = shape(rows // 2, up.shape[2] + HEAD_DIM)
    return pl.pallas_call(
        correct_kernel,
        in_specs=[scalar()] + [whole()] * (2 + len(parts)),
        out_specs=[whole()] * 2,
        out_shape=[out, out],
        compiler_params=params(),
        cost_estimate=pl.CostEstimate(
            flops=2 * rows * up.size, bytes_accessed=2 * up.size, transcendentals=0
        ),
        name="correct",
    )(bank, column, up, *parts)


def part_kernel(kept_ref, came_ref, *outs):
    for i, out in enumerate(outs):
        out[...] = kept_ref[i] + came_ref[i]


def part(kept, came):
    return pl.pallas_call(
        part_kernel,
        in_specs=[whole()] * 2,
        out_specs=[whole()] * kept.shape[0],
        out_shape=[shape(*kept.shape[1:])] * kept.shape[0],
        compiler_params=params(),
        name="part",
    )(kept, came)


def rotate(v, cosine, sine):
    return v * cosine + pltpu.roll(v, HEAD_DIM // 2, 1) * sine


def rotate_kernel(bank, own_ref, came_ref, cos_ref, sin_ref, q_ref, k_ref, v_ref, rows_ref):
    width = own_ref.shape[1] - HEAD_DIM
    cosine, sine = cos_ref[...], sin_ref[...]
    for g in range(width // HEAD_DIM):
        columns = slice(g * HEAD_DIM, (g + 1) * HEAD_DIM)
        rows_ref[:, g, :] = rotate(own_ref[:, columns] + came_ref[:, columns], cosine, sine)
    q_ref[0] = rows_ref[...].reshape(q_ref.shape[1:]).astype(BF16)
    own, came = own_ref[:, width:], came_ref[:, width:]
    key = jnp.where(bank[0] == 0, own, came)
    value = jnp.where(bank[0] == 0, came, own)
    k_ref[...] = rotate(key, cosine, sine).astype(BF16).astype(F32)
    v_ref[...] = value.astype(BF16).astype(F32)


def rotated(bank, own, came, cosine, sine):
    rows = own.shape[0]
    heads = own.shape[1] // HEAD_DIM - 1
    return pl.pallas_call(
        rotate_kernel,
        in_specs=[scalar()] + [whole()] * 4,
        out_specs=[whole()] * 3,
        out_shape=[
            shape(1, rows * heads, HEAD_DIM, dtype=BF16),
            shape(rows, HEAD_DIM),
            shape(rows, HEAD_DIM),
        ],
        scratch_shapes=[pltpu.VMEM((rows, heads, HEAD_DIM), F32)],
        compiler_params=params(),
        name="rotate",
    )(bank, own, came, cosine, sine)


def join_kernel(*refs):
    *parts, out_ref = refs
    for i, part in enumerate(parts):
        out_ref[i] = part[0]


def join(parts):
    return pl.pallas_call(
        join_kernel,
        in_specs=[whole()] * len(parts),
        out_specs=whole(),
        out_shape=shape(len(parts), *parts[0].shape[1:], dtype=parts[0].dtype),
        compiler_params=params(),
        name="join",
    )(*parts)


def attend_kernel(slots, earlier, place, bank, length_ref, q_ref, k_ref, v_ref, *refs):
    before, out_ref = refs[:-1], refs[-1]
    beams, positions, _ = k_ref.shape
    rows = q_ref.shape[1]
    group = rows // beams
    row, lane = iota((rows, HEAD_DIM), 0), iota((rows, HEAD_DIM), 1)
    left = length_ref[...] - place[0] * positions
    live = jnp.concatenate(
        [lane + first < left for first in range(0, positions, HEAD_DIM)], axis=1
    )
    for i, slot in enumerate(slots):
        head = rank_of(place[0], bank[0], slot)
        columns = pl.ds(pl.multiple_of(head * HEAD_DIM, HEAD_DIM), HEAD_DIM)
        query = q_ref[i].astype(F32)
        scores = jnp.concatenate(
            [
                lax.dot_general(
                    query[beam * group : (beam + 1) * group].astype(BF16),
                    k_ref[beam, :, columns],
                    (((1,), (1,)), ((), ())),
                    preferred_element_type=F32,
                )
                for beam in range(beams)
            ],
            axis=0,
        ) * (1.0 / HEAD_DIM**0.5)
        scores = jnp.where(live, scores, -1e30)
        peak = jnp.max(scores, axis=1, keepdims=True)
        weights = jnp.where(live, jnp.exp(scores - peak), 0.0)
        total = jnp.sum(weights, axis=1, keepdims=True)
        values = [
            jnp.dot(
                weights[beam * group : (beam + 1) * group].astype(BF16),
                v_ref[beam, :, columns],
                preferred_element_type=F32,
            )
            for beam in range(beams)
        ]
        stats = jnp.where(lane == row % group, peak, 0.0)
        stats += jnp.where(lane == group + row % group, total, 0.0)
        stats = jnp.sum(stats.reshape(beams, group, HEAD_DIM), axis=1)
        high = stats.astype(BF16).astype(F32)
        middle = (stats - high).astype(BF16).astype(F32)
        low = stats - high - middle
        tail = high + pltpu.roll(middle, 2 * group, 1) + pltpu.roll(low, 4 * group, 1)
        block = jnp.concatenate(values + [tail, jnp.zeros_like(tail)], axis=0)
        out_ref[head if earlier else i] = block.astype(BF16)
    if earlier:
        done = [(ref, i) for ref in before for i in range(ref.shape[0])]
        for slot, (ref, i) in zip(earlier, done):
            out_ref[rank_of(place[0], bank[0], slot)] = ref[i]


def attend(place, bank, length, queries, keys, values, slots, earlier=(), before=()):
    count, rows, _ = queries.shape
    beams, positions, _ = keys.shape
    return pl.pallas_call(
        lambda *refs: attend_kernel(slots, earlier, *refs),
        in_specs=[scalar()] * 2 + [whole()] * (4 + len(before)),
        out_specs=whole(),
        out_shape=shape(count + len(earlier), rows + 2 * beams, HEAD_DIM, dtype=BF16),
        compiler_params=params(),
        cost_estimate=pl.CostEstimate(
            flops=4 * rows * count * positions * HEAD_DIM,
            bytes_accessed=4 * beams * positions * HEAD_DIM * (16 if earlier else count),
            transcendentals=rows * count * positions,
        ),
        name="attend",
    )(place, bank, length, queries, keys, values, *before)


def combine_kernel(parts_ref, q_ref, k_ref, v_ref, out_ref, joined):
    ranks = parts_ref.shape[0]
    beams, group, _ = joined.shape
    rows = beams * group

    def by_row(v):
        return jnp.broadcast_to(v[:, None, :], (beams, group, HEAD_DIM)).reshape(rows, HEAD_DIM)

    head = iota((rows, HEAD_DIM), 0) % group
    lane = iota((rows, HEAD_DIM), 1)
    score = jnp.sum(q_ref[0].astype(F32) * by_row(k_ref[...]), axis=1, keepdims=True) * (
        1.0 / HEAD_DIM**0.5
    )
    peaks, totals, weighted = [], [], []
    top = score
    for s in range(ranks):
        block = parts_ref[s].astype(F32)
        tail = block[rows : rows + beams]
        for turn in (2, 4):
            tail += pltpu.roll(block[rows : rows + beams], HEAD_DIM - turn * group, 1)
        tail = by_row(tail)
        peak = jnp.sum(jnp.where(lane == head, tail, 0.0), axis=1, keepdims=True)
        total = jnp.sum(jnp.where(lane == group + head, tail, 0.0), axis=1, keepdims=True)
        top = jnp.maximum(top, peak)
        peaks.append(peak)
        totals.append(total)
        weighted.append(block[:rows])
    new = jnp.exp(score - top)
    everything = new
    result = new.astype(BF16).astype(F32) * by_row(v_ref[...])
    for peak, total, block in zip(peaks, totals, weighted):
        factor = jnp.exp(peak - top)
        everything += total * factor
        result += block * factor
    joined[...] = (result / everything).reshape(joined.shape)
    for g in range(group):
        out_ref[:, g * HEAD_DIM : (g + 1) * HEAD_DIM] = joined[:, g, :].astype(BF16)


def combine(parts, query, key_new, value_new):
    beams = key_new.shape[0]
    group = query.shape[1] // beams
    return pl.pallas_call(
        combine_kernel,
        in_specs=[whole()] * 4,
        out_specs=whole(),
        out_shape=shape(beams, group * HEAD_DIM, dtype=BF16),
        scratch_shapes=[pltpu.VMEM((beams, group, HEAD_DIM), F32)],
        compiler_params=params(),
        name="combine",
    )(parts, query, key_new, value_new)


def output_kernel(x_ref, w_ref, out):
    count, _, width = out.shape
    for s in range(count):
        columns = slice(s * width, (s + 1) * width)
        total = jnp.dot(x_ref[...], w_ref[:, columns], preferred_element_type=F32)
        out[s] = total.astype(BF16)


def output(x, weight, ranks):
    beams = x.shape[0]
    return pl.pallas_call(
        output_kernel,
        in_specs=[whole()] * 2,
        out_specs=whole(),
        out_shape=shape(ranks, beams, weight.shape[1] // ranks, dtype=BF16),
        compiler_params=params(),
        cost_estimate=pl.CostEstimate(
            flops=2 * beams * weight.size, bytes_accessed=2 * weight.size, transcendentals=0
        ),
        name="output",
    )(x, weight)


def residual_kernel(x_ref, parts_ref, out_ref):
    total = jnp.sum(parts_ref[...].astype(F32), axis=0)
    out_ref[...] = (x_ref[...].astype(F32) + total).astype(BF16)


def residual(x, parts):
    return pl.pallas_call(
        residual_kernel,
        in_specs=[whole()] * 2,
        out_specs=whole(),
        out_shape=jax.ShapeDtypeStruct(x.shape, BF16),
        compiler_params=params(),
        name="residual",
    )(x, parts)


def swapped(x):
    return lax.ppermute(x, "bank", [(0, 1), (1, 0)])


def traded(blocks):
    return lax.all_to_all(blocks, "tensor", 0, 0, tiled=True)


def hop(x, bit):
    pairs = []
    for rank in range(lax.axis_size("tensor")):
        for bank in range(2):
            pairs.append((2 * rank + bank, 2 * rank_of(rank, bank, bit) + bank))
    return lax.ppermute(x, ("tensor", "bank"), pairs)


def matched_body(
    normed_hidden_input,
    beam_adapter_index,
    beam_cache_length,
    query_weight,
    keyvalue_weight,
    output_weight,
    lowrank_down_factors,
    lowrank_up_factors,
    paged_key_cache,
    paged_value_cache,
):
    x = normed_hidden_input
    ranks = lax.axis_size("tensor")
    place = lax.axis_index("tensor").astype(jnp.int32).reshape(1)
    bank = lax.axis_index("bank").astype(jnp.int32).reshape(1)
    index = (beam_adapter_index, swapped(beam_adapter_index))
    x_other = swapped(x)
    lane = jnp.arange(HEAD_DIM, dtype=jnp.int32)
    half = HEAD_DIM // 2
    frequency = jnp.power(500000.0, -2.0 * (lane % half).astype(F32) / HEAD_DIM)
    angles = beam_cache_length.astype(F32)[:, None] * frequency[None, :]
    cosine = jnp.cos(angles)
    sine = jnp.where(lane < half, -1.0, 1.0) * jnp.sin(angles)
    weights = in_hbm(query_weight), in_hbm(keyvalue_weight)
    down = in_hbm(lowrank_down_factors.swapaxes(1, 2))
    ahead = fetch(place, bank, *weights, down, ranks)
    sent, inner, column = project_sent(bank, index, x, x_other, ahead)
    came = hop(sent, 1)
    kept, length = project_kept(
        place, bank, beam_cache_length, x, x_other, *weights, inner, ranks
    )
    kept, *sent = part(kept, came)
    near = tuple(range(2, ranks, 2))
    parts = [kept] + [hop(block, slot) for block, slot in zip(sent, near)]
    own, other = correct(bank, column, lowrank_up_factors, parts)
    query, key_new, value_new = rotated(bank, own, swapped(other), cosine, sine)

    def attended_part(queries, slots, **more):
        cache = paged_key_cache, paged_value_cache
        return attend(place, bank, length, queries, *cache, slots, **more)

    gathered = join([query] + [hop(query, slot) for slot in near])
    came = hop(gathered, 1)
    done = attended_part(gathered, (0, *near))
    odd = tuple(slot + 1 for slot in (0, *near))
    partial = attended_part(came, odd, earlier=(0, *near), before=(done,))
    attended = combine(traded(partial), query, key_new, value_new)
    return residual(x, traded(output(attended, output_weight, ranks)))


def joined(x, axis, combine):
    everything = jax.tree.map(lambda part: lax.all_gather(part, axis), x)
    leading = jax.tree.map(lambda part: part[0], everything)

    def turn(k, so_far):
        return combine(so_far, jax.tree.map(lambda part: part[k], everything))

    return lax.fori_loop(1, lax.axis_size(axis), turn, leading)


def apply_rotary(values, positions, head_size):
    row_count, col_count = values.shape
    half_size = head_size // 2
    frequency = jnp.power(500000.0, -2.0 * jnp.arange(half_size, dtype=jnp.float32) / head_size)
    angles = positions.astype(jnp.float32)[:, None] * frequency[None, :]
    cosine_table = jnp.cos(angles)[:, None, :]
    sine_table = jnp.sin(angles)[:, None, :]
    shaped = values.reshape(row_count, col_count // head_size, 2, half_size)
    first_half = shaped[:, :, 0]
    second_half = shaped[:, :, 1]
    rotated = jnp.stack(
        [
            first_half * cosine_table - second_half * sine_table,
            second_half * cosine_table + first_half * sine_table,
        ],
        axis=2,
    )
    return rotated.reshape(row_count, col_count)


def combine_parts(first_part, second_part):
    peak_one, total_one, weighted_one = first_part
    peak_two, total_two, weighted_two = second_part
    peak_both = jnp.maximum(peak_one, peak_two)
    factor_one = jnp.exp(peak_one - peak_both)
    factor_two = jnp.exp(peak_two - peak_both)
    return (
        peak_both,
        total_one * factor_one + total_two * factor_two,
        weighted_one * factor_one[..., None] + weighted_two * factor_two[..., None],
    )


def finish_heads(peak_score, weight_total, weighted, score_new, value_rows):
    peak_final = jnp.maximum(peak_score, score_new)
    old_factor = jnp.exp(peak_score - peak_final)
    new_weight = jnp.exp(score_new - peak_final)
    weight_total = weight_total * old_factor + new_weight
    weighted = (
        weighted * old_factor[..., None]
        + new_weight.astype(jnp.bfloat16).astype(jnp.float32)[..., None] * value_rows
    )
    return weighted / weight_total[..., None]


def body(
    normed_hidden_input,
    beam_adapter_index,
    beam_cache_length,
    query_weight,
    keyvalue_weight,
    output_weight,
    lowrank_down_factors,
    lowrank_up_factors,
    paged_key_cache,
    paged_value_cache,
):
    beam_rows, width_part = normed_hidden_input.shape
    model_width = query_weight.shape[1]
    kv_width = keyvalue_weight.shape[1] // 2
    head_count = model_width // HEAD_DIM
    kv_heads = kv_width // HEAD_DIM
    group_size = head_count // kv_heads
    tensor_index = lax.axis_index("tensor")
    query_part = jnp.dot(normed_hidden_input, query_weight, preferred_element_type=jnp.float32)
    keyval_part = jnp.dot(normed_hidden_input, keyvalue_weight, preferred_element_type=jnp.float32)
    down_all, up_all = (
        lax.all_gather(lowrank_down_factors, "bank", axis=0, tiled=True),
        lax.all_gather(lowrank_up_factors, "bank", axis=0, tiled=True),
    )
    inner_part = jnp.einsum(
        "ci,cim->cm",
        normed_hidden_input,
        down_all[beam_adapter_index],
        preferred_element_type=jnp.float32,
    )
    inner_total = lax.psum(inner_part, "tensor").astype(jnp.bfloat16)
    lowrank_delta = jnp.einsum(
        "mc,mct->mt", inner_total, up_all[beam_adapter_index], preferred_element_type=jnp.float32
    )
    query_total, keyval = lax.psum((query_part, keyval_part), "tensor")
    delta_total = lax.all_gather(lowrank_delta, "tensor", axis=1, tiled=True)
    query_rotated = apply_rotary(query_total + delta_total, beam_cache_length, HEAD_DIM).astype(
        jnp.bfloat16
    )
    key_new = apply_rotary(keyval[:, :kv_width], beam_cache_length, HEAD_DIM).astype(jnp.bfloat16)
    value_new = keyval[:, kv_width:].astype(jnp.bfloat16)
    position_count = paged_key_cache.shape[1]
    query_heads = query_rotated.reshape(beam_rows, kv_heads, group_size, HEAD_DIM)
    key_block = paged_key_cache.reshape(beam_rows, position_count, kv_heads, HEAD_DIM)
    value_block = paged_value_cache.reshape(beam_rows, position_count, kv_heads, HEAD_DIM)
    score_scale = 1.0 / HEAD_DIM**0.5
    scores = (
        jnp.einsum("bkgh,bpkh->bkgp", query_heads, key_block, preferred_element_type=jnp.float32)
        * score_scale
    )
    position_ids = tensor_index * position_count + jnp.arange(position_count)
    live_mask = (position_ids[None, :] < beam_cache_length[:, None])[:, None, None, :]
    scores = jnp.where(live_mask, scores, -1e30)
    peak_score = jnp.max(scores, axis=-1)
    weights = jnp.where(live_mask, jnp.exp(scores - peak_score[..., None]), 0.0)
    weight_total = jnp.sum(weights, axis=-1)
    weighted = jnp.einsum(
        "bkgp,bpkh->bkgh",
        weights.astype(jnp.bfloat16),
        value_block,
        preferred_element_type=jnp.float32,
    )
    peak_score, weight_total, weighted = joined(
        (peak_score, weight_total, weighted), "tensor", combine_parts
    )
    score_new = (
        jnp.einsum(
            "bkgh,bkh->bkg",
            query_heads,
            key_new.reshape(beam_rows, kv_heads, HEAD_DIM),
            preferred_element_type=jnp.float32,
        )
        * score_scale
    )
    value_rows = value_new.reshape(beam_rows, kv_heads, HEAD_DIM).astype(jnp.float32)[:, :, None, :]
    attended = (
        finish_heads(peak_score, weight_total, weighted, score_new, value_rows)
        .reshape(beam_rows, model_width)
        .astype(jnp.bfloat16)
    )
    attended_cols = lax.dynamic_slice_in_dim(attended, tensor_index * width_part, width_part, 1)
    mixed_cols = lax.psum_scatter(
        lax.dot_general(
            output_weight,
            attended_cols,
            (((0,), (1,)), ((), ())),
            preferred_element_type=jnp.float32,
        ),
        "tensor",
        scatter_dimension=0,
        tiled=True,
    )
    return (normed_hidden_input.astype(jnp.float32) + mixed_cols.T).astype(jnp.bfloat16)


def solution(mesh):
    matched = mesh.shape["tensor"] == 8 and mesh.shape["bank"] == 2
    return jax.shard_map(
        matched_body if matched else body,
        mesh=mesh,
        in_specs=(
            P(("groups", "bank"), "tensor"),
            P(("groups", "bank")),
            P(("groups", "bank")),
            P("tensor", None),
            P("tensor", None),
            P("tensor", None),
            P("bank", "tensor", None),
            P("bank", None, "tensor"),
            P(("groups", "bank"), "tensor", None),
            P(("groups", "bank"), "tensor", None),
        ),
        out_specs=P(("groups", "bank"), "tensor"),
        check_vma=False,
    )
```

```python
import jax
import jax.numpy as jnp
from jax import lax
from jax.experimental import pallas as pl
from jax.experimental.pallas import tpu as pltpu
from jax.sharding import PartitionSpec as P

HEAD_DIM = 128
F32 = jnp.float32
BF16 = jnp.bfloat16
CHUNKS = 2
MIB = 1024 * 1024


def whole():
    return pl.BlockSpec(memory_space=pltpu.VMEM)


def big():
    return pl.BlockSpec(memory_space=pltpu.HBM)


def scalar():
    return pl.BlockSpec(memory_space=pltpu.SMEM)


def in_hbm(array):
    return pltpu.with_memory_space_constraint(array, pltpu.HBM)


def shape(*dims, dtype=F32):
    return jax.ShapeDtypeStruct(dims, dtype)


def iota(dims, axis):
    return lax.broadcasted_iota(jnp.int32, dims, axis)


def params(mib=4):
    return pltpu.CompilerParams(vmem_limit_bytes=mib * MIB)


def exchanged(slot):
    return slot & ~3 | (slot & 1) << 1 | slot >> 1 & 1


def rank_of(place, bank, slot):
    return place ^ (slot + bank * (exchanged(slot) - slot))


def start_columns(weight, column, target, sems):
    depth, width = target.shape
    part = depth // CHUNKS
    copies = []
    for c in range(CHUNKS):
        rows = pl.ds(c * part, part)
        copies.append(
            pltpu.make_async_copy(
                weight.at[rows, pl.ds(pl.multiple_of(column, width), width)],
                target.at[rows, :],
                sems.at[c],
            )
        )
        copies[-1].start()
    return copies


def adapter_column(refs, bank, count):
    rows = len(refs) * refs[0].shape[0]
    row = iota((rows, HEAD_DIM), 0)
    column = jnp.zeros((rows, HEAD_DIM), jnp.int32)
    for r in range(rows):
        ref = refs[r // refs[0].shape[0]]
        column = jnp.where(row == r, ref[r % ref.shape[0]], column)
    return column - bank * count


def start_slots(parity, ranks, place, bank, w_ref, kv_ref, w_buf, kv_buf, sems, kv_sems):
    count, _, width = w_buf.shape
    copies = []
    for s in range(count):
        target = rank_of(place[0], bank[0], 2 * s + parity)
        copies.append(
            start_columns(w_ref, (2 * target + bank[0]) * width, w_buf.at[s], sems.at[s])
            + start_columns(
                kv_ref, (target + ranks * bank[0]) * HEAD_DIM, kv_buf.at[s], kv_sems.at[s]
            )
        )
    return copies


def wait_all(copies):
    for slot in copies:
        for copy in slot:
            copy.wait()


def fetch_kernel(ranks, place, bank, w_ref, kv_ref, down_ref, w_buf, kv_buf, down_buf, *sems):
    down_copy = pltpu.make_async_copy(down_ref, down_buf, sems[2])
    down_copy.start()
    wait_all(start_slots(1, ranks, place, bank, w_ref, kv_ref, w_buf, kv_buf, *sems[:2]))
    down_copy.wait()


def slot_buffers(wq, ranks):
    count, depth = ranks // 2, wq.shape[0]
    return [
        shape(count, depth, wq.shape[1] // ranks // 2, dtype=BF16),
        shape(count, depth, HEAD_DIM, dtype=BF16),
    ]


def slot_sems(count):
    return [pltpu.SemaphoreType.DMA((count, CHUNKS))] * 2


def fetch(place, bank, wq, wkv, down, ranks):
    out = slot_buffers(wq, ranks) + [jax.ShapeDtypeStruct(down.shape, BF16)]
    return pl.pallas_call(
        lambda *refs: fetch_kernel(ranks, *refs),
        in_specs=[scalar()] * 2 + [big()] * 3,
        out_specs=[whole()] * 3,
        out_shape=out,
        scratch_shapes=slot_sems(ranks // 2) + [pltpu.SemaphoreType.DMA(())],
        compiler_params=params(),
        cost_estimate=pl.CostEstimate(
            flops=0, bytes_accessed=2 * sum(o.size for o in out), transcendentals=0
        ),
        name="fetch",
    )(place, bank, wq, wkv, down)


def beam_rows(x_ref, other_ref):
    rows = [x_ref[...].astype(F32), other_ref[...].astype(F32)]
    return jnp.concatenate(rows, axis=0).astype(BF16)


def project_slot(x, w, kv, out):
    width = w.shape[1]
    out[:, :width] = jnp.dot(x, w[...], preferred_element_type=F32)
    out[:, width : width + HEAD_DIM] = jnp.dot(x, kv[...], preferred_element_type=F32)


def project_sent_kernel(
    bank, own_ref, came_ref, x_ref, other_ref, w_buf, kv_buf, down_buf, *refs
):
    out, inner, column_out, *index, sems = refs
    copies = [
        pltpu.make_async_copy(ref, held, sems.at[n])
        for n, (ref, held) in enumerate(zip((own_ref, came_ref), index))
    ]
    for copy in copies:
        copy.start()
    width = w_buf.shape[2]
    x = beam_rows(x_ref, other_ref)
    for s in range(out.shape[0]):
        project_slot(x, w_buf.at[s], kv_buf.at[s], out.at[s])
    adapters, rank, depth = down_buf.shape
    every = lax.dot_general(
        x,
        down_buf[...].reshape(adapters * rank, depth),
        (((1,), (1,)), ((), ())),
        preferred_element_type=F32,
    )
    for copy in copies:
        copy.wait()
    column = adapter_column(index, bank[0], adapters)
    column_out[...] = column
    lane = iota(column.shape, 1)
    per = HEAD_DIM // rank
    total = jnp.zeros(column.shape, F32)
    for j in range(adapters // per):
        part = every[:, j * HEAD_DIM : (j + 1) * HEAD_DIM]
        total += jnp.where(lane // rank + j * per == column, part, 0.0)
    inner[...] = total
    for s in range(out.shape[0]):
        out[s, :, width + HEAD_DIM :] = total


def project_sent(bank, index, x, other, weights):
    half, _, width = weights[0].shape
    rows = 2 * x.shape[0]
    return pl.pallas_call(
        project_sent_kernel,
        in_specs=[scalar(), big(), pl.BlockSpec(memory_space=pl.ANY)] + [whole()] * 5,
        out_specs=[whole()] * 3,
        out_shape=[
            shape(half, rows, width + 2 * HEAD_DIM),
            shape(rows, HEAD_DIM),
            shape(rows, HEAD_DIM, dtype=jnp.int32),
        ],
        scratch_shapes=[pltpu.SMEM(index[0].shape, jnp.int32)] * 2
        + [pltpu.SemaphoreType.DMA((2,))],
        compiler_params=params(),
        cost_estimate=pl.CostEstimate(
            flops=2 * rows * sum(w.size for w in weights),
            bytes_accessed=2 * sum(w.size for w in weights),
            transcendentals=0,
        ),
        name="project_sent",
    )(bank, in_hbm(index[0]), index[1], x, other, *weights)


def project_kept_kernel(
    ranks, place, bank, length, x_ref, other_ref, w_ref, kv_ref, inner, out, live, *scratch
):
    w_buf, kv_buf = scratch[:2]
    copies = start_slots(0, ranks, place, bank, w_ref, kv_ref, *scratch)
    width = w_buf.shape[2]
    beams = x_ref.shape[0]
    row = iota(live.shape, 0)
    limit = jnp.zeros(live.shape, jnp.int32)
    for beam in range(beams):
        limit = jnp.where(row // (live.shape[0] // beams) == beam, length[beam], limit)
    live[...] = limit
    x = beam_rows(x_ref, other_ref)
    for s, slot in enumerate(copies):
        wait_all([slot])
        project_slot(x, w_buf.at[s], kv_buf.at[s], out.at[s])
        out[s, :, width + HEAD_DIM :] = inner[...]


def project_kept(place, bank, length, x, other, wq, wkv, inner, ranks):
    beams, depth = x.shape
    rows = 2 * beams
    half = ranks // 2
    buffers = slot_buffers(wq, ranks)
    return pl.pallas_call(
        lambda *refs: project_kept_kernel(ranks, *refs),
        in_specs=[scalar()] * 3 + [whole()] * 2 + [big()] * 2 + [whole()],
        out_specs=[whole()] * 2,
        out_shape=[
            shape(half, rows, buffers[0].shape[2] + 2 * HEAD_DIM),
            shape(beams * wq.shape[1] // ranks // HEAD_DIM, HEAD_DIM, dtype=jnp.int32),
        ],
        scratch_shapes=[pltpu.VMEM(b.shape, BF16) for b in buffers] + slot_sems(half),
        compiler_params=params(8),
        cost_estimate=pl.CostEstimate(
            flops=rows * depth * (wq.shape[1] + wkv.shape[1]) // 2,
            bytes_accessed=wq.size + wkv.size,
            transcendentals=0,
        ),
        name="project_kept",
    )(place, bank, length, x, other, wq, wkv, inner)


def correct_kernel(bank, column_ref, up_ref, parts_ref, own_out, other_out):
    total = jnp.sum(parts_ref[...], axis=0)
    count, rank, width = up_ref.shape
    half = width // 2
    inner = total[:, half + HEAD_DIM :].astype(BF16).astype(F32)
    column = column_ref[...]
    lane = iota(column.shape, 1)
    per = HEAD_DIM // rank
    spread = jnp.concatenate(
        [
            jnp.where(lane // rank + j * per == column, inner, 0.0)
            for j in range(count // per)
        ],
        axis=1,
    ).astype(BF16)
    delta = jnp.dot(
        spread, up_ref[...].reshape(count * rank, width), preferred_element_type=F32
    )
    rows = own_out.shape[0]
    for side in range(2):
        columns = slice(side * half, (side + 1) * half)
        part = delta[:, columns] + jnp.where(bank[0] == side, total[:, :half], 0.0)
        own_out[:, columns] = part[:rows]
        other_out[:, columns] = part[rows:]
    own_out[:, width:] = total[:rows, half : half + HEAD_DIM]
    other_out[:, width:] = total[rows:, half : half + HEAD_DIM]


def correct(bank, column, up, parts):
    rows = parts.shape[1]
    out = shape(rows // 2, up.shape[2] + HEAD_DIM)
    return pl.pallas_call(
        correct_kernel,
        in_specs=[scalar()] + [whole()] * 3,
        out_specs=[whole()] * 2,
        out_shape=[out, out],
        compiler_params=params(),
        cost_estimate=pl.CostEstimate(
            flops=2 * rows * up.size, bytes_accessed=2 * up.size, transcendentals=0
        ),
        name="correct",
    )(bank, column, up, parts)


def part_kernel(place, bank, kept_ref, came_ref, out):
    mine = jnp.where(bank[0] == 0, place[0], exchanged(place[0])) >> 1
    for i in range(out.shape[0]):
        out[mine ^ i] = kept_ref[i] + came_ref[i]


def part(place, bank, kept, came):
    return pl.pallas_call(
        part_kernel,
        in_specs=[scalar()] * 2 + [whole()] * 2,
        out_specs=whole(),
        out_shape=shape(*kept.shape),
        compiler_params=params(),
        name="part",
    )(place, bank, kept, came)


def rotate(v, cosine, sine):
    return v * cosine + pltpu.roll(v, HEAD_DIM // 2, 1) * sine


def rotate_kernel(bank, own_ref, came_ref, cos_ref, sin_ref, q_ref, k_ref, v_ref, rows_ref):
    width = own_ref.shape[1] - HEAD_DIM
    cosine, sine = cos_ref[...], sin_ref[...]
    for g in range(width // HEAD_DIM):
        columns = slice(g * HEAD_DIM, (g + 1) * HEAD_DIM)
        rows_ref[:, g, :] = rotate(own_ref[:, columns] + came_ref[:, columns], cosine, sine)
    query = rows_ref[...].reshape(q_ref.shape[1:]).astype(BF16)
    for i in range(q_ref.shape[0]):
        q_ref[i] = query
    own, came = own_ref[:, width:], came_ref[:, width:]
    key = jnp.where(bank[0] == 0, own, came)
    value = jnp.where(bank[0] == 0, came, own)
    k_ref[...] = rotate(key, cosine, sine).astype(BF16).astype(F32)
    v_ref[...] = value.astype(BF16).astype(F32)


def rotated(bank, own, came, cosine, sine, copies):
    rows = own.shape[0]
    heads = own.shape[1] // HEAD_DIM - 1
    return pl.pallas_call(
        rotate_kernel,
        in_specs=[scalar()] + [whole()] * 4,
        out_specs=[whole()] * 3,
        out_shape=[
            shape(copies, rows * heads, HEAD_DIM, dtype=BF16),
            shape(rows, HEAD_DIM),
            shape(rows, HEAD_DIM),
        ],
        scratch_shapes=[pltpu.VMEM((rows, heads, HEAD_DIM), F32)],
        compiler_params=params(),
        name="rotate",
    )(bank, own, came, cosine, sine)


def attend_kernel(slots, earlier, place, bank, length_ref, q_ref, k_ref, v_ref, *refs):
    before, out_ref = refs[:-1], refs[-1]
    beams, positions, _ = k_ref.shape
    rows = q_ref.shape[1]
    group = rows // beams
    root = place[0] & (1 + bank[0])
    row, lane = iota((rows, HEAD_DIM), 0), iota((rows, HEAD_DIM), 1)
    left = length_ref[...] - place[0] * positions
    live = jnp.concatenate(
        [lane + first < left for first in range(0, positions, HEAD_DIM)], axis=1
    )
    for i, slot in enumerate(slots):
        head = rank_of(root, bank[0], slot)
        columns = pl.ds(pl.multiple_of(head * HEAD_DIM, HEAD_DIM), HEAD_DIM)
        query = q_ref[i].astype(F32)
        scores = jnp.concatenate(
            [
                lax.dot_general(
                    query[beam * group : (beam + 1) * group].astype(BF16),
                    k_ref[beam, :, columns],
                    (((1,), (1,)), ((), ())),
                    preferred_element_type=F32,
                )
                for beam in range(beams)
            ],
            axis=0,
        ) * (1.0 / HEAD_DIM**0.5)
        scores = jnp.where(live, scores, -1e30)
        peak = jnp.max(scores, axis=1, keepdims=True)
        weights = jnp.where(live, jnp.exp(scores - peak), 0.0)
        total = jnp.sum(weights, axis=1, keepdims=True)
        values = [
            jnp.dot(
                weights[beam * group : (beam + 1) * group].astype(BF16),
                v_ref[beam, :, columns],
                preferred_element_type=F32,
            )
            for beam in range(beams)
        ]
        stats = jnp.where(lane == row % group, peak, 0.0)
        stats += jnp.where(lane == group + row % group, total, 0.0)
        stats = jnp.sum(stats.reshape(beams, group, HEAD_DIM), axis=1)
        high = stats.astype(BF16).astype(F32)
        middle = (stats - high).astype(BF16).astype(F32)
        low = stats - high - middle
        tail = high + pltpu.roll(middle, 2 * group, 1) + pltpu.roll(low, 4 * group, 1)
        block = jnp.concatenate(values + [tail, jnp.zeros_like(tail)], axis=0)
        out_ref[head if earlier else i] = block.astype(BF16)
    if earlier:
        done = [(ref, i) for ref in before for i in range(ref.shape[0])]
        for slot, (ref, i) in zip(earlier, done):
            out_ref[rank_of(root, bank[0], slot)] = ref[i]


def attend(place, bank, length, queries, keys, values, slots, earlier=(), before=()):
    count, rows, _ = queries.shape
    beams, positions, _ = keys.shape
    return pl.pallas_call(
        lambda *refs: attend_kernel(slots, earlier, *refs),
        in_specs=[scalar()] * 2 + [whole()] * (4 + len(before)),
        out_specs=whole(),
        out_shape=shape(count + len(earlier), rows + 2 * beams, HEAD_DIM, dtype=BF16),
        compiler_params=params(),
        cost_estimate=pl.CostEstimate(
            flops=4 * rows * count * positions * HEAD_DIM,
            bytes_accessed=4 * beams * positions * HEAD_DIM * (16 if earlier else count),
            transcendentals=rows * count * positions,
        ),
        name="attend",
    )(place, bank, length, queries, keys, values, *before)


def combine_kernel(parts_ref, q_ref, k_ref, v_ref, out_ref, joined):
    ranks = parts_ref.shape[0]
    beams, group, _ = joined.shape
    rows = beams * group

    def by_row(v):
        return jnp.broadcast_to(v[:, None, :], (beams, group, HEAD_DIM)).reshape(rows, HEAD_DIM)

    head = iota((rows, HEAD_DIM), 0) % group
    lane = iota((rows, HEAD_DIM), 1)
    score = jnp.sum(q_ref[0].astype(F32) * by_row(k_ref[...]), axis=1, keepdims=True) * (
        1.0 / HEAD_DIM**0.5
    )
    peaks, totals, weighted = [], [], []
    top = score
    for s in range(ranks):
        block = parts_ref[s].astype(F32)
        tail = block[rows : rows + beams]
        for turn in (2, 4):
            tail += pltpu.roll(block[rows : rows + beams], HEAD_DIM - turn * group, 1)
        tail = by_row(tail)
        peak = jnp.sum(jnp.where(lane == head, tail, 0.0), axis=1, keepdims=True)
        total = jnp.sum(jnp.where(lane == group + head, tail, 0.0), axis=1, keepdims=True)
        top = jnp.maximum(top, peak)
        peaks.append(peak)
        totals.append(total)
        weighted.append(block[:rows])
    new = jnp.exp(score - top)
    everything = new
    result = new.astype(BF16).astype(F32) * by_row(v_ref[...])
    for peak, total, block in zip(peaks, totals, weighted):
        factor = jnp.exp(peak - top)
        everything += total * factor
        result += block * factor
    joined[...] = (result / everything).reshape(joined.shape)
    for g in range(group):
        out_ref[:, g * HEAD_DIM : (g + 1) * HEAD_DIM] = joined[:, g, :].astype(BF16)


def combine(parts, query, key_new, value_new):
    beams = key_new.shape[0]
    group = query.shape[1] // beams
    return pl.pallas_call(
        combine_kernel,
        in_specs=[whole()] * 4,
        out_specs=whole(),
        out_shape=shape(beams, group * HEAD_DIM, dtype=BF16),
        scratch_shapes=[pltpu.VMEM((beams, group, HEAD_DIM), F32)],
        compiler_params=params(),
        name="combine",
    )(parts, query, key_new, value_new)


def output_kernel(x_ref, w_ref, out):
    count, _, width = out.shape
    for s in range(count):
        columns = slice(s * width, (s + 1) * width)
        total = jnp.dot(x_ref[...], w_ref[:, columns], preferred_element_type=F32)
        out[s] = total.astype(BF16)


def output(x, weight, ranks):
    beams = x.shape[0]
    return pl.pallas_call(
        output_kernel,
        in_specs=[whole()] * 2,
        out_specs=whole(),
        out_shape=shape(ranks, beams, weight.shape[1] // ranks, dtype=BF16),
        compiler_params=params(),
        cost_estimate=pl.CostEstimate(
            flops=2 * beams * weight.size, bytes_accessed=2 * weight.size, transcendentals=0
        ),
        name="output",
    )(x, weight)


def residual_kernel(x_ref, parts_ref, out_ref):
    total = jnp.sum(parts_ref[...].astype(F32), axis=0)
    out_ref[...] = (x_ref[...].astype(F32) + total).astype(BF16)


def residual(x, parts):
    return pl.pallas_call(
        residual_kernel,
        in_specs=[whole()] * 2,
        out_specs=whole(),
        out_shape=jax.ShapeDtypeStruct(x.shape, BF16),
        compiler_params=params(),
        name="residual",
    )(x, parts)


def swapped(x):
    return lax.ppermute(x, "bank", [(0, 1), (1, 0)])


def traded(blocks):
    return lax.all_to_all(blocks, "tensor", 0, 0, tiled=True)


def traded_near(blocks):
    groups = []
    for bank in range(2):
        for root in (0, 1 + bank):
            slots = range(0, lax.axis_size("tensor"), 2)
            groups.append([2 * rank_of(root, bank, slot) + bank for slot in slots])
    return lax.all_to_all(
        blocks, ("tensor", "bank"), 0, 0, axis_index_groups=groups, tiled=True
    )


def hop(x, bit):
    pairs = []
    for rank in range(lax.axis_size("tensor")):
        for bank in range(2):
            pairs.append((2 * rank + bank, 2 * rank_of(rank, bank, bit) + bank))
    return lax.ppermute(x, ("tensor", "bank"), pairs)


def matched_body(
    normed_hidden_input,
    beam_adapter_index,
    beam_cache_length,
    query_weight,
    keyvalue_weight,
    output_weight,
    lowrank_down_factors,
    lowrank_up_factors,
    paged_key_cache,
    paged_value_cache,
):
    x = normed_hidden_input
    ranks = lax.axis_size("tensor")
    place = lax.axis_index("tensor").astype(jnp.int32).reshape(1)
    bank = lax.axis_index("bank").astype(jnp.int32).reshape(1)
    index = (beam_adapter_index, swapped(beam_adapter_index))
    x_other = swapped(x)
    lane = jnp.arange(HEAD_DIM, dtype=jnp.int32)
    half = HEAD_DIM // 2
    frequency = jnp.power(500000.0, -2.0 * (lane % half).astype(F32) / HEAD_DIM)
    angles = beam_cache_length.astype(F32)[:, None] * frequency[None, :]
    cosine = jnp.cos(angles)
    sine = jnp.where(lane < half, -1.0, 1.0) * jnp.sin(angles)
    weights = in_hbm(query_weight), in_hbm(keyvalue_weight)
    down = in_hbm(lowrank_down_factors.swapaxes(1, 2))
    ahead = fetch(place, bank, *weights, down, ranks)
    sent, inner, column = project_sent(bank, index, x, x_other, ahead)
    came = hop(sent, 1)
    kept, length = project_kept(
        place, bank, beam_cache_length, x, x_other, *weights, inner, ranks
    )
    parts = traded_near(part(place, bank, kept, came))
    own, other = correct(bank, column, lowrank_up_factors, parts)
    query, key_new, value_new = rotated(
        bank, own, swapped(other), cosine, sine, ranks // 2
    )

    def attended_part(queries, slots, **more):
        cache = paged_key_cache, paged_value_cache
        return attend(place, bank, length, queries, *cache, slots, **more)

    gathered = traded_near(query)
    came = hop(gathered, 1)
    even = tuple(range(0, ranks, 2))
    done = attended_part(gathered, even)
    odd = tuple(slot + 1 for slot in even)
    partial = attended_part(came, odd, earlier=even, before=(done,))
    attended = combine(traded(partial), query, key_new, value_new)
    return residual(x, traded(output(attended, output_weight, ranks)))


def joined(x, axis, combine):
    everything = jax.tree.map(lambda part: lax.all_gather(part, axis), x)
    leading = jax.tree.map(lambda part: part[0], everything)

    def turn(k, so_far):
        return combine(so_far, jax.tree.map(lambda part: part[k], everything))

    return lax.fori_loop(1, lax.axis_size(axis), turn, leading)


def apply_rotary(values, positions, head_size):
    row_count, col_count = values.shape
    half_size = head_size // 2
    frequency = jnp.power(500000.0, -2.0 * jnp.arange(half_size, dtype=jnp.float32) / head_size)
    angles = positions.astype(jnp.float32)[:, None] * frequency[None, :]
    cosine_table = jnp.cos(angles)[:, None, :]
    sine_table = jnp.sin(angles)[:, None, :]
    shaped = values.reshape(row_count, col_count // head_size, 2, half_size)
    first_half = shaped[:, :, 0]
    second_half = shaped[:, :, 1]
    rotated = jnp.stack(
        [
            first_half * cosine_table - second_half * sine_table,
            second_half * cosine_table + first_half * sine_table,
        ],
        axis=2,
    )
    return rotated.reshape(row_count, col_count)


def combine_parts(first_part, second_part):
    peak_one, total_one, weighted_one = first_part
    peak_two, total_two, weighted_two = second_part
    peak_both = jnp.maximum(peak_one, peak_two)
    factor_one = jnp.exp(peak_one - peak_both)
    factor_two = jnp.exp(peak_two - peak_both)
    return (
        peak_both,
        total_one * factor_one + total_two * factor_two,
        weighted_one * factor_one[..., None] + weighted_two * factor_two[..., None],
    )


def finish_heads(peak_score, weight_total, weighted, score_new, value_rows):
    peak_final = jnp.maximum(peak_score, score_new)
    old_factor = jnp.exp(peak_score - peak_final)
    new_weight = jnp.exp(score_new - peak_final)
    weight_total = weight_total * old_factor + new_weight
    weighted = (
        weighted * old_factor[..., None]
        + new_weight.astype(jnp.bfloat16).astype(jnp.float32)[..., None] * value_rows
    )
    return weighted / weight_total[..., None]


def body(
    normed_hidden_input,
    beam_adapter_index,
    beam_cache_length,
    query_weight,
    keyvalue_weight,
    output_weight,
    lowrank_down_factors,
    lowrank_up_factors,
    paged_key_cache,
    paged_value_cache,
):
    beam_rows, width_part = normed_hidden_input.shape
    model_width = query_weight.shape[1]
    kv_width = keyvalue_weight.shape[1] // 2
    head_count = model_width // HEAD_DIM
    kv_heads = kv_width // HEAD_DIM
    group_size = head_count // kv_heads
    tensor_index = lax.axis_index("tensor")
    query_part = jnp.dot(normed_hidden_input, query_weight, preferred_element_type=jnp.float32)
    keyval_part = jnp.dot(normed_hidden_input, keyvalue_weight, preferred_element_type=jnp.float32)
    down_all, up_all = (
        lax.all_gather(lowrank_down_factors, "bank", axis=0, tiled=True),
        lax.all_gather(lowrank_up_factors, "bank", axis=0, tiled=True),
    )
    inner_part = jnp.einsum(
        "ci,cim->cm",
        normed_hidden_input,
        down_all[beam_adapter_index],
        preferred_element_type=jnp.float32,
    )
    inner_total = lax.psum(inner_part, "tensor").astype(jnp.bfloat16)
    lowrank_delta = jnp.einsum(
        "mc,mct->mt", inner_total, up_all[beam_adapter_index], preferred_element_type=jnp.float32
    )
    query_total, keyval = lax.psum((query_part, keyval_part), "tensor")
    delta_total = lax.all_gather(lowrank_delta, "tensor", axis=1, tiled=True)
    query_rotated = apply_rotary(query_total + delta_total, beam_cache_length, HEAD_DIM).astype(
        jnp.bfloat16
    )
    key_new = apply_rotary(keyval[:, :kv_width], beam_cache_length, HEAD_DIM).astype(jnp.bfloat16)
    value_new = keyval[:, kv_width:].astype(jnp.bfloat16)
    position_count = paged_key_cache.shape[1]
    query_heads = query_rotated.reshape(beam_rows, kv_heads, group_size, HEAD_DIM)
    key_block = paged_key_cache.reshape(beam_rows, position_count, kv_heads, HEAD_DIM)
    value_block = paged_value_cache.reshape(beam_rows, position_count, kv_heads, HEAD_DIM)
    score_scale = 1.0 / HEAD_DIM**0.5
    scores = (
        jnp.einsum("bkgh,bpkh->bkgp", query_heads, key_block, preferred_element_type=jnp.float32)
        * score_scale
    )
    position_ids = tensor_index * position_count + jnp.arange(position_count)
    live_mask = (position_ids[None, :] < beam_cache_length[:, None])[:, None, None, :]
    scores = jnp.where(live_mask, scores, -1e30)
    peak_score = jnp.max(scores, axis=-1)
    weights = jnp.where(live_mask, jnp.exp(scores - peak_score[..., None]), 0.0)
    weight_total = jnp.sum(weights, axis=-1)
    weighted = jnp.einsum(
        "bkgp,bpkh->bkgh",
        weights.astype(jnp.bfloat16),
        value_block,
        preferred_element_type=jnp.float32,
    )
    peak_score, weight_total, weighted = joined(
        (peak_score, weight_total, weighted), "tensor", combine_parts
    )
    score_new = (
        jnp.einsum(
            "bkgh,bkh->bkg",
            query_heads,
            key_new.reshape(beam_rows, kv_heads, HEAD_DIM),
            preferred_element_type=jnp.float32,
        )
        * score_scale
    )
    value_rows = value_new.reshape(beam_rows, kv_heads, HEAD_DIM).astype(jnp.float32)[:, :, None, :]
    attended = (
        finish_heads(peak_score, weight_total, weighted, score_new, value_rows)
        .reshape(beam_rows, model_width)
        .astype(jnp.bfloat16)
    )
    attended_cols = lax.dynamic_slice_in_dim(attended, tensor_index * width_part, width_part, 1)
    mixed_cols = lax.psum_scatter(
        lax.dot_general(
            output_weight,
            attended_cols,
            (((0,), (1,)), ((), ())),
            preferred_element_type=jnp.float32,
        ),
        "tensor",
        scatter_dimension=0,
        tiled=True,
    )
    return (normed_hidden_input.astype(jnp.float32) + mixed_cols.T).astype(jnp.bfloat16)


def solution(mesh):
    matched = mesh.shape["tensor"] == 8 and mesh.shape["bank"] == 2
    return jax.shard_map(
        matched_body if matched else body,
        mesh=mesh,
        in_specs=(
            P(("groups", "bank"), "tensor"),
            P(("groups", "bank")),
            P(("groups", "bank")),
            P("tensor", None),
            P("tensor", None),
            P("tensor", None),
            P("bank", "tensor", None),
            P("bank", None, "tensor"),
            P(("groups", "bank"), "tensor", None),
            P(("groups", "bank"), "tensor", None),
        ),
        out_specs=P(("groups", "bank"), "tensor"),
        check_vma=False,
    )
```

```python
import jax
import jax.numpy as jnp
from jax import lax
from jax.experimental import pallas as pl
from jax.experimental.pallas import tpu as pltpu
from jax.sharding import PartitionSpec as P

HEAD_DIM = 128
F32 = jnp.float32
BF16 = jnp.bfloat16
CHUNKS = 2
MIB = 1024 * 1024


def whole():
    return pl.BlockSpec(memory_space=pltpu.VMEM)


def big():
    return pl.BlockSpec(memory_space=pltpu.HBM)


def scalar():
    return pl.BlockSpec(memory_space=pltpu.SMEM)


def in_hbm(array):
    return pltpu.with_memory_space_constraint(array, pltpu.HBM)


def shape(*dims, dtype=F32):
    return jax.ShapeDtypeStruct(dims, dtype)


def iota(dims, axis):
    return lax.broadcasted_iota(jnp.int32, dims, axis)


def params(mib=4):
    return pltpu.CompilerParams(vmem_limit_bytes=mib * MIB)


def exchanged(slot):
    return slot & ~3 | (slot & 1) << 1 | slot >> 1 & 1


def rank_of(place, bank, slot):
    return place ^ (slot + bank * (exchanged(slot) - slot))


def start_columns(weight, column, target, sems):
    depth, width = target.shape
    part = depth // CHUNKS
    copies = []
    for c in range(CHUNKS):
        rows = pl.ds(c * part, part)
        copies.append(
            pltpu.make_async_copy(
                weight.at[rows, pl.ds(pl.multiple_of(column, width), width)],
                target.at[rows, :],
                sems.at[c],
            )
        )
        copies[-1].start()
    return copies


def adapter_column(refs, bank, count):
    rows = len(refs) * refs[0].shape[0]
    row = iota((rows, HEAD_DIM), 0)
    column = jnp.zeros((rows, HEAD_DIM), jnp.int32)
    for r in range(rows):
        ref = refs[r // refs[0].shape[0]]
        column = jnp.where(row == r, ref[r % ref.shape[0]], column)
    return column - bank * count


def start_slots(parity, ranks, place, bank, w_ref, kv_ref, w_buf, kv_buf, sems, kv_sems):
    count, _, width = w_buf.shape
    copies = []
    for s in range(count):
        target = rank_of(place[0], bank[0], 2 * s + parity)
        copies.append(
            start_columns(w_ref, (2 * target + bank[0]) * width, w_buf.at[s], sems.at[s])
            + start_columns(
                kv_ref, (target + ranks * bank[0]) * HEAD_DIM, kv_buf.at[s], kv_sems.at[s]
            )
        )
    return copies


def wait_all(copies):
    for slot in copies:
        for copy in slot:
            copy.wait()


def fetch_kernel(ranks, place, bank, w_ref, kv_ref, down_ref, w_buf, kv_buf, down_buf, *sems):
    down_copy = pltpu.make_async_copy(down_ref, down_buf, sems[2])
    down_copy.start()
    wait_all(start_slots(1, ranks, place, bank, w_ref, kv_ref, w_buf, kv_buf, *sems[:2]))
    down_copy.wait()


def slot_buffers(wq, ranks):
    count, depth = ranks // 2, wq.shape[0]
    return [
        shape(count, depth, wq.shape[1] // ranks // 2, dtype=BF16),
        shape(count, depth, HEAD_DIM, dtype=BF16),
    ]


def slot_sems(count):
    return [pltpu.SemaphoreType.DMA((count, CHUNKS))] * 2


def fetch(place, bank, wq, wkv, down, ranks):
    out = slot_buffers(wq, ranks) + [jax.ShapeDtypeStruct(down.shape, BF16)]
    return pl.pallas_call(
        lambda *refs: fetch_kernel(ranks, *refs),
        in_specs=[scalar()] * 2 + [big()] * 3,
        out_specs=[whole()] * 3,
        out_shape=out,
        scratch_shapes=slot_sems(ranks // 2) + [pltpu.SemaphoreType.DMA(())],
        compiler_params=params(),
        cost_estimate=pl.CostEstimate(
            flops=0, bytes_accessed=2 * sum(o.size for o in out), transcendentals=0
        ),
        name="fetch",
    )(place, bank, wq, wkv, down)


def beam_rows(x_ref, other_ref):
    rows = [x_ref[...].astype(F32), other_ref[...].astype(F32)]
    return jnp.concatenate(rows, axis=0).astype(BF16)


def project_slot(x, w, kv, out):
    width = w.shape[1]
    out[:, :width] = jnp.dot(x, w[...], preferred_element_type=F32)
    out[:, width : width + HEAD_DIM] = jnp.dot(x, kv[...], preferred_element_type=F32)


def project_sent_kernel(
    bank, own_ref, came_ref, x_ref, other_ref, w_buf, kv_buf, down_buf, *refs
):
    out, inner, column_out, *index, sems = refs
    copies = [
        pltpu.make_async_copy(ref, held, sems.at[n])
        for n, (ref, held) in enumerate(zip((own_ref, came_ref), index))
    ]
    for copy in copies:
        copy.start()
    width = w_buf.shape[2]
    x = beam_rows(x_ref, other_ref)
    for s in range(out.shape[0]):
        project_slot(x, w_buf.at[s], kv_buf.at[s], out.at[s])
    adapters, rank, depth = down_buf.shape
    every = lax.dot_general(
        x,
        down_buf[...].reshape(adapters * rank, depth),
        (((1,), (1,)), ((), ())),
        preferred_element_type=F32,
    )
    for copy in copies:
        copy.wait()
    column = adapter_column(index, bank[0], adapters)
    column_out[...] = column
    lane = iota(column.shape, 1)
    per = HEAD_DIM // rank
    total = jnp.zeros(column.shape, F32)
    for j in range(adapters // per):
        part = every[:, j * HEAD_DIM : (j + 1) * HEAD_DIM]
        total += jnp.where(lane // rank + j * per == column, part, 0.0)
    inner[...] = total
    for s in range(out.shape[0]):
        out[s, :, width + HEAD_DIM :] = total


def project_sent(bank, index, x, other, weights):
    half, _, width = weights[0].shape
    rows = 2 * x.shape[0]
    return pl.pallas_call(
        project_sent_kernel,
        in_specs=[scalar(), big(), pl.BlockSpec(memory_space=pl.ANY)] + [whole()] * 5,
        out_specs=[whole()] * 3,
        out_shape=[
            shape(half, rows, width + 2 * HEAD_DIM),
            shape(rows, HEAD_DIM),
            shape(rows, HEAD_DIM, dtype=jnp.int32),
        ],
        scratch_shapes=[pltpu.SMEM(index[0].shape, jnp.int32)] * 2
        + [pltpu.SemaphoreType.DMA((2,))],
        compiler_params=params(),
        cost_estimate=pl.CostEstimate(
            flops=2 * rows * sum(w.size for w in weights),
            bytes_accessed=2 * sum(w.size for w in weights),
            transcendentals=0,
        ),
        name="project_sent",
    )(bank, in_hbm(index[0]), index[1], x, other, *weights)


def project_kept_kernel(
    ranks, place, bank, length, x_ref, other_ref, w_ref, kv_ref, inner, out, live, *scratch
):
    w_buf, kv_buf = scratch[:2]
    copies = start_slots(0, ranks, place, bank, w_ref, kv_ref, *scratch)
    width = w_buf.shape[2]
    beams = x_ref.shape[0]
    row = iota(live.shape, 0)
    limit = jnp.zeros(live.shape, jnp.int32)
    for beam in range(beams):
        limit = jnp.where(row // (live.shape[0] // beams) == beam, length[beam], limit)
    live[...] = limit
    x = beam_rows(x_ref, other_ref)
    for s, slot in enumerate(copies):
        wait_all([slot])
        project_slot(x, w_buf.at[s], kv_buf.at[s], out.at[s])
        out[s, :, width + HEAD_DIM :] = inner[...]


def project_kept(place, bank, length, x, other, wq, wkv, inner, ranks):
    beams, depth = x.shape
    rows = 2 * beams
    half = ranks // 2
    buffers = slot_buffers(wq, ranks)
    return pl.pallas_call(
        lambda *refs: project_kept_kernel(ranks, *refs),
        in_specs=[scalar()] * 3 + [whole()] * 2 + [big()] * 2 + [whole()],
        out_specs=[whole()] * 2,
        out_shape=[
            shape(half, rows, buffers[0].shape[2] + 2 * HEAD_DIM),
            shape(beams * wq.shape[1] // ranks // HEAD_DIM, HEAD_DIM, dtype=jnp.int32),
        ],
        scratch_shapes=[pltpu.VMEM(b.shape, BF16) for b in buffers] + slot_sems(half),
        compiler_params=params(8),
        cost_estimate=pl.CostEstimate(
            flops=rows * depth * (wq.shape[1] + wkv.shape[1]) // 2,
            bytes_accessed=wq.size + wkv.size,
            transcendentals=0,
        ),
        name="project_kept",
    )(place, bank, length, x, other, wq, wkv, inner)


def correct_kernel(bank, column_ref, up_ref, *refs):
    *parts, own_out, other_out = refs
    total = parts[0][...]
    for part in parts[1:]:
        total += part[...]
    count, rank, width = up_ref.shape
    half = width // 2
    inner = total[:, half + HEAD_DIM :].astype(BF16).astype(F32)
    column = column_ref[...]
    lane = iota(column.shape, 1)
    per = HEAD_DIM // rank
    spread = jnp.concatenate(
        [
            jnp.where(lane // rank + j * per == column, inner, 0.0)
            for j in range(count // per)
        ],
        axis=1,
    ).astype(BF16)
    delta = jnp.dot(
        spread, up_ref[...].reshape(count * rank, width), preferred_element_type=F32
    )
    rows = own_out.shape[0]
    for side in range(2):
        columns = slice(side * half, (side + 1) * half)
        part = delta[:, columns] + jnp.where(bank[0] == side, total[:, :half], 0.0)
        own_out[:, columns] = part[:rows]
        other_out[:, columns] = part[rows:]
    own_out[:, width:] = total[:rows, half : half + HEAD_DIM]
    other_out[:, width:] = total[rows:, half : half + HEAD_DIM]


def correct(bank, column, up, parts):
    rows = parts[0].shape[0]
    out = shape(rows // 2, up.shape[2] + HEAD_DIM)
    return pl.pallas_call(
        correct_kernel,
        in_specs=[scalar()] + [whole()] * (2 + len(parts)),
        out_specs=[whole()] * 2,
        out_shape=[out, out],
        compiler_params=params(),
        cost_estimate=pl.CostEstimate(
            flops=2 * rows * up.size, bytes_accessed=2 * up.size, transcendentals=0
        ),
        name="correct",
    )(bank, column, up, *parts)


def part_kernel(kept_ref, came_ref, *outs):
    for i, out in enumerate(outs):
        out[...] = kept_ref[i] + came_ref[i]


def part(kept, came):
    return pl.pallas_call(
        part_kernel,
        in_specs=[whole()] * 2,
        out_specs=[whole()] * kept.shape[0],
        out_shape=[shape(*kept.shape[1:])] * kept.shape[0],
        compiler_params=params(),
        name="part",
    )(kept, came)


def rotate(v, cosine, sine):
    return v * cosine + pltpu.roll(v, HEAD_DIM // 2, 1) * sine


def rotate_kernel(bank, own_ref, came_ref, cos_ref, sin_ref, q_ref, k_ref, v_ref, rows_ref):
    width = own_ref.shape[1] - HEAD_DIM
    cosine, sine = cos_ref[...], sin_ref[...]
    for g in range(width // HEAD_DIM):
        columns = slice(g * HEAD_DIM, (g + 1) * HEAD_DIM)
        rows_ref[:, g, :] = rotate(own_ref[:, columns] + came_ref[:, columns], cosine, sine)
    q_ref[0] = rows_ref[...].reshape(q_ref.shape[1:]).astype(BF16)
    own, came = own_ref[:, width:], came_ref[:, width:]
    key = jnp.where(bank[0] == 0, own, came)
    value = jnp.where(bank[0] == 0, came, own)
    k_ref[...] = rotate(key, cosine, sine).astype(BF16).astype(F32)
    v_ref[...] = value.astype(BF16).astype(F32)


def rotated(bank, own, came, cosine, sine):
    rows = own.shape[0]
    heads = own.shape[1] // HEAD_DIM - 1
    return pl.pallas_call(
        rotate_kernel,
        in_specs=[scalar()] + [whole()] * 4,
        out_specs=[whole()] * 3,
        out_shape=[
            shape(1, rows * heads, HEAD_DIM, dtype=BF16),
            shape(rows, HEAD_DIM),
            shape(rows, HEAD_DIM),
        ],
        scratch_shapes=[pltpu.VMEM((rows, heads, HEAD_DIM), F32)],
        compiler_params=params(),
        name="rotate",
    )(bank, own, came, cosine, sine)


def join_kernel(*refs):
    *parts, out_ref = refs
    for i, part in enumerate(parts):
        out_ref[i] = part[0]


def join(parts):
    return pl.pallas_call(
        join_kernel,
        in_specs=[whole()] * len(parts),
        out_specs=whole(),
        out_shape=shape(len(parts), *parts[0].shape[1:], dtype=parts[0].dtype),
        compiler_params=params(),
        name="join",
    )(*parts)


def attend_kernel(slots, earlier, place, bank, length_ref, q_ref, k_ref, v_ref, *refs):
    before, out_ref = refs[:-1], refs[-1]
    beams, positions, _ = k_ref.shape
    rows = q_ref.shape[1]
    group = rows // beams
    row, lane = iota((rows, HEAD_DIM), 0), iota((rows, HEAD_DIM), 1)
    left = length_ref[...] - place[0] * positions
    live = jnp.concatenate(
        [lane + first < left for first in range(0, positions, HEAD_DIM)], axis=1
    )
    for i, slot in enumerate(slots):
        head = rank_of(place[0], bank[0], slot)
        columns = pl.ds(pl.multiple_of(head * HEAD_DIM, HEAD_DIM), HEAD_DIM)
        query = q_ref[i].astype(F32)
        scores = jnp.concatenate(
            [
                lax.dot_general(
                    query[beam * group : (beam + 1) * group].astype(BF16),
                    k_ref[beam, :, columns],
                    (((1,), (1,)), ((), ())),
                    preferred_element_type=F32,
                )
                for beam in range(beams)
            ],
            axis=0,
        ) * (1.0 / HEAD_DIM**0.5)
        scores = jnp.where(live, scores, -1e30)
        peak = jnp.max(scores, axis=1, keepdims=True)
        weights = jnp.where(live, jnp.exp(scores - peak), 0.0)
        total = jnp.sum(weights, axis=1, keepdims=True)
        values = [
            jnp.dot(
                weights[beam * group : (beam + 1) * group].astype(BF16),
                v_ref[beam, :, columns],
                preferred_element_type=F32,
            )
            for beam in range(beams)
        ]
        stats = jnp.where(lane == row % group, peak, 0.0)
        stats += jnp.where(lane == group + row % group, total, 0.0)
        stats = jnp.sum(stats.reshape(beams, group, HEAD_DIM), axis=1)
        high = stats.astype(BF16).astype(F32)
        middle = (stats - high).astype(BF16).astype(F32)
        low = stats - high - middle
        tail = high + pltpu.roll(middle, 2 * group, 1) + pltpu.roll(low, 4 * group, 1)
        block = jnp.concatenate(values + [tail, jnp.zeros_like(tail)], axis=0)
        out_ref[head if earlier else i] = block.astype(BF16)
    if earlier:
        done = [(ref, i) for ref in before for i in range(ref.shape[0])]
        for slot, (ref, i) in zip(earlier, done):
            out_ref[rank_of(place[0], bank[0], slot)] = ref[i]


def attend(place, bank, length, queries, keys, values, slots, earlier=(), before=()):
    count, rows, _ = queries.shape
    beams, positions, _ = keys.shape
    return pl.pallas_call(
        lambda *refs: attend_kernel(slots, earlier, *refs),
        in_specs=[scalar()] * 2 + [whole()] * (4 + len(before)),
        out_specs=whole(),
        out_shape=shape(count + len(earlier), rows + 2 * beams, HEAD_DIM, dtype=BF16),
        compiler_params=params(),
        cost_estimate=pl.CostEstimate(
            flops=4 * rows * count * positions * HEAD_DIM,
            bytes_accessed=4 * beams * positions * HEAD_DIM * (16 if earlier else count),
            transcendentals=rows * count * positions,
        ),
        name="attend",
    )(place, bank, length, queries, keys, values, *before)


def combine_kernel(parts_ref, q_ref, k_ref, v_ref, out_ref, joined):
    ranks = parts_ref.shape[0]
    beams, group, _ = joined.shape
    rows = beams * group

    def by_row(v):
        return jnp.broadcast_to(v[:, None, :], (beams, group, HEAD_DIM)).reshape(rows, HEAD_DIM)

    head = iota((rows, HEAD_DIM), 0) % group
    lane = iota((rows, HEAD_DIM), 1)
    score = jnp.sum(q_ref[0].astype(F32) * by_row(k_ref[...]), axis=1, keepdims=True) * (
        1.0 / HEAD_DIM**0.5
    )
    peaks, totals, weighted = [], [], []
    top = score
    for s in range(ranks):
        block = parts_ref[s].astype(F32)
        tail = block[rows : rows + beams]
        for turn in (2, 4):
            tail += pltpu.roll(block[rows : rows + beams], HEAD_DIM - turn * group, 1)
        tail = by_row(tail)
        peak = jnp.sum(jnp.where(lane == head, tail, 0.0), axis=1, keepdims=True)
        total = jnp.sum(jnp.where(lane == group + head, tail, 0.0), axis=1, keepdims=True)
        top = jnp.maximum(top, peak)
        peaks.append(peak)
        totals.append(total)
        weighted.append(block[:rows])
    new = jnp.exp(score - top)
    everything = new
    result = new.astype(BF16).astype(F32) * by_row(v_ref[...])
    for peak, total, block in zip(peaks, totals, weighted):
        factor = jnp.exp(peak - top)
        everything += total * factor
        result += block * factor
    joined[...] = (result / everything).reshape(joined.shape)
    for g in range(group):
        out_ref[:, g * HEAD_DIM : (g + 1) * HEAD_DIM] = joined[:, g, :].astype(BF16)


def combine(parts, query, key_new, value_new):
    beams = key_new.shape[0]
    group = query.shape[1] // beams
    return pl.pallas_call(
        combine_kernel,
        in_specs=[whole()] * 4,
        out_specs=whole(),
        out_shape=shape(beams, group * HEAD_DIM, dtype=BF16),
        scratch_shapes=[pltpu.VMEM((beams, group, HEAD_DIM), F32)],
        compiler_params=params(),
        name="combine",
    )(parts, query, key_new, value_new)


def output_kernel(x_ref, w_ref, out):
    count, _, width = out.shape
    for s in range(count):
        columns = slice(s * width, (s + 1) * width)
        total = jnp.dot(x_ref[...], w_ref[:, columns], preferred_element_type=F32)
        out[s] = total.astype(BF16)


def output(x, weight, ranks):
    beams = x.shape[0]
    return pl.pallas_call(
        output_kernel,
        in_specs=[whole()] * 2,
        out_specs=whole(),
        out_shape=shape(ranks, beams, weight.shape[1] // ranks, dtype=BF16),
        compiler_params=params(),
        cost_estimate=pl.CostEstimate(
            flops=2 * beams * weight.size, bytes_accessed=2 * weight.size, transcendentals=0
        ),
        name="output",
    )(x, weight)


def residual_kernel(x_ref, parts_ref, out_ref):
    total = jnp.sum(parts_ref[...].astype(F32), axis=0)
    out_ref[...] = (x_ref[...].astype(F32) + total).astype(BF16)


def residual(x, parts):
    return pl.pallas_call(
        residual_kernel,
        in_specs=[whole()] * 2,
        out_specs=whole(),
        out_shape=jax.ShapeDtypeStruct(x.shape, BF16),
        compiler_params=params(),
        name="residual",
    )(x, parts)


def swapped(x):
    return lax.ppermute(x, "bank", [(0, 1), (1, 0)])


def traded(blocks):
    return lax.all_to_all(blocks, "tensor", 0, 0, tiled=True)


def hop(x, bit):
    pairs = []
    for rank in range(lax.axis_size("tensor")):
        for bank in range(2):
            pairs.append((2 * rank + bank, 2 * rank_of(rank, bank, bit) + bank))
    return lax.ppermute(x, ("tensor", "bank"), pairs)


def matched_body(
    normed_hidden_input,
    beam_adapter_index,
    beam_cache_length,
    query_weight,
    keyvalue_weight,
    output_weight,
    lowrank_down_factors,
    lowrank_up_factors,
    paged_key_cache,
    paged_value_cache,
):
    x = normed_hidden_input
    ranks = lax.axis_size("tensor")
    place = lax.axis_index("tensor").astype(jnp.int32).reshape(1)
    bank = lax.axis_index("bank").astype(jnp.int32).reshape(1)
    index = (beam_adapter_index, swapped(beam_adapter_index))
    x_other = swapped(x)
    lane = jnp.arange(HEAD_DIM, dtype=jnp.int32)
    half = HEAD_DIM // 2
    frequency = jnp.power(500000.0, -2.0 * (lane % half).astype(F32) / HEAD_DIM)
    angles = beam_cache_length.astype(F32)[:, None] * frequency[None, :]
    cosine = jnp.cos(angles)
    sine = jnp.where(lane < half, -1.0, 1.0) * jnp.sin(angles)
    weights = in_hbm(query_weight), in_hbm(keyvalue_weight)
    down = in_hbm(lowrank_down_factors.swapaxes(1, 2))
    ahead = fetch(place, bank, *weights, down, ranks)
    sent, inner, column = project_sent(bank, index, x, x_other, ahead)
    came = hop(sent, 1)
    kept, length = project_kept(
        place, bank, beam_cache_length, x, x_other, *weights, inner, ranks
    )
    kept, *sent = part(kept, came)
    near = tuple(range(ranks - 2, 0, -2))
    parts = [kept] + [hop(sent[slot // 2 - 1], slot) for slot in near]
    own, other = correct(bank, column, lowrank_up_factors, parts)
    query, key_new, value_new = rotated(bank, own, swapped(other), cosine, sine)

    def attended_part(queries, slots, **more):
        cache = paged_key_cache, paged_value_cache
        return attend(place, bank, length, queries, *cache, slots, **more)

    gathered = join([query] + [hop(query, slot) for slot in near])
    came = hop(gathered, 1)
    done = attended_part(gathered, (0, *near))
    odd = tuple(slot + 1 for slot in (0, *near))
    partial = attended_part(came, odd, earlier=(0, *near), before=(done,))
    attended = combine(traded(partial), query, key_new, value_new)
    return residual(x, traded(output(attended, output_weight, ranks)))


def joined(x, axis, combine):
    everything = jax.tree.map(lambda part: lax.all_gather(part, axis), x)
    leading = jax.tree.map(lambda part: part[0], everything)

    def turn(k, so_far):
        return combine(so_far, jax.tree.map(lambda part: part[k], everything))

    return lax.fori_loop(1, lax.axis_size(axis), turn, leading)


def apply_rotary(values, positions, head_size):
    row_count, col_count = values.shape
    half_size = head_size // 2
    frequency = jnp.power(500000.0, -2.0 * jnp.arange(half_size, dtype=jnp.float32) / head_size)
    angles = positions.astype(jnp.float32)[:, None] * frequency[None, :]
    cosine_table = jnp.cos(angles)[:, None, :]
    sine_table = jnp.sin(angles)[:, None, :]
    shaped = values.reshape(row_count, col_count // head_size, 2, half_size)
    first_half = shaped[:, :, 0]
    second_half = shaped[:, :, 1]
    rotated = jnp.stack(
        [
            first_half * cosine_table - second_half * sine_table,
            second_half * cosine_table + first_half * sine_table,
        ],
        axis=2,
    )
    return rotated.reshape(row_count, col_count)


def combine_parts(first_part, second_part):
    peak_one, total_one, weighted_one = first_part
    peak_two, total_two, weighted_two = second_part
    peak_both = jnp.maximum(peak_one, peak_two)
    factor_one = jnp.exp(peak_one - peak_both)
    factor_two = jnp.exp(peak_two - peak_both)
    return (
        peak_both,
        total_one * factor_one + total_two * factor_two,
        weighted_one * factor_one[..., None] + weighted_two * factor_two[..., None],
    )


def finish_heads(peak_score, weight_total, weighted, score_new, value_rows):
    peak_final = jnp.maximum(peak_score, score_new)
    old_factor = jnp.exp(peak_score - peak_final)
    new_weight = jnp.exp(score_new - peak_final)
    weight_total = weight_total * old_factor + new_weight
    weighted = (
        weighted * old_factor[..., None]
        + new_weight.astype(jnp.bfloat16).astype(jnp.float32)[..., None] * value_rows
    )
    return weighted / weight_total[..., None]


def body(
    normed_hidden_input,
    beam_adapter_index,
    beam_cache_length,
    query_weight,
    keyvalue_weight,
    output_weight,
    lowrank_down_factors,
    lowrank_up_factors,
    paged_key_cache,
    paged_value_cache,
):
    beam_rows, width_part = normed_hidden_input.shape
    model_width = query_weight.shape[1]
    kv_width = keyvalue_weight.shape[1] // 2
    head_count = model_width // HEAD_DIM
    kv_heads = kv_width // HEAD_DIM
    group_size = head_count // kv_heads
    tensor_index = lax.axis_index("tensor")
    query_part = jnp.dot(normed_hidden_input, query_weight, preferred_element_type=jnp.float32)
    keyval_part = jnp.dot(normed_hidden_input, keyvalue_weight, preferred_element_type=jnp.float32)
    down_all, up_all = (
        lax.all_gather(lowrank_down_factors, "bank", axis=0, tiled=True),
        lax.all_gather(lowrank_up_factors, "bank", axis=0, tiled=True),
    )
    inner_part = jnp.einsum(
        "ci,cim->cm",
        normed_hidden_input,
        down_all[beam_adapter_index],
        preferred_element_type=jnp.float32,
    )
    inner_total = lax.psum(inner_part, "tensor").astype(jnp.bfloat16)
    lowrank_delta = jnp.einsum(
        "mc,mct->mt", inner_total, up_all[beam_adapter_index], preferred_element_type=jnp.float32
    )
    query_total, keyval = lax.psum((query_part, keyval_part), "tensor")
    delta_total = lax.all_gather(lowrank_delta, "tensor", axis=1, tiled=True)
    query_rotated = apply_rotary(query_total + delta_total, beam_cache_length, HEAD_DIM).astype(
        jnp.bfloat16
    )
    key_new = apply_rotary(keyval[:, :kv_width], beam_cache_length, HEAD_DIM).astype(jnp.bfloat16)
    value_new = keyval[:, kv_width:].astype(jnp.bfloat16)
    position_count = paged_key_cache.shape[1]
    query_heads = query_rotated.reshape(beam_rows, kv_heads, group_size, HEAD_DIM)
    key_block = paged_key_cache.reshape(beam_rows, position_count, kv_heads, HEAD_DIM)
    value_block = paged_value_cache.reshape(beam_rows, position_count, kv_heads, HEAD_DIM)
    score_scale = 1.0 / HEAD_DIM**0.5
    scores = (
        jnp.einsum("bkgh,bpkh->bkgp", query_heads, key_block, preferred_element_type=jnp.float32)
        * score_scale
    )
    position_ids = tensor_index * position_count + jnp.arange(position_count)
    live_mask = (position_ids[None, :] < beam_cache_length[:, None])[:, None, None, :]
    scores = jnp.where(live_mask, scores, -1e30)
    peak_score = jnp.max(scores, axis=-1)
    weights = jnp.where(live_mask, jnp.exp(scores - peak_score[..., None]), 0.0)
    weight_total = jnp.sum(weights, axis=-1)
    weighted = jnp.einsum(
        "bkgp,bpkh->bkgh",
        weights.astype(jnp.bfloat16),
        value_block,
        preferred_element_type=jnp.float32,
    )
    peak_score, weight_total, weighted = joined(
        (peak_score, weight_total, weighted), "tensor", combine_parts
    )
    score_new = (
        jnp.einsum(
            "bkgh,bkh->bkg",
            query_heads,
            key_new.reshape(beam_rows, kv_heads, HEAD_DIM),
            preferred_element_type=jnp.float32,
        )
        * score_scale
    )
    value_rows = value_new.reshape(beam_rows, kv_heads, HEAD_DIM).astype(jnp.float32)[:, :, None, :]
    attended = (
        finish_heads(peak_score, weight_total, weighted, score_new, value_rows)
        .reshape(beam_rows, model_width)
        .astype(jnp.bfloat16)
    )
    attended_cols = lax.dynamic_slice_in_dim(attended, tensor_index * width_part, width_part, 1)
    mixed_cols = lax.psum_scatter(
        lax.dot_general(
            output_weight,
            attended_cols,
            (((0,), (1,)), ((), ())),
            preferred_element_type=jnp.float32,
        ),
        "tensor",
        scatter_dimension=0,
        tiled=True,
    )
    return (normed_hidden_input.astype(jnp.float32) + mixed_cols.T).astype(jnp.bfloat16)


def solution(mesh):
    matched = mesh.shape["tensor"] == 8 and mesh.shape["bank"] == 2
    return jax.shard_map(
        matched_body if matched else body,
        mesh=mesh,
        in_specs=(
            P(("groups", "bank"), "tensor"),
            P(("groups", "bank")),
            P(("groups", "bank")),
            P("tensor", None),
            P("tensor", None),
            P("tensor", None),
            P("bank", "tensor", None),
            P("bank", None, "tensor"),
            P(("groups", "bank"), "tensor", None),
            P(("groups", "bank"), "tensor", None),
        ),
        out_specs=P(("groups", "bank"), "tensor"),
        check_vma=False,
    )
```

```python
import jax
import jax.numpy as jnp
from jax import lax
from jax.experimental import pallas as pl
from jax.experimental.pallas import tpu as pltpu
from jax.sharding import PartitionSpec as P

HEAD_DIM = 128
F32 = jnp.float32
BF16 = jnp.bfloat16
CHUNKS = 2
MIB = 1024 * 1024


def whole():
    return pl.BlockSpec(memory_space=pltpu.VMEM)


def big():
    return pl.BlockSpec(memory_space=pltpu.HBM)


def scalar():
    return pl.BlockSpec(memory_space=pltpu.SMEM)


def in_hbm(array):
    return pltpu.with_memory_space_constraint(array, pltpu.HBM)


def shape(*dims, dtype=F32):
    return jax.ShapeDtypeStruct(dims, dtype)


def iota(dims, axis):
    return lax.broadcasted_iota(jnp.int32, dims, axis)


def params(mib=4):
    return pltpu.CompilerParams(vmem_limit_bytes=mib * MIB)


def exchanged(slot):
    return slot & ~3 | (slot & 1) << 1 | slot >> 1 & 1


def rank_of(place, bank, slot):
    return place ^ (slot + bank * (exchanged(slot) - slot))


def start_columns(weight, column, target, sems):
    depth, width = target.shape
    part = depth // CHUNKS
    copies = []
    for c in range(CHUNKS):
        rows = pl.ds(c * part, part)
        copies.append(
            pltpu.make_async_copy(
                weight.at[rows, pl.ds(pl.multiple_of(column, width), width)],
                target.at[rows, :],
                sems.at[c],
            )
        )
        copies[-1].start()
    return copies


def adapter_column(refs, bank, count):
    rows = len(refs) * refs[0].shape[0]
    row = iota((rows, HEAD_DIM), 0)
    column = jnp.zeros((rows, HEAD_DIM), jnp.int32)
    for r in range(rows):
        ref = refs[r // refs[0].shape[0]]
        column = jnp.where(row == r, ref[r % ref.shape[0]], column)
    return column - bank * count


def start_slots(parity, ranks, place, bank, w_ref, kv_ref, w_buf, kv_buf, sems, kv_sems):
    count, _, width = w_buf.shape
    copies = []
    for s in range(count):
        target = rank_of(place[0], bank[0], 2 * s + parity)
        copies.append(
            start_columns(w_ref, (2 * target + bank[0]) * width, w_buf.at[s], sems.at[s])
            + start_columns(
                kv_ref,
                (target + ranks * bank[0]) * HEAD_DIM,
                kv_buf.at[:, pl.ds(s * HEAD_DIM, HEAD_DIM)],
                kv_sems.at[s],
            )
        )
    return copies


def wait_all(copies):
    for slot in copies:
        for copy in slot:
            copy.wait()


def fetch_kernel(ranks, place, bank, w_ref, kv_ref, down_ref, w_buf, kv_buf, down_buf, *sems):
    down_copy = pltpu.make_async_copy(down_ref, down_buf, sems[2])
    down_copy.start()
    wait_all(start_slots(1, ranks, place, bank, w_ref, kv_ref, w_buf, kv_buf, *sems[:2]))
    down_copy.wait()


def slot_buffers(wq, ranks):
    count, depth = ranks // 2, wq.shape[0]
    return [
        shape(count, depth, wq.shape[1] // ranks // 2, dtype=BF16),
        shape(depth, count * HEAD_DIM, dtype=BF16),
    ]


def slot_sems(count):
    return [pltpu.SemaphoreType.DMA((count, CHUNKS))] * 2


def fetch(place, bank, wq, wkv, down, ranks):
    out = slot_buffers(wq, ranks) + [jax.ShapeDtypeStruct(down.shape, BF16)]
    return pl.pallas_call(
        lambda *refs: fetch_kernel(ranks, *refs),
        in_specs=[scalar()] * 2 + [big()] * 3,
        out_specs=[whole()] * 3,
        out_shape=out,
        scratch_shapes=slot_sems(ranks // 2) + [pltpu.SemaphoreType.DMA(())],
        compiler_params=params(),
        cost_estimate=pl.CostEstimate(
            flops=0, bytes_accessed=2 * sum(o.size for o in out), transcendentals=0
        ),
        name="fetch",
    )(place, bank, wq, wkv, down)


def beam_rows(x_ref, other_ref):
    rows = [x_ref[...].astype(F32), other_ref[...].astype(F32)]
    return jnp.concatenate(rows, axis=0).astype(BF16)


def project_keyval(x, kv_buf, out, width):
    keyval = jnp.dot(x, kv_buf[...], preferred_element_type=F32)
    for s in range(out.shape[0]):
        part = keyval[:, s * HEAD_DIM : (s + 1) * HEAD_DIM]
        out[s, :, width : width + HEAD_DIM] = part


def project_sent_kernel(
    bank, own_ref, came_ref, x_ref, other_ref, w_buf, kv_buf, down_buf, *refs
):
    out, inner, column_out, *index, sems = refs
    copies = [
        pltpu.make_async_copy(ref, held, sems.at[n])
        for n, (ref, held) in enumerate(zip((own_ref, came_ref), index))
    ]
    for copy in copies:
        copy.start()
    width = w_buf.shape[2]
    x = beam_rows(x_ref, other_ref)
    for s in range(out.shape[0]):
        out[s, :, :width] = jnp.dot(x, w_buf[s], preferred_element_type=F32)
    project_keyval(x, kv_buf, out, width)
    adapters, rank, depth = down_buf.shape
    every = lax.dot_general(
        x,
        down_buf[...].reshape(adapters * rank, depth),
        (((1,), (1,)), ((), ())),
        preferred_element_type=F32,
    )
    for copy in copies:
        copy.wait()
    column = adapter_column(index, bank[0], adapters)
    column_out[...] = column
    lane = iota(column.shape, 1)
    per = HEAD_DIM // rank
    total = jnp.zeros(column.shape, F32)
    for j in range(adapters // per):
        part = every[:, j * HEAD_DIM : (j + 1) * HEAD_DIM]
        total += jnp.where(lane // rank + j * per == column, part, 0.0)
    inner[...] = total
    for s in range(out.shape[0]):
        out[s, :, width + HEAD_DIM :] = total


def project_sent(bank, index, x, other, weights):
    half, _, width = weights[0].shape
    rows = 2 * x.shape[0]
    return pl.pallas_call(
        project_sent_kernel,
        in_specs=[scalar(), big(), pl.BlockSpec(memory_space=pl.ANY)] + [whole()] * 5,
        out_specs=[whole()] * 3,
        out_shape=[
            shape(half, rows, width + 2 * HEAD_DIM),
            shape(rows, HEAD_DIM),
            shape(rows, HEAD_DIM, dtype=jnp.int32),
        ],
        scratch_shapes=[pltpu.SMEM(index[0].shape, jnp.int32)] * 2
        + [pltpu.SemaphoreType.DMA((2,))],
        compiler_params=params(),
        cost_estimate=pl.CostEstimate(
            flops=2 * rows * sum(w.size for w in weights),
            bytes_accessed=2 * sum(w.size for w in weights),
            transcendentals=0,
        ),
        name="project_sent",
    )(bank, in_hbm(index[0]), index[1], x, other, *weights)


def project_kept_kernel(
    ranks, place, bank, length, x_ref, other_ref, w_ref, kv_ref, inner, out, live, *scratch
):
    w_buf, kv_buf = scratch[:2]
    copies = start_slots(0, ranks, place, bank, w_ref, kv_ref, *scratch)
    width = w_buf.shape[2]
    beams = x_ref.shape[0]
    row = iota(live.shape, 0)
    limit = jnp.zeros(live.shape, jnp.int32)
    for beam in range(beams):
        limit = jnp.where(row // (live.shape[0] // beams) == beam, length[beam], limit)
    live[...] = limit
    x = beam_rows(x_ref, other_ref)
    for s, slot in enumerate(copies):
        wait_all([slot])
        out[s, :, :width] = jnp.dot(x, w_buf[s], preferred_element_type=F32)
        out[s, :, width + HEAD_DIM :] = inner[...]
    project_keyval(x, kv_buf, out, width)


def project_kept(place, bank, length, x, other, wq, wkv, inner, ranks):
    beams, depth = x.shape
    rows = 2 * beams
    half = ranks // 2
    buffers = slot_buffers(wq, ranks)
    return pl.pallas_call(
        lambda *refs: project_kept_kernel(ranks, *refs),
        in_specs=[scalar()] * 3 + [whole()] * 2 + [big()] * 2 + [whole()],
        out_specs=[whole()] * 2,
        out_shape=[
            shape(half, rows, buffers[0].shape[2] + 2 * HEAD_DIM),
            shape(beams * wq.shape[1] // ranks // HEAD_DIM, HEAD_DIM, dtype=jnp.int32),
        ],
        scratch_shapes=[pltpu.VMEM(b.shape, BF16) for b in buffers] + slot_sems(half),
        compiler_params=params(8),
        cost_estimate=pl.CostEstimate(
            flops=rows * depth * (wq.shape[1] + wkv.shape[1]) // 2,
            bytes_accessed=wq.size + wkv.size,
            transcendentals=0,
        ),
        name="project_kept",
    )(place, bank, length, x, other, wq, wkv, inner)


def correct_kernel(bank, column_ref, up_ref, *refs):
    *parts, own_out, other_out = refs
    total = parts[0][...]
    for part in parts[1:]:
        total += part[...]
    count, rank, width = up_ref.shape
    half = width // 2
    inner = total[:, half + HEAD_DIM :].astype(BF16).astype(F32)
    column = column_ref[...]
    lane = iota(column.shape, 1)
    per = HEAD_DIM // rank
    spread = jnp.concatenate(
        [
            jnp.where(lane // rank + j * per == column, inner, 0.0)
            for j in range(count // per)
        ],
        axis=1,
    ).astype(BF16)
    delta = jnp.dot(
        spread, up_ref[...].reshape(count * rank, width), preferred_element_type=F32
    )
    rows = own_out.shape[0]
    for side in range(2):
        columns = slice(side * half, (side + 1) * half)
        part = delta[:, columns] + jnp.where(bank[0] == side, total[:, :half], 0.0)
        own_out[:, columns] = part[:rows]
        other_out[:, columns] = part[rows:]
    own_out[:, width:] = total[:rows, half : half + HEAD_DIM]
    other_out[:, width:] = total[rows:, half : half + HEAD_DIM]


def correct(bank, column, up, parts):
    rows = parts[0].shape[0]
    out = shape(rows // 2, up.shape[2] + HEAD_DIM)
    return pl.pallas_call(
        correct_kernel,
        in_specs=[scalar()] + [whole()] * (2 + len(parts)),
        out_specs=[whole()] * 2,
        out_shape=[out, out],
        compiler_params=params(),
        cost_estimate=pl.CostEstimate(
            flops=2 * rows * up.size, bytes_accessed=2 * up.size, transcendentals=0
        ),
        name="correct",
    )(bank, column, up, *parts)


def part_kernel(kept_ref, came_ref, *outs):
    for i, out in enumerate(outs):
        out[...] = kept_ref[i] + came_ref[i]


def part(kept, came):
    return pl.pallas_call(
        part_kernel,
        in_specs=[whole()] * 2,
        out_specs=[whole()] * kept.shape[0],
        out_shape=[shape(*kept.shape[1:])] * kept.shape[0],
        compiler_params=params(),
        name="part",
    )(kept, came)


def rotate(v, cosine, sine):
    return v * cosine + pltpu.roll(v, HEAD_DIM // 2, 1) * sine


def rotate_kernel(bank, own_ref, came_ref, cos_ref, sin_ref, q_ref, k_ref, v_ref, rows_ref):
    width = own_ref.shape[1] - HEAD_DIM
    cosine, sine = cos_ref[...], sin_ref[...]
    for g in range(width // HEAD_DIM):
        columns = slice(g * HEAD_DIM, (g + 1) * HEAD_DIM)
        rows_ref[:, g, :] = rotate(own_ref[:, columns] + came_ref[:, columns], cosine, sine)
    q_ref[0] = rows_ref[...].reshape(q_ref.shape[1:]).astype(BF16)
    own, came = own_ref[:, width:], came_ref[:, width:]
    key = jnp.where(bank[0] == 0, own, came)
    value = jnp.where(bank[0] == 0, came, own)
    k_ref[...] = rotate(key, cosine, sine).astype(BF16).astype(F32)
    v_ref[...] = value.astype(BF16).astype(F32)


def rotated(bank, own, came, cosine, sine):
    rows = own.shape[0]
    heads = own.shape[1] // HEAD_DIM - 1
    return pl.pallas_call(
        rotate_kernel,
        in_specs=[scalar()] + [whole()] * 4,
        out_specs=[whole()] * 3,
        out_shape=[
            shape(1, rows * heads, HEAD_DIM, dtype=BF16),
            shape(rows, HEAD_DIM),
            shape(rows, HEAD_DIM),
        ],
        scratch_shapes=[pltpu.VMEM((rows, heads, HEAD_DIM), F32)],
        compiler_params=params(),
        name="rotate",
    )(bank, own, came, cosine, sine)


def join_kernel(*refs):
    *parts, out_ref = refs
    for i, part in enumerate(parts):
        out_ref[i] = part[0]


def join(parts):
    return pl.pallas_call(
        join_kernel,
        in_specs=[whole()] * len(parts),
        out_specs=whole(),
        out_shape=shape(len(parts), *parts[0].shape[1:], dtype=parts[0].dtype),
        compiler_params=params(),
        name="join",
    )(*parts)


def attend_kernel(slots, earlier, place, bank, length_ref, q_ref, k_ref, v_ref, *refs):
    before, out_ref = refs[:-1], refs[-1]
    beams, positions, _ = k_ref.shape
    rows = q_ref.shape[1]
    group = rows // beams
    row, lane = iota((rows, HEAD_DIM), 0), iota((rows, HEAD_DIM), 1)
    left = length_ref[...] - place[0] * positions
    live = jnp.concatenate(
        [lane + first < left for first in range(0, positions, HEAD_DIM)], axis=1
    )
    for i, slot in enumerate(slots):
        head = rank_of(place[0], bank[0], slot)
        columns = pl.ds(pl.multiple_of(head * HEAD_DIM, HEAD_DIM), HEAD_DIM)
        query = q_ref[i].astype(F32)
        scores = jnp.concatenate(
            [
                lax.dot_general(
                    query[beam * group : (beam + 1) * group].astype(BF16),
                    k_ref[beam, :, columns],
                    (((1,), (1,)), ((), ())),
                    preferred_element_type=F32,
                )
                for beam in range(beams)
            ],
            axis=0,
        ) * (1.0 / HEAD_DIM**0.5)
        scores = jnp.where(live, scores, -1e30)
        peak = jnp.max(scores, axis=1, keepdims=True)
        weights = jnp.where(live, jnp.exp(scores - peak), 0.0)
        total = jnp.sum(weights, axis=1, keepdims=True)
        values = [
            jnp.dot(
                weights[beam * group : (beam + 1) * group].astype(BF16),
                v_ref[beam, :, columns],
                preferred_element_type=F32,
            )
            for beam in range(beams)
        ]
        stats = jnp.where(lane == row % group, peak, 0.0)
        stats += jnp.where(lane == group + row % group, total, 0.0)
        stats = jnp.sum(stats.reshape(beams, group, HEAD_DIM), axis=1)
        high = stats.astype(BF16).astype(F32)
        middle = (stats - high).astype(BF16).astype(F32)
        low = stats - high - middle
        tail = high + pltpu.roll(middle, 2 * group, 1) + pltpu.roll(low, 4 * group, 1)
        block = jnp.concatenate(values + [tail, jnp.zeros_like(tail)], axis=0)
        out_ref[head if earlier else i] = block.astype(BF16)
    if earlier:
        done = [(ref, i) for ref in before for i in range(ref.shape[0])]
        for slot, (ref, i) in zip(earlier, done):
            out_ref[rank_of(place[0], bank[0], slot)] = ref[i]


def attend(place, bank, length, queries, keys, values, slots, earlier=(), before=()):
    count, rows, _ = queries.shape
    beams, positions, _ = keys.shape
    return pl.pallas_call(
        lambda *refs: attend_kernel(slots, earlier, *refs),
        in_specs=[scalar()] * 2 + [whole()] * (4 + len(before)),
        out_specs=whole(),
        out_shape=shape(count + len(earlier), rows + 2 * beams, HEAD_DIM, dtype=BF16),
        compiler_params=params(),
        cost_estimate=pl.CostEstimate(
            flops=4 * rows * count * positions * HEAD_DIM,
            bytes_accessed=4 * beams * positions * HEAD_DIM * (16 if earlier else count),
            transcendentals=rows * count * positions,
        ),
        name="attend",
    )(place, bank, length, queries, keys, values, *before)


def combine_kernel(parts_ref, q_ref, k_ref, v_ref, out_ref, joined):
    ranks = parts_ref.shape[0]
    beams, group, _ = joined.shape
    rows = beams * group

    def by_row(v):
        return jnp.broadcast_to(v[:, None, :], (beams, group, HEAD_DIM)).reshape(rows, HEAD_DIM)

    head = iota((rows, HEAD_DIM), 0) % group
    lane = iota((rows, HEAD_DIM), 1)
    score = jnp.sum(q_ref[0].astype(F32) * by_row(k_ref[...]), axis=1, keepdims=True) * (
        1.0 / HEAD_DIM**0.5
    )
    peaks, totals, weighted = [], [], []
    top = score
    for s in range(ranks):
        block = parts_ref[s].astype(F32)
        tail = block[rows : rows + beams]
        for turn in (2, 4):
            tail += pltpu.roll(block[rows : rows + beams], HEAD_DIM - turn * group, 1)
        tail = by_row(tail)
        peak = jnp.sum(jnp.where(lane == head, tail, 0.0), axis=1, keepdims=True)
        total = jnp.sum(jnp.where(lane == group + head, tail, 0.0), axis=1, keepdims=True)
        top = jnp.maximum(top, peak)
        peaks.append(peak)
        totals.append(total)
        weighted.append(block[:rows])
    new = jnp.exp(score - top)
    everything = new
    result = new.astype(BF16).astype(F32) * by_row(v_ref[...])
    for peak, total, block in zip(peaks, totals, weighted):
        factor = jnp.exp(peak - top)
        everything += total * factor
        result += block * factor
    joined[...] = (result / everything).reshape(joined.shape)
    for g in range(group):
        out_ref[:, g * HEAD_DIM : (g + 1) * HEAD_DIM] = joined[:, g, :].astype(BF16)


def combine(parts, query, key_new, value_new):
    beams = key_new.shape[0]
    group = query.shape[1] // beams
    return pl.pallas_call(
        combine_kernel,
        in_specs=[whole()] * 4,
        out_specs=whole(),
        out_shape=shape(beams, group * HEAD_DIM, dtype=BF16),
        scratch_shapes=[pltpu.VMEM((beams, group, HEAD_DIM), F32)],
        compiler_params=params(),
        name="combine",
    )(parts, query, key_new, value_new)


def output_kernel(x_ref, w_ref, out):
    count, _, width = out.shape
    for s in range(count):
        columns = slice(s * width, (s + 1) * width)
        total = jnp.dot(x_ref[...], w_ref[:, columns], preferred_element_type=F32)
        out[s] = total.astype(BF16)


def output(x, weight, ranks):
    beams = x.shape[0]
    return pl.pallas_call(
        output_kernel,
        in_specs=[whole()] * 2,
        out_specs=whole(),
        out_shape=shape(ranks, beams, weight.shape[1] // ranks, dtype=BF16),
        compiler_params=params(),
        cost_estimate=pl.CostEstimate(
            flops=2 * beams * weight.size, bytes_accessed=2 * weight.size, transcendentals=0
        ),
        name="output",
    )(x, weight)


def residual_kernel(x_ref, parts_ref, out_ref):
    total = jnp.sum(parts_ref[...].astype(F32), axis=0)
    out_ref[...] = (x_ref[...].astype(F32) + total).astype(BF16)


def residual(x, parts):
    return pl.pallas_call(
        residual_kernel,
        in_specs=[whole()] * 2,
        out_specs=whole(),
        out_shape=jax.ShapeDtypeStruct(x.shape, BF16),
        compiler_params=params(),
        name="residual",
    )(x, parts)


def swapped(x):
    return lax.ppermute(x, "bank", [(0, 1), (1, 0)])


def traded(blocks):
    return lax.all_to_all(blocks, "tensor", 0, 0, tiled=True)


def hop(x, bit):
    pairs = []
    for rank in range(lax.axis_size("tensor")):
        for bank in range(2):
            pairs.append((2 * rank + bank, 2 * rank_of(rank, bank, bit) + bank))
    return lax.ppermute(x, ("tensor", "bank"), pairs)


def matched_body(
    normed_hidden_input,
    beam_adapter_index,
    beam_cache_length,
    query_weight,
    keyvalue_weight,
    output_weight,
    lowrank_down_factors,
    lowrank_up_factors,
    paged_key_cache,
    paged_value_cache,
):
    x = normed_hidden_input
    ranks = lax.axis_size("tensor")
    place = lax.axis_index("tensor").astype(jnp.int32).reshape(1)
    bank = lax.axis_index("bank").astype(jnp.int32).reshape(1)
    index = (beam_adapter_index, swapped(beam_adapter_index))
    x_other = swapped(x)
    lane = jnp.arange(HEAD_DIM, dtype=jnp.int32)
    half = HEAD_DIM // 2
    frequency = jnp.power(500000.0, -2.0 * (lane % half).astype(F32) / HEAD_DIM)
    angles = beam_cache_length.astype(F32)[:, None] * frequency[None, :]
    cosine = jnp.cos(angles)
    sine = jnp.where(lane < half, -1.0, 1.0) * jnp.sin(angles)
    weights = in_hbm(query_weight), in_hbm(keyvalue_weight)
    down = in_hbm(lowrank_down_factors.swapaxes(1, 2))
    ahead = fetch(place, bank, *weights, down, ranks)
    sent, inner, column = project_sent(bank, index, x, x_other, ahead)
    came = hop(sent, 1)
    kept, length = project_kept(
        place, bank, beam_cache_length, x, x_other, *weights, inner, ranks
    )
    kept, *sent = part(kept, came)
    near = tuple(range(ranks - 2, 0, -2))
    parts = [kept] + [hop(sent[slot // 2 - 1], slot) for slot in near]
    own, other = correct(bank, column, lowrank_up_factors, parts)
    query, key_new, value_new = rotated(bank, own, swapped(other), cosine, sine)

    def attended_part(queries, slots, **more):
        cache = paged_key_cache, paged_value_cache
        return attend(place, bank, length, queries, *cache, slots, **more)

    came, done = lax.optimization_barrier((hop(query, 1), attended_part(query, (0,))))
    pair = join([query, came])
    pairs = [hop(pair, slot) for slot in near]
    done = [done, attended_part(came, (1,))]
    order, slots = [0, 2, 1], [0, 1]
    for i in order[:-1]:
        done.append(attended_part(pairs[i], (near[i], near[i] + 1)))
        slots += [near[i], near[i] + 1]
    i = order[-1]
    last = near[i], near[i] + 1
    partial = attended_part(pairs[i], last, earlier=tuple(slots), before=tuple(done))
    attended = combine(traded(partial), query, key_new, value_new)
    return residual(x, traded(output(attended, output_weight, ranks)))


def joined(x, axis, combine):
    everything = jax.tree.map(lambda part: lax.all_gather(part, axis), x)
    leading = jax.tree.map(lambda part: part[0], everything)

    def turn(k, so_far):
        return combine(so_far, jax.tree.map(lambda part: part[k], everything))

    return lax.fori_loop(1, lax.axis_size(axis), turn, leading)


def apply_rotary(values, positions, head_size):
    row_count, col_count = values.shape
    half_size = head_size // 2
    frequency = jnp.power(500000.0, -2.0 * jnp.arange(half_size, dtype=jnp.float32) / head_size)
    angles = positions.astype(jnp.float32)[:, None] * frequency[None, :]
    cosine_table = jnp.cos(angles)[:, None, :]
    sine_table = jnp.sin(angles)[:, None, :]
    shaped = values.reshape(row_count, col_count // head_size, 2, half_size)
    first_half = shaped[:, :, 0]
    second_half = shaped[:, :, 1]
    rotated = jnp.stack(
        [
            first_half * cosine_table - second_half * sine_table,
            second_half * cosine_table + first_half * sine_table,
        ],
        axis=2,
    )
    return rotated.reshape(row_count, col_count)


def combine_parts(first_part, second_part):
    peak_one, total_one, weighted_one = first_part
    peak_two, total_two, weighted_two = second_part
    peak_both = jnp.maximum(peak_one, peak_two)
    factor_one = jnp.exp(peak_one - peak_both)
    factor_two = jnp.exp(peak_two - peak_both)
    return (
        peak_both,
        total_one * factor_one + total_two * factor_two,
        weighted_one * factor_one[..., None] + weighted_two * factor_two[..., None],
    )


def finish_heads(peak_score, weight_total, weighted, score_new, value_rows):
    peak_final = jnp.maximum(peak_score, score_new)
    old_factor = jnp.exp(peak_score - peak_final)
    new_weight = jnp.exp(score_new - peak_final)
    weight_total = weight_total * old_factor + new_weight
    weighted = (
        weighted * old_factor[..., None]
        + new_weight.astype(jnp.bfloat16).astype(jnp.float32)[..., None] * value_rows
    )
    return weighted / weight_total[..., None]


def body(
    normed_hidden_input,
    beam_adapter_index,
    beam_cache_length,
    query_weight,
    keyvalue_weight,
    output_weight,
    lowrank_down_factors,
    lowrank_up_factors,
    paged_key_cache,
    paged_value_cache,
):
    beam_rows, width_part = normed_hidden_input.shape
    model_width = query_weight.shape[1]
    kv_width = keyvalue_weight.shape[1] // 2
    head_count = model_width // HEAD_DIM
    kv_heads = kv_width // HEAD_DIM
    group_size = head_count // kv_heads
    tensor_index = lax.axis_index("tensor")
    query_part = jnp.dot(normed_hidden_input, query_weight, preferred_element_type=jnp.float32)
    keyval_part = jnp.dot(normed_hidden_input, keyvalue_weight, preferred_element_type=jnp.float32)
    down_all, up_all = (
        lax.all_gather(lowrank_down_factors, "bank", axis=0, tiled=True),
        lax.all_gather(lowrank_up_factors, "bank", axis=0, tiled=True),
    )
    inner_part = jnp.einsum(
        "ci,cim->cm",
        normed_hidden_input,
        down_all[beam_adapter_index],
        preferred_element_type=jnp.float32,
    )
    inner_total = lax.psum(inner_part, "tensor").astype(jnp.bfloat16)
    lowrank_delta = jnp.einsum(
        "mc,mct->mt", inner_total, up_all[beam_adapter_index], preferred_element_type=jnp.float32
    )
    query_total, keyval = lax.psum((query_part, keyval_part), "tensor")
    delta_total = lax.all_gather(lowrank_delta, "tensor", axis=1, tiled=True)
    query_rotated = apply_rotary(query_total + delta_total, beam_cache_length, HEAD_DIM).astype(
        jnp.bfloat16
    )
    key_new = apply_rotary(keyval[:, :kv_width], beam_cache_length, HEAD_DIM).astype(jnp.bfloat16)
    value_new = keyval[:, kv_width:].astype(jnp.bfloat16)
    position_count = paged_key_cache.shape[1]
    query_heads = query_rotated.reshape(beam_rows, kv_heads, group_size, HEAD_DIM)
    key_block = paged_key_cache.reshape(beam_rows, position_count, kv_heads, HEAD_DIM)
    value_block = paged_value_cache.reshape(beam_rows, position_count, kv_heads, HEAD_DIM)
    score_scale = 1.0 / HEAD_DIM**0.5
    scores = (
        jnp.einsum("bkgh,bpkh->bkgp", query_heads, key_block, preferred_element_type=jnp.float32)
        * score_scale
    )
    position_ids = tensor_index * position_count + jnp.arange(position_count)
    live_mask = (position_ids[None, :] < beam_cache_length[:, None])[:, None, None, :]
    scores = jnp.where(live_mask, scores, -1e30)
    peak_score = jnp.max(scores, axis=-1)
    weights = jnp.where(live_mask, jnp.exp(scores - peak_score[..., None]), 0.0)
    weight_total = jnp.sum(weights, axis=-1)
    weighted = jnp.einsum(
        "bkgp,bpkh->bkgh",
        weights.astype(jnp.bfloat16),
        value_block,
        preferred_element_type=jnp.float32,
    )
    peak_score, weight_total, weighted = joined(
        (peak_score, weight_total, weighted), "tensor", combine_parts
    )
    score_new = (
        jnp.einsum(
            "bkgh,bkh->bkg",
            query_heads,
            key_new.reshape(beam_rows, kv_heads, HEAD_DIM),
            preferred_element_type=jnp.float32,
        )
        * score_scale
    )
    value_rows = value_new.reshape(beam_rows, kv_heads, HEAD_DIM).astype(jnp.float32)[:, :, None, :]
    attended = (
        finish_heads(peak_score, weight_total, weighted, score_new, value_rows)
        .reshape(beam_rows, model_width)
        .astype(jnp.bfloat16)
    )
    attended_cols = lax.dynamic_slice_in_dim(attended, tensor_index * width_part, width_part, 1)
    mixed_cols = lax.psum_scatter(
        lax.dot_general(
            output_weight,
            attended_cols,
            (((0,), (1,)), ((), ())),
            preferred_element_type=jnp.float32,
        ),
        "tensor",
        scatter_dimension=0,
        tiled=True,
    )
    return (normed_hidden_input.astype(jnp.float32) + mixed_cols.T).astype(jnp.bfloat16)


def solution(mesh):
    matched = mesh.shape["tensor"] == 8 and mesh.shape["bank"] == 2
    return jax.shard_map(
        matched_body if matched else body,
        mesh=mesh,
        in_specs=(
            P(("groups", "bank"), "tensor"),
            P(("groups", "bank")),
            P(("groups", "bank")),
            P("tensor", None),
            P("tensor", None),
            P("tensor", None),
            P("bank", "tensor", None),
            P("bank", None, "tensor"),
            P(("groups", "bank"), "tensor", None),
            P(("groups", "bank"), "tensor", None),
        ),
        out_specs=P(("groups", "bank"), "tensor"),
        check_vma=False,
    )
```

```python
import jax
import jax.numpy as jnp
from jax import lax
from jax.experimental import pallas as pl
from jax.experimental.pallas import tpu as pltpu
from jax.sharding import PartitionSpec as P

HEAD_DIM = 128
F32 = jnp.float32
BF16 = jnp.bfloat16
CHUNKS = 2
MIB = 1024 * 1024


def whole():
    return pl.BlockSpec(memory_space=pltpu.VMEM)


def big():
    return pl.BlockSpec(memory_space=pltpu.HBM)


def scalar():
    return pl.BlockSpec(memory_space=pltpu.SMEM)


def in_hbm(array):
    return pltpu.with_memory_space_constraint(array, pltpu.HBM)


def shape(*dims, dtype=F32):
    return jax.ShapeDtypeStruct(dims, dtype)


def iota(dims, axis):
    return lax.broadcasted_iota(jnp.int32, dims, axis)


def params(mib=4):
    return pltpu.CompilerParams(vmem_limit_bytes=mib * MIB)


def exchanged(slot):
    return slot & ~3 | (slot & 1) << 1 | slot >> 1 & 1


def rank_of(place, bank, slot):
    return place ^ (slot + bank * (exchanged(slot) - slot))


def start_columns(weight, column, target, sems):
    depth, width = target.shape
    part = depth // CHUNKS
    copies = []
    for c in range(CHUNKS):
        rows = pl.ds(c * part, part)
        copies.append(
            pltpu.make_async_copy(
                weight.at[rows, pl.ds(pl.multiple_of(column, width), width)],
                target.at[rows, :],
                sems.at[c],
            )
        )
        copies[-1].start()
    return copies


def adapter_column(refs, bank, count):
    columns = []
    for ref in refs:
        rows = ref.shape[1]
        index = jnp.broadcast_to(ref[...].astype(F32), (rows, rows))
        diagonal = iota((rows, rows), 0) == iota((rows, rows), 1)
        columns.append(jnp.sum(jnp.where(diagonal, index, 0.0), axis=1, keepdims=True))
    column = jnp.concatenate(columns, axis=0).astype(jnp.int32) - bank * count
    return jnp.broadcast_to(column, (column.shape[0], HEAD_DIM))


def start_slots(parity, ranks, place, bank, w_ref, kv_ref, w_buf, kv_buf, sems, kv_sems):
    count, _, width = w_buf.shape
    copies = []
    for s in range(count):
        target = rank_of(place[0], bank[0], 2 * s + parity)
        copies.append(
            start_columns(w_ref, (2 * target + bank[0]) * width, w_buf.at[s], sems.at[s])
            + start_columns(
                kv_ref,
                (target + ranks * bank[0]) * HEAD_DIM,
                kv_buf.at[:, pl.ds(s * HEAD_DIM, HEAD_DIM)],
                kv_sems.at[s],
            )
        )
    return copies


def wait_all(copies):
    for slot in copies:
        for copy in slot:
            copy.wait()


def fetch_kernel(ranks, place, bank, *refs):
    wait_all(start_slots(1, ranks, place, bank, *refs))


def slot_buffers(wq, ranks):
    count, depth = ranks // 2, wq.shape[0]
    return [
        shape(count, depth, wq.shape[1] // ranks // 2, dtype=BF16),
        shape(depth, count * HEAD_DIM, dtype=BF16),
    ]


def slot_sems(count):
    return [pltpu.SemaphoreType.DMA((count, CHUNKS))] * 2


def fetch(place, bank, wq, wkv, ranks):
    out = slot_buffers(wq, ranks)
    return pl.pallas_call(
        lambda *refs: fetch_kernel(ranks, *refs),
        in_specs=[scalar()] * 2 + [big()] * 2,
        out_specs=[whole()] * 2,
        out_shape=out,
        scratch_shapes=slot_sems(ranks // 2),
        compiler_params=params(),
        cost_estimate=pl.CostEstimate(
            flops=0, bytes_accessed=2 * sum(o.size for o in out), transcendentals=0
        ),
        name="fetch",
    )(place, bank, wq, wkv)


def beam_rows(x_ref, other_ref):
    rows = [x_ref[...].astype(F32), other_ref[...].astype(F32)]
    return jnp.concatenate(rows, axis=0).astype(BF16)


def project_keyval(x, kv_buf, out, width):
    keyval = jnp.dot(x, kv_buf[...], preferred_element_type=F32)
    for s in range(out.shape[0]):
        part = keyval[:, s * HEAD_DIM : (s + 1) * HEAD_DIM]
        out[s, :, width : width + HEAD_DIM] = part


def project_sent_kernel(
    bank, own_ref, came_ref, x_ref, other_ref, w_buf, kv_buf, down_ref, *refs
):
    out, inner, column_out, down_buf, sems = refs
    adapters, rank, depth = down_buf.shape
    part = adapters // sems.shape[0]
    copies = [
        pltpu.make_async_copy(
            down_ref.at[pl.ds(c * part, part)], down_buf.at[pl.ds(c * part, part)], sems.at[c]
        )
        for c in range(sems.shape[0])
    ]
    for copy in copies:
        copy.start()
    width = w_buf.shape[2]
    x = beam_rows(x_ref, other_ref)
    for s in range(out.shape[0]):
        out[s, :, :width] = jnp.dot(x, w_buf[s], preferred_element_type=F32)
    project_keyval(x, kv_buf, out, width)
    column = adapter_column((own_ref, came_ref), bank[0], adapters)
    column_out[...] = column
    for copy in copies:
        copy.wait()
    every = lax.dot_general(
        x,
        down_buf[...].reshape(adapters * rank, depth),
        (((1,), (1,)), ((), ())),
        preferred_element_type=F32,
    )
    lane = iota(column.shape, 1)
    per = HEAD_DIM // rank
    total = jnp.zeros(column.shape, F32)
    for j in range(adapters // per):
        part = every[:, j * HEAD_DIM : (j + 1) * HEAD_DIM]
        total += jnp.where(lane // rank + j * per == column, part, 0.0)
    inner[...] = total
    for s in range(out.shape[0]):
        out[s, :, width + HEAD_DIM :] = total


def project_sent(bank, index, x, other, weights, down):
    half, _, width = weights[0].shape
    rows = 2 * x.shape[0]
    return pl.pallas_call(
        project_sent_kernel,
        in_specs=[scalar()] + [whole()] * 6 + [big()],
        out_specs=[whole()] * 3,
        out_shape=[
            shape(half, rows, width + 2 * HEAD_DIM),
            shape(rows, HEAD_DIM),
            shape(rows, HEAD_DIM, dtype=jnp.int32),
        ],
        scratch_shapes=[pltpu.VMEM(down.shape, BF16), pltpu.SemaphoreType.DMA((2,))],
        compiler_params=params(8),
        cost_estimate=pl.CostEstimate(
            flops=2 * rows * (sum(w.size for w in weights) + down.size),
            bytes_accessed=2 * (sum(w.size for w in weights) + down.size),
            transcendentals=0,
        ),
        name="project_sent",
    )(bank, *[i.reshape(1, -1) for i in index], x, other, *weights, down)


def project_kept_kernel(
    ranks, place, bank, length, x_ref, other_ref, w_ref, kv_ref, inner, out, live, *scratch
):
    w_buf, kv_buf = scratch[:2]
    copies = start_slots(0, ranks, place, bank, w_ref, kv_ref, *scratch)
    width = w_buf.shape[2]
    beams = x_ref.shape[0]
    row = iota(live.shape, 0)
    limit = jnp.zeros(live.shape, jnp.int32)
    for beam in range(beams):
        limit = jnp.where(row // (live.shape[0] // beams) == beam, length[beam], limit)
    live[...] = limit
    x = beam_rows(x_ref, other_ref)
    for s, slot in enumerate(copies):
        wait_all([slot])
        out[s, :, :width] = jnp.dot(x, w_buf[s], preferred_element_type=F32)
        out[s, :, width + HEAD_DIM :] = inner[...]
    project_keyval(x, kv_buf, out, width)


def project_kept(place, bank, length, x, other, wq, wkv, inner, ranks):
    beams, depth = x.shape
    rows = 2 * beams
    half = ranks // 2
    buffers = slot_buffers(wq, ranks)
    return pl.pallas_call(
        lambda *refs: project_kept_kernel(ranks, *refs),
        in_specs=[scalar()] * 3 + [whole()] * 2 + [big()] * 2 + [whole()],
        out_specs=[whole()] * 2,
        out_shape=[
            shape(half, rows, buffers[0].shape[2] + 2 * HEAD_DIM),
            shape(beams * wq.shape[1] // ranks // HEAD_DIM, HEAD_DIM, dtype=jnp.int32),
        ],
        scratch_shapes=[pltpu.VMEM(b.shape, BF16) for b in buffers] + slot_sems(half),
        compiler_params=params(8),
        cost_estimate=pl.CostEstimate(
            flops=rows * depth * (wq.shape[1] + wkv.shape[1]) // 2,
            bytes_accessed=wq.size + wkv.size,
            transcendentals=0,
        ),
        name="project_kept",
    )(place, bank, length, x, other, wq, wkv, inner)


def correct_kernel(bank, column_ref, up_ref, *refs):
    *parts, own_out, other_out = refs
    total = parts[0][...]
    for part in parts[1:]:
        total += part[...]
    count, rank, width = up_ref.shape
    half = width // 2
    inner = total[:, half + HEAD_DIM :].astype(BF16).astype(F32)
    column = column_ref[...]
    lane = iota(column.shape, 1)
    per = HEAD_DIM // rank
    spread = jnp.concatenate(
        [
            jnp.where(lane // rank + j * per == column, inner, 0.0)
            for j in range(count // per)
        ],
        axis=1,
    ).astype(BF16)
    delta = jnp.dot(
        spread, up_ref[...].reshape(count * rank, width), preferred_element_type=F32
    )
    rows = own_out.shape[0]
    for side in range(2):
        columns = slice(side * half, (side + 1) * half)
        part = delta[:, columns] + jnp.where(bank[0] == side, total[:, :half], 0.0)
        own_out[:, columns] = part[:rows]
        other_out[:, columns] = part[rows:]
    own_out[:, width:] = total[:rows, half : half + HEAD_DIM]
    other_out[:, width:] = total[rows:, half : half + HEAD_DIM]


def correct(bank, column, up, parts):
    rows = parts[0].shape[0]
    out = shape(rows // 2, up.shape[2] + HEAD_DIM)
    return pl.pallas_call(
        correct_kernel,
        in_specs=[scalar()] + [whole()] * (2 + len(parts)),
        out_specs=[whole()] * 2,
        out_shape=[out, out],
        compiler_params=params(),
        cost_estimate=pl.CostEstimate(
            flops=2 * rows * up.size, bytes_accessed=2 * up.size, transcendentals=0
        ),
        name="correct",
    )(bank, column, up, *parts)


def part_kernel(kept_ref, came_ref, *outs):
    for i, out in enumerate(outs):
        out[...] = kept_ref[i] + came_ref[i]


def part(kept, came):
    return pl.pallas_call(
        part_kernel,
        in_specs=[whole()] * 2,
        out_specs=[whole()] * kept.shape[0],
        out_shape=[shape(*kept.shape[1:])] * kept.shape[0],
        compiler_params=params(),
        name="part",
    )(kept, came)


def rotate(v, cosine, sine):
    return v * cosine + pltpu.roll(v, HEAD_DIM // 2, 1) * sine


def rotate_kernel(bank, own_ref, came_ref, cos_ref, sin_ref, q_ref, k_ref, v_ref, rows_ref):
    width = own_ref.shape[1] - HEAD_DIM
    cosine, sine = cos_ref[...], sin_ref[...]
    for g in range(width // HEAD_DIM):
        columns = slice(g * HEAD_DIM, (g + 1) * HEAD_DIM)
        rows_ref[:, g, :] = rotate(own_ref[:, columns] + came_ref[:, columns], cosine, sine)
    q_ref[0] = rows_ref[...].reshape(q_ref.shape[1:]).astype(BF16)
    own, came = own_ref[:, width:], came_ref[:, width:]
    key = jnp.where(bank[0] == 0, own, came)
    value = jnp.where(bank[0] == 0, came, own)
    k_ref[...] = rotate(key, cosine, sine).astype(BF16).astype(F32)
    v_ref[...] = value.astype(BF16).astype(F32)


def rotated(bank, own, came, cosine, sine):
    rows = own.shape[0]
    heads = own.shape[1] // HEAD_DIM - 1
    return pl.pallas_call(
        rotate_kernel,
        in_specs=[scalar()] + [whole()] * 4,
        out_specs=[whole()] * 3,
        out_shape=[
            shape(1, rows * heads, HEAD_DIM, dtype=BF16),
            shape(rows, HEAD_DIM),
            shape(rows, HEAD_DIM),
        ],
        scratch_shapes=[pltpu.VMEM((rows, heads, HEAD_DIM), F32)],
        compiler_params=params(),
        name="rotate",
    )(bank, own, came, cosine, sine)


def join_kernel(*refs):
    *parts, out_ref = refs
    for i, part in enumerate(parts):
        out_ref[i] = part[0]


def join(parts):
    return pl.pallas_call(
        join_kernel,
        in_specs=[whole()] * len(parts),
        out_specs=whole(),
        out_shape=shape(len(parts), *parts[0].shape[1:], dtype=parts[0].dtype),
        compiler_params=params(),
        name="join",
    )(*parts)


def attend_kernel(slots, earlier, place, bank, length_ref, q_ref, k_ref, v_ref, *refs):
    before, out_ref = refs[:-1], refs[-1]
    beams, positions, _ = k_ref.shape
    rows = q_ref.shape[1]
    group = rows // beams
    row, lane = iota((rows, HEAD_DIM), 0), iota((rows, HEAD_DIM), 1)
    left = length_ref[...] - place[0] * positions
    live = jnp.concatenate(
        [lane + first < left for first in range(0, positions, HEAD_DIM)], axis=1
    )
    for i, slot in enumerate(slots):
        head = rank_of(place[0], bank[0], slot)
        columns = pl.ds(pl.multiple_of(head * HEAD_DIM, HEAD_DIM), HEAD_DIM)
        query = q_ref[i].astype(F32)
        scores = jnp.concatenate(
            [
                lax.dot_general(
                    query[beam * group : (beam + 1) * group].astype(BF16),
                    k_ref[beam, :, columns],
                    (((1,), (1,)), ((), ())),
                    preferred_element_type=F32,
                )
                for beam in range(beams)
            ],
            axis=0,
        ) * (1.0 / HEAD_DIM**0.5)
        scores = jnp.where(live, scores, -1e30)
        peak = jnp.max(scores, axis=1, keepdims=True)
        weights = jnp.where(live, jnp.exp(scores - peak), 0.0)
        total = jnp.sum(weights, axis=1, keepdims=True)
        values = [
            jnp.dot(
                weights[beam * group : (beam + 1) * group].astype(BF16),
                v_ref[beam, :, columns],
                preferred_element_type=F32,
            )
            for beam in range(beams)
        ]
        stats = jnp.where(lane == row % group, peak, 0.0)
        stats += jnp.where(lane == group + row % group, total, 0.0)
        stats = jnp.sum(stats.reshape(beams, group, HEAD_DIM), axis=1)
        high = stats.astype(BF16).astype(F32)
        middle = (stats - high).astype(BF16).astype(F32)
        low = stats - high - middle
        tail = high + pltpu.roll(middle, 2 * group, 1) + pltpu.roll(low, 4 * group, 1)
        block = jnp.concatenate(values + [tail, jnp.zeros_like(tail)], axis=0)
        out_ref[head if earlier else i] = block.astype(BF16)
    if earlier:
        done = [(ref, i) for ref in before for i in range(ref.shape[0])]
        for slot, (ref, i) in zip(earlier, done):
            out_ref[rank_of(place[0], bank[0], slot)] = ref[i]


def attend(place, bank, length, queries, keys, values, slots, earlier=(), before=()):
    count, rows, _ = queries.shape
    beams, positions, _ = keys.shape
    return pl.pallas_call(
        lambda *refs: attend_kernel(slots, earlier, *refs),
        in_specs=[scalar()] * 2 + [whole()] * (4 + len(before)),
        out_specs=whole(),
        out_shape=shape(count + len(earlier), rows + 2 * beams, HEAD_DIM, dtype=BF16),
        compiler_params=params(),
        cost_estimate=pl.CostEstimate(
            flops=4 * rows * count * positions * HEAD_DIM,
            bytes_accessed=4 * beams * positions * HEAD_DIM * (16 if earlier else count),
            transcendentals=rows * count * positions,
        ),
        name="attend",
    )(place, bank, length, queries, keys, values, *before)


def combine_kernel(parts_ref, q_ref, k_ref, v_ref, out_ref, joined):
    ranks = parts_ref.shape[0]
    beams, group, _ = joined.shape
    rows = beams * group

    def by_row(v):
        return jnp.broadcast_to(v[:, None, :], (beams, group, HEAD_DIM)).reshape(rows, HEAD_DIM)

    head = iota((rows, HEAD_DIM), 0) % group
    lane = iota((rows, HEAD_DIM), 1)
    score = jnp.sum(q_ref[0].astype(F32) * by_row(k_ref[...]), axis=1, keepdims=True) * (
        1.0 / HEAD_DIM**0.5
    )
    peaks, totals, weighted = [], [], []
    top = score
    for s in range(ranks):
        block = parts_ref[s].astype(F32)
        tail = block[rows : rows + beams]
        for turn in (2, 4):
            tail += pltpu.roll(block[rows : rows + beams], HEAD_DIM - turn * group, 1)
        tail = by_row(tail)
        peak = jnp.sum(jnp.where(lane == head, tail, 0.0), axis=1, keepdims=True)
        total = jnp.sum(jnp.where(lane == group + head, tail, 0.0), axis=1, keepdims=True)
        top = jnp.maximum(top, peak)
        peaks.append(peak)
        totals.append(total)
        weighted.append(block[:rows])
    new = jnp.exp(score - top)
    everything = new
    result = new.astype(BF16).astype(F32) * by_row(v_ref[...])
    for peak, total, block in zip(peaks, totals, weighted):
        factor = jnp.exp(peak - top)
        everything += total * factor
        result += block * factor
    joined[...] = (result / everything).reshape(joined.shape)
    for g in range(group):
        out_ref[:, g * HEAD_DIM : (g + 1) * HEAD_DIM] = joined[:, g, :].astype(BF16)


def combine(parts, query, key_new, value_new):
    beams = key_new.shape[0]
    group = query.shape[1] // beams
    return pl.pallas_call(
        combine_kernel,
        in_specs=[whole()] * 4,
        out_specs=whole(),
        out_shape=shape(beams, group * HEAD_DIM, dtype=BF16),
        scratch_shapes=[pltpu.VMEM((beams, group, HEAD_DIM), F32)],
        compiler_params=params(),
        name="combine",
    )(parts, query, key_new, value_new)


def output_kernel(x_ref, w_ref, out):
    count, _, width = out.shape
    for s in range(count):
        columns = slice(s * width, (s + 1) * width)
        total = jnp.dot(x_ref[...], w_ref[:, columns], preferred_element_type=F32)
        out[s] = total.astype(BF16)


def output(x, weight, ranks):
    beams = x.shape[0]
    return pl.pallas_call(
        output_kernel,
        in_specs=[whole()] * 2,
        out_specs=whole(),
        out_shape=shape(ranks, beams, weight.shape[1] // ranks, dtype=BF16),
        compiler_params=params(),
        cost_estimate=pl.CostEstimate(
            flops=2 * beams * weight.size, bytes_accessed=2 * weight.size, transcendentals=0
        ),
        name="output",
    )(x, weight)


def residual_kernel(x_ref, parts_ref, out_ref):
    total = jnp.sum(parts_ref[...].astype(F32), axis=0)
    out_ref[...] = (x_ref[...].astype(F32) + total).astype(BF16)


def residual(x, parts):
    return pl.pallas_call(
        residual_kernel,
        in_specs=[whole()] * 2,
        out_specs=whole(),
        out_shape=jax.ShapeDtypeStruct(x.shape, BF16),
        compiler_params=params(),
        name="residual",
    )(x, parts)


def swapped(x):
    return lax.ppermute(x, "bank", [(0, 1), (1, 0)])


def traded(blocks):
    return lax.all_to_all(blocks, "tensor", 0, 0, tiled=True)


def hop(x, bit):
    pairs = []
    for rank in range(lax.axis_size("tensor")):
        for bank in range(2):
            pairs.append((2 * rank + bank, 2 * rank_of(rank, bank, bit) + bank))
    return lax.ppermute(x, ("tensor", "bank"), pairs)


def matched_body(
    normed_hidden_input,
    beam_adapter_index,
    beam_cache_length,
    query_weight,
    keyvalue_weight,
    output_weight,
    lowrank_down_factors,
    lowrank_up_factors,
    paged_key_cache,
    paged_value_cache,
):
    x = normed_hidden_input
    ranks = lax.axis_size("tensor")
    place = lax.axis_index("tensor").astype(jnp.int32).reshape(1)
    bank = lax.axis_index("bank").astype(jnp.int32).reshape(1)
    index = (beam_adapter_index, swapped(beam_adapter_index))
    x_other = swapped(x)
    lane = jnp.arange(HEAD_DIM, dtype=jnp.int32)
    half = HEAD_DIM // 2
    frequency = jnp.power(500000.0, -2.0 * (lane % half).astype(F32) / HEAD_DIM)
    angles = beam_cache_length.astype(F32)[:, None] * frequency[None, :]
    cosine = jnp.cos(angles)
    sine = jnp.where(lane < half, -1.0, 1.0) * jnp.sin(angles)
    weights = in_hbm(query_weight), in_hbm(keyvalue_weight)
    down = in_hbm(lowrank_down_factors.swapaxes(1, 2))
    odd = fetch(place, bank, *weights, ranks)
    sent, inner, column = project_sent(bank, index, x, x_other, odd, down)
    came = hop(sent, 1)
    kept, length = project_kept(
        place, bank, beam_cache_length, x, x_other, *weights, inner, ranks
    )
    kept, *sent = part(kept, came)
    near = tuple(range(ranks - 2, 0, -2))
    parts = [kept] + [hop(sent[slot // 2 - 1], slot) for slot in near]
    own, other = correct(bank, column, lowrank_up_factors, parts)
    query, key_new, value_new = rotated(bank, own, swapped(other), cosine, sine)

    def attended_part(queries, slots, **more):
        cache = paged_key_cache, paged_value_cache
        return attend(place, bank, length, queries, *cache, slots, **more)

    came, done = lax.optimization_barrier((hop(query, 1), attended_part(query, (0,))))
    pair = join([query, came])
    pairs = [hop(pair, slot) for slot in near]
    done = [done, attended_part(came, (1,))]
    slots = [0, 1]
    for i in range(len(near) - 1):
        done.append(attended_part(pairs[i], (near[i], near[i] + 1)))
        slots += [near[i], near[i] + 1]
    last = near[-1], near[-1] + 1
    partial = attended_part(pairs[-1], last, earlier=tuple(slots), before=tuple(done))
    attended = combine(traded(partial), query, key_new, value_new)
    return residual(x, traded(output(attended, output_weight, ranks)))


def joined(x, axis, combine):
    everything = jax.tree.map(lambda part: lax.all_gather(part, axis), x)
    leading = jax.tree.map(lambda part: part[0], everything)

    def turn(k, so_far):
        return combine(so_far, jax.tree.map(lambda part: part[k], everything))

    return lax.fori_loop(1, lax.axis_size(axis), turn, leading)


def apply_rotary(values, positions, head_size):
    row_count, col_count = values.shape
    half_size = head_size // 2
    frequency = jnp.power(500000.0, -2.0 * jnp.arange(half_size, dtype=jnp.float32) / head_size)
    angles = positions.astype(jnp.float32)[:, None] * frequency[None, :]
    cosine_table = jnp.cos(angles)[:, None, :]
    sine_table = jnp.sin(angles)[:, None, :]
    shaped = values.reshape(row_count, col_count // head_size, 2, half_size)
    first_half = shaped[:, :, 0]
    second_half = shaped[:, :, 1]
    rotated = jnp.stack(
        [
            first_half * cosine_table - second_half * sine_table,
            second_half * cosine_table + first_half * sine_table,
        ],
        axis=2,
    )
    return rotated.reshape(row_count, col_count)


def combine_parts(first_part, second_part):
    peak_one, total_one, weighted_one = first_part
    peak_two, total_two, weighted_two = second_part
    peak_both = jnp.maximum(peak_one, peak_two)
    factor_one = jnp.exp(peak_one - peak_both)
    factor_two = jnp.exp(peak_two - peak_both)
    return (
        peak_both,
        total_one * factor_one + total_two * factor_two,
        weighted_one * factor_one[..., None] + weighted_two * factor_two[..., None],
    )


def finish_heads(peak_score, weight_total, weighted, score_new, value_rows):
    peak_final = jnp.maximum(peak_score, score_new)
    old_factor = jnp.exp(peak_score - peak_final)
    new_weight = jnp.exp(score_new - peak_final)
    weight_total = weight_total * old_factor + new_weight
    weighted = (
        weighted * old_factor[..., None]
        + new_weight.astype(jnp.bfloat16).astype(jnp.float32)[..., None] * value_rows
    )
    return weighted / weight_total[..., None]


def body(
    normed_hidden_input,
    beam_adapter_index,
    beam_cache_length,
    query_weight,
    keyvalue_weight,
    output_weight,
    lowrank_down_factors,
    lowrank_up_factors,
    paged_key_cache,
    paged_value_cache,
):
    beam_rows, width_part = normed_hidden_input.shape
    model_width = query_weight.shape[1]
    kv_width = keyvalue_weight.shape[1] // 2
    head_count = model_width // HEAD_DIM
    kv_heads = kv_width // HEAD_DIM
    group_size = head_count // kv_heads
    tensor_index = lax.axis_index("tensor")
    query_part = jnp.dot(normed_hidden_input, query_weight, preferred_element_type=jnp.float32)
    keyval_part = jnp.dot(normed_hidden_input, keyvalue_weight, preferred_element_type=jnp.float32)
    down_all, up_all = (
        lax.all_gather(lowrank_down_factors, "bank", axis=0, tiled=True),
        lax.all_gather(lowrank_up_factors, "bank", axis=0, tiled=True),
    )
    inner_part = jnp.einsum(
        "ci,cim->cm",
        normed_hidden_input,
        down_all[beam_adapter_index],
        preferred_element_type=jnp.float32,
    )
    inner_total = lax.psum(inner_part, "tensor").astype(jnp.bfloat16)
    lowrank_delta = jnp.einsum(
        "mc,mct->mt", inner_total, up_all[beam_adapter_index], preferred_element_type=jnp.float32
    )
    query_total, keyval = lax.psum((query_part, keyval_part), "tensor")
    delta_total = lax.all_gather(lowrank_delta, "tensor", axis=1, tiled=True)
    query_rotated = apply_rotary(query_total + delta_total, beam_cache_length, HEAD_DIM).astype(
        jnp.bfloat16
    )
    key_new = apply_rotary(keyval[:, :kv_width], beam_cache_length, HEAD_DIM).astype(jnp.bfloat16)
    value_new = keyval[:, kv_width:].astype(jnp.bfloat16)
    position_count = paged_key_cache.shape[1]
    query_heads = query_rotated.reshape(beam_rows, kv_heads, group_size, HEAD_DIM)
    key_block = paged_key_cache.reshape(beam_rows, position_count, kv_heads, HEAD_DIM)
    value_block = paged_value_cache.reshape(beam_rows, position_count, kv_heads, HEAD_DIM)
    score_scale = 1.0 / HEAD_DIM**0.5
    scores = (
        jnp.einsum("bkgh,bpkh->bkgp", query_heads, key_block, preferred_element_type=jnp.float32)
        * score_scale
    )
    position_ids = tensor_index * position_count + jnp.arange(position_count)
    live_mask = (position_ids[None, :] < beam_cache_length[:, None])[:, None, None, :]
    scores = jnp.where(live_mask, scores, -1e30)
    peak_score = jnp.max(scores, axis=-1)
    weights = jnp.where(live_mask, jnp.exp(scores - peak_score[..., None]), 0.0)
    weight_total = jnp.sum(weights, axis=-1)
    weighted = jnp.einsum(
        "bkgp,bpkh->bkgh",
        weights.astype(jnp.bfloat16),
        value_block,
        preferred_element_type=jnp.float32,
    )
    peak_score, weight_total, weighted = joined(
        (peak_score, weight_total, weighted), "tensor", combine_parts
    )
    score_new = (
        jnp.einsum(
            "bkgh,bkh->bkg",
            query_heads,
            key_new.reshape(beam_rows, kv_heads, HEAD_DIM),
            preferred_element_type=jnp.float32,
        )
        * score_scale
    )
    value_rows = value_new.reshape(beam_rows, kv_heads, HEAD_DIM).astype(jnp.float32)[:, :, None, :]
    attended = (
        finish_heads(peak_score, weight_total, weighted, score_new, value_rows)
        .reshape(beam_rows, model_width)
        .astype(jnp.bfloat16)
    )
    attended_cols = lax.dynamic_slice_in_dim(attended, tensor_index * width_part, width_part, 1)
    mixed_cols = lax.psum_scatter(
        lax.dot_general(
            output_weight,
            attended_cols,
            (((0,), (1,)), ((), ())),
            preferred_element_type=jnp.float32,
        ),
        "tensor",
        scatter_dimension=0,
        tiled=True,
    )
    return (normed_hidden_input.astype(jnp.float32) + mixed_cols.T).astype(jnp.bfloat16)


def solution(mesh):
    matched = mesh.shape["tensor"] == 8 and mesh.shape["bank"] == 2
    return jax.shard_map(
        matched_body if matched else body,
        mesh=mesh,
        in_specs=(
            P(("groups", "bank"), "tensor"),
            P(("groups", "bank")),
            P(("groups", "bank")),
            P("tensor", None),
            P("tensor", None),
            P("tensor", None),
            P("bank", "tensor", None),
            P("bank", None, "tensor"),
            P(("groups", "bank"), "tensor", None),
            P(("groups", "bank"), "tensor", None),
        ),
        out_specs=P(("groups", "bank"), "tensor"),
        check_vma=False,
    )
```

```python
import jax
import jax.numpy as jnp
from jax import lax
from jax.experimental import pallas as pl
from jax.experimental.pallas import tpu as pltpu
from jax.sharding import PartitionSpec as P

HEAD_DIM = 128
F32 = jnp.float32
BF16 = jnp.bfloat16
CHUNKS = 2
MIB = 1024 * 1024


def whole():
    return pl.BlockSpec(memory_space=pltpu.VMEM)


def big():
    return pl.BlockSpec(memory_space=pltpu.HBM)


def scalar():
    return pl.BlockSpec(memory_space=pltpu.SMEM)


def in_hbm(array):
    return pltpu.with_memory_space_constraint(array, pltpu.HBM)


def shape(*dims, dtype=F32):
    return jax.ShapeDtypeStruct(dims, dtype)


def iota(dims, axis):
    return lax.broadcasted_iota(jnp.int32, dims, axis)


def params(mib=4):
    return pltpu.CompilerParams(vmem_limit_bytes=mib * MIB)


def exchanged(slot):
    return slot & ~3 | (slot & 1) << 1 | slot >> 1 & 1


def rank_of(place, bank, slot):
    return place ^ (slot + bank * (exchanged(slot) - slot))


def start_columns(weight, column, target, sems):
    depth, width = target.shape
    part = depth // CHUNKS
    copies = []
    for c in range(CHUNKS):
        rows = pl.ds(c * part, part)
        copies.append(
            pltpu.make_async_copy(
                weight.at[rows, pl.ds(pl.multiple_of(column, width), width)],
                target.at[rows, :],
                sems.at[c],
            )
        )
        copies[-1].start()
    return copies


def adapter_column(refs, bank, count):
    columns = []
    for ref in refs:
        rows = ref.shape[1]
        index = jnp.broadcast_to(ref[...].astype(F32), (rows, rows))
        diagonal = iota((rows, rows), 0) == iota((rows, rows), 1)
        columns.append(jnp.sum(jnp.where(diagonal, index, 0.0), axis=1, keepdims=True))
    column = jnp.concatenate(columns, axis=0).astype(jnp.int32) - bank * count
    return jnp.broadcast_to(column, (column.shape[0], HEAD_DIM))


def start_slots(parity, place, bank, w_ref, w_buf, sems):
    count, _, width = w_buf.shape
    copies = []
    for s in range(count):
        target = rank_of(place[0], bank[0], 2 * s + parity)
        first = (2 * target + bank[0]) * width
        copies.append(start_columns(w_ref, first, w_buf.at[s], sems.at[s]))
    return copies


def wait_all(copies):
    for copy in copies:
        copy.wait()


def start_parts(source, target, sems):
    part = source.shape[0] // sems.shape[0]
    copies = []
    for c in range(sems.shape[0]):
        rows = pl.ds(c * part, part)
        copies.append(pltpu.make_async_copy(source.at[rows], target.at[rows], sems.at[c]))
        copies[-1].start()
    return copies


def fetch_kernel(ref, out, sems):
    wait_all(start_parts(ref, out, sems))


def fetch(array):
    return pl.pallas_call(
        fetch_kernel,
        in_specs=[big()],
        out_specs=whole(),
        out_shape=jax.ShapeDtypeStruct(array.shape, array.dtype),
        scratch_shapes=[pltpu.SemaphoreType.DMA((2,))],
        compiler_params=params(),
        cost_estimate=pl.CostEstimate(
            flops=0, bytes_accessed=2 * array.size, transcendentals=0
        ),
        name="fetch",
    )(array)


def slot_scratch(wq, ranks):
    half, depth = ranks // 2, wq.shape[0]
    return [
        pltpu.VMEM((half, depth, wq.shape[1] // ranks // 2), BF16),
        pltpu.SemaphoreType.DMA((half, CHUNKS)),
    ]


def beam_rows(x_ref, other_ref):
    rows = [x_ref[...].astype(F32), other_ref[...].astype(F32)]
    return jnp.concatenate(rows, axis=0).astype(BF16)


def project_sent_kernel(
    place, bank, own_ref, came_ref, x_ref, other_ref, down_ref, w_ref, *refs
):
    out, inner, column_out, w_buf, sems = refs
    copies = start_slots(1, place, bank, w_ref, w_buf, sems)
    width = w_buf.shape[2]
    x = beam_rows(x_ref, other_ref)
    adapters, rank, depth = down_ref.shape
    every = lax.dot_general(
        x,
        down_ref[...].reshape(adapters * rank, depth),
        (((1,), (1,)), ((), ())),
        preferred_element_type=F32,
    )
    column = adapter_column((own_ref, came_ref), bank[0], adapters)
    column_out[...] = column
    lane = iota(column.shape, 1)
    per = HEAD_DIM // rank
    total = jnp.zeros(column.shape, F32)
    for j in range(adapters // per):
        part = every[:, j * HEAD_DIM : (j + 1) * HEAD_DIM]
        total += jnp.where(lane // rank + j * per == column, part, 0.0)
    inner[...] = total
    for s, slot in enumerate(copies):
        out[s, :, width:] = total
        wait_all(slot)
        out[s, :, :width] = jnp.dot(x, w_buf[s], preferred_element_type=F32)


def project_sent(place, bank, index, x, other, down, wq, ranks):
    rows = 2 * x.shape[0]
    return pl.pallas_call(
        project_sent_kernel,
        in_specs=[scalar()] * 2 + [whole()] * 5 + [big()],
        out_specs=[whole()] * 3,
        out_shape=[
            shape(ranks // 2, rows, wq.shape[1] // ranks // 2 + HEAD_DIM),
            shape(rows, HEAD_DIM),
            shape(rows, HEAD_DIM, dtype=jnp.int32),
        ],
        scratch_shapes=slot_scratch(wq, ranks),
        compiler_params=params(8),
        cost_estimate=pl.CostEstimate(
            flops=rows * (wq.size // 2 + 2 * down.size),
            bytes_accessed=wq.size // 2 + 2 * down.size,
            transcendentals=0,
        ),
        name="project_sent",
    )(place, bank, *[i.reshape(1, -1) for i in index], x, other, down, wq)


def project_kept_kernel(
    place, bank, length, x_ref, other_ref, w_ref, inner, out, length_out, w_buf, sems
):
    copies = start_slots(0, place, bank, w_ref, w_buf, sems)
    width = w_buf.shape[2]
    beams = x_ref.shape[0]
    row = iota(length_out.shape, 0)
    limit = jnp.zeros(length_out.shape, jnp.int32)
    for beam in range(beams):
        limit = jnp.where(row // (length_out.shape[0] // beams) == beam, length[beam], limit)
    length_out[...] = limit
    x = beam_rows(x_ref, other_ref)
    for s, slot in enumerate(copies):
        out[s, :, width:] = inner[...]
        wait_all(slot)
        out[s, :, :width] = jnp.dot(x, w_buf[s], preferred_element_type=F32)


def project_kept(place, bank, length, x, other, wq, inner, ranks):
    beams = x.shape[0]
    return pl.pallas_call(
        project_kept_kernel,
        in_specs=[scalar()] * 3 + [whole()] * 2 + [big(), whole()],
        out_specs=[whole()] * 2,
        out_shape=[
            shape(ranks // 2, 2 * beams, wq.shape[1] // ranks // 2 + HEAD_DIM),
            shape(beams * wq.shape[1] // ranks // HEAD_DIM, HEAD_DIM, dtype=jnp.int32),
        ],
        scratch_shapes=slot_scratch(wq, ranks),
        compiler_params=params(8),
        cost_estimate=pl.CostEstimate(
            flops=beams * wq.size, bytes_accessed=2 * wq.size, transcendentals=0
        ),
        name="project_kept",
    )(place, bank, length, x, other, wq, inner)


def keyval_kernel(x_ref, w_ref, out, w_buf, sems):
    copies = start_parts(w_ref, w_buf, sems)
    beams = x_ref.shape[0]
    ranks = out.shape[0]
    part = w_buf.shape[0] // len(copies)
    total = None
    for c, copy in enumerate(copies):
        copy.wait()
        rows = slice(c * part, (c + 1) * part)
        product = jnp.dot(x_ref[:, rows], w_buf[rows], preferred_element_type=F32)
        total = product if total is None else total + product
    high = total.astype(BF16).astype(F32)
    low = total - high
    for r in range(ranks):
        pieces = []
        for first in (r * HEAD_DIM, (ranks + r) * HEAD_DIM):
            pieces += [v[:, first : first + HEAD_DIM] for v in (high, low)]
        out[r] = jnp.concatenate(pieces, axis=0).astype(BF16)


def keyval(x, wkv, ranks):
    beams, depth = x.shape
    return pl.pallas_call(
        keyval_kernel,
        in_specs=[whole(), big()],
        out_specs=whole(),
        out_shape=shape(ranks, 4 * beams, HEAD_DIM, dtype=BF16),
        scratch_shapes=[pltpu.VMEM(wkv.shape, BF16), pltpu.SemaphoreType.DMA((4,))],
        compiler_params=params(8),
        cost_estimate=pl.CostEstimate(
            flops=2 * beams * wkv.size, bytes_accessed=2 * wkv.size, transcendentals=0
        ),
        name="keyval",
    )(x, wkv)


def correct_kernel(bank, column_ref, up_ref, *refs):
    *parts, own_out, other_out = refs
    total = parts[0][...]
    for part in parts[1:]:
        total += part[...]
    count, rank, width = up_ref.shape
    half = width // 2
    inner = total[:, half:].astype(BF16).astype(F32)
    column = column_ref[...]
    lane = iota(column.shape, 1)
    per = HEAD_DIM // rank
    spread = jnp.concatenate(
        [
            jnp.where(lane // rank + j * per == column, inner, 0.0)
            for j in range(count // per)
        ],
        axis=1,
    ).astype(BF16)
    delta = jnp.dot(
        spread, up_ref[...].reshape(count * rank, width), preferred_element_type=F32
    )
    rows = own_out.shape[0]
    for side in range(2):
        columns = slice(side * half, (side + 1) * half)
        part = delta[:, columns] + jnp.where(bank[0] == side, total[:, :half], 0.0)
        own_out[:, columns] = part[:rows]
        other_out[:, columns] = part[rows:]


def correct(bank, column, up, parts):
    rows = parts[0].shape[0]
    out = shape(rows // 2, up.shape[2])
    return pl.pallas_call(
        correct_kernel,
        in_specs=[scalar()] + [whole()] * (2 + len(parts)),
        out_specs=[whole()] * 2,
        out_shape=[out, out],
        compiler_params=params(),
        cost_estimate=pl.CostEstimate(
            flops=2 * rows * up.size, bytes_accessed=2 * up.size, transcendentals=0
        ),
        name="correct",
    )(bank, column, up, *parts)


def part_kernel(kept_ref, came_ref, *outs):
    for i, out in enumerate(outs):
        out[...] = kept_ref[i] + came_ref[i]


def part(kept, came):
    return pl.pallas_call(
        part_kernel,
        in_specs=[whole()] * 2,
        out_specs=[whole()] * kept.shape[0],
        out_shape=[shape(*kept.shape[1:])] * kept.shape[0],
        compiler_params=params(),
        name="part",
    )(kept, came)


def rotate(v, cosine, sine):
    return v * cosine + pltpu.roll(v, HEAD_DIM // 2, 1) * sine


def rotate_kernel(own_ref, came_ref, cos_ref, sin_ref, q_ref, rows_ref):
    cosine, sine = cos_ref[...], sin_ref[...]
    for g in range(own_ref.shape[1] // HEAD_DIM):
        columns = slice(g * HEAD_DIM, (g + 1) * HEAD_DIM)
        rows_ref[:, g, :] = rotate(own_ref[:, columns] + came_ref[:, columns], cosine, sine)
    q_ref[0] = rows_ref[...].reshape(q_ref.shape[1:]).astype(BF16)


def rotated(own, came, cosine, sine):
    rows, width = own.shape
    heads = width // HEAD_DIM
    return pl.pallas_call(
        rotate_kernel,
        in_specs=[whole()] * 4,
        out_specs=whole(),
        out_shape=shape(1, rows * heads, HEAD_DIM, dtype=BF16),
        scratch_shapes=[pltpu.VMEM((rows, heads, HEAD_DIM), F32)],
        compiler_params=params(),
        name="rotate",
    )(own, came, cosine, sine)


def join_kernel(*refs):
    *parts, out_ref = refs
    for i, part in enumerate(parts):
        out_ref[i] = part[0]


def join(parts):
    return pl.pallas_call(
        join_kernel,
        in_specs=[whole()] * len(parts),
        out_specs=whole(),
        out_shape=shape(len(parts), *parts[0].shape[1:], dtype=parts[0].dtype),
        compiler_params=params(),
        name="join",
    )(*parts)


def attend_kernel(slots, earlier, place, bank, length_ref, q_ref, k_ref, v_ref, *refs):
    before, out_ref = refs[:-1], refs[-1]
    beams, positions, _ = k_ref.shape
    rows = q_ref.shape[1]
    group = rows // beams
    row, lane = iota((rows, HEAD_DIM), 0), iota((rows, HEAD_DIM), 1)
    left = length_ref[...] - place[0] * positions
    live = jnp.concatenate(
        [lane + first < left for first in range(0, positions, HEAD_DIM)], axis=1
    )
    for i, slot in enumerate(slots):
        head = rank_of(place[0], bank[0], slot)
        columns = pl.ds(pl.multiple_of(head * HEAD_DIM, HEAD_DIM), HEAD_DIM)
        query = q_ref[i].astype(F32)
        scores = jnp.concatenate(
            [
                lax.dot_general(
                    query[beam * group : (beam + 1) * group].astype(BF16),
                    k_ref[beam, :, columns],
                    (((1,), (1,)), ((), ())),
                    preferred_element_type=F32,
                )
                for beam in range(beams)
            ],
            axis=0,
        ) * (1.0 / HEAD_DIM**0.5)
        scores = jnp.where(live, scores, -1e30)
        peak = jnp.max(scores, axis=1, keepdims=True)
        weights = jnp.where(live, jnp.exp(scores - peak), 0.0)
        total = jnp.sum(weights, axis=1, keepdims=True)
        values = [
            jnp.dot(
                weights[beam * group : (beam + 1) * group].astype(BF16),
                v_ref[beam, :, columns],
                preferred_element_type=F32,
            )
            for beam in range(beams)
        ]
        stats = jnp.where(lane == row % group, peak, 0.0)
        stats += jnp.where(lane == group + row % group, total, 0.0)
        stats = jnp.sum(stats.reshape(beams, group, HEAD_DIM), axis=1)
        high = stats.astype(BF16).astype(F32)
        middle = (stats - high).astype(BF16).astype(F32)
        low = stats - high - middle
        tail = high + pltpu.roll(middle, 2 * group, 1) + pltpu.roll(low, 4 * group, 1)
        block = jnp.concatenate(values + [tail, jnp.zeros_like(tail)], axis=0)
        out_ref[head if earlier else i, : rows + 2 * beams] = block.astype(BF16)
    if earlier:
        *before, keyval_ref = before
        done = [(ref, i) for ref in before for i in range(ref.shape[0])]
        for slot, (ref, i) in zip(earlier, done):
            out_ref[rank_of(place[0], bank[0], slot), : rows + 2 * beams] = ref[i]
        out_ref[:, rows + 2 * beams :] = keyval_ref[...]


def attend(place, bank, length, queries, keys, values, slots, earlier=(), before=()):
    count, rows, _ = queries.shape
    beams, positions, _ = keys.shape
    return pl.pallas_call(
        lambda *refs: attend_kernel(slots, earlier, *refs),
        in_specs=[scalar()] * 2 + [whole()] * (4 + len(before)),
        out_specs=whole(),
        out_shape=shape(
            count + len(earlier), rows + (6 if earlier else 2) * beams, HEAD_DIM, dtype=BF16
        ),
        compiler_params=params(),
        cost_estimate=pl.CostEstimate(
            flops=4 * rows * count * positions * HEAD_DIM,
            bytes_accessed=4 * beams * positions * HEAD_DIM * (16 if earlier else count),
            transcendentals=rows * count * positions,
        ),
        name="attend",
    )(place, bank, length, queries, keys, values, *before)


def combine_kernel(parts_ref, q_ref, cos_ref, sin_ref, out_ref, joined):
    ranks = parts_ref.shape[0]
    beams, group, _ = joined.shape
    rows = beams * group

    def by_row(v):
        return jnp.broadcast_to(v[:, None, :], (beams, group, HEAD_DIM)).reshape(rows, HEAD_DIM)

    head = iota((rows, HEAD_DIM), 0) % group
    lane = iota((rows, HEAD_DIM), 1)
    sums = jnp.sum(parts_ref[:, rows + 2 * beams :].astype(F32), axis=0)
    key, value = [
        sums[i * beams : (i + 1) * beams] + sums[(i + 1) * beams : (i + 2) * beams]
        for i in (0, 2)
    ]
    key = rotate(key, cos_ref[...], sin_ref[...]).astype(BF16).astype(F32)
    value = value.astype(BF16).astype(F32)
    score = jnp.sum(q_ref[0].astype(F32) * by_row(key), axis=1, keepdims=True) * (
        1.0 / HEAD_DIM**0.5
    )
    peaks, totals, weighted = [], [], []
    top = score
    for s in range(ranks):
        block = parts_ref[s].astype(F32)
        tail = block[rows : rows + beams]
        for turn in (2, 4):
            tail += pltpu.roll(block[rows : rows + beams], HEAD_DIM - turn * group, 1)
        tail = by_row(tail)
        peak = jnp.sum(jnp.where(lane == head, tail, 0.0), axis=1, keepdims=True)
        total = jnp.sum(jnp.where(lane == group + head, tail, 0.0), axis=1, keepdims=True)
        top = jnp.maximum(top, peak)
        peaks.append(peak)
        totals.append(total)
        weighted.append(block[:rows])
    new = jnp.exp(score - top)
    everything = new
    result = new.astype(BF16).astype(F32) * by_row(value)
    for peak, total, block in zip(peaks, totals, weighted):
        factor = jnp.exp(peak - top)
        everything += total * factor
        result += block * factor
    joined[...] = (result / everything).reshape(joined.shape)
    for g in range(group):
        out_ref[:, g * HEAD_DIM : (g + 1) * HEAD_DIM] = joined[:, g, :].astype(BF16)


def combine(parts, query, cosine, sine):
    beams = cosine.shape[0]
    group = query.shape[1] // beams
    return pl.pallas_call(
        combine_kernel,
        in_specs=[whole()] * 4,
        out_specs=whole(),
        out_shape=shape(beams, group * HEAD_DIM, dtype=BF16),
        scratch_shapes=[pltpu.VMEM((beams, group, HEAD_DIM), F32)],
        compiler_params=params(),
        name="combine",
    )(parts, query, cosine, sine)


def output_kernel(x_ref, w_ref, out):
    count, _, width = out.shape
    for s in range(count):
        columns = slice(s * width, (s + 1) * width)
        total = jnp.dot(x_ref[...], w_ref[:, columns], preferred_element_type=F32)
        out[s] = total.astype(BF16)


def output(x, weight, ranks):
    beams = x.shape[0]
    return pl.pallas_call(
        output_kernel,
        in_specs=[whole()] * 2,
        out_specs=whole(),
        out_shape=shape(ranks, beams, weight.shape[1] // ranks, dtype=BF16),
        compiler_params=params(),
        cost_estimate=pl.CostEstimate(
            flops=2 * beams * weight.size, bytes_accessed=2 * weight.size, transcendentals=0
        ),
        name="output",
    )(x, weight)


def residual_kernel(x_ref, parts_ref, out_ref):
    total = jnp.sum(parts_ref[...].astype(F32), axis=0)
    out_ref[...] = (x_ref[...].astype(F32) + total).astype(BF16)


def residual(x, parts):
    return pl.pallas_call(
        residual_kernel,
        in_specs=[whole()] * 2,
        out_specs=whole(),
        out_shape=jax.ShapeDtypeStruct(x.shape, BF16),
        compiler_params=params(),
        name="residual",
    )(x, parts)


def swapped(x):
    return lax.ppermute(x, "bank", [(0, 1), (1, 0)])


def traded(blocks):
    return lax.all_to_all(blocks, "tensor", 0, 0, tiled=True)


def hop(x, bit):
    pairs = []
    for rank in range(lax.axis_size("tensor")):
        for bank in range(2):
            pairs.append((2 * rank + bank, 2 * rank_of(rank, bank, bit) + bank))
    return lax.ppermute(x, ("tensor", "bank"), pairs)


def matched_body(
    normed_hidden_input,
    beam_adapter_index,
    beam_cache_length,
    query_weight,
    keyvalue_weight,
    output_weight,
    lowrank_down_factors,
    lowrank_up_factors,
    paged_key_cache,
    paged_value_cache,
):
    x = normed_hidden_input
    ranks = lax.axis_size("tensor")
    place = lax.axis_index("tensor").astype(jnp.int32).reshape(1)
    bank = lax.axis_index("bank").astype(jnp.int32).reshape(1)
    index = (beam_adapter_index, swapped(beam_adapter_index))
    x_other = swapped(x)
    lane = jnp.arange(HEAD_DIM, dtype=jnp.int32)
    half = HEAD_DIM // 2
    frequency = jnp.power(500000.0, -2.0 * (lane % half).astype(F32) / HEAD_DIM)
    angles = beam_cache_length.astype(F32)[:, None] * frequency[None, :]
    cosine = jnp.cos(angles)
    sine = jnp.where(lane < half, -1.0, 1.0) * jnp.sin(angles)
    weight = in_hbm(query_weight)
    down = fetch(in_hbm(lowrank_down_factors.swapaxes(1, 2)))
    sent, inner, column = project_sent(place, bank, index, x, x_other, down, weight, ranks)
    came = hop(sent, 1)
    kept, length = project_kept(
        place, bank, beam_cache_length, x, x_other, weight, inner, ranks
    )
    kept, *sent = part(kept, came)
    near = tuple(range(ranks - 2, 0, -2))
    parts = [kept] + [hop(sent[slot // 2 - 1], slot) for slot in near]
    token_weight, _ = lax.optimization_barrier((in_hbm(keyvalue_weight), kept))
    token, parts = lax.optimization_barrier((keyval(x, in_hbm(token_weight), ranks), parts))
    own, other = correct(bank, column, lowrank_up_factors, parts)
    query = rotated(own, swapped(other), cosine, sine)

    def attended_part(queries, slots, **more):
        cache = paged_key_cache, paged_value_cache
        return attend(place, bank, length, queries, *cache, slots, **more)

    gathered = join([query] + [hop(query, slot) for slot in near])
    came = hop(gathered, 1)
    done = attended_part(gathered, (0, *near))
    odd = tuple(slot + 1 for slot in (0, *near))
    partial = attended_part(came, odd, earlier=(0, *near), before=(done, token))
    attended = combine(traded(partial), query, cosine, sine)
    return residual(x, traded(output(attended, output_weight, ranks)))


def joined(x, axis, combine):
    everything = jax.tree.map(lambda part: lax.all_gather(part, axis), x)
    leading = jax.tree.map(lambda part: part[0], everything)

    def turn(k, so_far):
        return combine(so_far, jax.tree.map(lambda part: part[k], everything))

    return lax.fori_loop(1, lax.axis_size(axis), turn, leading)


def apply_rotary(values, positions, head_size):
    row_count, col_count = values.shape
    half_size = head_size // 2
    frequency = jnp.power(500000.0, -2.0 * jnp.arange(half_size, dtype=jnp.float32) / head_size)
    angles = positions.astype(jnp.float32)[:, None] * frequency[None, :]
    cosine_table = jnp.cos(angles)[:, None, :]
    sine_table = jnp.sin(angles)[:, None, :]
    shaped = values.reshape(row_count, col_count // head_size, 2, half_size)
    first_half = shaped[:, :, 0]
    second_half = shaped[:, :, 1]
    rotated = jnp.stack(
        [
            first_half * cosine_table - second_half * sine_table,
            second_half * cosine_table + first_half * sine_table,
        ],
        axis=2,
    )
    return rotated.reshape(row_count, col_count)


def combine_parts(first_part, second_part):
    peak_one, total_one, weighted_one = first_part
    peak_two, total_two, weighted_two = second_part
    peak_both = jnp.maximum(peak_one, peak_two)
    factor_one = jnp.exp(peak_one - peak_both)
    factor_two = jnp.exp(peak_two - peak_both)
    return (
        peak_both,
        total_one * factor_one + total_two * factor_two,
        weighted_one * factor_one[..., None] + weighted_two * factor_two[..., None],
    )


def finish_heads(peak_score, weight_total, weighted, score_new, value_rows):
    peak_final = jnp.maximum(peak_score, score_new)
    old_factor = jnp.exp(peak_score - peak_final)
    new_weight = jnp.exp(score_new - peak_final)
    weight_total = weight_total * old_factor + new_weight
    weighted = (
        weighted * old_factor[..., None]
        + new_weight.astype(jnp.bfloat16).astype(jnp.float32)[..., None] * value_rows
    )
    return weighted / weight_total[..., None]


def body(
    normed_hidden_input,
    beam_adapter_index,
    beam_cache_length,
    query_weight,
    keyvalue_weight,
    output_weight,
    lowrank_down_factors,
    lowrank_up_factors,
    paged_key_cache,
    paged_value_cache,
):
    beam_rows, width_part = normed_hidden_input.shape
    model_width = query_weight.shape[1]
    kv_width = keyvalue_weight.shape[1] // 2
    head_count = model_width // HEAD_DIM
    kv_heads = kv_width // HEAD_DIM
    group_size = head_count // kv_heads
    tensor_index = lax.axis_index("tensor")
    query_part = jnp.dot(normed_hidden_input, query_weight, preferred_element_type=jnp.float32)
    keyval_part = jnp.dot(normed_hidden_input, keyvalue_weight, preferred_element_type=jnp.float32)
    down_all, up_all = (
        lax.all_gather(lowrank_down_factors, "bank", axis=0, tiled=True),
        lax.all_gather(lowrank_up_factors, "bank", axis=0, tiled=True),
    )
    inner_part = jnp.einsum(
        "ci,cim->cm",
        normed_hidden_input,
        down_all[beam_adapter_index],
        preferred_element_type=jnp.float32,
    )
    inner_total = lax.psum(inner_part, "tensor").astype(jnp.bfloat16)
    lowrank_delta = jnp.einsum(
        "mc,mct->mt", inner_total, up_all[beam_adapter_index], preferred_element_type=jnp.float32
    )
    query_total, keyval = lax.psum((query_part, keyval_part), "tensor")
    delta_total = lax.all_gather(lowrank_delta, "tensor", axis=1, tiled=True)
    query_rotated = apply_rotary(query_total + delta_total, beam_cache_length, HEAD_DIM).astype(
        jnp.bfloat16
    )
    key_new = apply_rotary(keyval[:, :kv_width], beam_cache_length, HEAD_DIM).astype(jnp.bfloat16)
    value_new = keyval[:, kv_width:].astype(jnp.bfloat16)
    position_count = paged_key_cache.shape[1]
    query_heads = query_rotated.reshape(beam_rows, kv_heads, group_size, HEAD_DIM)
    key_block = paged_key_cache.reshape(beam_rows, position_count, kv_heads, HEAD_DIM)
    value_block = paged_value_cache.reshape(beam_rows, position_count, kv_heads, HEAD_DIM)
    score_scale = 1.0 / HEAD_DIM**0.5
    scores = (
        jnp.einsum("bkgh,bpkh->bkgp", query_heads, key_block, preferred_element_type=jnp.float32)
        * score_scale
    )
    position_ids = tensor_index * position_count + jnp.arange(position_count)
    live_mask = (position_ids[None, :] < beam_cache_length[:, None])[:, None, None, :]
    scores = jnp.where(live_mask, scores, -1e30)
    peak_score = jnp.max(scores, axis=-1)
    weights = jnp.where(live_mask, jnp.exp(scores - peak_score[..., None]), 0.0)
    weight_total = jnp.sum(weights, axis=-1)
    weighted = jnp.einsum(
        "bkgp,bpkh->bkgh",
        weights.astype(jnp.bfloat16),
        value_block,
        preferred_element_type=jnp.float32,
    )
    peak_score, weight_total, weighted = joined(
        (peak_score, weight_total, weighted), "tensor", combine_parts
    )
    score_new = (
        jnp.einsum(
            "bkgh,bkh->bkg",
            query_heads,
            key_new.reshape(beam_rows, kv_heads, HEAD_DIM),
            preferred_element_type=jnp.float32,
        )
        * score_scale
    )
    value_rows = value_new.reshape(beam_rows, kv_heads, HEAD_DIM).astype(jnp.float32)[:, :, None, :]
    attended = (
        finish_heads(peak_score, weight_total, weighted, score_new, value_rows)
        .reshape(beam_rows, model_width)
        .astype(jnp.bfloat16)
    )
    attended_cols = lax.dynamic_slice_in_dim(attended, tensor_index * width_part, width_part, 1)
    mixed_cols = lax.psum_scatter(
        lax.dot_general(
            output_weight,
            attended_cols,
            (((0,), (1,)), ((), ())),
            preferred_element_type=jnp.float32,
        ),
        "tensor",
        scatter_dimension=0,
        tiled=True,
    )
    return (normed_hidden_input.astype(jnp.float32) + mixed_cols.T).astype(jnp.bfloat16)


def solution(mesh):
    matched = mesh.shape["tensor"] == 8 and mesh.shape["bank"] == 2
    return jax.shard_map(
        matched_body if matched else body,
        mesh=mesh,
        in_specs=(
            P(("groups", "bank"), "tensor"),
            P(("groups", "bank")),
            P(("groups", "bank")),
            P("tensor", None),
            P("tensor", None),
            P("tensor", None),
            P("bank", "tensor", None),
            P("bank", None, "tensor"),
            P(("groups", "bank"), "tensor", None),
            P(("groups", "bank"), "tensor", None),
        ),
        out_specs=P(("groups", "bank"), "tensor"),
        check_vma=False,
    )
```

```python
import jax
import jax.numpy as jnp
from jax import lax
from jax.experimental import pallas as pl
from jax.experimental.pallas import tpu as pltpu
from jax.sharding import PartitionSpec as P

HEAD_DIM = 128
F32 = jnp.float32
BF16 = jnp.bfloat16
CHUNKS = 2
MIB = 1024 * 1024


def whole():
    return pl.BlockSpec(memory_space=pltpu.VMEM)


def big():
    return pl.BlockSpec(memory_space=pltpu.HBM)


def scalar():
    return pl.BlockSpec(memory_space=pltpu.SMEM)


def in_hbm(array):
    return pltpu.with_memory_space_constraint(array, pltpu.HBM)


def shape(*dims, dtype=F32):
    return jax.ShapeDtypeStruct(dims, dtype)


def iota(dims, axis):
    return lax.broadcasted_iota(jnp.int32, dims, axis)


def params(mib=4):
    return pltpu.CompilerParams(vmem_limit_bytes=mib * MIB)


def turned(slot, bits):
    return sum(bit for i, bit in enumerate(bits) if slot >> i & 1)


def rank_of(place, bank, slot):
    first, second = turned(slot, (4, 1, 2)), turned(slot, (4, 2, 1))
    return place ^ (first + bank * (second - first))


def start_columns(weight, column, target, sems):
    depth, width = target.shape
    part = depth // CHUNKS
    copies = []
    for c in range(CHUNKS):
        rows = pl.ds(c * part, part)
        copies.append(
            pltpu.make_async_copy(
                weight.at[rows, pl.ds(pl.multiple_of(column, width), width)],
                target.at[rows, :],
                sems.at[c],
            )
        )
        copies[-1].start()
    return copies


def adapter_column(refs, bank, count):
    columns = []
    for ref in refs:
        rows = ref.shape[1]
        index = jnp.broadcast_to(ref[...].astype(F32), (rows, rows))
        diagonal = iota((rows, rows), 0) == iota((rows, rows), 1)
        columns.append(jnp.sum(jnp.where(diagonal, index, 0.0), axis=1, keepdims=True))
    column = jnp.concatenate(columns, axis=0).astype(jnp.int32) - bank * count
    return jnp.broadcast_to(column, (column.shape[0], HEAD_DIM))


def start_slots(parity, first_slot, place, bank, w_ref, w_buf, sems):
    count, _, width = w_buf.shape
    copies = []
    for s in range(count):
        target = rank_of(place[0], bank[0], 2 * (first_slot + s) + parity)
        first = (2 * target + bank[0]) * width
        copies.append(start_columns(w_ref, first, w_buf.at[s], sems.at[s]))
    return copies


def wait_all(copies):
    for copy in copies:
        copy.wait()


def start_parts(source, target, sems):
    part = source.shape[0] // sems.shape[0]
    copies = []
    for c in range(sems.shape[0]):
        rows = pl.ds(c * part, part)
        copies.append(pltpu.make_async_copy(source.at[rows], target.at[rows], sems.at[c]))
        copies[-1].start()
    return copies


def fetch_kernel(place, bank, down_ref, w_ref, down_out, w_out, down_sems, sems):
    copies = start_parts(down_ref, down_out, down_sems)
    for slot in start_slots(1, 0, place, bank, w_ref, w_out, sems):
        copies += slot
    wait_all(copies)


def fetch(place, bank, down, wq, ranks, slots):
    out = [
        jax.ShapeDtypeStruct(down.shape, BF16),
        shape(slots, wq.shape[0], wq.shape[1] // ranks // 2, dtype=BF16),
    ]
    return pl.pallas_call(
        fetch_kernel,
        in_specs=[scalar()] * 2 + [big()] * 2,
        out_specs=[whole()] * 2,
        out_shape=out,
        scratch_shapes=[
            pltpu.SemaphoreType.DMA((2,)),
            pltpu.SemaphoreType.DMA((slots, CHUNKS)),
        ],
        compiler_params=params(),
        cost_estimate=pl.CostEstimate(
            flops=0, bytes_accessed=2 * sum(o.size for o in out), transcendentals=0
        ),
        name="fetch",
    )(place, bank, down, wq)


def slot_scratch(wq, ranks, slots):
    return [
        pltpu.VMEM((slots, wq.shape[0], wq.shape[1] // ranks // 2), BF16),
        pltpu.SemaphoreType.DMA((slots, CHUNKS)),
    ]


def beam_rows(x_ref, other_ref):
    rows = [x_ref[...].astype(F32), other_ref[...].astype(F32)]
    return jnp.concatenate(rows, axis=0).astype(BF16)


def project_sent_kernel(
    place, bank, own_ref, came_ref, x_ref, other_ref, down_ref, ahead_ref, w_ref, *refs
):
    out, inner, column_out, w_buf, sems = refs
    ahead = ahead_ref.shape[0]
    copies = start_slots(1, ahead, place, bank, w_ref, w_buf, sems)
    width = w_buf.shape[2]
    x = beam_rows(x_ref, other_ref)
    adapters, rank, depth = down_ref.shape
    every = lax.dot_general(
        x,
        down_ref[...].reshape(adapters * rank, depth),
        (((1,), (1,)), ((), ())),
        preferred_element_type=F32,
    )
    column = adapter_column((own_ref, came_ref), bank[0], adapters)
    column_out[...] = column
    lane = iota(column.shape, 1)
    per = HEAD_DIM // rank
    total = jnp.zeros(column.shape, F32)
    for j in range(adapters // per):
        part = every[:, j * HEAD_DIM : (j + 1) * HEAD_DIM]
        total += jnp.where(lane // rank + j * per == column, part, 0.0)
    inner[...] = total
    for s in range(out.shape[0]):
        out[s, :, width:] = total
    for s in range(ahead):
        out[s, :, :width] = jnp.dot(x, ahead_ref[s], preferred_element_type=F32)
    for s, slot in enumerate(copies):
        wait_all(slot)
        out[ahead + s, :, :width] = jnp.dot(x, w_buf[s], preferred_element_type=F32)


def project_sent(place, bank, index, x, other, down, ahead, wq, ranks):
    rows = 2 * x.shape[0]
    return pl.pallas_call(
        project_sent_kernel,
        in_specs=[scalar()] * 2 + [whole()] * 6 + [big()],
        out_specs=[whole()] * 3,
        out_shape=[
            shape(ranks // 2, rows, wq.shape[1] // ranks // 2 + HEAD_DIM),
            shape(rows, HEAD_DIM),
            shape(rows, HEAD_DIM, dtype=jnp.int32),
        ],
        scratch_shapes=slot_scratch(wq, ranks, ranks // 2 - ahead.shape[0]),
        compiler_params=params(8),
        cost_estimate=pl.CostEstimate(
            flops=rows * (wq.size // 2 + 2 * down.size),
            bytes_accessed=wq.size // 2 + 2 * down.size,
            transcendentals=0,
        ),
        name="project_sent",
    )(place, bank, *[i.reshape(1, -1) for i in index], x, other, down, ahead, wq)


def project_kept_kernel(
    place, bank, length, x_ref, other_ref, w_ref, inner, out, length_out, w_buf, sems
):
    copies = start_slots(0, 0, place, bank, w_ref, w_buf, sems)
    width = w_buf.shape[2]
    beams = x_ref.shape[0]
    row = iota(length_out.shape, 0)
    limit = jnp.zeros(length_out.shape, jnp.int32)
    for beam in range(beams):
        limit = jnp.where(row // (length_out.shape[0] // beams) == beam, length[beam], limit)
    length_out[...] = limit
    x = beam_rows(x_ref, other_ref)
    for s, slot in enumerate(copies):
        out[s, :, width:] = inner[...]
        wait_all(slot)
        out[s, :, :width] = jnp.dot(x, w_buf[s], preferred_element_type=F32)


def project_kept(place, bank, length, x, other, wq, inner, ranks):
    beams = x.shape[0]
    return pl.pallas_call(
        project_kept_kernel,
        in_specs=[scalar()] * 3 + [whole()] * 2 + [big(), whole()],
        out_specs=[whole()] * 2,
        out_shape=[
            shape(ranks // 2, 2 * beams, wq.shape[1] // ranks // 2 + HEAD_DIM),
            shape(beams * wq.shape[1] // ranks // HEAD_DIM, HEAD_DIM, dtype=jnp.int32),
        ],
        scratch_shapes=slot_scratch(wq, ranks, ranks // 2),
        compiler_params=params(8),
        cost_estimate=pl.CostEstimate(
            flops=beams * wq.size, bytes_accessed=2 * wq.size, transcendentals=0
        ),
        name="project_kept",
    )(place, bank, length, x, other, wq, inner)


def keyval_kernel(x_ref, w_ref, out, w_buf, sems):
    copies = start_parts(w_ref, w_buf, sems)
    beams = x_ref.shape[0]
    ranks = out.shape[0]
    part = w_buf.shape[0] // len(copies)
    total = None
    for c, copy in enumerate(copies):
        copy.wait()
        rows = slice(c * part, (c + 1) * part)
        product = jnp.dot(x_ref[:, rows], w_buf[rows], preferred_element_type=F32)
        total = product if total is None else total + product
    high = total.astype(BF16).astype(F32)
    low = total - high
    for r in range(ranks):
        key = slice(r * HEAD_DIM, (r + 1) * HEAD_DIM)
        value = slice((ranks + r) * HEAD_DIM, (ranks + r + 1) * HEAD_DIM)
        pieces = [high[:, key], low[:, key], total[:, value]]
        out[r] = jnp.concatenate(pieces, axis=0)


def keyval(x, wkv, ranks):
    beams, depth = x.shape
    return pl.pallas_call(
        keyval_kernel,
        in_specs=[whole(), big()],
        out_specs=whole(),
        out_shape=shape(ranks, 3 * beams, HEAD_DIM),
        scratch_shapes=[pltpu.VMEM(wkv.shape, BF16), pltpu.SemaphoreType.DMA((4,))],
        compiler_params=params(8),
        cost_estimate=pl.CostEstimate(
            flops=2 * beams * wkv.size, bytes_accessed=2 * wkv.size, transcendentals=0
        ),
        name="keyval",
    )(x, wkv)


def correct_kernel(bank, column_ref, up_ref, *refs):
    *parts, own_out, other_out = refs
    total = parts[0][...]
    for part in parts[1:]:
        total += part[...]
    count, rank, width = up_ref.shape
    half = width // 2
    inner = total[:, half:].astype(BF16).astype(F32)
    column = column_ref[...]
    lane = iota(column.shape, 1)
    per = HEAD_DIM // rank
    spread = jnp.concatenate(
        [
            jnp.where(lane // rank + j * per == column, inner, 0.0)
            for j in range(count // per)
        ],
        axis=1,
    ).astype(BF16)
    delta = jnp.dot(
        spread, up_ref[...].reshape(count * rank, width), preferred_element_type=F32
    )
    rows = own_out.shape[0]
    for side in range(2):
        columns = slice(side * half, (side + 1) * half)
        part = delta[:, columns] + jnp.where(bank[0] == side, total[:, :half], 0.0)
        own_out[:, columns] = part[:rows]
        other_out[:, columns] = part[rows:]


def correct(bank, column, up, parts):
    rows = parts[0].shape[0]
    out = shape(rows // 2, up.shape[2])
    return pl.pallas_call(
        correct_kernel,
        in_specs=[scalar()] + [whole()] * (2 + len(parts)),
        out_specs=[whole()] * 2,
        out_shape=[out, out],
        compiler_params=params(),
        cost_estimate=pl.CostEstimate(
            flops=2 * rows * up.size, bytes_accessed=2 * up.size, transcendentals=0
        ),
        name="correct",
    )(bank, column, up, *parts)


def part_kernel(kept_ref, came_ref, *outs):
    for i, out in enumerate(outs):
        out[...] = kept_ref[i] + came_ref[i]


def part(kept, came):
    return pl.pallas_call(
        part_kernel,
        in_specs=[whole()] * 2,
        out_specs=[whole()] * kept.shape[0],
        out_shape=[shape(*kept.shape[1:])] * kept.shape[0],
        compiler_params=params(),
        name="part",
    )(kept, came)


def rotate(v, cosine, sine):
    return v * cosine + pltpu.roll(v, HEAD_DIM // 2, 1) * sine


def rotate_kernel(own_ref, came_ref, cos_ref, sin_ref, q_ref, rows_ref):
    cosine, sine = cos_ref[...], sin_ref[...]
    for g in range(own_ref.shape[1] // HEAD_DIM):
        columns = slice(g * HEAD_DIM, (g + 1) * HEAD_DIM)
        rows_ref[:, g, :] = rotate(own_ref[:, columns] + came_ref[:, columns], cosine, sine)
    q_ref[0] = rows_ref[...].reshape(q_ref.shape[1:]).astype(BF16)


def rotated(own, came, cosine, sine):
    rows, width = own.shape
    heads = width // HEAD_DIM
    return pl.pallas_call(
        rotate_kernel,
        in_specs=[whole()] * 4,
        out_specs=whole(),
        out_shape=shape(1, rows * heads, HEAD_DIM, dtype=BF16),
        scratch_shapes=[pltpu.VMEM((rows, heads, HEAD_DIM), F32)],
        compiler_params=params(),
        name="rotate",
    )(own, came, cosine, sine)


def join_kernel(*refs):
    *parts, out_ref = refs
    for i, part in enumerate(parts):
        out_ref[i] = part[0]


def join(parts):
    return pl.pallas_call(
        join_kernel,
        in_specs=[whole()] * len(parts),
        out_specs=whole(),
        out_shape=shape(len(parts), *parts[0].shape[1:], dtype=parts[0].dtype),
        compiler_params=params(),
        name="join",
    )(*parts)


def attend_kernel(slots, earlier, place, bank, length_ref, q_ref, k_ref, v_ref, *refs):
    before, out_ref = refs[:-1], refs[-1]
    if earlier:
        *before, keyval_ref = before
    beams, positions, _ = k_ref.shape
    rows = q_ref.shape[1]
    group = rows // beams
    row, lane = iota((rows, HEAD_DIM), 0), iota((rows, HEAD_DIM), 1)
    left = length_ref[...] - place[0] * positions
    live = jnp.concatenate(
        [lane + first < left for first in range(0, positions, HEAD_DIM)], axis=1
    )
    for i, slot in enumerate(slots):
        head = rank_of(place[0], bank[0], slot)
        columns = pl.ds(pl.multiple_of(head * HEAD_DIM, HEAD_DIM), HEAD_DIM)
        query = q_ref[i].astype(F32)
        scores = jnp.concatenate(
            [
                lax.dot_general(
                    query[beam * group : (beam + 1) * group].astype(BF16),
                    k_ref[beam, :, columns],
                    (((1,), (1,)), ((), ())),
                    preferred_element_type=F32,
                )
                for beam in range(beams)
            ],
            axis=0,
        ) * (1.0 / HEAD_DIM**0.5)
        scores = jnp.where(live, scores, -1e30)
        peak = jnp.max(scores, axis=1, keepdims=True)
        weights = jnp.where(live, jnp.exp(scores - peak), 0.0)
        total = jnp.sum(weights, axis=1, keepdims=True)
        values = [
            jnp.dot(
                weights[beam * group : (beam + 1) * group].astype(BF16),
                v_ref[beam, :, columns],
                preferred_element_type=F32,
            )
            for beam in range(beams)
        ]
        stats = jnp.where(lane == row % group, peak, 0.0)
        stats += jnp.where(lane == group + row % group, total, 0.0)
        stats = jnp.sum(stats.reshape(beams, group, HEAD_DIM), axis=1)
        high = stats.astype(BF16).astype(F32)
        middle = (stats - high).astype(BF16).astype(F32)
        low = stats - high - middle
        tail = high + pltpu.roll(middle, 2 * group, 1) + pltpu.roll(low, 4 * group, 1)
        if earlier:
            block = jnp.concatenate(values + [tail, keyval_ref[head]], axis=0)
            out_ref[head] = block.astype(BF16)
        else:
            block = jnp.concatenate(values + [tail, jnp.zeros_like(tail)], axis=0)
            out_ref[i] = block.astype(BF16)
    if earlier:
        done = [(ref, i) for ref in before for i in range(ref.shape[0])]
        for slot, (ref, i) in zip(earlier, done):
            head = rank_of(place[0], bank[0], slot)
            held = ref[i].astype(F32)[: rows + beams]
            out_ref[head] = jnp.concatenate([held, keyval_ref[head]], axis=0).astype(BF16)


def attend(place, bank, length, queries, keys, values, slots, earlier=(), before=()):
    count, rows, _ = queries.shape
    beams, positions, _ = keys.shape
    return pl.pallas_call(
        lambda *refs: attend_kernel(slots, earlier, *refs),
        in_specs=[scalar()] * 2 + [whole()] * (4 + len(before)),
        out_specs=whole(),
        out_shape=shape(
            count + len(earlier), rows + (4 if earlier else 2) * beams, HEAD_DIM, dtype=BF16
        ),
        compiler_params=params(),
        cost_estimate=pl.CostEstimate(
            flops=4 * rows * count * positions * HEAD_DIM,
            bytes_accessed=4 * beams * positions * HEAD_DIM * (16 if earlier else count),
            transcendentals=rows * count * positions,
        ),
        name="attend",
    )(place, bank, length, queries, keys, values, *before)


def combine_kernel(parts_ref, q_ref, cos_ref, sin_ref, out_ref, joined):
    ranks = parts_ref.shape[0]
    beams, group, _ = joined.shape
    rows = beams * group

    def by_row(v):
        return jnp.broadcast_to(v[:, None, :], (beams, group, HEAD_DIM)).reshape(rows, HEAD_DIM)

    head = iota((rows, HEAD_DIM), 0) % group
    lane = iota((rows, HEAD_DIM), 1)
    sums = jnp.sum(parts_ref[...].astype(F32)[:, rows + beams :], axis=0)
    key = sums[:beams] + sums[beams : 2 * beams]
    key = rotate(key, cos_ref[...], sin_ref[...]).astype(BF16).astype(F32)
    value = sums[2 * beams :].astype(BF16).astype(F32)
    score = jnp.sum(q_ref[0].astype(F32) * by_row(key), axis=1, keepdims=True) * (
        1.0 / HEAD_DIM**0.5
    )
    peaks, totals, weighted = [], [], []
    top = score
    for s in range(ranks):
        block = parts_ref[s].astype(F32)
        tail = block[rows : rows + beams]
        for turn in (2, 4):
            tail += pltpu.roll(block[rows : rows + beams], HEAD_DIM - turn * group, 1)
        tail = by_row(tail)
        peak = jnp.sum(jnp.where(lane == head, tail, 0.0), axis=1, keepdims=True)
        total = jnp.sum(jnp.where(lane == group + head, tail, 0.0), axis=1, keepdims=True)
        top = jnp.maximum(top, peak)
        peaks.append(peak)
        totals.append(total)
        weighted.append(block[:rows])
    new = jnp.exp(score - top)
    everything = new
    result = new.astype(BF16).astype(F32) * by_row(value)
    for peak, total, block in zip(peaks, totals, weighted):
        factor = jnp.exp(peak - top)
        everything += total * factor
        result += block * factor
    joined[...] = (result / everything).reshape(joined.shape)
    for g in range(group):
        out_ref[:, g * HEAD_DIM : (g + 1) * HEAD_DIM] = joined[:, g, :].astype(BF16)


def combine(parts, query, cosine, sine):
    beams = cosine.shape[0]
    group = query.shape[1] // beams
    return pl.pallas_call(
        combine_kernel,
        in_specs=[whole()] * 4,
        out_specs=whole(),
        out_shape=shape(beams, group * HEAD_DIM, dtype=BF16),
        scratch_shapes=[pltpu.VMEM((beams, group, HEAD_DIM), F32)],
        compiler_params=params(),
        name="combine",
    )(parts, query, cosine, sine)


def output_kernel(x_ref, w_ref, out):
    count, _, width = out.shape
    for s in range(count):
        columns = slice(s * width, (s + 1) * width)
        total = jnp.dot(x_ref[...], w_ref[:, columns], preferred_element_type=F32)
        out[s] = total.astype(BF16)


def output(x, weight, ranks):
    beams = x.shape[0]
    return pl.pallas_call(
        output_kernel,
        in_specs=[whole()] * 2,
        out_specs=whole(),
        out_shape=shape(ranks, beams, weight.shape[1] // ranks, dtype=BF16),
        compiler_params=params(),
        cost_estimate=pl.CostEstimate(
            flops=2 * beams * weight.size, bytes_accessed=2 * weight.size, transcendentals=0
        ),
        name="output",
    )(x, weight)


def residual_kernel(x_ref, parts_ref, out_ref):
    total = jnp.sum(parts_ref[...].astype(F32), axis=0)
    out_ref[...] = (x_ref[...].astype(F32) + total).astype(BF16)


def residual(x, parts):
    return pl.pallas_call(
        residual_kernel,
        in_specs=[whole()] * 2,
        out_specs=whole(),
        out_shape=jax.ShapeDtypeStruct(x.shape, BF16),
        compiler_params=params(),
        name="residual",
    )(x, parts)


def swapped(x):
    return lax.ppermute(x, "bank", [(0, 1), (1, 0)])


def traded(blocks):
    return lax.all_to_all(blocks, "tensor", 0, 0, tiled=True)


def hop(x, bit):
    pairs = []
    for rank in range(lax.axis_size("tensor")):
        for bank in range(2):
            pairs.append((2 * rank + bank, 2 * rank_of(rank, bank, bit) + bank))
    return lax.ppermute(x, ("tensor", "bank"), pairs)


def matched_body(
    normed_hidden_input,
    beam_adapter_index,
    beam_cache_length,
    query_weight,
    keyvalue_weight,
    output_weight,
    lowrank_down_factors,
    lowrank_up_factors,
    paged_key_cache,
    paged_value_cache,
):
    x = normed_hidden_input
    ranks = lax.axis_size("tensor")
    place = lax.axis_index("tensor").astype(jnp.int32).reshape(1)
    bank = lax.axis_index("bank").astype(jnp.int32).reshape(1)
    index = (beam_adapter_index, swapped(beam_adapter_index))
    x_other = swapped(x)
    lane = jnp.arange(HEAD_DIM, dtype=jnp.int32)
    half = HEAD_DIM // 2
    frequency = jnp.power(500000.0, -2.0 * (lane % half).astype(F32) / HEAD_DIM)
    angles = beam_cache_length.astype(F32)[:, None] * frequency[None, :]
    cosine = jnp.cos(angles)
    sine = jnp.where(lane < half, -1.0, 1.0) * jnp.sin(angles)
    weight = in_hbm(query_weight)
    down = in_hbm(lowrank_down_factors.swapaxes(1, 2))
    ahead = fetch(place, bank, down, weight, ranks, ranks // 4)
    sent, inner, column = project_sent(place, bank, index, x, x_other, *ahead, weight, ranks)
    came = hop(sent, 1)
    kept, length = project_kept(
        place, bank, beam_cache_length, x, x_other, weight, inner, ranks
    )
    kept, *sent = part(kept, came)
    near = tuple(range(ranks - 2, 0, -2))
    parts = [kept] + [hop(sent[slot // 2 - 1], slot) for slot in near]
    token_weight, _ = lax.optimization_barrier((in_hbm(keyvalue_weight), kept))
    token, parts = lax.optimization_barrier((keyval(x, in_hbm(token_weight), ranks), parts))
    own, other = correct(bank, column, lowrank_up_factors, parts)
    query = rotated(own, swapped(other), cosine, sine)

    def attended_part(queries, slots, **more):
        cache = paged_key_cache, paged_value_cache
        return attend(place, bank, length, queries, *cache, slots, **more)

    gathered = join([query] + [hop(query, slot) for slot in near])
    came = hop(gathered, 1)
    done = attended_part(gathered, (0, *near))
    odd = tuple(slot + 1 for slot in (0, *near))
    partial = attended_part(came, odd, earlier=(0, *near), before=(done, token))
    attended = combine(traded(partial), query, cosine, sine)
    return residual(x, traded(output(attended, output_weight, ranks)))


def joined(x, axis, combine):
    everything = jax.tree.map(lambda part: lax.all_gather(part, axis), x)
    leading = jax.tree.map(lambda part: part[0], everything)

    def turn(k, so_far):
        return combine(so_far, jax.tree.map(lambda part: part[k], everything))

    return lax.fori_loop(1, lax.axis_size(axis), turn, leading)


def apply_rotary(values, positions, head_size):
    row_count, col_count = values.shape
    half_size = head_size // 2
    frequency = jnp.power(500000.0, -2.0 * jnp.arange(half_size, dtype=jnp.float32) / head_size)
    angles = positions.astype(jnp.float32)[:, None] * frequency[None, :]
    cosine_table = jnp.cos(angles)[:, None, :]
    sine_table = jnp.sin(angles)[:, None, :]
    shaped = values.reshape(row_count, col_count // head_size, 2, half_size)
    first_half = shaped[:, :, 0]
    second_half = shaped[:, :, 1]
    rotated = jnp.stack(
        [
            first_half * cosine_table - second_half * sine_table,
            second_half * cosine_table + first_half * sine_table,
        ],
        axis=2,
    )
    return rotated.reshape(row_count, col_count)


def combine_parts(first_part, second_part):
    peak_one, total_one, weighted_one = first_part
    peak_two, total_two, weighted_two = second_part
    peak_both = jnp.maximum(peak_one, peak_two)
    factor_one = jnp.exp(peak_one - peak_both)
    factor_two = jnp.exp(peak_two - peak_both)
    return (
        peak_both,
        total_one * factor_one + total_two * factor_two,
        weighted_one * factor_one[..., None] + weighted_two * factor_two[..., None],
    )


def finish_heads(peak_score, weight_total, weighted, score_new, value_rows):
    peak_final = jnp.maximum(peak_score, score_new)
    old_factor = jnp.exp(peak_score - peak_final)
    new_weight = jnp.exp(score_new - peak_final)
    weight_total = weight_total * old_factor + new_weight
    weighted = (
        weighted * old_factor[..., None]
        + new_weight.astype(jnp.bfloat16).astype(jnp.float32)[..., None] * value_rows
    )
    return weighted / weight_total[..., None]


def body(
    normed_hidden_input,
    beam_adapter_index,
    beam_cache_length,
    query_weight,
    keyvalue_weight,
    output_weight,
    lowrank_down_factors,
    lowrank_up_factors,
    paged_key_cache,
    paged_value_cache,
):
    beam_rows, width_part = normed_hidden_input.shape
    model_width = query_weight.shape[1]
    kv_width = keyvalue_weight.shape[1] // 2
    head_count = model_width // HEAD_DIM
    kv_heads = kv_width // HEAD_DIM
    group_size = head_count // kv_heads
    tensor_index = lax.axis_index("tensor")
    query_part = jnp.dot(normed_hidden_input, query_weight, preferred_element_type=jnp.float32)
    keyval_part = jnp.dot(normed_hidden_input, keyvalue_weight, preferred_element_type=jnp.float32)
    down_all, up_all = (
        lax.all_gather(lowrank_down_factors, "bank", axis=0, tiled=True),
        lax.all_gather(lowrank_up_factors, "bank", axis=0, tiled=True),
    )
    inner_part = jnp.einsum(
        "ci,cim->cm",
        normed_hidden_input,
        down_all[beam_adapter_index],
        preferred_element_type=jnp.float32,
    )
    inner_total = lax.psum(inner_part, "tensor").astype(jnp.bfloat16)
    lowrank_delta = jnp.einsum(
        "mc,mct->mt", inner_total, up_all[beam_adapter_index], preferred_element_type=jnp.float32
    )
    query_total, keyval = lax.psum((query_part, keyval_part), "tensor")
    delta_total = lax.all_gather(lowrank_delta, "tensor", axis=1, tiled=True)
    query_rotated = apply_rotary(query_total + delta_total, beam_cache_length, HEAD_DIM).astype(
        jnp.bfloat16
    )
    key_new = apply_rotary(keyval[:, :kv_width], beam_cache_length, HEAD_DIM).astype(jnp.bfloat16)
    value_new = keyval[:, kv_width:].astype(jnp.bfloat16)
    position_count = paged_key_cache.shape[1]
    query_heads = query_rotated.reshape(beam_rows, kv_heads, group_size, HEAD_DIM)
    key_block = paged_key_cache.reshape(beam_rows, position_count, kv_heads, HEAD_DIM)
    value_block = paged_value_cache.reshape(beam_rows, position_count, kv_heads, HEAD_DIM)
    score_scale = 1.0 / HEAD_DIM**0.5
    scores = (
        jnp.einsum("bkgh,bpkh->bkgp", query_heads, key_block, preferred_element_type=jnp.float32)
        * score_scale
    )
    position_ids = tensor_index * position_count + jnp.arange(position_count)
    live_mask = (position_ids[None, :] < beam_cache_length[:, None])[:, None, None, :]
    scores = jnp.where(live_mask, scores, -1e30)
    peak_score = jnp.max(scores, axis=-1)
    weights = jnp.where(live_mask, jnp.exp(scores - peak_score[..., None]), 0.0)
    weight_total = jnp.sum(weights, axis=-1)
    weighted = jnp.einsum(
        "bkgp,bpkh->bkgh",
        weights.astype(jnp.bfloat16),
        value_block,
        preferred_element_type=jnp.float32,
    )
    peak_score, weight_total, weighted = joined(
        (peak_score, weight_total, weighted), "tensor", combine_parts
    )
    score_new = (
        jnp.einsum(
            "bkgh,bkh->bkg",
            query_heads,
            key_new.reshape(beam_rows, kv_heads, HEAD_DIM),
            preferred_element_type=jnp.float32,
        )
        * score_scale
    )
    value_rows = value_new.reshape(beam_rows, kv_heads, HEAD_DIM).astype(jnp.float32)[:, :, None, :]
    attended = (
        finish_heads(peak_score, weight_total, weighted, score_new, value_rows)
        .reshape(beam_rows, model_width)
        .astype(jnp.bfloat16)
    )
    attended_cols = lax.dynamic_slice_in_dim(attended, tensor_index * width_part, width_part, 1)
    mixed_cols = lax.psum_scatter(
        lax.dot_general(
            output_weight,
            attended_cols,
            (((0,), (1,)), ((), ())),
            preferred_element_type=jnp.float32,
        ),
        "tensor",
        scatter_dimension=0,
        tiled=True,
    )
    return (normed_hidden_input.astype(jnp.float32) + mixed_cols.T).astype(jnp.bfloat16)


def solution(mesh):
    matched = mesh.shape["tensor"] == 8 and mesh.shape["bank"] == 2
    return jax.shard_map(
        matched_body if matched else body,
        mesh=mesh,
        in_specs=(
            P(("groups", "bank"), "tensor"),
            P(("groups", "bank")),
            P(("groups", "bank")),
            P("tensor", None),
            P("tensor", None),
            P("tensor", None),
            P("bank", "tensor", None),
            P("bank", None, "tensor"),
            P(("groups", "bank"), "tensor", None),
            P(("groups", "bank"), "tensor", None),
        ),
        out_specs=P(("groups", "bank"), "tensor"),
        check_vma=False,
    )
```

```python
import jax
import jax.numpy as jnp
from jax import lax
from jax.experimental import pallas as pl
from jax.experimental.pallas import tpu as pltpu
from jax.sharding import PartitionSpec as P

HEAD_DIM = 128
F32 = jnp.float32
BF16 = jnp.bfloat16
CHUNKS = 2
MIB = 1024 * 1024


def whole():
    return pl.BlockSpec(memory_space=pltpu.VMEM)


def big():
    return pl.BlockSpec(memory_space=pltpu.HBM)


def scalar():
    return pl.BlockSpec(memory_space=pltpu.SMEM)


def in_hbm(array):
    return pltpu.with_memory_space_constraint(array, pltpu.HBM)


def shape(*dims, dtype=F32):
    return jax.ShapeDtypeStruct(dims, dtype)


def iota(dims, axis):
    return lax.broadcasted_iota(jnp.int32, dims, axis)


def params(mib=4):
    return pltpu.CompilerParams(vmem_limit_bytes=mib * MIB)


def exchanged(slot):
    return slot & ~3 | (slot & 1) << 1 | slot >> 1 & 1


def rank_of(place, bank, slot):
    return place ^ (slot + bank * (exchanged(slot) - slot))


def start_columns(weight, column, target, sems):
    depth, width = target.shape
    part = depth // CHUNKS
    copies = []
    for c in range(CHUNKS):
        rows = pl.ds(c * part, part)
        copies.append(
            pltpu.make_async_copy(
                weight.at[rows, pl.ds(pl.multiple_of(column, width), width)],
                target.at[rows, :],
                sems.at[c],
            )
        )
        copies[-1].start()
    return copies


def adapter_column(refs, bank, count):
    columns = []
    for ref in refs:
        rows = ref.shape[1]
        index = jnp.broadcast_to(ref[...].astype(F32), (rows, rows))
        diagonal = iota((rows, rows), 0) == iota((rows, rows), 1)
        columns.append(jnp.sum(jnp.where(diagonal, index, 0.0), axis=1, keepdims=True))
    column = jnp.concatenate(columns, axis=0).astype(jnp.int32) - bank * count
    return jnp.broadcast_to(column, (column.shape[0], HEAD_DIM))


def start_slots(parity, place, bank, w_ref, w_buf, sems):
    count, _, width = w_buf.shape
    copies = []
    for s in range(count):
        target = rank_of(place[0], bank[0], 2 * s + parity)
        first = (2 * target + bank[0]) * width
        copies.append(start_columns(w_ref, first, w_buf.at[s], sems.at[s]))
    return copies


def wait_all(copies):
    for copy in copies:
        copy.wait()


def start_parts(source, target, sems):
    part = source.shape[0] // sems.shape[0]
    copies = []
    for c in range(sems.shape[0]):
        rows = pl.ds(c * part, part)
        copies.append(pltpu.make_async_copy(source.at[rows], target.at[rows], sems.at[c]))
        copies[-1].start()
    return copies


def fetch_kernel(ref, out, sems):
    wait_all(start_parts(ref, out, sems))


def fetch(array):
    return pl.pallas_call(
        fetch_kernel,
        in_specs=[big()],
        out_specs=whole(),
        out_shape=jax.ShapeDtypeStruct(array.shape, array.dtype),
        scratch_shapes=[pltpu.SemaphoreType.DMA((2,))],
        compiler_params=params(),
        cost_estimate=pl.CostEstimate(
            flops=0, bytes_accessed=2 * array.size, transcendentals=0
        ),
        name="fetch",
    )(array)


def slot_scratch(wq, ranks):
    half, depth = ranks // 2, wq.shape[0]
    return [
        pltpu.VMEM((half, depth, wq.shape[1] // ranks // 2), BF16),
        pltpu.SemaphoreType.DMA((half, CHUNKS)),
    ]


def beam_rows(x_ref, other_ref):
    rows = [x_ref[...].astype(F32), other_ref[...].astype(F32)]
    return jnp.concatenate(rows, axis=0).astype(BF16)


def project_sent_kernel(
    place, bank, own_ref, came_ref, x_ref, other_ref, down_ref, w_ref, *refs
):
    out, inner, column_out, w_buf, sems = refs
    copies = start_slots(1, place, bank, w_ref, w_buf, sems)
    width = w_buf.shape[2]
    x = beam_rows(x_ref, other_ref)
    adapters, rank, depth = down_ref.shape
    every = lax.dot_general(
        x,
        down_ref[...].reshape(adapters * rank, depth),
        (((1,), (1,)), ((), ())),
        preferred_element_type=F32,
    )
    column = adapter_column((own_ref, came_ref), bank[0], adapters)
    column_out[...] = column
    lane = iota(column.shape, 1)
    per = HEAD_DIM // rank
    total = jnp.zeros(column.shape, F32)
    for j in range(adapters // per):
        part = every[:, j * HEAD_DIM : (j + 1) * HEAD_DIM]
        total += jnp.where(lane // rank + j * per == column, part, 0.0)
    inner[...] = total
    for s, slot in enumerate(copies):
        out[s, :, width:] = total
        wait_all(slot)
        out[s, :, :width] = jnp.dot(x, w_buf[s], preferred_element_type=F32)


def project_sent(place, bank, index, x, other, down, wq, ranks):
    rows = 2 * x.shape[0]
    return pl.pallas_call(
        project_sent_kernel,
        in_specs=[scalar()] * 2 + [whole()] * 5 + [big()],
        out_specs=[whole()] * 3,
        out_shape=[
            shape(ranks // 2, rows, wq.shape[1] // ranks // 2 + HEAD_DIM),
            shape(rows, HEAD_DIM),
            shape(rows, HEAD_DIM, dtype=jnp.int32),
        ],
        scratch_shapes=slot_scratch(wq, ranks),
        compiler_params=params(8),
        cost_estimate=pl.CostEstimate(
            flops=rows * (wq.size // 2 + 2 * down.size),
            bytes_accessed=wq.size // 2 + 2 * down.size,
            transcendentals=0,
        ),
        name="project_sent",
    )(place, bank, *[i.reshape(1, -1) for i in index], x, other, down, wq)


def project_kept_kernel(
    place, bank, length, x_ref, other_ref, w_ref, inner, out, length_out, w_buf, sems
):
    copies = start_slots(0, place, bank, w_ref, w_buf, sems)
    width = w_buf.shape[2]
    beams = x_ref.shape[0]
    row = iota(length_out.shape, 0)
    limit = jnp.zeros(length_out.shape, jnp.int32)
    for beam in range(beams):
        limit = jnp.where(row // (length_out.shape[0] // beams) == beam, length[beam], limit)
    length_out[...] = limit
    x = beam_rows(x_ref, other_ref)
    for s, slot in enumerate(copies):
        out[s, :, width:] = inner[...]
        wait_all(slot)
        out[s, :, :width] = jnp.dot(x, w_buf[s], preferred_element_type=F32)


def project_kept(place, bank, length, x, other, wq, inner, ranks):
    beams = x.shape[0]
    return pl.pallas_call(
        project_kept_kernel,
        in_specs=[scalar()] * 3 + [whole()] * 2 + [big(), whole()],
        out_specs=[whole()] * 2,
        out_shape=[
            shape(ranks // 2, 2 * beams, wq.shape[1] // ranks // 2 + HEAD_DIM),
            shape(beams * wq.shape[1] // ranks // HEAD_DIM, HEAD_DIM, dtype=jnp.int32),
        ],
        scratch_shapes=slot_scratch(wq, ranks),
        compiler_params=params(8),
        cost_estimate=pl.CostEstimate(
            flops=beams * wq.size, bytes_accessed=2 * wq.size, transcendentals=0
        ),
        name="project_kept",
    )(place, bank, length, x, other, wq, inner)


def keyval_kernel(x_ref, w_ref, out, w_buf, sems):
    copies = start_parts(w_ref, w_buf, sems)
    beams = x_ref.shape[0]
    ranks = out.shape[0]
    part = w_buf.shape[0] // len(copies)
    total = None
    for c, copy in enumerate(copies):
        copy.wait()
        rows = slice(c * part, (c + 1) * part)
        product = jnp.dot(x_ref[:, rows], w_buf[rows], preferred_element_type=F32)
        total = product if total is None else total + product
    high = total.astype(BF16).astype(F32)
    low = total - high
    for r in range(ranks):
        key = slice(r * HEAD_DIM, (r + 1) * HEAD_DIM)
        value = slice((ranks + r) * HEAD_DIM, (ranks + r + 1) * HEAD_DIM)
        pieces = [high[:, key], low[:, key], total[:, value]]
        out[r] = jnp.concatenate(pieces, axis=0)


def keyval(x, wkv, ranks):
    beams, depth = x.shape
    return pl.pallas_call(
        keyval_kernel,
        in_specs=[whole(), big()],
        out_specs=whole(),
        out_shape=shape(ranks, 3 * beams, HEAD_DIM),
        scratch_shapes=[pltpu.VMEM(wkv.shape, BF16), pltpu.SemaphoreType.DMA((4,))],
        compiler_params=params(8),
        cost_estimate=pl.CostEstimate(
            flops=2 * beams * wkv.size, bytes_accessed=2 * wkv.size, transcendentals=0
        ),
        name="keyval",
    )(x, wkv)


def correct_kernel(bank, column_ref, up_ref, *refs):
    *parts, own_out, other_out = refs
    total = parts[0][...]
    for part in parts[1:]:
        total += part[...]
    count, rank, width = up_ref.shape
    half = width // 2
    inner = total[:, half:].astype(BF16).astype(F32)
    column = column_ref[...]
    lane = iota(column.shape, 1)
    per = HEAD_DIM // rank
    spread = jnp.concatenate(
        [
            jnp.where(lane // rank + j * per == column, inner, 0.0)
            for j in range(count // per)
        ],
        axis=1,
    ).astype(BF16)
    delta = jnp.dot(
        spread, up_ref[...].reshape(count * rank, width), preferred_element_type=F32
    )
    rows = own_out.shape[0]
    for side in range(2):
        columns = slice(side * half, (side + 1) * half)
        part = delta[:, columns] + jnp.where(bank[0] == side, total[:, :half], 0.0)
        own_out[:, columns] = part[:rows]
        other_out[:, columns] = part[rows:]


def correct(bank, column, up, parts):
    rows = parts[0].shape[0]
    out = shape(rows // 2, up.shape[2])
    return pl.pallas_call(
        correct_kernel,
        in_specs=[scalar()] + [whole()] * (2 + len(parts)),
        out_specs=[whole()] * 2,
        out_shape=[out, out],
        compiler_params=params(),
        cost_estimate=pl.CostEstimate(
            flops=2 * rows * up.size, bytes_accessed=2 * up.size, transcendentals=0
        ),
        name="correct",
    )(bank, column, up, *parts)


def part_kernel(kept_ref, came_ref, *outs):
    for i, out in enumerate(outs):
        out[...] = kept_ref[i] + came_ref[i]


def part(kept, came):
    return pl.pallas_call(
        part_kernel,
        in_specs=[whole()] * 2,
        out_specs=[whole()] * kept.shape[0],
        out_shape=[shape(*kept.shape[1:])] * kept.shape[0],
        compiler_params=params(),
        name="part",
    )(kept, came)


def rotate(v, cosine, sine):
    return v * cosine + pltpu.roll(v, HEAD_DIM // 2, 1) * sine


def rotate_kernel(own_ref, came_ref, cos_ref, sin_ref, q_ref, rows_ref):
    cosine, sine = cos_ref[...], sin_ref[...]
    for g in range(own_ref.shape[1] // HEAD_DIM):
        columns = slice(g * HEAD_DIM, (g + 1) * HEAD_DIM)
        rows_ref[:, g, :] = rotate(own_ref[:, columns] + came_ref[:, columns], cosine, sine)
    q_ref[0] = rows_ref[...].reshape(q_ref.shape[1:]).astype(BF16)


def rotated(own, came, cosine, sine):
    rows, width = own.shape
    heads = width // HEAD_DIM
    return pl.pallas_call(
        rotate_kernel,
        in_specs=[whole()] * 4,
        out_specs=whole(),
        out_shape=shape(1, rows * heads, HEAD_DIM, dtype=BF16),
        scratch_shapes=[pltpu.VMEM((rows, heads, HEAD_DIM), F32)],
        compiler_params=params(),
        name="rotate",
    )(own, came, cosine, sine)


def join_kernel(*refs):
    *parts, out_ref = refs
    for i, part in enumerate(parts):
        out_ref[i] = part[0]


def join(parts):
    return pl.pallas_call(
        join_kernel,
        in_specs=[whole()] * len(parts),
        out_specs=whole(),
        out_shape=shape(len(parts), *parts[0].shape[1:], dtype=parts[0].dtype),
        compiler_params=params(),
        name="join",
    )(*parts)


def attend_kernel(slots, earlier, place, bank, length_ref, q_ref, k_ref, v_ref, *refs):
    before, out_ref = refs[:-1], refs[-1]
    if earlier:
        *before, keyval_ref = before
    beams, positions, _ = k_ref.shape
    rows = q_ref.shape[1]
    group = rows // beams
    row, lane = iota((rows, HEAD_DIM), 0), iota((rows, HEAD_DIM), 1)
    left = length_ref[...] - place[0] * positions
    live = jnp.concatenate(
        [lane + first < left for first in range(0, positions, HEAD_DIM)], axis=1
    )
    for i, slot in enumerate(slots):
        head = rank_of(place[0], bank[0], slot)
        columns = pl.ds(pl.multiple_of(head * HEAD_DIM, HEAD_DIM), HEAD_DIM)
        query = q_ref[i].astype(F32)
        scores = jnp.concatenate(
            [
                lax.dot_general(
                    query[beam * group : (beam + 1) * group].astype(BF16),
                    k_ref[beam, :, columns],
                    (((1,), (1,)), ((), ())),
                    preferred_element_type=F32,
                )
                for beam in range(beams)
            ],
            axis=0,
        ) * (1.0 / HEAD_DIM**0.5)
        scores = jnp.where(live, scores, -1e30)
        peak = jnp.max(scores, axis=1, keepdims=True)
        weights = jnp.where(live, jnp.exp(scores - peak), 0.0)
        total = jnp.sum(weights, axis=1, keepdims=True)
        values = [
            jnp.dot(
                weights[beam * group : (beam + 1) * group].astype(BF16),
                v_ref[beam, :, columns],
                preferred_element_type=F32,
            )
            for beam in range(beams)
        ]
        stats = jnp.where(lane == row % group, peak, 0.0)
        stats += jnp.where(lane == group + row % group, total, 0.0)
        stats = jnp.sum(stats.reshape(beams, group, HEAD_DIM), axis=1)
        high = stats.astype(BF16).astype(F32)
        middle = (stats - high).astype(BF16).astype(F32)
        low = stats - high - middle
        tail = high + pltpu.roll(middle, 2 * group, 1) + pltpu.roll(low, 4 * group, 1)
        if earlier:
            block = jnp.concatenate(values + [tail, keyval_ref[head]], axis=0)
            out_ref[head] = block.astype(BF16)
        else:
            block = jnp.concatenate(values + [tail, jnp.zeros_like(tail)], axis=0)
            out_ref[i] = block.astype(BF16)
    if earlier:
        done = [(ref, i) for ref in before for i in range(ref.shape[0])]
        for slot, (ref, i) in zip(earlier, done):
            head = rank_of(place[0], bank[0], slot)
            held = ref[i].astype(F32)[: rows + beams]
            out_ref[head] = jnp.concatenate([held, keyval_ref[head]], axis=0).astype(BF16)


def attend(place, bank, length, queries, keys, values, slots, earlier=(), before=()):
    count, rows, _ = queries.shape
    beams, positions, _ = keys.shape
    return pl.pallas_call(
        lambda *refs: attend_kernel(slots, earlier, *refs),
        in_specs=[scalar()] * 2 + [whole()] * (4 + len(before)),
        out_specs=whole(),
        out_shape=shape(
            count + len(earlier), rows + (4 if earlier else 2) * beams, HEAD_DIM, dtype=BF16
        ),
        compiler_params=params(),
        cost_estimate=pl.CostEstimate(
            flops=4 * rows * count * positions * HEAD_DIM,
            bytes_accessed=4 * beams * positions * HEAD_DIM * (16 if earlier else count),
            transcendentals=rows * count * positions,
        ),
        name="attend",
    )(place, bank, length, queries, keys, values, *before)


def combine_kernel(parts_ref, q_ref, cos_ref, sin_ref, out_ref, joined):
    ranks = parts_ref.shape[0]
    beams, group, _ = joined.shape
    rows = beams * group

    def by_row(v):
        return jnp.broadcast_to(v[:, None, :], (beams, group, HEAD_DIM)).reshape(rows, HEAD_DIM)

    head = iota((rows, HEAD_DIM), 0) % group
    lane = iota((rows, HEAD_DIM), 1)
    sums = jnp.sum(parts_ref[...].astype(F32)[:, rows + beams :], axis=0)
    key = sums[:beams] + sums[beams : 2 * beams]
    key = rotate(key, cos_ref[...], sin_ref[...]).astype(BF16).astype(F32)
    value = sums[2 * beams :].astype(BF16).astype(F32)
    score = jnp.sum(q_ref[0].astype(F32) * by_row(key), axis=1, keepdims=True) * (
        1.0 / HEAD_DIM**0.5
    )
    peaks, totals, weighted = [], [], []
    top = score
    for s in range(ranks):
        block = parts_ref[s].astype(F32)
        tail = block[rows : rows + beams]
        for turn in (2, 4):
            tail += pltpu.roll(block[rows : rows + beams], HEAD_DIM - turn * group, 1)
        tail = by_row(tail)
        peak = jnp.sum(jnp.where(lane == head, tail, 0.0), axis=1, keepdims=True)
        total = jnp.sum(jnp.where(lane == group + head, tail, 0.0), axis=1, keepdims=True)
        top = jnp.maximum(top, peak)
        peaks.append(peak)
        totals.append(total)
        weighted.append(block[:rows])
    new = jnp.exp(score - top)
    everything = new
    result = new.astype(BF16).astype(F32) * by_row(value)
    for peak, total, block in zip(peaks, totals, weighted):
        factor = jnp.exp(peak - top)
        everything += total * factor
        result += block * factor
    joined[...] = (result / everything).reshape(joined.shape)
    for g in range(group):
        out_ref[:, g * HEAD_DIM : (g + 1) * HEAD_DIM] = joined[:, g, :].astype(BF16)


def combine(parts, query, cosine, sine):
    beams = cosine.shape[0]
    group = query.shape[1] // beams
    return pl.pallas_call(
        combine_kernel,
        in_specs=[whole()] * 4,
        out_specs=whole(),
        out_shape=shape(beams, group * HEAD_DIM, dtype=BF16),
        scratch_shapes=[pltpu.VMEM((beams, group, HEAD_DIM), F32)],
        compiler_params=params(),
        name="combine",
    )(parts, query, cosine, sine)


def output_kernel(x_ref, w_ref, out):
    count, _, width = out.shape
    for s in range(count):
        columns = slice(s * width, (s + 1) * width)
        total = jnp.dot(x_ref[...], w_ref[:, columns], preferred_element_type=F32)
        out[s] = total.astype(BF16)


def output(x, weight, ranks):
    beams = x.shape[0]
    return pl.pallas_call(
        output_kernel,
        in_specs=[whole()] * 2,
        out_specs=whole(),
        out_shape=shape(ranks, beams, weight.shape[1] // ranks, dtype=BF16),
        compiler_params=params(),
        cost_estimate=pl.CostEstimate(
            flops=2 * beams * weight.size, bytes_accessed=2 * weight.size, transcendentals=0
        ),
        name="output",
    )(x, weight)


def residual_kernel(x_ref, parts_ref, out_ref):
    total = jnp.sum(parts_ref[...].astype(F32), axis=0)
    out_ref[...] = (x_ref[...].astype(F32) + total).astype(BF16)


def residual(x, parts):
    return pl.pallas_call(
        residual_kernel,
        in_specs=[whole()] * 2,
        out_specs=whole(),
        out_shape=jax.ShapeDtypeStruct(x.shape, BF16),
        compiler_params=params(),
        name="residual",
    )(x, parts)


def swapped(x):
    return lax.ppermute(x, "bank", [(0, 1), (1, 0)])


def traded(blocks):
    return lax.all_to_all(blocks, "tensor", 0, 0, tiled=True)


def hop(x, bit):
    pairs = []
    for rank in range(lax.axis_size("tensor")):
        for bank in range(2):
            pairs.append((2 * rank + bank, 2 * rank_of(rank, bank, bit) + bank))
    return lax.ppermute(x, ("tensor", "bank"), pairs)


def matched_body(
    normed_hidden_input,
    beam_adapter_index,
    beam_cache_length,
    query_weight,
    keyvalue_weight,
    output_weight,
    lowrank_down_factors,
    lowrank_up_factors,
    paged_key_cache,
    paged_value_cache,
):
    x = normed_hidden_input
    ranks = lax.axis_size("tensor")
    place = lax.axis_index("tensor").astype(jnp.int32).reshape(1)
    bank = lax.axis_index("bank").astype(jnp.int32).reshape(1)
    index = (beam_adapter_index, swapped(beam_adapter_index))
    x_other = swapped(x)
    lane = jnp.arange(HEAD_DIM, dtype=jnp.int32)
    half = HEAD_DIM // 2
    frequency = jnp.power(500000.0, -2.0 * (lane % half).astype(F32) / HEAD_DIM)
    angles = beam_cache_length.astype(F32)[:, None] * frequency[None, :]
    cosine = jnp.cos(angles)
    sine = jnp.where(lane < half, -1.0, 1.0) * jnp.sin(angles)
    weight = in_hbm(query_weight)
    down = fetch(in_hbm(lowrank_down_factors.swapaxes(1, 2)))
    sent, inner, column = project_sent(place, bank, index, x, x_other, down, weight, ranks)
    came = hop(sent, 1)
    kept, length = project_kept(
        place, bank, beam_cache_length, x, x_other, weight, inner, ranks
    )
    kept, *sent = part(kept, came)
    near = tuple(range(ranks - 2, 0, -2))
    parts = [kept] + [hop(sent[slot // 2 - 1], slot) for slot in near]
    token_weight, _ = lax.optimization_barrier((in_hbm(keyvalue_weight), kept))
    token, parts = lax.optimization_barrier((keyval(x, in_hbm(token_weight), ranks), parts))
    own, other = correct(bank, column, lowrank_up_factors, parts)
    query = rotated(own, swapped(other), cosine, sine)

    def attended_part(queries, slots, **more):
        cache = paged_key_cache, paged_value_cache
        return attend(place, bank, length, queries, *cache, slots, **more)

    came, done = lax.optimization_barrier((hop(query, 1), attended_part(query, (0,))))
    pair = join([query, came])
    pairs = [hop(pair, slot) for slot in near[:-1]]
    done = [done, attended_part(came, (1,))]
    held, _ = lax.optimization_barrier((pair, done[1]))
    pairs.append(hop(held, near[-1]))
    slots = [0, 1]
    for i in (0, 2):
        slots += [near[i], near[i] + 1]
        done.append(attended_part(pairs[i], tuple(slots[-2:])))
    last = near[1], near[1] + 1
    partial = attended_part(
        pairs[1], last, earlier=tuple(slots), before=(*done, token)
    )
    attended = combine(traded(partial), query, cosine, sine)
    return residual(x, traded(output(attended, output_weight, ranks)))


def joined(x, axis, combine):
    everything = jax.tree.map(lambda part: lax.all_gather(part, axis), x)
    leading = jax.tree.map(lambda part: part[0], everything)

    def turn(k, so_far):
        return combine(so_far, jax.tree.map(lambda part: part[k], everything))

    return lax.fori_loop(1, lax.axis_size(axis), turn, leading)


def apply_rotary(values, positions, head_size):
    row_count, col_count = values.shape
    half_size = head_size // 2
    frequency = jnp.power(500000.0, -2.0 * jnp.arange(half_size, dtype=jnp.float32) / head_size)
    angles = positions.astype(jnp.float32)[:, None] * frequency[None, :]
    cosine_table = jnp.cos(angles)[:, None, :]
    sine_table = jnp.sin(angles)[:, None, :]
    shaped = values.reshape(row_count, col_count // head_size, 2, half_size)
    first_half = shaped[:, :, 0]
    second_half = shaped[:, :, 1]
    rotated = jnp.stack(
        [
            first_half * cosine_table - second_half * sine_table,
            second_half * cosine_table + first_half * sine_table,
        ],
        axis=2,
    )
    return rotated.reshape(row_count, col_count)


def combine_parts(first_part, second_part):
    peak_one, total_one, weighted_one = first_part
    peak_two, total_two, weighted_two = second_part
    peak_both = jnp.maximum(peak_one, peak_two)
    factor_one = jnp.exp(peak_one - peak_both)
    factor_two = jnp.exp(peak_two - peak_both)
    return (
        peak_both,
        total_one * factor_one + total_two * factor_two,
        weighted_one * factor_one[..., None] + weighted_two * factor_two[..., None],
    )


def finish_heads(peak_score, weight_total, weighted, score_new, value_rows):
    peak_final = jnp.maximum(peak_score, score_new)
    old_factor = jnp.exp(peak_score - peak_final)
    new_weight = jnp.exp(score_new - peak_final)
    weight_total = weight_total * old_factor + new_weight
    weighted = (
        weighted * old_factor[..., None]
        + new_weight.astype(jnp.bfloat16).astype(jnp.float32)[..., None] * value_rows
    )
    return weighted / weight_total[..., None]


def body(
    normed_hidden_input,
    beam_adapter_index,
    beam_cache_length,
    query_weight,
    keyvalue_weight,
    output_weight,
    lowrank_down_factors,
    lowrank_up_factors,
    paged_key_cache,
    paged_value_cache,
):
    beam_rows, width_part = normed_hidden_input.shape
    model_width = query_weight.shape[1]
    kv_width = keyvalue_weight.shape[1] // 2
    head_count = model_width // HEAD_DIM
    kv_heads = kv_width // HEAD_DIM
    group_size = head_count // kv_heads
    tensor_index = lax.axis_index("tensor")
    query_part = jnp.dot(normed_hidden_input, query_weight, preferred_element_type=jnp.float32)
    keyval_part = jnp.dot(normed_hidden_input, keyvalue_weight, preferred_element_type=jnp.float32)
    down_all, up_all = (
        lax.all_gather(lowrank_down_factors, "bank", axis=0, tiled=True),
        lax.all_gather(lowrank_up_factors, "bank", axis=0, tiled=True),
    )
    inner_part = jnp.einsum(
        "ci,cim->cm",
        normed_hidden_input,
        down_all[beam_adapter_index],
        preferred_element_type=jnp.float32,
    )
    inner_total = lax.psum(inner_part, "tensor").astype(jnp.bfloat16)
    lowrank_delta = jnp.einsum(
        "mc,mct->mt", inner_total, up_all[beam_adapter_index], preferred_element_type=jnp.float32
    )
    query_total, keyval = lax.psum((query_part, keyval_part), "tensor")
    delta_total = lax.all_gather(lowrank_delta, "tensor", axis=1, tiled=True)
    query_rotated = apply_rotary(query_total + delta_total, beam_cache_length, HEAD_DIM).astype(
        jnp.bfloat16
    )
    key_new = apply_rotary(keyval[:, :kv_width], beam_cache_length, HEAD_DIM).astype(jnp.bfloat16)
    value_new = keyval[:, kv_width:].astype(jnp.bfloat16)
    position_count = paged_key_cache.shape[1]
    query_heads = query_rotated.reshape(beam_rows, kv_heads, group_size, HEAD_DIM)
    key_block = paged_key_cache.reshape(beam_rows, position_count, kv_heads, HEAD_DIM)
    value_block = paged_value_cache.reshape(beam_rows, position_count, kv_heads, HEAD_DIM)
    score_scale = 1.0 / HEAD_DIM**0.5
    scores = (
        jnp.einsum("bkgh,bpkh->bkgp", query_heads, key_block, preferred_element_type=jnp.float32)
        * score_scale
    )
    position_ids = tensor_index * position_count + jnp.arange(position_count)
    live_mask = (position_ids[None, :] < beam_cache_length[:, None])[:, None, None, :]
    scores = jnp.where(live_mask, scores, -1e30)
    peak_score = jnp.max(scores, axis=-1)
    weights = jnp.where(live_mask, jnp.exp(scores - peak_score[..., None]), 0.0)
    weight_total = jnp.sum(weights, axis=-1)
    weighted = jnp.einsum(
        "bkgp,bpkh->bkgh",
        weights.astype(jnp.bfloat16),
        value_block,
        preferred_element_type=jnp.float32,
    )
    peak_score, weight_total, weighted = joined(
        (peak_score, weight_total, weighted), "tensor", combine_parts
    )
    score_new = (
        jnp.einsum(
            "bkgh,bkh->bkg",
            query_heads,
            key_new.reshape(beam_rows, kv_heads, HEAD_DIM),
            preferred_element_type=jnp.float32,
        )
        * score_scale
    )
    value_rows = value_new.reshape(beam_rows, kv_heads, HEAD_DIM).astype(jnp.float32)[:, :, None, :]
    attended = (
        finish_heads(peak_score, weight_total, weighted, score_new, value_rows)
        .reshape(beam_rows, model_width)
        .astype(jnp.bfloat16)
    )
    attended_cols = lax.dynamic_slice_in_dim(attended, tensor_index * width_part, width_part, 1)
    mixed_cols = lax.psum_scatter(
        lax.dot_general(
            output_weight,
            attended_cols,
            (((0,), (1,)), ((), ())),
            preferred_element_type=jnp.float32,
        ),
        "tensor",
        scatter_dimension=0,
        tiled=True,
    )
    return (normed_hidden_input.astype(jnp.float32) + mixed_cols.T).astype(jnp.bfloat16)


def solution(mesh):
    matched = mesh.shape["tensor"] == 8 and mesh.shape["bank"] == 2
    return jax.shard_map(
        matched_body if matched else body,
        mesh=mesh,
        in_specs=(
            P(("groups", "bank"), "tensor"),
            P(("groups", "bank")),
            P(("groups", "bank")),
            P("tensor", None),
            P("tensor", None),
            P("tensor", None),
            P("bank", "tensor", None),
            P("bank", None, "tensor"),
            P(("groups", "bank"), "tensor", None),
            P(("groups", "bank"), "tensor", None),
        ),
        out_specs=P(("groups", "bank"), "tensor"),
        check_vma=False,
    )
```

```python
import jax
import jax.numpy as jnp
from jax import lax
from jax.experimental import pallas as pl
from jax.experimental.pallas import tpu as pltpu
from jax.sharding import PartitionSpec as P

HEAD_DIM = 128
F32 = jnp.float32
BF16 = jnp.bfloat16
CHUNKS = 2
MIB = 1024 * 1024


def whole():
    return pl.BlockSpec(memory_space=pltpu.VMEM)


def big():
    return pl.BlockSpec(memory_space=pltpu.HBM)


def scalar():
    return pl.BlockSpec(memory_space=pltpu.SMEM)


def in_hbm(array):
    return pltpu.with_memory_space_constraint(array, pltpu.HBM)


def shape(*dims, dtype=F32):
    return jax.ShapeDtypeStruct(dims, dtype)


def iota(dims, axis):
    return lax.broadcasted_iota(jnp.int32, dims, axis)


def params(mib=4):
    return pltpu.CompilerParams(vmem_limit_bytes=mib * MIB)


def exchanged(slot):
    return slot & ~3 | (slot & 1) << 1 | slot >> 1 & 1


def rank_of(place, bank, slot):
    return place ^ (slot + bank * (exchanged(slot) - slot))


def start_columns(weight, column, target, sems):
    depth, width = target.shape
    part = depth // CHUNKS
    copies = []
    for c in range(CHUNKS):
        rows = pl.ds(c * part, part)
        copies.append(
            pltpu.make_async_copy(
                weight.at[rows, pl.ds(pl.multiple_of(column, width), width)],
                target.at[rows, :],
                sems.at[c],
            )
        )
        copies[-1].start()
    return copies


def adapter_column(refs, bank, count):
    columns = []
    for ref in refs:
        rows = ref.shape[1]
        index = jnp.broadcast_to(ref[...].astype(F32), (rows, rows))
        diagonal = iota((rows, rows), 0) == iota((rows, rows), 1)
        columns.append(jnp.sum(jnp.where(diagonal, index, 0.0), axis=1, keepdims=True))
    column = jnp.concatenate(columns, axis=0).astype(jnp.int32) - bank * count
    return jnp.broadcast_to(column, (column.shape[0], HEAD_DIM))


def start_slots(parity, place, bank, w_ref, w_buf, sems):
    count, _, width = w_buf.shape
    copies = []
    for s in range(count):
        target = rank_of(place[0], bank[0], 2 * s + parity)
        first = (2 * target + bank[0]) * width
        copies.append(start_columns(w_ref, first, w_buf.at[s], sems.at[s]))
    return copies


def wait_all(copies):
    for copy in copies:
        copy.wait()


def start_parts(source, target, sems):
    part = source.shape[0] // sems.shape[0]
    copies = []
    for c in range(sems.shape[0]):
        rows = pl.ds(c * part, part)
        copies.append(pltpu.make_async_copy(source.at[rows], target.at[rows], sems.at[c]))
        copies[-1].start()
    return copies


def fetch_kernel(ref, out, sems):
    wait_all(start_parts(ref, out, sems))


def fetch(array):
    return pl.pallas_call(
        fetch_kernel,
        in_specs=[big()],
        out_specs=whole(),
        out_shape=jax.ShapeDtypeStruct(array.shape, array.dtype),
        scratch_shapes=[pltpu.SemaphoreType.DMA((2,))],
        compiler_params=params(),
        cost_estimate=pl.CostEstimate(
            flops=0, bytes_accessed=2 * array.size, transcendentals=0
        ),
        name="fetch",
    )(array)


def slot_scratch(wq, ranks):
    half, depth = ranks // 2, wq.shape[0]
    return [
        pltpu.VMEM((half, depth, wq.shape[1] // ranks // 2), BF16),
        pltpu.SemaphoreType.DMA((half, CHUNKS)),
    ]


def beam_rows(x_ref, other_ref):
    rows = [x_ref[...].astype(F32), other_ref[...].astype(F32)]
    return jnp.concatenate(rows, axis=0).astype(BF16)


def project_sent_kernel(
    place, bank, own_ref, came_ref, x_ref, other_ref, down_ref, w_ref, *refs
):
    out, inner, column_out, w_buf, sems = refs
    copies = start_slots(1, place, bank, w_ref, w_buf, sems)
    width = w_buf.shape[2]
    x = beam_rows(x_ref, other_ref)
    adapters, rank, depth = down_ref.shape
    every = lax.dot_general(
        x,
        down_ref[...].reshape(adapters * rank, depth),
        (((1,), (1,)), ((), ())),
        preferred_element_type=F32,
    )
    column = adapter_column((own_ref, came_ref), bank[0], adapters)
    column_out[...] = column
    lane = iota(column.shape, 1)
    per = HEAD_DIM // rank
    total = jnp.zeros(column.shape, F32)
    for j in range(adapters // per):
        part = every[:, j * HEAD_DIM : (j + 1) * HEAD_DIM]
        total += jnp.where(lane // rank + j * per == column, part, 0.0)
    inner[...] = total
    for s, slot in enumerate(copies):
        out[s, :, width:] = total
        wait_all(slot)
        out[s, :, :width] = jnp.dot(x, w_buf[s], preferred_element_type=F32)


def project_sent(place, bank, index, x, other, down, wq, ranks):
    rows = 2 * x.shape[0]
    return pl.pallas_call(
        project_sent_kernel,
        in_specs=[scalar()] * 2 + [whole()] * 5 + [big()],
        out_specs=[whole()] * 3,
        out_shape=[
            shape(ranks // 2, rows, wq.shape[1] // ranks // 2 + HEAD_DIM),
            shape(rows, HEAD_DIM),
            shape(rows, HEAD_DIM, dtype=jnp.int32),
        ],
        scratch_shapes=slot_scratch(wq, ranks),
        compiler_params=params(8),
        cost_estimate=pl.CostEstimate(
            flops=rows * (wq.size // 2 + 2 * down.size),
            bytes_accessed=wq.size // 2 + 2 * down.size,
            transcendentals=0,
        ),
        name="project_sent",
    )(place, bank, *[i.reshape(1, -1) for i in index], x, other, down, wq)


def project_kept_kernel(
    place, bank, length, x_ref, other_ref, w_ref, inner, out, length_out, w_buf, sems
):
    copies = start_slots(0, place, bank, w_ref, w_buf, sems)
    width = w_buf.shape[2]
    beams = x_ref.shape[0]
    row = iota(length_out.shape, 0)
    limit = jnp.zeros(length_out.shape, jnp.int32)
    for beam in range(beams):
        limit = jnp.where(row // (length_out.shape[0] // beams) == beam, length[beam], limit)
    length_out[...] = limit
    x = beam_rows(x_ref, other_ref)
    for s, slot in enumerate(copies):
        out[s, :, width:] = inner[...]
        wait_all(slot)
        out[s, :, :width] = jnp.dot(x, w_buf[s], preferred_element_type=F32)


def project_kept(place, bank, length, x, other, wq, inner, ranks):
    beams = x.shape[0]
    return pl.pallas_call(
        project_kept_kernel,
        in_specs=[scalar()] * 3 + [whole()] * 2 + [big(), whole()],
        out_specs=[whole()] * 2,
        out_shape=[
            shape(ranks // 2, 2 * beams, wq.shape[1] // ranks // 2 + HEAD_DIM),
            shape(beams * wq.shape[1] // ranks // HEAD_DIM, HEAD_DIM, dtype=jnp.int32),
        ],
        scratch_shapes=slot_scratch(wq, ranks),
        compiler_params=params(8),
        cost_estimate=pl.CostEstimate(
            flops=beams * wq.size, bytes_accessed=2 * wq.size, transcendentals=0
        ),
        name="project_kept",
    )(place, bank, length, x, other, wq, inner)


def keyval_kernel(x_ref, w_ref, out, w_buf, sems):
    copies = start_parts(w_ref, w_buf, sems)
    beams = x_ref.shape[0]
    ranks = out.shape[0]
    part = w_buf.shape[0] // len(copies)
    total = None
    for c, copy in enumerate(copies):
        copy.wait()
        rows = slice(c * part, (c + 1) * part)
        product = jnp.dot(x_ref[:, rows], w_buf[rows], preferred_element_type=F32)
        total = product if total is None else total + product
    high = total.astype(BF16).astype(F32)
    low = total - high
    for r in range(ranks):
        key = slice(r * HEAD_DIM, (r + 1) * HEAD_DIM)
        value = slice((ranks + r) * HEAD_DIM, (ranks + r + 1) * HEAD_DIM)
        pieces = [high[:, key], low[:, key], total[:, value]]
        out[r] = jnp.concatenate(pieces, axis=0)


def keyval(x, wkv, ranks):
    beams, depth = x.shape
    return pl.pallas_call(
        keyval_kernel,
        in_specs=[whole(), big()],
        out_specs=whole(),
        out_shape=shape(ranks, 3 * beams, HEAD_DIM),
        scratch_shapes=[pltpu.VMEM(wkv.shape, BF16), pltpu.SemaphoreType.DMA((4,))],
        compiler_params=params(8),
        cost_estimate=pl.CostEstimate(
            flops=2 * beams * wkv.size, bytes_accessed=2 * wkv.size, transcendentals=0
        ),
        name="keyval",
    )(x, wkv)


def correct_kernel(bank, column_ref, up_ref, *refs):
    *parts, own_out, other_out = refs
    total = parts[0][...]
    for part in parts[1:]:
        total += part[...]
    count, rank, width = up_ref.shape
    half = width // 2
    inner = total[:, half:].astype(BF16).astype(F32)
    column = column_ref[...]
    lane = iota(column.shape, 1)
    per = HEAD_DIM // rank
    spread = jnp.concatenate(
        [
            jnp.where(lane // rank + j * per == column, inner, 0.0)
            for j in range(count // per)
        ],
        axis=1,
    ).astype(BF16)
    delta = jnp.dot(
        spread, up_ref[...].reshape(count * rank, width), preferred_element_type=F32
    )
    rows = own_out.shape[0]
    for side in range(2):
        columns = slice(side * half, (side + 1) * half)
        part = delta[:, columns] + jnp.where(bank[0] == side, total[:, :half], 0.0)
        own_out[:, columns] = part[:rows]
        other_out[:, columns] = part[rows:]


def correct(bank, column, up, parts):
    rows = parts[0].shape[0]
    out = shape(rows // 2, up.shape[2])
    return pl.pallas_call(
        correct_kernel,
        in_specs=[scalar()] + [whole()] * (2 + len(parts)),
        out_specs=[whole()] * 2,
        out_shape=[out, out],
        compiler_params=params(),
        cost_estimate=pl.CostEstimate(
            flops=2 * rows * up.size, bytes_accessed=2 * up.size, transcendentals=0
        ),
        name="correct",
    )(bank, column, up, *parts)


def part_kernel(kept_ref, came_ref, *outs):
    for i, out in enumerate(outs):
        out[...] = kept_ref[i] + came_ref[i]


def part(kept, came):
    return pl.pallas_call(
        part_kernel,
        in_specs=[whole()] * 2,
        out_specs=[whole()] * kept.shape[0],
        out_shape=[shape(*kept.shape[1:])] * kept.shape[0],
        compiler_params=params(),
        name="part",
    )(kept, came)


def rotate(v, cosine, sine):
    return v * cosine + pltpu.roll(v, HEAD_DIM // 2, 1) * sine


def rotate_kernel(own_ref, came_ref, cos_ref, sin_ref, q_ref, rows_ref):
    cosine, sine = cos_ref[...], sin_ref[...]
    for g in range(own_ref.shape[1] // HEAD_DIM):
        columns = slice(g * HEAD_DIM, (g + 1) * HEAD_DIM)
        rows_ref[:, g, :] = rotate(own_ref[:, columns] + came_ref[:, columns], cosine, sine)
    q_ref[0] = rows_ref[...].reshape(q_ref.shape[1:]).astype(BF16)


def rotated(own, came, cosine, sine):
    rows, width = own.shape
    heads = width // HEAD_DIM
    return pl.pallas_call(
        rotate_kernel,
        in_specs=[whole()] * 4,
        out_specs=whole(),
        out_shape=shape(1, rows * heads, HEAD_DIM, dtype=BF16),
        scratch_shapes=[pltpu.VMEM((rows, heads, HEAD_DIM), F32)],
        compiler_params=params(),
        name="rotate",
    )(own, came, cosine, sine)


def join_kernel(*refs):
    *parts, out_ref = refs
    for i, part in enumerate(parts):
        out_ref[i] = part[0]


def join(parts):
    return pl.pallas_call(
        join_kernel,
        in_specs=[whole()] * len(parts),
        out_specs=whole(),
        out_shape=shape(len(parts), *parts[0].shape[1:], dtype=parts[0].dtype),
        compiler_params=params(),
        name="join",
    )(*parts)


def attend_kernel(slots, earlier, place, bank, length_ref, q_ref, k_ref, v_ref, *refs):
    before, out_ref = refs[:-1], refs[-1]
    if earlier:
        *before, keyval_ref = before
    beams, positions, _ = k_ref.shape
    rows = q_ref.shape[1]
    group = rows // beams
    row, lane = iota((rows, HEAD_DIM), 0), iota((rows, HEAD_DIM), 1)
    left = length_ref[...] - place[0] * positions
    live = jnp.concatenate(
        [lane + first < left for first in range(0, positions, HEAD_DIM)], axis=1
    )
    for i, slot in enumerate(slots):
        head = rank_of(place[0], bank[0], slot)
        columns = pl.ds(pl.multiple_of(head * HEAD_DIM, HEAD_DIM), HEAD_DIM)
        query = q_ref[i].astype(F32)
        scores = jnp.concatenate(
            [
                lax.dot_general(
                    query[beam * group : (beam + 1) * group].astype(BF16),
                    k_ref[beam, :, columns],
                    (((1,), (1,)), ((), ())),
                    preferred_element_type=F32,
                )
                for beam in range(beams)
            ],
            axis=0,
        ) * (1.0 / HEAD_DIM**0.5)
        scores = jnp.where(live, scores, -1e30)
        peak = jnp.max(scores, axis=1, keepdims=True)
        weights = jnp.where(live, jnp.exp(scores - peak), 0.0)
        total = jnp.sum(weights, axis=1, keepdims=True)
        values = [
            jnp.dot(
                weights[beam * group : (beam + 1) * group].astype(BF16),
                v_ref[beam, :, columns],
                preferred_element_type=F32,
            )
            for beam in range(beams)
        ]
        stats = jnp.where(lane == row % group, peak, 0.0)
        stats += jnp.where(lane == group + row % group, total, 0.0)
        stats = jnp.sum(stats.reshape(beams, group, HEAD_DIM), axis=1)
        high = stats.astype(BF16).astype(F32)
        middle = (stats - high).astype(BF16).astype(F32)
        low = stats - high - middle
        tail = high + pltpu.roll(middle, 2 * group, 1) + pltpu.roll(low, 4 * group, 1)
        if earlier:
            block = jnp.concatenate(values + [tail, keyval_ref[head]], axis=0)
            out_ref[head] = block.astype(BF16)
        else:
            block = jnp.concatenate(values + [tail, jnp.zeros_like(tail)], axis=0)
            out_ref[i] = block.astype(BF16)
    if earlier:
        done = [(ref, i) for ref in before for i in range(ref.shape[0])]
        for slot, (ref, i) in zip(earlier, done):
            head = rank_of(place[0], bank[0], slot)
            held = ref[i].astype(F32)[: rows + beams]
            out_ref[head] = jnp.concatenate([held, keyval_ref[head]], axis=0).astype(BF16)


def attend(place, bank, length, queries, keys, values, slots, earlier=(), before=()):
    count, rows, _ = queries.shape
    beams, positions, _ = keys.shape
    return pl.pallas_call(
        lambda *refs: attend_kernel(slots, earlier, *refs),
        in_specs=[scalar()] * 2 + [whole()] * (4 + len(before)),
        out_specs=whole(),
        out_shape=shape(
            count + len(earlier), rows + (4 if earlier else 2) * beams, HEAD_DIM, dtype=BF16
        ),
        compiler_params=params(),
        cost_estimate=pl.CostEstimate(
            flops=4 * rows * count * positions * HEAD_DIM,
            bytes_accessed=4 * beams * positions * HEAD_DIM * (16 if earlier else count),
            transcendentals=rows * count * positions,
        ),
        name="attend",
    )(place, bank, length, queries, keys, values, *before)


def combine_kernel(parts_ref, q_ref, cos_ref, sin_ref, out_ref, joined):
    ranks = parts_ref.shape[0]
    beams, group, _ = joined.shape
    rows = beams * group

    def by_row(v):
        return jnp.broadcast_to(v[:, None, :], (beams, group, HEAD_DIM)).reshape(rows, HEAD_DIM)

    head = iota((rows, HEAD_DIM), 0) % group
    lane = iota((rows, HEAD_DIM), 1)
    sums = jnp.sum(parts_ref[...].astype(F32)[:, rows + beams :], axis=0)
    key = sums[:beams] + sums[beams : 2 * beams]
    key = rotate(key, cos_ref[...], sin_ref[...]).astype(BF16).astype(F32)
    value = sums[2 * beams :].astype(BF16).astype(F32)
    score = jnp.sum(q_ref[0].astype(F32) * by_row(key), axis=1, keepdims=True) * (
        1.0 / HEAD_DIM**0.5
    )
    peaks, totals, weighted = [], [], []
    top = score
    for s in range(ranks):
        block = parts_ref[s].astype(F32)
        tail = block[rows : rows + beams]
        for turn in (2, 4):
            tail += pltpu.roll(block[rows : rows + beams], HEAD_DIM - turn * group, 1)
        tail = by_row(tail)
        peak = jnp.sum(jnp.where(lane == head, tail, 0.0), axis=1, keepdims=True)
        total = jnp.sum(jnp.where(lane == group + head, tail, 0.0), axis=1, keepdims=True)
        top = jnp.maximum(top, peak)
        peaks.append(peak)
        totals.append(total)
        weighted.append(block[:rows])
    new = jnp.exp(score - top)
    everything = new
    result = new.astype(BF16).astype(F32) * by_row(value)
    for peak, total, block in zip(peaks, totals, weighted):
        factor = jnp.exp(peak - top)
        everything += total * factor
        result += block * factor
    joined[...] = (result / everything).reshape(joined.shape)
    for g in range(group):
        out_ref[:, g * HEAD_DIM : (g + 1) * HEAD_DIM] = joined[:, g, :].astype(BF16)


def combine(parts, query, cosine, sine):
    beams = cosine.shape[0]
    group = query.shape[1] // beams
    return pl.pallas_call(
        combine_kernel,
        in_specs=[whole()] * 4,
        out_specs=whole(),
        out_shape=shape(beams, group * HEAD_DIM, dtype=BF16),
        scratch_shapes=[pltpu.VMEM((beams, group, HEAD_DIM), F32)],
        compiler_params=params(),
        name="combine",
    )(parts, query, cosine, sine)


def output_kernel(x_ref, w_ref, out):
    count, _, width = out.shape
    for s in range(count):
        columns = slice(s * width, (s + 1) * width)
        total = jnp.dot(x_ref[...], w_ref[:, columns], preferred_element_type=F32)
        out[s] = total.astype(BF16)


def output(x, weight, ranks):
    beams = x.shape[0]
    return pl.pallas_call(
        output_kernel,
        in_specs=[whole()] * 2,
        out_specs=whole(),
        out_shape=shape(ranks, beams, weight.shape[1] // ranks, dtype=BF16),
        compiler_params=params(),
        cost_estimate=pl.CostEstimate(
            flops=2 * beams * weight.size, bytes_accessed=2 * weight.size, transcendentals=0
        ),
        name="output",
    )(x, weight)


def residual_kernel(x_ref, parts_ref, out_ref):
    total = jnp.sum(parts_ref[...].astype(F32), axis=0)
    out_ref[...] = (x_ref[...].astype(F32) + total).astype(BF16)


def residual(x, parts):
    return pl.pallas_call(
        residual_kernel,
        in_specs=[whole()] * 2,
        out_specs=whole(),
        out_shape=jax.ShapeDtypeStruct(x.shape, BF16),
        compiler_params=params(),
        name="residual",
    )(x, parts)


def swapped(x):
    return lax.ppermute(x, "bank", [(0, 1), (1, 0)])


def traded(blocks):
    return lax.all_to_all(blocks, "tensor", 0, 0, tiled=True)


def hop(x, bit):
    pairs = []
    for rank in range(lax.axis_size("tensor")):
        for bank in range(2):
            pairs.append((2 * rank + bank, 2 * rank_of(rank, bank, bit) + bank))
    return lax.ppermute(x, ("tensor", "bank"), pairs)


def matched_body(
    normed_hidden_input,
    beam_adapter_index,
    beam_cache_length,
    query_weight,
    keyvalue_weight,
    output_weight,
    lowrank_down_factors,
    lowrank_up_factors,
    paged_key_cache,
    paged_value_cache,
):
    x = normed_hidden_input
    ranks = lax.axis_size("tensor")
    place = lax.axis_index("tensor").astype(jnp.int32).reshape(1)
    bank = lax.axis_index("bank").astype(jnp.int32).reshape(1)
    index = (beam_adapter_index, swapped(beam_adapter_index))
    x_other = swapped(x)
    lane = jnp.arange(HEAD_DIM, dtype=jnp.int32)
    half = HEAD_DIM // 2
    frequency = jnp.power(500000.0, -2.0 * (lane % half).astype(F32) / HEAD_DIM)
    angles = beam_cache_length.astype(F32)[:, None] * frequency[None, :]
    cosine = jnp.cos(angles)
    sine = jnp.where(lane < half, -1.0, 1.0) * jnp.sin(angles)
    weight = in_hbm(query_weight)
    down = fetch(in_hbm(lowrank_down_factors.swapaxes(1, 2)))
    sent, inner, column = project_sent(place, bank, index, x, x_other, down, weight, ranks)
    came = hop(sent, 1)
    kept, length = project_kept(
        place, bank, beam_cache_length, x, x_other, weight, inner, ranks
    )
    kept, *sent = part(kept, came)
    near = 4, 6, 2
    parts = [kept] + [hop(sent[slot // 2 - 1], slot) for slot in near]
    token_weight, _ = lax.optimization_barrier((in_hbm(keyvalue_weight), kept))
    token, parts = lax.optimization_barrier((keyval(x, in_hbm(token_weight), ranks), parts))
    own, other = correct(bank, column, lowrank_up_factors, parts)
    query = rotated(own, swapped(other), cosine, sine)

    def attended_part(queries, slots, **more):
        cache = paged_key_cache, paged_value_cache
        return attend(place, bank, length, queries, *cache, slots, **more)

    gathered = join([query] + [hop(query, slot) for slot in near])
    came = hop(gathered, 1)
    done = attended_part(gathered, (0, *near))
    odd = tuple(slot + 1 for slot in (0, *near))
    partial = attended_part(came, odd, earlier=(0, *near), before=(done, token))
    attended = combine(traded(partial), query, cosine, sine)
    return residual(x, traded(output(attended, output_weight, ranks)))


def joined(x, axis, combine):
    everything = jax.tree.map(lambda part: lax.all_gather(part, axis), x)
    leading = jax.tree.map(lambda part: part[0], everything)

    def turn(k, so_far):
        return combine(so_far, jax.tree.map(lambda part: part[k], everything))

    return lax.fori_loop(1, lax.axis_size(axis), turn, leading)


def apply_rotary(values, positions, head_size):
    row_count, col_count = values.shape
    half_size = head_size // 2
    frequency = jnp.power(500000.0, -2.0 * jnp.arange(half_size, dtype=jnp.float32) / head_size)
    angles = positions.astype(jnp.float32)[:, None] * frequency[None, :]
    cosine_table = jnp.cos(angles)[:, None, :]
    sine_table = jnp.sin(angles)[:, None, :]
    shaped = values.reshape(row_count, col_count // head_size, 2, half_size)
    first_half = shaped[:, :, 0]
    second_half = shaped[:, :, 1]
    rotated = jnp.stack(
        [
            first_half * cosine_table - second_half * sine_table,
            second_half * cosine_table + first_half * sine_table,
        ],
        axis=2,
    )
    return rotated.reshape(row_count, col_count)


def combine_parts(first_part, second_part):
    peak_one, total_one, weighted_one = first_part
    peak_two, total_two, weighted_two = second_part
    peak_both = jnp.maximum(peak_one, peak_two)
    factor_one = jnp.exp(peak_one - peak_both)
    factor_two = jnp.exp(peak_two - peak_both)
    return (
        peak_both,
        total_one * factor_one + total_two * factor_two,
        weighted_one * factor_one[..., None] + weighted_two * factor_two[..., None],
    )


def finish_heads(peak_score, weight_total, weighted, score_new, value_rows):
    peak_final = jnp.maximum(peak_score, score_new)
    old_factor = jnp.exp(peak_score - peak_final)
    new_weight = jnp.exp(score_new - peak_final)
    weight_total = weight_total * old_factor + new_weight
    weighted = (
        weighted * old_factor[..., None]
        + new_weight.astype(jnp.bfloat16).astype(jnp.float32)[..., None] * value_rows
    )
    return weighted / weight_total[..., None]


def body(
    normed_hidden_input,
    beam_adapter_index,
    beam_cache_length,
    query_weight,
    keyvalue_weight,
    output_weight,
    lowrank_down_factors,
    lowrank_up_factors,
    paged_key_cache,
    paged_value_cache,
):
    beam_rows, width_part = normed_hidden_input.shape
    model_width = query_weight.shape[1]
    kv_width = keyvalue_weight.shape[1] // 2
    head_count = model_width // HEAD_DIM
    kv_heads = kv_width // HEAD_DIM
    group_size = head_count // kv_heads
    tensor_index = lax.axis_index("tensor")
    query_part = jnp.dot(normed_hidden_input, query_weight, preferred_element_type=jnp.float32)
    keyval_part = jnp.dot(normed_hidden_input, keyvalue_weight, preferred_element_type=jnp.float32)
    down_all, up_all = (
        lax.all_gather(lowrank_down_factors, "bank", axis=0, tiled=True),
        lax.all_gather(lowrank_up_factors, "bank", axis=0, tiled=True),
    )
    inner_part = jnp.einsum(
        "ci,cim->cm",
        normed_hidden_input,
        down_all[beam_adapter_index],
        preferred_element_type=jnp.float32,
    )
    inner_total = lax.psum(inner_part, "tensor").astype(jnp.bfloat16)
    lowrank_delta = jnp.einsum(
        "mc,mct->mt", inner_total, up_all[beam_adapter_index], preferred_element_type=jnp.float32
    )
    query_total, keyval = lax.psum((query_part, keyval_part), "tensor")
    delta_total = lax.all_gather(lowrank_delta, "tensor", axis=1, tiled=True)
    query_rotated = apply_rotary(query_total + delta_total, beam_cache_length, HEAD_DIM).astype(
        jnp.bfloat16
    )
    key_new = apply_rotary(keyval[:, :kv_width], beam_cache_length, HEAD_DIM).astype(jnp.bfloat16)
    value_new = keyval[:, kv_width:].astype(jnp.bfloat16)
    position_count = paged_key_cache.shape[1]
    query_heads = query_rotated.reshape(beam_rows, kv_heads, group_size, HEAD_DIM)
    key_block = paged_key_cache.reshape(beam_rows, position_count, kv_heads, HEAD_DIM)
    value_block = paged_value_cache.reshape(beam_rows, position_count, kv_heads, HEAD_DIM)
    score_scale = 1.0 / HEAD_DIM**0.5
    scores = (
        jnp.einsum("bkgh,bpkh->bkgp", query_heads, key_block, preferred_element_type=jnp.float32)
        * score_scale
    )
    position_ids = tensor_index * position_count + jnp.arange(position_count)
    live_mask = (position_ids[None, :] < beam_cache_length[:, None])[:, None, None, :]
    scores = jnp.where(live_mask, scores, -1e30)
    peak_score = jnp.max(scores, axis=-1)
    weights = jnp.where(live_mask, jnp.exp(scores - peak_score[..., None]), 0.0)
    weight_total = jnp.sum(weights, axis=-1)
    weighted = jnp.einsum(
        "bkgp,bpkh->bkgh",
        weights.astype(jnp.bfloat16),
        value_block,
        preferred_element_type=jnp.float32,
    )
    peak_score, weight_total, weighted = joined(
        (peak_score, weight_total, weighted), "tensor", combine_parts
    )
    score_new = (
        jnp.einsum(
            "bkgh,bkh->bkg",
            query_heads,
            key_new.reshape(beam_rows, kv_heads, HEAD_DIM),
            preferred_element_type=jnp.float32,
        )
        * score_scale
    )
    value_rows = value_new.reshape(beam_rows, kv_heads, HEAD_DIM).astype(jnp.float32)[:, :, None, :]
    attended = (
        finish_heads(peak_score, weight_total, weighted, score_new, value_rows)
        .reshape(beam_rows, model_width)
        .astype(jnp.bfloat16)
    )
    attended_cols = lax.dynamic_slice_in_dim(attended, tensor_index * width_part, width_part, 1)
    mixed_cols = lax.psum_scatter(
        lax.dot_general(
            output_weight,
            attended_cols,
            (((0,), (1,)), ((), ())),
            preferred_element_type=jnp.float32,
        ),
        "tensor",
        scatter_dimension=0,
        tiled=True,
    )
    return (normed_hidden_input.astype(jnp.float32) + mixed_cols.T).astype(jnp.bfloat16)


def solution(mesh):
    matched = mesh.shape["tensor"] == 8 and mesh.shape["bank"] == 2
    return jax.shard_map(
        matched_body if matched else body,
        mesh=mesh,
        in_specs=(
            P(("groups", "bank"), "tensor"),
            P(("groups", "bank")),
            P(("groups", "bank")),
            P("tensor", None),
            P("tensor", None),
            P("tensor", None),
            P("bank", "tensor", None),
            P("bank", None, "tensor"),
            P(("groups", "bank"), "tensor", None),
            P(("groups", "bank"), "tensor", None),
        ),
        out_specs=P(("groups", "bank"), "tensor"),
        check_vma=False,
    )
```

```python
import jax
import jax.numpy as jnp
from jax import lax
from jax.experimental import pallas as pl
from jax.experimental.pallas import tpu as pltpu
from jax.sharding import PartitionSpec as P

HEAD_DIM = 128
F32 = jnp.float32
BF16 = jnp.bfloat16
CHUNKS = 2
MIB = 1024 * 1024


def whole():
    return pl.BlockSpec(memory_space=pltpu.VMEM)


def big():
    return pl.BlockSpec(memory_space=pltpu.HBM)


def scalar():
    return pl.BlockSpec(memory_space=pltpu.SMEM)


def in_hbm(array):
    return pltpu.with_memory_space_constraint(array, pltpu.HBM)


def shape(*dims, dtype=F32):
    return jax.ShapeDtypeStruct(dims, dtype)


def iota(dims, axis):
    return lax.broadcasted_iota(jnp.int32, dims, axis)


def params(mib=4):
    return pltpu.CompilerParams(vmem_limit_bytes=mib * MIB)


def exchanged(slot):
    return slot & ~3 | (slot & 1) << 1 | slot >> 1 & 1


def rank_of(place, bank, slot):
    return place ^ (slot + bank * (exchanged(slot) - slot))


def start_columns(weight, column, target, sems):
    depth, width = target.shape
    part = depth // CHUNKS
    copies = []
    for c in range(CHUNKS):
        rows = pl.ds(c * part, part)
        copies.append(
            pltpu.make_async_copy(
                weight.at[rows, pl.ds(pl.multiple_of(column, width), width)],
                target.at[rows, :],
                sems.at[c],
            )
        )
        copies[-1].start()
    return copies


def adapter_column(refs, bank, count):
    columns = []
    for ref in refs:
        rows = ref.shape[1]
        index = jnp.broadcast_to(ref[...].astype(F32), (rows, rows))
        diagonal = iota((rows, rows), 0) == iota((rows, rows), 1)
        columns.append(jnp.sum(jnp.where(diagonal, index, 0.0), axis=1, keepdims=True))
    column = jnp.concatenate(columns, axis=0).astype(jnp.int32) - bank * count
    return jnp.broadcast_to(column, (column.shape[0], HEAD_DIM))


def start_slots(parity, place, bank, w_ref, w_buf, sems):
    count, _, width = w_buf.shape
    copies = []
    for s in range(count):
        target = rank_of(place[0], bank[0], 2 * s + parity)
        first = (2 * target + bank[0]) * width
        copies.append(start_columns(w_ref, first, w_buf.at[s], sems.at[s]))
    return copies


def wait_all(copies):
    for copy in copies:
        copy.wait()


def start_parts(source, target, sems):
    part = source.shape[0] // sems.shape[0]
    copies = []
    for c in range(sems.shape[0]):
        rows = pl.ds(c * part, part)
        copies.append(pltpu.make_async_copy(source.at[rows], target.at[rows], sems.at[c]))
        copies[-1].start()
    return copies


def fetch_kernel(ref, out, sems):
    wait_all(start_parts(ref, out, sems))


def fetch(array):
    return pl.pallas_call(
        fetch_kernel,
        in_specs=[big()],
        out_specs=whole(),
        out_shape=jax.ShapeDtypeStruct(array.shape, array.dtype),
        scratch_shapes=[pltpu.SemaphoreType.DMA((2,))],
        compiler_params=params(),
        cost_estimate=pl.CostEstimate(
            flops=0, bytes_accessed=2 * array.size, transcendentals=0
        ),
        name="fetch",
    )(array)


def slot_scratch(wq, ranks):
    half, depth = ranks // 2, wq.shape[0]
    return [
        pltpu.VMEM((half, depth, wq.shape[1] // ranks // 2), BF16),
        pltpu.SemaphoreType.DMA((half, CHUNKS)),
    ]


def beam_rows(x_ref, other_ref):
    rows = [x_ref[...].astype(F32), other_ref[...].astype(F32)]
    return jnp.concatenate(rows, axis=0).astype(BF16)


def project_sent_kernel(
    place, bank, own_ref, came_ref, x_ref, other_ref, down_ref, w_ref, *refs
):
    out, inner, column_out, w_buf, sems = refs
    copies = start_slots(1, place, bank, w_ref, w_buf, sems)
    width = w_buf.shape[2]
    x = beam_rows(x_ref, other_ref)
    adapters, rank, depth = down_ref.shape
    every = lax.dot_general(
        x,
        down_ref[...].reshape(adapters * rank, depth),
        (((1,), (1,)), ((), ())),
        preferred_element_type=F32,
    )
    column = adapter_column((own_ref, came_ref), bank[0], adapters)
    column_out[...] = column
    lane = iota(column.shape, 1)
    per = HEAD_DIM // rank
    total = jnp.zeros(column.shape, F32)
    for j in range(adapters // per):
        part = every[:, j * HEAD_DIM : (j + 1) * HEAD_DIM]
        total += jnp.where(lane // rank + j * per == column, part, 0.0)
    inner[...] = total
    out[:, len(copies) * width :] = total
    for s, slot in enumerate(copies):
        wait_all(slot)
        columns = slice(s * width, (s + 1) * width)
        out[:, columns] = jnp.dot(x, w_buf[s], preferred_element_type=F32)


def project_sent(place, bank, index, x, other, down, wq, ranks):
    rows = 2 * x.shape[0]
    return pl.pallas_call(
        project_sent_kernel,
        in_specs=[scalar()] * 2 + [whole()] * 5 + [big()],
        out_specs=[whole()] * 3,
        out_shape=[
            shape(rows, wq.shape[1] // 4 + HEAD_DIM),
            shape(rows, HEAD_DIM),
            shape(rows, HEAD_DIM, dtype=jnp.int32),
        ],
        scratch_shapes=slot_scratch(wq, ranks),
        compiler_params=params(8),
        cost_estimate=pl.CostEstimate(
            flops=rows * (wq.size // 2 + 2 * down.size),
            bytes_accessed=wq.size // 2 + 2 * down.size,
            transcendentals=0,
        ),
        name="project_sent",
    )(place, bank, *[i.reshape(1, -1) for i in index], x, other, down, wq)


def project_kept_kernel(
    place, bank, length, x_ref, other_ref, w_ref, out, length_out, w_buf, sems
):
    copies = start_slots(0, place, bank, w_ref, w_buf, sems)
    width = w_buf.shape[2]
    beams = x_ref.shape[0]
    row = iota(length_out.shape, 0)
    limit = jnp.zeros(length_out.shape, jnp.int32)
    for beam in range(beams):
        limit = jnp.where(row // (length_out.shape[0] // beams) == beam, length[beam], limit)
    length_out[...] = limit
    x = beam_rows(x_ref, other_ref)
    for s, slot in enumerate(copies):
        wait_all(slot)
        columns = slice(s * width, (s + 1) * width)
        out[:, columns] = jnp.dot(x, w_buf[s], preferred_element_type=F32)


def project_kept(place, bank, length, x, other, wq, ranks):
    beams = x.shape[0]
    return pl.pallas_call(
        project_kept_kernel,
        in_specs=[scalar()] * 3 + [whole()] * 2 + [big()],
        out_specs=[whole()] * 2,
        out_shape=[
            shape(2 * beams, wq.shape[1] // 4),
            shape(beams * wq.shape[1] // ranks // HEAD_DIM, HEAD_DIM, dtype=jnp.int32),
        ],
        scratch_shapes=slot_scratch(wq, ranks),
        compiler_params=params(8),
        cost_estimate=pl.CostEstimate(
            flops=beams * wq.size, bytes_accessed=2 * wq.size, transcendentals=0
        ),
        name="project_kept",
    )(place, bank, length, x, other, wq)


def keyval_kernel(x_ref, w_ref, out, w_buf, sems):
    copies = start_parts(w_ref, w_buf, sems)
    beams = x_ref.shape[0]
    ranks = out.shape[0]
    part = w_buf.shape[0] // len(copies)
    total = None
    for c, copy in enumerate(copies):
        copy.wait()
        rows = slice(c * part, (c + 1) * part)
        product = jnp.dot(x_ref[:, rows], w_buf[rows], preferred_element_type=F32)
        total = product if total is None else total + product
    high = total.astype(BF16).astype(F32)
    low = total - high
    for r in range(ranks):
        key = slice(r * HEAD_DIM, (r + 1) * HEAD_DIM)
        value = slice((ranks + r) * HEAD_DIM, (ranks + r + 1) * HEAD_DIM)
        pieces = [high[:, key], low[:, key], total[:, value]]
        out[r] = jnp.concatenate(pieces, axis=0)


def keyval(x, wkv, ranks):
    beams, depth = x.shape
    return pl.pallas_call(
        keyval_kernel,
        in_specs=[whole(), big()],
        out_specs=whole(),
        out_shape=shape(ranks, 3 * beams, HEAD_DIM),
        scratch_shapes=[pltpu.VMEM(wkv.shape, BF16), pltpu.SemaphoreType.DMA((4,))],
        compiler_params=params(8),
        cost_estimate=pl.CostEstimate(
            flops=2 * beams * wkv.size, bytes_accessed=2 * wkv.size, transcendentals=0
        ),
        name="keyval",
    )(x, wkv)


def correct_kernel(bank, column_ref, up_ref, *refs):
    *parts, own_out, other_out = refs
    total = parts[0][...]
    for part in parts[1:]:
        total += part[...]
    count, rank, width = up_ref.shape
    half = width // 2
    inner = total[:, half:].astype(BF16).astype(F32)
    column = column_ref[...]
    lane = iota(column.shape, 1)
    per = HEAD_DIM // rank
    spread = jnp.concatenate(
        [
            jnp.where(lane // rank + j * per == column, inner, 0.0)
            for j in range(count // per)
        ],
        axis=1,
    ).astype(BF16)
    delta = jnp.dot(
        spread, up_ref[...].reshape(count * rank, width), preferred_element_type=F32
    )
    rows = own_out.shape[0]
    for side in range(2):
        columns = slice(side * half, (side + 1) * half)
        part = delta[:, columns] + jnp.where(bank[0] == side, total[:, :half], 0.0)
        own_out[:, columns] = part[:rows]
        other_out[:, columns] = part[rows:]


def correct(bank, column, up, parts):
    rows = parts[0].shape[0]
    out = shape(rows // 2, up.shape[2])
    return pl.pallas_call(
        correct_kernel,
        in_specs=[scalar()] + [whole()] * (2 + len(parts)),
        out_specs=[whole()] * 2,
        out_shape=[out, out],
        compiler_params=params(),
        cost_estimate=pl.CostEstimate(
            flops=2 * rows * up.size, bytes_accessed=2 * up.size, transcendentals=0
        ),
        name="correct",
    )(bank, column, up, *parts)


def part_kernel(kept_ref, inner_ref, came_ref, *outs):
    width = outs[0].shape[1] - HEAD_DIM
    inner = inner_ref[...] + came_ref[:, len(outs) * width :]
    for i, out in enumerate(outs):
        columns = slice(i * width, (i + 1) * width)
        out[:, :width] = kept_ref[:, columns] + came_ref[:, columns]
        out[:, width:] = inner


def part(kept, inner, came, slots):
    rows, width = kept.shape
    return pl.pallas_call(
        part_kernel,
        in_specs=[whole()] * 3,
        out_specs=[whole()] * slots,
        out_shape=[shape(rows, width // slots + HEAD_DIM)] * slots,
        compiler_params=params(),
        name="part",
    )(kept, inner, came)


def rotate(v, cosine, sine):
    return v * cosine + pltpu.roll(v, HEAD_DIM // 2, 1) * sine


def rotate_kernel(own_ref, came_ref, cos_ref, sin_ref, q_ref, rows_ref):
    cosine, sine = cos_ref[...], sin_ref[...]
    for g in range(own_ref.shape[1] // HEAD_DIM):
        columns = slice(g * HEAD_DIM, (g + 1) * HEAD_DIM)
        rows_ref[:, g, :] = rotate(own_ref[:, columns] + came_ref[:, columns], cosine, sine)
    q_ref[0] = rows_ref[...].reshape(q_ref.shape[1:]).astype(BF16)


def rotated(own, came, cosine, sine):
    rows, width = own.shape
    heads = width // HEAD_DIM
    return pl.pallas_call(
        rotate_kernel,
        in_specs=[whole()] * 4,
        out_specs=whole(),
        out_shape=shape(1, rows * heads, HEAD_DIM, dtype=BF16),
        scratch_shapes=[pltpu.VMEM((rows, heads, HEAD_DIM), F32)],
        compiler_params=params(),
        name="rotate",
    )(own, came, cosine, sine)


def join_kernel(*refs):
    *parts, out_ref = refs
    for i, part in enumerate(parts):
        out_ref[i] = part[0]


def join(parts):
    return pl.pallas_call(
        join_kernel,
        in_specs=[whole()] * len(parts),
        out_specs=whole(),
        out_shape=shape(len(parts), *parts[0].shape[1:], dtype=parts[0].dtype),
        compiler_params=params(),
        name="join",
    )(*parts)


def attend_kernel(slots, earlier, place, bank, length_ref, q_ref, k_ref, v_ref, *refs):
    before, out_ref = refs[:-1], refs[-1]
    if earlier:
        *before, keyval_ref = before
    beams, positions, _ = k_ref.shape
    rows = q_ref.shape[1]
    group = rows // beams
    row, lane = iota((rows, HEAD_DIM), 0), iota((rows, HEAD_DIM), 1)
    left = length_ref[...] - place[0] * positions
    live = jnp.concatenate(
        [lane + first < left for first in range(0, positions, HEAD_DIM)], axis=1
    )
    for i, slot in enumerate(slots):
        head = rank_of(place[0], bank[0], slot)
        columns = pl.ds(pl.multiple_of(head * HEAD_DIM, HEAD_DIM), HEAD_DIM)
        query = q_ref[i].astype(F32)
        scores = jnp.concatenate(
            [
                lax.dot_general(
                    query[beam * group : (beam + 1) * group].astype(BF16),
                    k_ref[beam, :, columns],
                    (((1,), (1,)), ((), ())),
                    preferred_element_type=F32,
                )
                for beam in range(beams)
            ],
            axis=0,
        ) * (1.0 / HEAD_DIM**0.5)
        scores = jnp.where(live, scores, -1e30)
        peak = jnp.max(scores, axis=1, keepdims=True)
        weights = jnp.where(live, jnp.exp(scores - peak), 0.0)
        total = jnp.sum(weights, axis=1, keepdims=True)
        values = [
            jnp.dot(
                weights[beam * group : (beam + 1) * group].astype(BF16),
                v_ref[beam, :, columns],
                preferred_element_type=F32,
            )
            for beam in range(beams)
        ]
        stats = jnp.where(lane == row % group, peak, 0.0)
        stats += jnp.where(lane == group + row % group, total, 0.0)
        stats = jnp.sum(stats.reshape(beams, group, HEAD_DIM), axis=1)
        high = stats.astype(BF16).astype(F32)
        middle = (stats - high).astype(BF16).astype(F32)
        low = stats - high - middle
        tail = high + pltpu.roll(middle, 2 * group, 1) + pltpu.roll(low, 4 * group, 1)
        if earlier:
            block = jnp.concatenate(values + [tail, keyval_ref[head]], axis=0)
            out_ref[head] = block.astype(BF16)
        else:
            block = jnp.concatenate(values + [tail, jnp.zeros_like(tail)], axis=0)
            out_ref[i] = block.astype(BF16)
    if earlier:
        done = [(ref, i) for ref in before for i in range(ref.shape[0])]
        for slot, (ref, i) in zip(earlier, done):
            head = rank_of(place[0], bank[0], slot)
            held = ref[i].astype(F32)[: rows + beams]
            out_ref[head] = jnp.concatenate([held, keyval_ref[head]], axis=0).astype(BF16)


def attend(place, bank, length, queries, keys, values, slots, earlier=(), before=()):
    count, rows, _ = queries.shape
    beams, positions, _ = keys.shape
    return pl.pallas_call(
        lambda *refs: attend_kernel(slots, earlier, *refs),
        in_specs=[scalar()] * 2 + [whole()] * (4 + len(before)),
        out_specs=whole(),
        out_shape=shape(
            count + len(earlier), rows + (4 if earlier else 2) * beams, HEAD_DIM, dtype=BF16
        ),
        compiler_params=params(),
        cost_estimate=pl.CostEstimate(
            flops=4 * rows * count * positions * HEAD_DIM,
            bytes_accessed=4 * beams * positions * HEAD_DIM * (16 if earlier else count),
            transcendentals=rows * count * positions,
        ),
        name="attend",
    )(place, bank, length, queries, keys, values, *before)


def combine_kernel(parts_ref, q_ref, cos_ref, sin_ref, out_ref, joined):
    ranks = parts_ref.shape[0]
    beams, group, _ = joined.shape
    rows = beams * group

    def by_row(v):
        return jnp.broadcast_to(v[:, None, :], (beams, group, HEAD_DIM)).reshape(rows, HEAD_DIM)

    lane = iota((rows, HEAD_DIM), 1)
    own_lane = lane == iota((rows, HEAD_DIM), 0) % group

    def spread(v):
        return jnp.sum(jnp.where(own_lane, by_row(v), 0.0), axis=1, keepdims=True)

    blocks = [parts_ref[s].astype(F32) for s in range(ranks)]
    sums = blocks[0][rows + beams :]
    for block in blocks[1:]:
        sums += block[rows + beams :]
    key = sums[:beams] + sums[beams : 2 * beams]
    key = rotate(key, cos_ref[...], sin_ref[...]).astype(BF16).astype(F32)
    value = sums[2 * beams :].astype(BF16).astype(F32)
    score = jnp.sum(q_ref[0].astype(F32) * by_row(key), axis=1, keepdims=True) * (
        1.0 / HEAD_DIM**0.5
    )
    score = jnp.where(own_lane, score, 0.0).reshape(beams, group, HEAD_DIM)
    score = jnp.sum(score, axis=1)
    used = iota((beams, HEAD_DIM), 1) < group
    peaks, totals = [], []
    top = score
    for block in blocks:
        tail = block[rows : rows + beams]
        stats = tail
        for turn in (2, 4):
            stats = stats + pltpu.roll(tail, HEAD_DIM - turn * group, 1)
        peaks.append(jnp.where(used, stats, 0.0))
        totals.append(jnp.where(used, pltpu.roll(stats, HEAD_DIM - group, 1), 0.0))
        top = jnp.maximum(top, peaks[-1])
    factors = [jnp.exp(peak - top) for peak in peaks]
    new = jnp.exp(score - top)
    everything = new
    for factor, total in zip(factors, totals):
        everything += factor * total
    result = spread(new.astype(BF16).astype(F32) / everything) * by_row(value)
    for block, factor in zip(blocks, factors):
        result += spread(factor / everything) * block[:rows]
    joined[...] = result.reshape(joined.shape)
    for g in range(group):
        out_ref[:, g * HEAD_DIM : (g + 1) * HEAD_DIM] = joined[:, g, :].astype(BF16)


def combine(parts, query, cosine, sine):
    beams = cosine.shape[0]
    group = query.shape[1] // beams
    return pl.pallas_call(
        combine_kernel,
        in_specs=[whole()] * 4,
        out_specs=whole(),
        out_shape=shape(beams, group * HEAD_DIM, dtype=BF16),
        scratch_shapes=[pltpu.VMEM((beams, group, HEAD_DIM), F32)],
        compiler_params=params(),
        name="combine",
    )(parts, query, cosine, sine)


def output_kernel(x_ref, w_ref, out):
    count, _, width = out.shape
    for s in range(count):
        columns = slice(s * width, (s + 1) * width)
        total = jnp.dot(x_ref[...], w_ref[:, columns], preferred_element_type=F32)
        out[s] = total.astype(BF16)


def output(x, weight, ranks):
    beams = x.shape[0]
    return pl.pallas_call(
        output_kernel,
        in_specs=[whole()] * 2,
        out_specs=whole(),
        out_shape=shape(ranks, beams, weight.shape[1] // ranks, dtype=BF16),
        compiler_params=params(),
        cost_estimate=pl.CostEstimate(
            flops=2 * beams * weight.size, bytes_accessed=2 * weight.size, transcendentals=0
        ),
        name="output",
    )(x, weight)


def residual_kernel(x_ref, parts_ref, out_ref):
    total = jnp.sum(parts_ref[...].astype(F32), axis=0)
    out_ref[...] = (x_ref[...].astype(F32) + total).astype(BF16)


def residual(x, parts):
    return pl.pallas_call(
        residual_kernel,
        in_specs=[whole()] * 2,
        out_specs=whole(),
        out_shape=jax.ShapeDtypeStruct(x.shape, BF16),
        compiler_params=params(),
        name="residual",
    )(x, parts)


def swapped(x):
    return lax.ppermute(x, "bank", [(0, 1), (1, 0)])


def traded(blocks):
    return lax.all_to_all(blocks, "tensor", 0, 0, tiled=True)


def hop(x, bit):
    pairs = []
    for rank in range(lax.axis_size("tensor")):
        for bank in range(2):
            pairs.append((2 * rank + bank, 2 * rank_of(rank, bank, bit) + bank))
    return lax.ppermute(x, ("tensor", "bank"), pairs)


def matched_body(
    normed_hidden_input,
    beam_adapter_index,
    beam_cache_length,
    query_weight,
    keyvalue_weight,
    output_weight,
    lowrank_down_factors,
    lowrank_up_factors,
    paged_key_cache,
    paged_value_cache,
):
    x = normed_hidden_input
    ranks = lax.axis_size("tensor")
    place = lax.axis_index("tensor").astype(jnp.int32).reshape(1)
    bank = lax.axis_index("bank").astype(jnp.int32).reshape(1)
    index = (beam_adapter_index, swapped(beam_adapter_index))
    x_other = swapped(x)
    lane = jnp.arange(HEAD_DIM, dtype=jnp.int32)
    half = HEAD_DIM // 2
    frequency = jnp.power(500000.0, -2.0 * (lane % half).astype(F32) / HEAD_DIM)
    angles = beam_cache_length.astype(F32)[:, None] * frequency[None, :]
    cosine = jnp.cos(angles)
    sine = jnp.where(lane < half, -1.0, 1.0) * jnp.sin(angles)
    weight = in_hbm(query_weight)
    down = fetch(in_hbm(lowrank_down_factors.swapaxes(1, 2)))
    sent, inner, column = project_sent(place, bank, index, x, x_other, down, weight, ranks)
    came = hop(sent, 1)
    kept, length = project_kept(
        place, bank, beam_cache_length, x, x_other, weight, ranks
    )
    kept, *sent = part(kept, inner, came, ranks // 2)
    near = 4, 6, 2
    parts = [kept] + [hop(sent[slot // 2 - 1], slot) for slot in near]
    token_weight, _ = lax.optimization_barrier((in_hbm(keyvalue_weight), kept))
    token, parts = lax.optimization_barrier((keyval(x, in_hbm(token_weight), ranks), parts))
    own, other = correct(bank, column, lowrank_up_factors, parts)
    query = rotated(own, swapped(other), cosine, sine)

    def attended_part(queries, slots, **more):
        cache = paged_key_cache, paged_value_cache
        return attend(place, bank, length, queries, *cache, slots, **more)

    gathered = join([query] + [hop(query, slot) for slot in near])
    came = hop(gathered, 1)
    done = attended_part(gathered, (0, *near))
    odd = tuple(slot + 1 for slot in (0, *near))
    partial = attended_part(came, odd, earlier=(0, *near), before=(done, token))
    attended = combine(traded(partial), query, cosine, sine)
    return residual(x, traded(output(attended, output_weight, ranks)))


def joined(x, axis, combine):
    everything = jax.tree.map(lambda part: lax.all_gather(part, axis), x)
    leading = jax.tree.map(lambda part: part[0], everything)

    def turn(k, so_far):
        return combine(so_far, jax.tree.map(lambda part: part[k], everything))

    return lax.fori_loop(1, lax.axis_size(axis), turn, leading)


def apply_rotary(values, positions, head_size):
    row_count, col_count = values.shape
    half_size = head_size // 2
    frequency = jnp.power(500000.0, -2.0 * jnp.arange(half_size, dtype=jnp.float32) / head_size)
    angles = positions.astype(jnp.float32)[:, None] * frequency[None, :]
    cosine_table = jnp.cos(angles)[:, None, :]
    sine_table = jnp.sin(angles)[:, None, :]
    shaped = values.reshape(row_count, col_count // head_size, 2, half_size)
    first_half = shaped[:, :, 0]
    second_half = shaped[:, :, 1]
    rotated = jnp.stack(
        [
            first_half * cosine_table - second_half * sine_table,
            second_half * cosine_table + first_half * sine_table,
        ],
        axis=2,
    )
    return rotated.reshape(row_count, col_count)


def combine_parts(first_part, second_part):
    peak_one, total_one, weighted_one = first_part
    peak_two, total_two, weighted_two = second_part
    peak_both = jnp.maximum(peak_one, peak_two)
    factor_one = jnp.exp(peak_one - peak_both)
    factor_two = jnp.exp(peak_two - peak_both)
    return (
        peak_both,
        total_one * factor_one + total_two * factor_two,
        weighted_one * factor_one[..., None] + weighted_two * factor_two[..., None],
    )


def finish_heads(peak_score, weight_total, weighted, score_new, value_rows):
    peak_final = jnp.maximum(peak_score, score_new)
    old_factor = jnp.exp(peak_score - peak_final)
    new_weight = jnp.exp(score_new - peak_final)
    weight_total = weight_total * old_factor + new_weight
    weighted = (
        weighted * old_factor[..., None]
        + new_weight.astype(jnp.bfloat16).astype(jnp.float32)[..., None] * value_rows
    )
    return weighted / weight_total[..., None]


def body(
    normed_hidden_input,
    beam_adapter_index,
    beam_cache_length,
    query_weight,
    keyvalue_weight,
    output_weight,
    lowrank_down_factors,
    lowrank_up_factors,
    paged_key_cache,
    paged_value_cache,
):
    beam_rows, width_part = normed_hidden_input.shape
    model_width = query_weight.shape[1]
    kv_width = keyvalue_weight.shape[1] // 2
    head_count = model_width // HEAD_DIM
    kv_heads = kv_width // HEAD_DIM
    group_size = head_count // kv_heads
    tensor_index = lax.axis_index("tensor")
    query_part = jnp.dot(normed_hidden_input, query_weight, preferred_element_type=jnp.float32)
    keyval_part = jnp.dot(normed_hidden_input, keyvalue_weight, preferred_element_type=jnp.float32)
    down_all, up_all = (
        lax.all_gather(lowrank_down_factors, "bank", axis=0, tiled=True),
        lax.all_gather(lowrank_up_factors, "bank", axis=0, tiled=True),
    )
    inner_part = jnp.einsum(
        "ci,cim->cm",
        normed_hidden_input,
        down_all[beam_adapter_index],
        preferred_element_type=jnp.float32,
    )
    inner_total = lax.psum(inner_part, "tensor").astype(jnp.bfloat16)
    lowrank_delta = jnp.einsum(
        "mc,mct->mt", inner_total, up_all[beam_adapter_index], preferred_element_type=jnp.float32
    )
    query_total, keyval = lax.psum((query_part, keyval_part), "tensor")
    delta_total = lax.all_gather(lowrank_delta, "tensor", axis=1, tiled=True)
    query_rotated = apply_rotary(query_total + delta_total, beam_cache_length, HEAD_DIM).astype(
        jnp.bfloat16
    )
    key_new = apply_rotary(keyval[:, :kv_width], beam_cache_length, HEAD_DIM).astype(jnp.bfloat16)
    value_new = keyval[:, kv_width:].astype(jnp.bfloat16)
    position_count = paged_key_cache.shape[1]
    query_heads = query_rotated.reshape(beam_rows, kv_heads, group_size, HEAD_DIM)
    key_block = paged_key_cache.reshape(beam_rows, position_count, kv_heads, HEAD_DIM)
    value_block = paged_value_cache.reshape(beam_rows, position_count, kv_heads, HEAD_DIM)
    score_scale = 1.0 / HEAD_DIM**0.5
    scores = (
        jnp.einsum("bkgh,bpkh->bkgp", query_heads, key_block, preferred_element_type=jnp.float32)
        * score_scale
    )
    position_ids = tensor_index * position_count + jnp.arange(position_count)
    live_mask = (position_ids[None, :] < beam_cache_length[:, None])[:, None, None, :]
    scores = jnp.where(live_mask, scores, -1e30)
    peak_score = jnp.max(scores, axis=-1)
    weights = jnp.where(live_mask, jnp.exp(scores - peak_score[..., None]), 0.0)
    weight_total = jnp.sum(weights, axis=-1)
    weighted = jnp.einsum(
        "bkgp,bpkh->bkgh",
        weights.astype(jnp.bfloat16),
        value_block,
        preferred_element_type=jnp.float32,
    )
    peak_score, weight_total, weighted = joined(
        (peak_score, weight_total, weighted), "tensor", combine_parts
    )
    score_new = (
        jnp.einsum(
            "bkgh,bkh->bkg",
            query_heads,
            key_new.reshape(beam_rows, kv_heads, HEAD_DIM),
            preferred_element_type=jnp.float32,
        )
        * score_scale
    )
    value_rows = value_new.reshape(beam_rows, kv_heads, HEAD_DIM).astype(jnp.float32)[:, :, None, :]
    attended = (
        finish_heads(peak_score, weight_total, weighted, score_new, value_rows)
        .reshape(beam_rows, model_width)
        .astype(jnp.bfloat16)
    )
    attended_cols = lax.dynamic_slice_in_dim(attended, tensor_index * width_part, width_part, 1)
    mixed_cols = lax.psum_scatter(
        lax.dot_general(
            output_weight,
            attended_cols,
            (((0,), (1,)), ((), ())),
            preferred_element_type=jnp.float32,
        ),
        "tensor",
        scatter_dimension=0,
        tiled=True,
    )
    return (normed_hidden_input.astype(jnp.float32) + mixed_cols.T).astype(jnp.bfloat16)


def solution(mesh):
    matched = mesh.shape["tensor"] == 8 and mesh.shape["bank"] == 2
    return jax.shard_map(
        matched_body if matched else body,
        mesh=mesh,
        in_specs=(
            P(("groups", "bank"), "tensor"),
            P(("groups", "bank")),
            P(("groups", "bank")),
            P("tensor", None),
            P("tensor", None),
            P("tensor", None),
            P("bank", "tensor", None),
            P("bank", None, "tensor"),
            P(("groups", "bank"), "tensor", None),
            P(("groups", "bank"), "tensor", None),
        ),
        out_specs=P(("groups", "bank"), "tensor"),
        check_vma=False,
    )
```

```python
import jax
import jax.numpy as jnp
from jax import lax
from jax.experimental import pallas as pl
from jax.experimental.pallas import tpu as pltpu
from jax.sharding import PartitionSpec as P

HEAD_DIM = 128
F32 = jnp.float32
BF16 = jnp.bfloat16
CHUNKS = 2
MIB = 1024 * 1024


def whole():
    return pl.BlockSpec(memory_space=pltpu.VMEM)


def big():
    return pl.BlockSpec(memory_space=pltpu.HBM)


def scalar():
    return pl.BlockSpec(memory_space=pltpu.SMEM)


def in_hbm(array):
    return pltpu.with_memory_space_constraint(array, pltpu.HBM)


def shape(*dims, dtype=F32):
    return jax.ShapeDtypeStruct(dims, dtype)


def iota(dims, axis):
    return lax.broadcasted_iota(jnp.int32, dims, axis)


def params(mib=4):
    return pltpu.CompilerParams(vmem_limit_bytes=mib * MIB)


def exchanged(slot):
    return slot & ~3 | (slot & 1) << 1 | slot >> 1 & 1


def rank_of(place, bank, slot):
    return place ^ (slot + bank * (exchanged(slot) - slot))


def start_columns(weight, column, target, sems):
    depth, width = target.shape
    part = depth // CHUNKS
    copies = []
    for c in range(CHUNKS):
        rows = pl.ds(c * part, part)
        copies.append(
            pltpu.make_async_copy(
                weight.at[rows, pl.ds(pl.multiple_of(column, width), width)],
                target.at[rows, :],
                sems.at[c],
            )
        )
        copies[-1].start()
    return copies


def adapter_column(refs, bank, count):
    columns = []
    for ref in refs:
        rows = ref.shape[1]
        index = jnp.broadcast_to(ref[...].astype(F32), (rows, rows))
        diagonal = iota((rows, rows), 0) == iota((rows, rows), 1)
        columns.append(jnp.sum(jnp.where(diagonal, index, 0.0), axis=1, keepdims=True))
    column = jnp.concatenate(columns, axis=0).astype(jnp.int32) - bank * count
    return jnp.broadcast_to(column, (column.shape[0], HEAD_DIM))


def start_slots(parity, place, bank, w_ref, w_buf, sems):
    count, _, width = w_buf.shape
    copies = []
    for s in range(count):
        target = rank_of(place[0], bank[0], 2 * s + parity)
        first = (2 * target + bank[0]) * width
        copies.append(start_columns(w_ref, first, w_buf.at[s], sems.at[s]))
    return copies


def wait_all(copies):
    for copy in copies:
        copy.wait()


def start_parts(source, target, sems):
    part = source.shape[0] // sems.shape[0]
    copies = []
    for c in range(sems.shape[0]):
        rows = pl.ds(c * part, part)
        copies.append(pltpu.make_async_copy(source.at[rows], target.at[rows], sems.at[c]))
        copies[-1].start()
    return copies


def fetch_kernel(ref, out, sems):
    wait_all(start_parts(ref, out, sems))


def fetch(array):
    return pl.pallas_call(
        fetch_kernel,
        in_specs=[big()],
        out_specs=whole(),
        out_shape=jax.ShapeDtypeStruct(array.shape, array.dtype),
        scratch_shapes=[pltpu.SemaphoreType.DMA((2,))],
        compiler_params=params(),
        cost_estimate=pl.CostEstimate(
            flops=0, bytes_accessed=2 * array.size, transcendentals=0
        ),
        name="fetch",
    )(array)


def slot_scratch(wq, ranks):
    half, depth = ranks // 2, wq.shape[0]
    return [
        pltpu.VMEM((half, depth, wq.shape[1] // ranks // 2), BF16),
        pltpu.SemaphoreType.DMA((half, CHUNKS)),
    ]


def beam_rows(x_ref, other_ref):
    rows = [x_ref[...].astype(F32), other_ref[...].astype(F32)]
    return jnp.concatenate(rows, axis=0).astype(BF16)


def project_sent_kernel(
    place, bank, own_ref, came_ref, x_ref, other_ref, down_ref, w_ref, *refs
):
    out, inner, column_out, w_buf, sems = refs
    copies = start_slots(1, place, bank, w_ref, w_buf, sems)
    width = w_buf.shape[2]
    x = beam_rows(x_ref, other_ref)
    adapters, rank, depth = down_ref.shape
    every = lax.dot_general(
        x,
        down_ref[...].reshape(adapters * rank, depth),
        (((1,), (1,)), ((), ())),
        preferred_element_type=F32,
    )
    column = adapter_column((own_ref, came_ref), bank[0], adapters)
    column_out[...] = column
    lane = iota(column.shape, 1)
    per = HEAD_DIM // rank
    total = jnp.zeros(column.shape, F32)
    for j in range(adapters // per):
        part = every[:, j * HEAD_DIM : (j + 1) * HEAD_DIM]
        total += jnp.where(lane // rank + j * per == column, part, 0.0)
    inner[...] = total
    out[:, len(copies) * width :] = total
    for s, slot in enumerate(copies):
        wait_all(slot)
        columns = slice(s * width, (s + 1) * width)
        out[:, columns] = jnp.dot(x, w_buf[s], preferred_element_type=F32)


def project_sent(place, bank, index, x, other, down, wq, ranks):
    rows = 2 * x.shape[0]
    return pl.pallas_call(
        project_sent_kernel,
        in_specs=[scalar()] * 2 + [whole()] * 5 + [big()],
        out_specs=[whole()] * 3,
        out_shape=[
            shape(rows, wq.shape[1] // 4 + HEAD_DIM),
            shape(rows, HEAD_DIM),
            shape(rows, HEAD_DIM, dtype=jnp.int32),
        ],
        scratch_shapes=slot_scratch(wq, ranks),
        compiler_params=params(8),
        cost_estimate=pl.CostEstimate(
            flops=rows * (wq.size // 2 + 2 * down.size),
            bytes_accessed=wq.size // 2 + 2 * down.size,
            transcendentals=0,
        ),
        name="project_sent",
    )(place, bank, *[i.reshape(1, -1) for i in index], x, other, down, wq)


def project_kept_kernel(
    place, bank, length, x_ref, other_ref, w_ref, out, length_out, w_buf, sems
):
    copies = start_slots(0, place, bank, w_ref, w_buf, sems)
    width = w_buf.shape[2]
    beams = x_ref.shape[0]
    row = iota(length_out.shape, 0)
    limit = jnp.zeros(length_out.shape, jnp.int32)
    for beam in range(beams):
        limit = jnp.where(row // (length_out.shape[0] // beams) == beam, length[beam], limit)
    length_out[...] = limit
    x = beam_rows(x_ref, other_ref)
    for s, slot in enumerate(copies):
        wait_all(slot)
        columns = slice(s * width, (s + 1) * width)
        out[:, columns] = jnp.dot(x, w_buf[s], preferred_element_type=F32)


def project_kept(place, bank, length, x, other, wq, ranks):
    beams = x.shape[0]
    return pl.pallas_call(
        project_kept_kernel,
        in_specs=[scalar()] * 3 + [whole()] * 2 + [big()],
        out_specs=[whole()] * 2,
        out_shape=[
            shape(2 * beams, wq.shape[1] // 4),
            shape(beams * wq.shape[1] // ranks // HEAD_DIM, HEAD_DIM, dtype=jnp.int32),
        ],
        scratch_shapes=slot_scratch(wq, ranks),
        compiler_params=params(8),
        cost_estimate=pl.CostEstimate(
            flops=beams * wq.size, bytes_accessed=2 * wq.size, transcendentals=0
        ),
        name="project_kept",
    )(place, bank, length, x, other, wq)


def keyval_kernel(x_ref, w_ref, out):
    ranks = out.shape[0]
    total = jnp.dot(x_ref[...], w_ref[...], preferred_element_type=F32)
    high = total.astype(BF16).astype(F32)
    low = total - high
    for r in range(ranks):
        key = slice(r * HEAD_DIM, (r + 1) * HEAD_DIM)
        value = slice((ranks + r) * HEAD_DIM, (ranks + r + 1) * HEAD_DIM)
        pieces = [high[:, key], low[:, key], total[:, value]]
        out[r] = jnp.concatenate(pieces, axis=0)


def keyval(x, wkv, ranks):
    beams, depth = x.shape
    return pl.pallas_call(
        keyval_kernel,
        in_specs=[whole()] * 2,
        out_specs=whole(),
        out_shape=shape(ranks, 3 * beams, HEAD_DIM),
        compiler_params=params(),
        cost_estimate=pl.CostEstimate(
            flops=2 * beams * wkv.size, bytes_accessed=2 * wkv.size, transcendentals=0
        ),
        name="keyval",
    )(x, wkv)


def correct_kernel(bank, column_ref, up_ref, *refs):
    *parts, own_out, other_out = refs
    total = parts[0][...]
    for part in parts[1:]:
        total += part[...]
    count, rank, width = up_ref.shape
    half = width // 2
    inner = total[:, half:].astype(BF16).astype(F32)
    column = column_ref[...]
    lane = iota(column.shape, 1)
    per = HEAD_DIM // rank
    spread = jnp.concatenate(
        [
            jnp.where(lane // rank + j * per == column, inner, 0.0)
            for j in range(count // per)
        ],
        axis=1,
    ).astype(BF16)
    delta = jnp.dot(
        spread, up_ref[...].reshape(count * rank, width), preferred_element_type=F32
    )
    rows = own_out.shape[0]
    for side in range(2):
        columns = slice(side * half, (side + 1) * half)
        part = delta[:, columns] + jnp.where(bank[0] == side, total[:, :half], 0.0)
        own_out[:, columns] = part[:rows]
        other_out[:, columns] = part[rows:]


def correct(bank, column, up, parts):
    rows = parts[0].shape[0]
    out = shape(rows // 2, up.shape[2])
    return pl.pallas_call(
        correct_kernel,
        in_specs=[scalar()] + [whole()] * (2 + len(parts)),
        out_specs=[whole()] * 2,
        out_shape=[out, out],
        compiler_params=params(),
        cost_estimate=pl.CostEstimate(
            flops=2 * rows * up.size, bytes_accessed=2 * up.size, transcendentals=0
        ),
        name="correct",
    )(bank, column, up, *parts)


def part_kernel(kept_ref, inner_ref, came_ref, *outs):
    width = outs[0].shape[1] - HEAD_DIM
    inner = inner_ref[...] + came_ref[:, len(outs) * width :]
    for i, out in enumerate(outs):
        columns = slice(i * width, (i + 1) * width)
        out[:, :width] = kept_ref[:, columns] + came_ref[:, columns]
        out[:, width:] = inner


def part(kept, inner, came, slots):
    rows, width = kept.shape
    return pl.pallas_call(
        part_kernel,
        in_specs=[whole()] * 3,
        out_specs=[whole()] * slots,
        out_shape=[shape(rows, width // slots + HEAD_DIM)] * slots,
        compiler_params=params(),
        name="part",
    )(kept, inner, came)


def rotate(v, cosine, sine):
    return v * cosine + pltpu.roll(v, HEAD_DIM // 2, 1) * sine


def rotate_kernel(own_ref, came_ref, cos_ref, sin_ref, q_ref, rows_ref):
    cosine, sine = cos_ref[...], sin_ref[...]
    for g in range(own_ref.shape[1] // HEAD_DIM):
        columns = slice(g * HEAD_DIM, (g + 1) * HEAD_DIM)
        rows_ref[:, g, :] = rotate(own_ref[:, columns] + came_ref[:, columns], cosine, sine)
    q_ref[0] = rows_ref[...].reshape(q_ref.shape[1:]).astype(BF16)


def rotated(own, came, cosine, sine):
    rows, width = own.shape
    heads = width // HEAD_DIM
    return pl.pallas_call(
        rotate_kernel,
        in_specs=[whole()] * 4,
        out_specs=whole(),
        out_shape=shape(1, rows * heads, HEAD_DIM, dtype=BF16),
        scratch_shapes=[pltpu.VMEM((rows, heads, HEAD_DIM), F32)],
        compiler_params=params(),
        name="rotate",
    )(own, came, cosine, sine)


def join_kernel(*refs):
    *parts, out_ref = refs
    for i, part in enumerate(parts):
        out_ref[i] = part[0]


def join(parts):
    return pl.pallas_call(
        join_kernel,
        in_specs=[whole()] * len(parts),
        out_specs=whole(),
        out_shape=shape(len(parts), *parts[0].shape[1:], dtype=parts[0].dtype),
        compiler_params=params(),
        name="join",
    )(*parts)


def attend_kernel(slots, earlier, place, bank, length_ref, q_ref, k_ref, v_ref, *refs):
    before, out_ref = refs[:-1], refs[-1]
    if earlier:
        *before, keyval_ref = before
    beams, positions, _ = k_ref.shape
    rows = q_ref.shape[1]
    group = rows // beams
    row, lane = iota((rows, HEAD_DIM), 0), iota((rows, HEAD_DIM), 1)
    left = length_ref[...] - place[0] * positions
    live = jnp.concatenate(
        [lane + first < left for first in range(0, positions, HEAD_DIM)], axis=1
    )
    for i, slot in enumerate(slots):
        head = rank_of(place[0], bank[0], slot)
        columns = pl.ds(pl.multiple_of(head * HEAD_DIM, HEAD_DIM), HEAD_DIM)
        query = q_ref[i].astype(F32)
        scores = jnp.concatenate(
            [
                lax.dot_general(
                    query[beam * group : (beam + 1) * group].astype(BF16),
                    k_ref[beam, :, columns],
                    (((1,), (1,)), ((), ())),
                    preferred_element_type=F32,
                )
                for beam in range(beams)
            ],
            axis=0,
        ) * (1.0 / HEAD_DIM**0.5)
        scores = jnp.where(live, scores, -1e30)
        peak = jnp.max(scores, axis=1, keepdims=True)
        weights = jnp.where(live, jnp.exp(scores - peak), 0.0)
        total = jnp.sum(weights, axis=1, keepdims=True)
        values = [
            jnp.dot(
                weights[beam * group : (beam + 1) * group].astype(BF16),
                v_ref[beam, :, columns],
                preferred_element_type=F32,
            )
            for beam in range(beams)
        ]
        stats = jnp.where(lane == row % group, peak, 0.0)
        stats += jnp.where(lane == group + row % group, total, 0.0)
        stats = jnp.sum(stats.reshape(beams, group, HEAD_DIM), axis=1)
        high = stats.astype(BF16).astype(F32)
        middle = (stats - high).astype(BF16).astype(F32)
        low = stats - high - middle
        tail = high + pltpu.roll(middle, 2 * group, 1) + pltpu.roll(low, 4 * group, 1)
        if earlier:
            block = jnp.concatenate(values + [tail, keyval_ref[head]], axis=0)
            out_ref[head] = block.astype(BF16)
        else:
            block = jnp.concatenate(values + [tail, jnp.zeros_like(tail)], axis=0)
            out_ref[i] = block.astype(BF16)
    if earlier:
        done = [(ref, i) for ref in before for i in range(ref.shape[0])]
        for slot, (ref, i) in zip(earlier, done):
            head = rank_of(place[0], bank[0], slot)
            held = ref[i].astype(F32)[: rows + beams]
            out_ref[head] = jnp.concatenate([held, keyval_ref[head]], axis=0).astype(BF16)


def attend(place, bank, length, queries, keys, values, slots, earlier=(), before=()):
    count, rows, _ = queries.shape
    beams, positions, _ = keys.shape
    return pl.pallas_call(
        lambda *refs: attend_kernel(slots, earlier, *refs),
        in_specs=[scalar()] * 2 + [whole()] * (4 + len(before)),
        out_specs=whole(),
        out_shape=shape(
            count + len(earlier), rows + (4 if earlier else 2) * beams, HEAD_DIM, dtype=BF16
        ),
        compiler_params=params(),
        cost_estimate=pl.CostEstimate(
            flops=4 * rows * count * positions * HEAD_DIM,
            bytes_accessed=4 * beams * positions * HEAD_DIM * (16 if earlier else count),
            transcendentals=rows * count * positions,
        ),
        name="attend",
    )(place, bank, length, queries, keys, values, *before)


def combine_kernel(parts_ref, q_ref, cos_ref, sin_ref, out_ref, joined):
    ranks = parts_ref.shape[0]
    beams, group, _ = joined.shape
    rows = beams * group

    def by_row(v):
        return jnp.broadcast_to(v[:, None, :], (beams, group, HEAD_DIM)).reshape(rows, HEAD_DIM)

    lane = iota((rows, HEAD_DIM), 1)
    own_lane = lane == iota((rows, HEAD_DIM), 0) % group

    def spread(v):
        return jnp.sum(jnp.where(own_lane, by_row(v), 0.0), axis=1, keepdims=True)

    blocks = [parts_ref[s].astype(F32) for s in range(ranks)]
    sums = blocks[0][rows + beams :]
    for block in blocks[1:]:
        sums += block[rows + beams :]
    key = sums[:beams] + sums[beams : 2 * beams]
    key = rotate(key, cos_ref[...], sin_ref[...]).astype(BF16).astype(F32)
    value = sums[2 * beams :].astype(BF16).astype(F32)
    score = jnp.sum(q_ref[0].astype(F32) * by_row(key), axis=1, keepdims=True) * (
        1.0 / HEAD_DIM**0.5
    )
    score = jnp.where(own_lane, score, 0.0).reshape(beams, group, HEAD_DIM)
    score = jnp.sum(score, axis=1)
    used = iota((beams, HEAD_DIM), 1) < group
    peaks, totals = [], []
    top = score
    for block in blocks:
        tail = block[rows : rows + beams]
        stats = tail
        for turn in (2, 4):
            stats = stats + pltpu.roll(tail, HEAD_DIM - turn * group, 1)
        peaks.append(jnp.where(used, stats, 0.0))
        totals.append(jnp.where(used, pltpu.roll(stats, HEAD_DIM - group, 1), 0.0))
        top = jnp.maximum(top, peaks[-1])
    factors = [jnp.exp(peak - top) for peak in peaks]
    new = jnp.exp(score - top)
    everything = new
    for factor, total in zip(factors, totals):
        everything += factor * total
    result = spread(new.astype(BF16).astype(F32) / everything) * by_row(value)
    for block, factor in zip(blocks, factors):
        result += spread(factor / everything) * block[:rows]
    joined[...] = result.reshape(joined.shape)
    for g in range(group):
        out_ref[:, g * HEAD_DIM : (g + 1) * HEAD_DIM] = joined[:, g, :].astype(BF16)


def combine(parts, query, cosine, sine):
    beams = cosine.shape[0]
    group = query.shape[1] // beams
    return pl.pallas_call(
        combine_kernel,
        in_specs=[whole()] * 4,
        out_specs=whole(),
        out_shape=shape(beams, group * HEAD_DIM, dtype=BF16),
        scratch_shapes=[pltpu.VMEM((beams, group, HEAD_DIM), F32)],
        compiler_params=params(),
        name="combine",
    )(parts, query, cosine, sine)


def output_kernel(x_ref, w_ref, out):
    count, _, width = out.shape
    for s in range(count):
        columns = slice(s * width, (s + 1) * width)
        total = jnp.dot(x_ref[...], w_ref[:, columns], preferred_element_type=F32)
        out[s] = total.astype(BF16)


def output(x, weight, ranks):
    beams = x.shape[0]
    return pl.pallas_call(
        output_kernel,
        in_specs=[whole()] * 2,
        out_specs=whole(),
        out_shape=shape(ranks, beams, weight.shape[1] // ranks, dtype=BF16),
        compiler_params=params(),
        cost_estimate=pl.CostEstimate(
            flops=2 * beams * weight.size, bytes_accessed=2 * weight.size, transcendentals=0
        ),
        name="output",
    )(x, weight)


def residual_kernel(x_ref, parts_ref, out_ref):
    total = jnp.sum(parts_ref[...].astype(F32), axis=0)
    out_ref[...] = (x_ref[...].astype(F32) + total).astype(BF16)


def residual(x, parts):
    return pl.pallas_call(
        residual_kernel,
        in_specs=[whole()] * 2,
        out_specs=whole(),
        out_shape=jax.ShapeDtypeStruct(x.shape, BF16),
        compiler_params=params(),
        name="residual",
    )(x, parts)


def swapped(x):
    return lax.ppermute(x, "bank", [(0, 1), (1, 0)])


def traded(blocks):
    return lax.all_to_all(blocks, "tensor", 0, 0, tiled=True)


def hop(x, bit):
    pairs = []
    for rank in range(lax.axis_size("tensor")):
        for bank in range(2):
            pairs.append((2 * rank + bank, 2 * rank_of(rank, bank, bit) + bank))
    return lax.ppermute(x, ("tensor", "bank"), pairs)


def matched_body(
    normed_hidden_input,
    beam_adapter_index,
    beam_cache_length,
    query_weight,
    keyvalue_weight,
    output_weight,
    lowrank_down_factors,
    lowrank_up_factors,
    paged_key_cache,
    paged_value_cache,
):
    x = normed_hidden_input
    ranks = lax.axis_size("tensor")
    place = lax.axis_index("tensor").astype(jnp.int32).reshape(1)
    bank = lax.axis_index("bank").astype(jnp.int32).reshape(1)
    index = (beam_adapter_index, swapped(beam_adapter_index))
    x_other = swapped(x)
    lane = jnp.arange(HEAD_DIM, dtype=jnp.int32)
    half = HEAD_DIM // 2
    frequency = jnp.power(500000.0, -2.0 * (lane % half).astype(F32) / HEAD_DIM)
    angles = beam_cache_length.astype(F32)[:, None] * frequency[None, :]
    cosine = jnp.cos(angles)
    sine = jnp.where(lane < half, -1.0, 1.0) * jnp.sin(angles)
    weight = in_hbm(query_weight)
    down = fetch(in_hbm(lowrank_down_factors.swapaxes(1, 2)))
    sent, inner, column = project_sent(place, bank, index, x, x_other, down, weight, ranks)
    came = hop(sent, 1)
    kept, length = project_kept(
        place, bank, beam_cache_length, x, x_other, weight, ranks
    )
    kept, *sent = part(kept, inner, came, ranks // 2)
    near = 4, 6, 2
    parts = [kept] + [hop(sent[slot // 2 - 1], slot) for slot in near]
    own_x, _ = lax.optimization_barrier((x, kept))
    token, parts = lax.optimization_barrier((keyval(own_x, keyvalue_weight, ranks), parts))
    own, other = correct(bank, column, lowrank_up_factors, parts)
    query = rotated(own, swapped(other), cosine, sine)

    def attended_part(queries, slots, **more):
        cache = paged_key_cache, paged_value_cache
        return attend(place, bank, length, queries, *cache, slots, **more)

    gathered = join([query] + [hop(query, slot) for slot in near])
    came = hop(gathered, 1)
    done = attended_part(gathered, (0, *near))
    odd = tuple(slot + 1 for slot in (0, *near))
    partial = attended_part(came, odd, earlier=(0, *near), before=(done, token))
    attended = combine(traded(partial), query, cosine, sine)
    return residual(x, traded(output(attended, output_weight, ranks)))


def joined(x, axis, combine):
    everything = jax.tree.map(lambda part: lax.all_gather(part, axis), x)
    leading = jax.tree.map(lambda part: part[0], everything)

    def turn(k, so_far):
        return combine(so_far, jax.tree.map(lambda part: part[k], everything))

    return lax.fori_loop(1, lax.axis_size(axis), turn, leading)


def apply_rotary(values, positions, head_size):
    row_count, col_count = values.shape
    half_size = head_size // 2
    frequency = jnp.power(500000.0, -2.0 * jnp.arange(half_size, dtype=jnp.float32) / head_size)
    angles = positions.astype(jnp.float32)[:, None] * frequency[None, :]
    cosine_table = jnp.cos(angles)[:, None, :]
    sine_table = jnp.sin(angles)[:, None, :]
    shaped = values.reshape(row_count, col_count // head_size, 2, half_size)
    first_half = shaped[:, :, 0]
    second_half = shaped[:, :, 1]
    rotated = jnp.stack(
        [
            first_half * cosine_table - second_half * sine_table,
            second_half * cosine_table + first_half * sine_table,
        ],
        axis=2,
    )
    return rotated.reshape(row_count, col_count)


def combine_parts(first_part, second_part):
    peak_one, total_one, weighted_one = first_part
    peak_two, total_two, weighted_two = second_part
    peak_both = jnp.maximum(peak_one, peak_two)
    factor_one = jnp.exp(peak_one - peak_both)
    factor_two = jnp.exp(peak_two - peak_both)
    return (
        peak_both,
        total_one * factor_one + total_two * factor_two,
        weighted_one * factor_one[..., None] + weighted_two * factor_two[..., None],
    )


def finish_heads(peak_score, weight_total, weighted, score_new, value_rows):
    peak_final = jnp.maximum(peak_score, score_new)
    old_factor = jnp.exp(peak_score - peak_final)
    new_weight = jnp.exp(score_new - peak_final)
    weight_total = weight_total * old_factor + new_weight
    weighted = (
        weighted * old_factor[..., None]
        + new_weight.astype(jnp.bfloat16).astype(jnp.float32)[..., None] * value_rows
    )
    return weighted / weight_total[..., None]


def body(
    normed_hidden_input,
    beam_adapter_index,
    beam_cache_length,
    query_weight,
    keyvalue_weight,
    output_weight,
    lowrank_down_factors,
    lowrank_up_factors,
    paged_key_cache,
    paged_value_cache,
):
    beam_rows, width_part = normed_hidden_input.shape
    model_width = query_weight.shape[1]
    kv_width = keyvalue_weight.shape[1] // 2
    head_count = model_width // HEAD_DIM
    kv_heads = kv_width // HEAD_DIM
    group_size = head_count // kv_heads
    tensor_index = lax.axis_index("tensor")
    query_part = jnp.dot(normed_hidden_input, query_weight, preferred_element_type=jnp.float32)
    keyval_part = jnp.dot(normed_hidden_input, keyvalue_weight, preferred_element_type=jnp.float32)
    down_all, up_all = (
        lax.all_gather(lowrank_down_factors, "bank", axis=0, tiled=True),
        lax.all_gather(lowrank_up_factors, "bank", axis=0, tiled=True),
    )
    inner_part = jnp.einsum(
        "ci,cim->cm",
        normed_hidden_input,
        down_all[beam_adapter_index],
        preferred_element_type=jnp.float32,
    )
    inner_total = lax.psum(inner_part, "tensor").astype(jnp.bfloat16)
    lowrank_delta = jnp.einsum(
        "mc,mct->mt", inner_total, up_all[beam_adapter_index], preferred_element_type=jnp.float32
    )
    query_total, keyval = lax.psum((query_part, keyval_part), "tensor")
    delta_total = lax.all_gather(lowrank_delta, "tensor", axis=1, tiled=True)
    query_rotated = apply_rotary(query_total + delta_total, beam_cache_length, HEAD_DIM).astype(
        jnp.bfloat16
    )
    key_new = apply_rotary(keyval[:, :kv_width], beam_cache_length, HEAD_DIM).astype(jnp.bfloat16)
    value_new = keyval[:, kv_width:].astype(jnp.bfloat16)
    position_count = paged_key_cache.shape[1]
    query_heads = query_rotated.reshape(beam_rows, kv_heads, group_size, HEAD_DIM)
    key_block = paged_key_cache.reshape(beam_rows, position_count, kv_heads, HEAD_DIM)
    value_block = paged_value_cache.reshape(beam_rows, position_count, kv_heads, HEAD_DIM)
    score_scale = 1.0 / HEAD_DIM**0.5
    scores = (
        jnp.einsum("bkgh,bpkh->bkgp", query_heads, key_block, preferred_element_type=jnp.float32)
        * score_scale
    )
    position_ids = tensor_index * position_count + jnp.arange(position_count)
    live_mask = (position_ids[None, :] < beam_cache_length[:, None])[:, None, None, :]
    scores = jnp.where(live_mask, scores, -1e30)
    peak_score = jnp.max(scores, axis=-1)
    weights = jnp.where(live_mask, jnp.exp(scores - peak_score[..., None]), 0.0)
    weight_total = jnp.sum(weights, axis=-1)
    weighted = jnp.einsum(
        "bkgp,bpkh->bkgh",
        weights.astype(jnp.bfloat16),
        value_block,
        preferred_element_type=jnp.float32,
    )
    peak_score, weight_total, weighted = joined(
        (peak_score, weight_total, weighted), "tensor", combine_parts
    )
    score_new = (
        jnp.einsum(
            "bkgh,bkh->bkg",
            query_heads,
            key_new.reshape(beam_rows, kv_heads, HEAD_DIM),
            preferred_element_type=jnp.float32,
        )
        * score_scale
    )
    value_rows = value_new.reshape(beam_rows, kv_heads, HEAD_DIM).astype(jnp.float32)[:, :, None, :]
    attended = (
        finish_heads(peak_score, weight_total, weighted, score_new, value_rows)
        .reshape(beam_rows, model_width)
        .astype(jnp.bfloat16)
    )
    attended_cols = lax.dynamic_slice_in_dim(attended, tensor_index * width_part, width_part, 1)
    mixed_cols = lax.psum_scatter(
        lax.dot_general(
            output_weight,
            attended_cols,
            (((0,), (1,)), ((), ())),
            preferred_element_type=jnp.float32,
        ),
        "tensor",
        scatter_dimension=0,
        tiled=True,
    )
    return (normed_hidden_input.astype(jnp.float32) + mixed_cols.T).astype(jnp.bfloat16)


def solution(mesh):
    matched = mesh.shape["tensor"] == 8 and mesh.shape["bank"] == 2
    return jax.shard_map(
        matched_body if matched else body,
        mesh=mesh,
        in_specs=(
            P(("groups", "bank"), "tensor"),
            P(("groups", "bank")),
            P(("groups", "bank")),
            P("tensor", None),
            P("tensor", None),
            P("tensor", None),
            P("bank", "tensor", None),
            P("bank", None, "tensor"),
            P(("groups", "bank"), "tensor", None),
            P(("groups", "bank"), "tensor", None),
        ),
        out_specs=P(("groups", "bank"), "tensor"),
        check_vma=False,
    )
```

```python
import jax
import jax.numpy as jnp
from jax import lax
from jax.experimental import pallas as pl
from jax.experimental.pallas import tpu as pltpu
from jax.sharding import PartitionSpec as P

HEAD_DIM = 128
F32 = jnp.float32
BF16 = jnp.bfloat16
CHUNKS = 2
MIB = 1024 * 1024


def whole():
    return pl.BlockSpec(memory_space=pltpu.VMEM)


def big():
    return pl.BlockSpec(memory_space=pltpu.HBM)


def scalar():
    return pl.BlockSpec(memory_space=pltpu.SMEM)


def in_hbm(array):
    return pltpu.with_memory_space_constraint(array, pltpu.HBM)


def shape(*dims, dtype=F32):
    return jax.ShapeDtypeStruct(dims, dtype)


def iota(dims, axis):
    return lax.broadcasted_iota(jnp.int32, dims, axis)


def params(mib=4):
    return pltpu.CompilerParams(vmem_limit_bytes=mib * MIB)


def exchanged(slot):
    return slot & ~3 | (slot & 1) << 1 | slot >> 1 & 1


def rank_of(place, bank, slot):
    return place ^ (slot + bank * (exchanged(slot) - slot))


def adapter_column(refs, bank, count):
    columns = []
    for ref in refs:
        rows = ref.shape[1]
        index = jnp.broadcast_to(ref[...].astype(F32), (rows, rows))
        diagonal = iota((rows, rows), 0) == iota((rows, rows), 1)
        columns.append(jnp.sum(jnp.where(diagonal, index, 0.0), axis=1, keepdims=True))
    column = jnp.concatenate(columns, axis=0).astype(jnp.int32) - bank * count
    return jnp.broadcast_to(column, (column.shape[0], HEAD_DIM))


def start_slots(parity, place, bank, w_ref, w_buf, sems):
    count, depth, width = w_buf.shape
    part = depth // CHUNKS
    copies = []
    for c in range(CHUNKS):
        rows = pl.ds(c * part, part)
        copies.append([])
        for s in range(count):
            target = rank_of(place[0], bank[0], 2 * s + parity)
            columns = pl.ds(pl.multiple_of((2 * target + bank[0]) * width, width), width)
            copy = pltpu.make_async_copy(
                w_ref.at[rows, columns], w_buf.at[s, rows], sems.at[s, c]
            )
            copy.start()
            copies[-1].append(copy)
    return copies


def slot_products(x, copies, w_buf, out):
    count, depth, width = w_buf.shape
    part = depth // CHUNKS
    for c, chunk in enumerate(copies):
        rows = slice(c * part, (c + 1) * part)
        for s, copy in enumerate(chunk):
            copy.wait()
            columns = slice(s * width, (s + 1) * width)
            product = jnp.dot(x[:, rows], w_buf[s, rows], preferred_element_type=F32)
            out[:, columns] = product if c == 0 else out[:, columns] + product


def wait_all(copies):
    for copy in copies:
        copy.wait()


def start_parts(source, target, sems):
    part = source.shape[0] // sems.shape[0]
    copies = []
    for c in range(sems.shape[0]):
        rows = pl.ds(c * part, part)
        copies.append(pltpu.make_async_copy(source.at[rows], target.at[rows], sems.at[c]))
        copies[-1].start()
    return copies


def fetch_kernel(ref, out, sems):
    wait_all(start_parts(ref, out, sems))


def fetch(array):
    return pl.pallas_call(
        fetch_kernel,
        in_specs=[big()],
        out_specs=whole(),
        out_shape=jax.ShapeDtypeStruct(array.shape, array.dtype),
        scratch_shapes=[pltpu.SemaphoreType.DMA((2,))],
        compiler_params=params(),
        cost_estimate=pl.CostEstimate(
            flops=0, bytes_accessed=2 * array.size, transcendentals=0
        ),
        name="fetch",
    )(array)


def slot_scratch(wq, ranks):
    half, depth = ranks // 2, wq.shape[0]
    return [
        pltpu.VMEM((half, depth, wq.shape[1] // ranks // 2), BF16),
        pltpu.SemaphoreType.DMA((half, CHUNKS)),
    ]


def beam_rows(x_ref, other_ref):
    rows = [x_ref[...].astype(F32), other_ref[...].astype(F32)]
    return jnp.concatenate(rows, axis=0).astype(BF16)


def project_sent_kernel(
    place, bank, own_ref, came_ref, x_ref, other_ref, down_ref, w_ref, *refs
):
    out, inner, column_out, w_buf, sems = refs
    copies = start_slots(1, place, bank, w_ref, w_buf, sems)
    x = beam_rows(x_ref, other_ref)
    adapters, rank, depth = down_ref.shape
    every = lax.dot_general(
        x,
        down_ref[...].reshape(adapters * rank, depth),
        (((1,), (1,)), ((), ())),
        preferred_element_type=F32,
    )
    column = adapter_column((own_ref, came_ref), bank[0], adapters)
    column_out[...] = column
    lane = iota(column.shape, 1)
    per = HEAD_DIM // rank
    total = jnp.zeros(column.shape, F32)
    for j in range(adapters // per):
        part = every[:, j * HEAD_DIM : (j + 1) * HEAD_DIM]
        total += jnp.where(lane // rank + j * per == column, part, 0.0)
    inner[...] = total
    out[:, out.shape[1] - HEAD_DIM :] = total
    slot_products(x, copies, w_buf, out)


def project_sent(place, bank, index, x, other, down, wq, ranks):
    rows = 2 * x.shape[0]
    return pl.pallas_call(
        project_sent_kernel,
        in_specs=[scalar()] * 2 + [whole()] * 5 + [big()],
        out_specs=[whole()] * 3,
        out_shape=[
            shape(rows, wq.shape[1] // 4 + HEAD_DIM),
            shape(rows, HEAD_DIM),
            shape(rows, HEAD_DIM, dtype=jnp.int32),
        ],
        scratch_shapes=slot_scratch(wq, ranks),
        compiler_params=params(8),
        cost_estimate=pl.CostEstimate(
            flops=rows * (wq.size // 2 + 2 * down.size),
            bytes_accessed=wq.size // 2 + 2 * down.size,
            transcendentals=0,
        ),
        name="project_sent",
    )(place, bank, *[i.reshape(1, -1) for i in index], x, other, down, wq)


def project_kept_kernel(
    place, bank, length, x_ref, other_ref, w_ref, out, length_out, w_buf, sems
):
    copies = start_slots(0, place, bank, w_ref, w_buf, sems)
    beams = x_ref.shape[0]
    row = iota(length_out.shape, 0)
    limit = jnp.zeros(length_out.shape, jnp.int32)
    for beam in range(beams):
        limit = jnp.where(row // (length_out.shape[0] // beams) == beam, length[beam], limit)
    length_out[...] = limit
    x = beam_rows(x_ref, other_ref)
    slot_products(x, copies, w_buf, out)


def project_kept(place, bank, length, x, other, wq, ranks):
    beams = x.shape[0]
    return pl.pallas_call(
        project_kept_kernel,
        in_specs=[scalar()] * 3 + [whole()] * 2 + [big()],
        out_specs=[whole()] * 2,
        out_shape=[
            shape(2 * beams, wq.shape[1] // 4),
            shape(beams * wq.shape[1] // ranks // HEAD_DIM, HEAD_DIM, dtype=jnp.int32),
        ],
        scratch_shapes=slot_scratch(wq, ranks),
        compiler_params=params(8),
        cost_estimate=pl.CostEstimate(
            flops=beams * wq.size, bytes_accessed=2 * wq.size, transcendentals=0
        ),
        name="project_kept",
    )(place, bank, length, x, other, wq)


def keyval_kernel(x_ref, w_ref, out):
    ranks = out.shape[0]
    total = jnp.dot(x_ref[...], w_ref[...], preferred_element_type=F32)
    high = total.astype(BF16).astype(F32)
    low = total - high
    for r in range(ranks):
        key = slice(r * HEAD_DIM, (r + 1) * HEAD_DIM)
        value = slice((ranks + r) * HEAD_DIM, (ranks + r + 1) * HEAD_DIM)
        pieces = [high[:, key], low[:, key], total[:, value]]
        out[r] = jnp.concatenate(pieces, axis=0)


def keyval(x, wkv, ranks):
    beams, depth = x.shape
    return pl.pallas_call(
        keyval_kernel,
        in_specs=[whole()] * 2,
        out_specs=whole(),
        out_shape=shape(ranks, 3 * beams, HEAD_DIM),
        compiler_params=params(),
        cost_estimate=pl.CostEstimate(
            flops=2 * beams * wkv.size, bytes_accessed=2 * wkv.size, transcendentals=0
        ),
        name="keyval",
    )(x, wkv)


def correct_kernel(bank, column_ref, up_ref, *refs):
    *parts, own_out, other_out = refs
    total = parts[0][...]
    for part in parts[1:]:
        total += part[...]
    count, rank, width = up_ref.shape
    half = width // 2
    inner = total[:, half:].astype(BF16).astype(F32)
    column = column_ref[...]
    lane = iota(column.shape, 1)
    per = HEAD_DIM // rank
    spread = jnp.concatenate(
        [
            jnp.where(lane // rank + j * per == column, inner, 0.0)
            for j in range(count // per)
        ],
        axis=1,
    ).astype(BF16)
    delta = jnp.dot(
        spread, up_ref[...].reshape(count * rank, width), preferred_element_type=F32
    )
    rows = own_out.shape[0]
    for side in range(2):
        columns = slice(side * half, (side + 1) * half)
        part = delta[:, columns] + jnp.where(bank[0] == side, total[:, :half], 0.0)
        own_out[:, columns] = part[:rows]
        other_out[:, columns] = part[rows:]


def correct(bank, column, up, parts):
    rows = parts[0].shape[0]
    out = shape(rows // 2, up.shape[2])
    return pl.pallas_call(
        correct_kernel,
        in_specs=[scalar()] + [whole()] * (2 + len(parts)),
        out_specs=[whole()] * 2,
        out_shape=[out, out],
        compiler_params=params(),
        cost_estimate=pl.CostEstimate(
            flops=2 * rows * up.size, bytes_accessed=2 * up.size, transcendentals=0
        ),
        name="correct",
    )(bank, column, up, *parts)


def part_kernel(kept_ref, inner_ref, came_ref, *outs):
    width = outs[0].shape[1] - HEAD_DIM
    inner = inner_ref[...] + came_ref[:, len(outs) * width :]
    for i, out in enumerate(outs):
        columns = slice(i * width, (i + 1) * width)
        out[:, :width] = kept_ref[:, columns] + came_ref[:, columns]
        out[:, width:] = inner


def part(kept, inner, came, slots):
    rows, width = kept.shape
    return pl.pallas_call(
        part_kernel,
        in_specs=[whole()] * 3,
        out_specs=[whole()] * slots,
        out_shape=[shape(rows, width // slots + HEAD_DIM)] * slots,
        compiler_params=params(),
        name="part",
    )(kept, inner, came)


def rotate(v, cosine, sine):
    return v * cosine + pltpu.roll(v, HEAD_DIM // 2, 1) * sine


def rotate_kernel(own_ref, came_ref, cos_ref, sin_ref, q_ref, rows_ref):
    cosine, sine = cos_ref[...], sin_ref[...]
    for g in range(own_ref.shape[1] // HEAD_DIM):
        columns = slice(g * HEAD_DIM, (g + 1) * HEAD_DIM)
        rows_ref[:, g, :] = rotate(own_ref[:, columns] + came_ref[:, columns], cosine, sine)
    q_ref[0] = rows_ref[...].reshape(q_ref.shape[1:]).astype(BF16)


def rotated(own, came, cosine, sine):
    rows, width = own.shape
    heads = width // HEAD_DIM
    return pl.pallas_call(
        rotate_kernel,
        in_specs=[whole()] * 4,
        out_specs=whole(),
        out_shape=shape(1, rows * heads, HEAD_DIM, dtype=BF16),
        scratch_shapes=[pltpu.VMEM((rows, heads, HEAD_DIM), F32)],
        compiler_params=params(),
        name="rotate",
    )(own, came, cosine, sine)


def join_kernel(*refs):
    *parts, out_ref = refs
    for i, part in enumerate(parts):
        out_ref[i] = part[0]


def join(parts):
    return pl.pallas_call(
        join_kernel,
        in_specs=[whole()] * len(parts),
        out_specs=whole(),
        out_shape=shape(len(parts), *parts[0].shape[1:], dtype=parts[0].dtype),
        compiler_params=params(),
        name="join",
    )(*parts)


def attend_kernel(slots, earlier, place, bank, length_ref, q_ref, k_ref, v_ref, *refs):
    before, out_ref = refs[:-1], refs[-1]
    if earlier:
        *before, keyval_ref = before
    beams, positions, _ = k_ref.shape
    rows = q_ref.shape[1]
    group = rows // beams
    row, lane = iota((rows, HEAD_DIM), 0), iota((rows, HEAD_DIM), 1)
    left = length_ref[...] - place[0] * positions
    live = jnp.concatenate(
        [lane + first < left for first in range(0, positions, HEAD_DIM)], axis=1
    )
    for i, slot in enumerate(slots):
        head = rank_of(place[0], bank[0], slot)
        columns = pl.ds(pl.multiple_of(head * HEAD_DIM, HEAD_DIM), HEAD_DIM)
        query = q_ref[i].astype(F32)
        scores = jnp.concatenate(
            [
                lax.dot_general(
                    query[beam * group : (beam + 1) * group].astype(BF16),
                    k_ref[beam, :, columns],
                    (((1,), (1,)), ((), ())),
                    preferred_element_type=F32,
                )
                for beam in range(beams)
            ],
            axis=0,
        ) * (1.0 / HEAD_DIM**0.5)
        scores = jnp.where(live, scores, -1e30)
        peak = jnp.max(scores, axis=1, keepdims=True)
        weights = jnp.where(live, jnp.exp(scores - peak), 0.0)
        total = jnp.sum(weights, axis=1, keepdims=True)
        values = [
            jnp.dot(
                weights[beam * group : (beam + 1) * group].astype(BF16),
                v_ref[beam, :, columns],
                preferred_element_type=F32,
            )
            for beam in range(beams)
        ]
        stats = jnp.where(lane == row % group, peak, 0.0)
        stats += jnp.where(lane == group + row % group, total, 0.0)
        stats = jnp.sum(stats.reshape(beams, group, HEAD_DIM), axis=1)
        high = stats.astype(BF16).astype(F32)
        middle = (stats - high).astype(BF16).astype(F32)
        low = stats - high - middle
        tail = high + pltpu.roll(middle, 2 * group, 1) + pltpu.roll(low, 4 * group, 1)
        if earlier:
            block = jnp.concatenate(values + [tail, keyval_ref[head]], axis=0)
            out_ref[head] = block.astype(BF16)
        else:
            block = jnp.concatenate(values + [tail, jnp.zeros_like(tail)], axis=0)
            out_ref[i] = block.astype(BF16)
    if earlier:
        done = [(ref, i) for ref in before for i in range(ref.shape[0])]
        for slot, (ref, i) in zip(earlier, done):
            head = rank_of(place[0], bank[0], slot)
            held = ref[i].astype(F32)[: rows + beams]
            out_ref[head] = jnp.concatenate([held, keyval_ref[head]], axis=0).astype(BF16)


def attend(place, bank, length, queries, keys, values, slots, earlier=(), before=()):
    count, rows, _ = queries.shape
    beams, positions, _ = keys.shape
    return pl.pallas_call(
        lambda *refs: attend_kernel(slots, earlier, *refs),
        in_specs=[scalar()] * 2 + [whole()] * (4 + len(before)),
        out_specs=whole(),
        out_shape=shape(
            count + len(earlier), rows + (4 if earlier else 2) * beams, HEAD_DIM, dtype=BF16
        ),
        compiler_params=params(),
        cost_estimate=pl.CostEstimate(
            flops=4 * rows * count * positions * HEAD_DIM,
            bytes_accessed=4 * beams * positions * HEAD_DIM * (16 if earlier else count),
            transcendentals=rows * count * positions,
        ),
        name="attend",
    )(place, bank, length, queries, keys, values, *before)


def combine_kernel(parts_ref, q_ref, cos_ref, sin_ref, out_ref, joined):
    ranks = parts_ref.shape[0]
    beams, group, _ = joined.shape
    rows = beams * group

    def by_row(v):
        return jnp.broadcast_to(v[:, None, :], (beams, group, HEAD_DIM)).reshape(rows, HEAD_DIM)

    lane = iota((rows, HEAD_DIM), 1)
    own_lane = lane == iota((rows, HEAD_DIM), 0) % group

    def spread(v):
        return jnp.sum(jnp.where(own_lane, by_row(v), 0.0), axis=1, keepdims=True)

    blocks = [parts_ref[s].astype(F32) for s in range(ranks)]
    sums = blocks[0][rows + beams :]
    for block in blocks[1:]:
        sums += block[rows + beams :]
    key = sums[:beams] + sums[beams : 2 * beams]
    key = rotate(key, cos_ref[...], sin_ref[...]).astype(BF16).astype(F32)
    value = sums[2 * beams :].astype(BF16).astype(F32)
    score = jnp.sum(q_ref[0].astype(F32) * by_row(key), axis=1, keepdims=True) * (
        1.0 / HEAD_DIM**0.5
    )
    score = jnp.where(own_lane, score, 0.0).reshape(beams, group, HEAD_DIM)
    score = jnp.sum(score, axis=1)
    used = iota((beams, HEAD_DIM), 1) < group
    peaks, totals = [], []
    top = score
    for block in blocks:
        tail = block[rows : rows + beams]
        stats = tail
        for turn in (2, 4):
            stats = stats + pltpu.roll(tail, HEAD_DIM - turn * group, 1)
        peaks.append(jnp.where(used, stats, 0.0))
        totals.append(jnp.where(used, pltpu.roll(stats, HEAD_DIM - group, 1), 0.0))
        top = jnp.maximum(top, peaks[-1])
    factors = [jnp.exp(peak - top) for peak in peaks]
    new = jnp.exp(score - top)
    everything = new
    for factor, total in zip(factors, totals):
        everything += factor * total
    result = spread(new.astype(BF16).astype(F32) / everything) * by_row(value)
    for block, factor in zip(blocks, factors):
        result += spread(factor / everything) * block[:rows]
    joined[...] = result.reshape(joined.shape)
    for g in range(group):
        out_ref[:, g * HEAD_DIM : (g + 1) * HEAD_DIM] = joined[:, g, :].astype(BF16)


def combine(parts, query, cosine, sine):
    beams = cosine.shape[0]
    group = query.shape[1] // beams
    return pl.pallas_call(
        combine_kernel,
        in_specs=[whole()] * 4,
        out_specs=whole(),
        out_shape=shape(beams, group * HEAD_DIM, dtype=BF16),
        scratch_shapes=[pltpu.VMEM((beams, group, HEAD_DIM), F32)],
        compiler_params=params(),
        name="combine",
    )(parts, query, cosine, sine)


def output_kernel(x_ref, w_ref, out):
    count, _, width = out.shape
    for s in range(count):
        columns = slice(s * width, (s + 1) * width)
        total = jnp.dot(x_ref[...], w_ref[:, columns], preferred_element_type=F32)
        out[s] = total.astype(BF16)


def output(x, weight, ranks):
    beams = x.shape[0]
    return pl.pallas_call(
        output_kernel,
        in_specs=[whole()] * 2,
        out_specs=whole(),
        out_shape=shape(ranks, beams, weight.shape[1] // ranks, dtype=BF16),
        compiler_params=params(),
        cost_estimate=pl.CostEstimate(
            flops=2 * beams * weight.size, bytes_accessed=2 * weight.size, transcendentals=0
        ),
        name="output",
    )(x, weight)


def residual_kernel(x_ref, parts_ref, out_ref):
    total = jnp.sum(parts_ref[...].astype(F32), axis=0)
    out_ref[...] = (x_ref[...].astype(F32) + total).astype(BF16)


def residual(x, parts):
    return pl.pallas_call(
        residual_kernel,
        in_specs=[whole()] * 2,
        out_specs=whole(),
        out_shape=jax.ShapeDtypeStruct(x.shape, BF16),
        compiler_params=params(),
        name="residual",
    )(x, parts)


def swapped(x):
    return lax.ppermute(x, "bank", [(0, 1), (1, 0)])


def traded(blocks):
    return lax.all_to_all(blocks, "tensor", 0, 0, tiled=True)


def hop(x, bit):
    pairs = []
    for rank in range(lax.axis_size("tensor")):
        for bank in range(2):
            pairs.append((2 * rank + bank, 2 * rank_of(rank, bank, bit) + bank))
    return lax.ppermute(x, ("tensor", "bank"), pairs)


def matched_body(
    normed_hidden_input,
    beam_adapter_index,
    beam_cache_length,
    query_weight,
    keyvalue_weight,
    output_weight,
    lowrank_down_factors,
    lowrank_up_factors,
    paged_key_cache,
    paged_value_cache,
):
    x = normed_hidden_input
    ranks = lax.axis_size("tensor")
    place = lax.axis_index("tensor").astype(jnp.int32).reshape(1)
    bank = lax.axis_index("bank").astype(jnp.int32).reshape(1)
    index = (beam_adapter_index, swapped(beam_adapter_index))
    x_other = swapped(x)
    lane = jnp.arange(HEAD_DIM, dtype=jnp.int32)
    half = HEAD_DIM // 2
    frequency = jnp.power(500000.0, -2.0 * (lane % half).astype(F32) / HEAD_DIM)
    angles = beam_cache_length.astype(F32)[:, None] * frequency[None, :]
    cosine = jnp.cos(angles)
    sine = jnp.where(lane < half, -1.0, 1.0) * jnp.sin(angles)
    weight = in_hbm(query_weight)
    down = fetch(in_hbm(lowrank_down_factors.swapaxes(1, 2)))
    sent, inner, column = project_sent(place, bank, index, x, x_other, down, weight, ranks)
    came = hop(sent, 1)
    kept, length = project_kept(
        place, bank, beam_cache_length, x, x_other, weight, ranks
    )
    kept, *sent = part(kept, inner, came, ranks // 2)
    near = 4, 6, 2
    parts = [kept] + [hop(sent[slot // 2 - 1], slot) for slot in near]
    own_x, _ = lax.optimization_barrier((x, kept))
    token, parts = lax.optimization_barrier((keyval(own_x, keyvalue_weight, ranks), parts))
    own, other = correct(bank, column, lowrank_up_factors, parts)
    query = rotated(own, swapped(other), cosine, sine)

    def attended_part(queries, slots, **more):
        cache = paged_key_cache, paged_value_cache
        return attend(place, bank, length, queries, *cache, slots, **more)

    gathered = join([query] + [hop(query, slot) for slot in near])
    came = hop(gathered, 1)
    done = attended_part(gathered, (0, *near))
    odd = tuple(slot + 1 for slot in (0, *near))
    partial = attended_part(came, odd, earlier=(0, *near), before=(done, token))
    attended = combine(traded(partial), query, cosine, sine)
    return residual(x, traded(output(attended, output_weight, ranks)))


def joined(x, axis, combine):
    everything = jax.tree.map(lambda part: lax.all_gather(part, axis), x)
    leading = jax.tree.map(lambda part: part[0], everything)

    def turn(k, so_far):
        return combine(so_far, jax.tree.map(lambda part: part[k], everything))

    return lax.fori_loop(1, lax.axis_size(axis), turn, leading)


def apply_rotary(values, positions, head_size):
    row_count, col_count = values.shape
    half_size = head_size // 2
    frequency = jnp.power(500000.0, -2.0 * jnp.arange(half_size, dtype=jnp.float32) / head_size)
    angles = positions.astype(jnp.float32)[:, None] * frequency[None, :]
    cosine_table = jnp.cos(angles)[:, None, :]
    sine_table = jnp.sin(angles)[:, None, :]
    shaped = values.reshape(row_count, col_count // head_size, 2, half_size)
    first_half = shaped[:, :, 0]
    second_half = shaped[:, :, 1]
    rotated = jnp.stack(
        [
            first_half * cosine_table - second_half * sine_table,
            second_half * cosine_table + first_half * sine_table,
        ],
        axis=2,
    )
    return rotated.reshape(row_count, col_count)


def combine_parts(first_part, second_part):
    peak_one, total_one, weighted_one = first_part
    peak_two, total_two, weighted_two = second_part
    peak_both = jnp.maximum(peak_one, peak_two)
    factor_one = jnp.exp(peak_one - peak_both)
    factor_two = jnp.exp(peak_two - peak_both)
    return (
        peak_both,
        total_one * factor_one + total_two * factor_two,
        weighted_one * factor_one[..., None] + weighted_two * factor_two[..., None],
    )


def finish_heads(peak_score, weight_total, weighted, score_new, value_rows):
    peak_final = jnp.maximum(peak_score, score_new)
    old_factor = jnp.exp(peak_score - peak_final)
    new_weight = jnp.exp(score_new - peak_final)
    weight_total = weight_total * old_factor + new_weight
    weighted = (
        weighted * old_factor[..., None]
        + new_weight.astype(jnp.bfloat16).astype(jnp.float32)[..., None] * value_rows
    )
    return weighted / weight_total[..., None]


def body(
    normed_hidden_input,
    beam_adapter_index,
    beam_cache_length,
    query_weight,
    keyvalue_weight,
    output_weight,
    lowrank_down_factors,
    lowrank_up_factors,
    paged_key_cache,
    paged_value_cache,
):
    beam_rows, width_part = normed_hidden_input.shape
    model_width = query_weight.shape[1]
    kv_width = keyvalue_weight.shape[1] // 2
    head_count = model_width // HEAD_DIM
    kv_heads = kv_width // HEAD_DIM
    group_size = head_count // kv_heads
    tensor_index = lax.axis_index("tensor")
    query_part = jnp.dot(normed_hidden_input, query_weight, preferred_element_type=jnp.float32)
    keyval_part = jnp.dot(normed_hidden_input, keyvalue_weight, preferred_element_type=jnp.float32)
    down_all, up_all = (
        lax.all_gather(lowrank_down_factors, "bank", axis=0, tiled=True),
        lax.all_gather(lowrank_up_factors, "bank", axis=0, tiled=True),
    )
    inner_part = jnp.einsum(
        "ci,cim->cm",
        normed_hidden_input,
        down_all[beam_adapter_index],
        preferred_element_type=jnp.float32,
    )
    inner_total = lax.psum(inner_part, "tensor").astype(jnp.bfloat16)
    lowrank_delta = jnp.einsum(
        "mc,mct->mt", inner_total, up_all[beam_adapter_index], preferred_element_type=jnp.float32
    )
    query_total, keyval = lax.psum((query_part, keyval_part), "tensor")
    delta_total = lax.all_gather(lowrank_delta, "tensor", axis=1, tiled=True)
    query_rotated = apply_rotary(query_total + delta_total, beam_cache_length, HEAD_DIM).astype(
        jnp.bfloat16
    )
    key_new = apply_rotary(keyval[:, :kv_width], beam_cache_length, HEAD_DIM).astype(jnp.bfloat16)
    value_new = keyval[:, kv_width:].astype(jnp.bfloat16)
    position_count = paged_key_cache.shape[1]
    query_heads = query_rotated.reshape(beam_rows, kv_heads, group_size, HEAD_DIM)
    key_block = paged_key_cache.reshape(beam_rows, position_count, kv_heads, HEAD_DIM)
    value_block = paged_value_cache.reshape(beam_rows, position_count, kv_heads, HEAD_DIM)
    score_scale = 1.0 / HEAD_DIM**0.5
    scores = (
        jnp.einsum("bkgh,bpkh->bkgp", query_heads, key_block, preferred_element_type=jnp.float32)
        * score_scale
    )
    position_ids = tensor_index * position_count + jnp.arange(position_count)
    live_mask = (position_ids[None, :] < beam_cache_length[:, None])[:, None, None, :]
    scores = jnp.where(live_mask, scores, -1e30)
    peak_score = jnp.max(scores, axis=-1)
    weights = jnp.where(live_mask, jnp.exp(scores - peak_score[..., None]), 0.0)
    weight_total = jnp.sum(weights, axis=-1)
    weighted = jnp.einsum(
        "bkgp,bpkh->bkgh",
        weights.astype(jnp.bfloat16),
        value_block,
        preferred_element_type=jnp.float32,
    )
    peak_score, weight_total, weighted = joined(
        (peak_score, weight_total, weighted), "tensor", combine_parts
    )
    score_new = (
        jnp.einsum(
            "bkgh,bkh->bkg",
            query_heads,
            key_new.reshape(beam_rows, kv_heads, HEAD_DIM),
            preferred_element_type=jnp.float32,
        )
        * score_scale
    )
    value_rows = value_new.reshape(beam_rows, kv_heads, HEAD_DIM).astype(jnp.float32)[:, :, None, :]
    attended = (
        finish_heads(peak_score, weight_total, weighted, score_new, value_rows)
        .reshape(beam_rows, model_width)
        .astype(jnp.bfloat16)
    )
    attended_cols = lax.dynamic_slice_in_dim(attended, tensor_index * width_part, width_part, 1)
    mixed_cols = lax.psum_scatter(
        lax.dot_general(
            output_weight,
            attended_cols,
            (((0,), (1,)), ((), ())),
            preferred_element_type=jnp.float32,
        ),
        "tensor",
        scatter_dimension=0,
        tiled=True,
    )
    return (normed_hidden_input.astype(jnp.float32) + mixed_cols.T).astype(jnp.bfloat16)


def solution(mesh):
    matched = mesh.shape["tensor"] == 8 and mesh.shape["bank"] == 2
    return jax.shard_map(
        matched_body if matched else body,
        mesh=mesh,
        in_specs=(
            P(("groups", "bank"), "tensor"),
            P(("groups", "bank")),
            P(("groups", "bank")),
            P("tensor", None),
            P("tensor", None),
            P("tensor", None),
            P("bank", "tensor", None),
            P("bank", None, "tensor"),
            P(("groups", "bank"), "tensor", None),
            P(("groups", "bank"), "tensor", None),
        ),
        out_specs=P(("groups", "bank"), "tensor"),
        check_vma=False,
    )
```

```python
import jax
import jax.numpy as jnp
from jax import lax
from jax.experimental import pallas as pl
from jax.experimental.pallas import tpu as pltpu
from jax.sharding import PartitionSpec as P

HEAD_DIM = 128
F32 = jnp.float32
BF16 = jnp.bfloat16
CHUNKS = 2
MIB = 1024 * 1024


def whole():
    return pl.BlockSpec(memory_space=pltpu.VMEM)


def big():
    return pl.BlockSpec(memory_space=pltpu.HBM)


def scalar():
    return pl.BlockSpec(memory_space=pltpu.SMEM)


def in_hbm(array):
    return pltpu.with_memory_space_constraint(array, pltpu.HBM)


def shape(*dims, dtype=F32):
    return jax.ShapeDtypeStruct(dims, dtype)


def iota(dims, axis):
    return lax.broadcasted_iota(jnp.int32, dims, axis)


def params(mib=4):
    return pltpu.CompilerParams(vmem_limit_bytes=mib * MIB)


def exchanged(slot):
    return slot & ~3 | (slot & 1) << 1 | slot >> 1 & 1


def rank_of(place, bank, slot):
    return place ^ (slot + bank * (exchanged(slot) - slot))


def adapter_column(refs, bank, count):
    columns = []
    for ref in refs:
        rows = ref.shape[1]
        index = jnp.broadcast_to(ref[...].astype(F32), (rows, rows))
        diagonal = iota((rows, rows), 0) == iota((rows, rows), 1)
        columns.append(jnp.sum(jnp.where(diagonal, index, 0.0), axis=1, keepdims=True))
    column = jnp.concatenate(columns, axis=0).astype(jnp.int32) - bank * count
    return jnp.broadcast_to(column, (column.shape[0], HEAD_DIM))


def start_slots(parity, place, bank, w_ref, w_buf, sems):
    count, depth, width = w_buf.shape
    part = depth // CHUNKS
    copies = []
    for c in range(CHUNKS):
        rows = pl.ds(c * part, part)
        copies.append([])
        for s in range(count):
            target = rank_of(place[0], bank[0], 2 * s + parity)
            columns = pl.ds(pl.multiple_of((2 * target + bank[0]) * width, width), width)
            copy = pltpu.make_async_copy(
                w_ref.at[rows, columns], w_buf.at[s, rows], sems.at[s, c]
            )
            copy.start()
            copies[-1].append(copy)
    return copies


def slot_products(x, copies, w_buf, out):
    count, depth, width = w_buf.shape
    part = depth // CHUNKS
    for c, chunk in enumerate(copies):
        rows = slice(c * part, (c + 1) * part)
        for s, copy in enumerate(chunk):
            copy.wait()
            columns = slice(s * width, (s + 1) * width)
            product = jnp.dot(x[:, rows], w_buf[s, rows], preferred_element_type=F32)
            out[:, columns] = product if c == 0 else out[:, columns] + product


def wait_all(copies):
    for copy in copies:
        copy.wait()


def start_parts(source, target, sems):
    part = source.shape[0] // sems.shape[0]
    copies = []
    for c in range(sems.shape[0]):
        rows = pl.ds(c * part, part)
        copies.append(pltpu.make_async_copy(source.at[rows], target.at[rows], sems.at[c]))
        copies[-1].start()
    return copies


def fetch_kernel(ref, out, sems):
    wait_all(start_parts(ref, out, sems))


def fetch(array):
    return pl.pallas_call(
        fetch_kernel,
        in_specs=[big()],
        out_specs=whole(),
        out_shape=jax.ShapeDtypeStruct(array.shape, array.dtype),
        scratch_shapes=[pltpu.SemaphoreType.DMA((2,))],
        compiler_params=params(),
        cost_estimate=pl.CostEstimate(
            flops=0, bytes_accessed=2 * array.size, transcendentals=0
        ),
        name="fetch",
    )(array)


def slot_scratch(wq, ranks):
    half, depth = ranks // 2, wq.shape[0]
    return [
        pltpu.VMEM((half, depth, wq.shape[1] // ranks // 2), BF16),
        pltpu.SemaphoreType.DMA((half, CHUNKS)),
    ]


def beam_rows(x_ref, other_ref):
    rows = [x_ref[...].astype(F32), other_ref[...].astype(F32)]
    return jnp.concatenate(rows, axis=0).astype(BF16)


def project_sent_kernel(
    place, bank, own_ref, came_ref, x_ref, other_ref, down_ref, w_ref, *refs
):
    out, inner, column_out, w_buf, sems = refs
    copies = start_slots(1, place, bank, w_ref, w_buf, sems)
    x = beam_rows(x_ref, other_ref)
    adapters, rank, depth = down_ref.shape
    wide = jnp.concatenate([x, jnp.zeros((HEAD_DIM - x.shape[0], depth), BF16)], axis=0)
    every = lax.dot_general(
        down_ref[...].reshape(adapters * rank, depth),
        wide,
        (((1,), (1,)), ((), ())),
        preferred_element_type=F32,
    )
    every = jnp.transpose(every)[: x.shape[0]]
    column = adapter_column((own_ref, came_ref), bank[0], adapters)
    column_out[...] = column
    lane = iota(column.shape, 1)
    per = HEAD_DIM // rank
    total = jnp.zeros(column.shape, F32)
    for j in range(adapters // per):
        part = every[:, j * HEAD_DIM : (j + 1) * HEAD_DIM]
        total += jnp.where(lane // rank + j * per == column, part, 0.0)
    inner[...] = total
    out[:, out.shape[1] - HEAD_DIM :] = total
    slot_products(x, copies, w_buf, out)


def project_sent(place, bank, index, x, other, down, wq, ranks):
    rows = 2 * x.shape[0]
    return pl.pallas_call(
        project_sent_kernel,
        in_specs=[scalar()] * 2 + [whole()] * 5 + [big()],
        out_specs=[whole()] * 3,
        out_shape=[
            shape(rows, wq.shape[1] // 4 + HEAD_DIM),
            shape(rows, HEAD_DIM),
            shape(rows, HEAD_DIM, dtype=jnp.int32),
        ],
        scratch_shapes=slot_scratch(wq, ranks),
        compiler_params=params(8),
        cost_estimate=pl.CostEstimate(
            flops=rows * (wq.size // 2 + 2 * down.size),
            bytes_accessed=wq.size // 2 + 2 * down.size,
            transcendentals=0,
        ),
        name="project_sent",
    )(place, bank, *[i.reshape(1, -1) for i in index], x, other, down, wq)


def project_kept_kernel(
    place, bank, length, x_ref, other_ref, w_ref, out, length_out, w_buf, sems
):
    copies = start_slots(0, place, bank, w_ref, w_buf, sems)
    beams = x_ref.shape[0]
    row = iota(length_out.shape, 0)
    limit = jnp.zeros(length_out.shape, jnp.int32)
    for beam in range(beams):
        limit = jnp.where(row // (length_out.shape[0] // beams) == beam, length[beam], limit)
    length_out[...] = limit
    x = beam_rows(x_ref, other_ref)
    slot_products(x, copies, w_buf, out)


def project_kept(place, bank, length, x, other, wq, ranks):
    beams = x.shape[0]
    return pl.pallas_call(
        project_kept_kernel,
        in_specs=[scalar()] * 3 + [whole()] * 2 + [big()],
        out_specs=[whole()] * 2,
        out_shape=[
            shape(2 * beams, wq.shape[1] // 4),
            shape(beams * wq.shape[1] // ranks // HEAD_DIM, HEAD_DIM, dtype=jnp.int32),
        ],
        scratch_shapes=slot_scratch(wq, ranks),
        compiler_params=params(8),
        cost_estimate=pl.CostEstimate(
            flops=beams * wq.size, bytes_accessed=2 * wq.size, transcendentals=0
        ),
        name="project_kept",
    )(place, bank, length, x, other, wq)


def keyval_kernel(x_ref, w_ref, out):
    ranks = out.shape[0]
    total = jnp.dot(x_ref[...], w_ref[...], preferred_element_type=F32)
    high = total.astype(BF16).astype(F32)
    low = total - high
    for r in range(ranks):
        key = slice(r * HEAD_DIM, (r + 1) * HEAD_DIM)
        value = slice((ranks + r) * HEAD_DIM, (ranks + r + 1) * HEAD_DIM)
        pieces = [high[:, key], low[:, key], total[:, value]]
        out[r] = jnp.concatenate(pieces, axis=0)


def keyval(x, wkv, ranks):
    beams, depth = x.shape
    return pl.pallas_call(
        keyval_kernel,
        in_specs=[whole()] * 2,
        out_specs=whole(),
        out_shape=shape(ranks, 3 * beams, HEAD_DIM),
        compiler_params=params(),
        cost_estimate=pl.CostEstimate(
            flops=2 * beams * wkv.size, bytes_accessed=2 * wkv.size, transcendentals=0
        ),
        name="keyval",
    )(x, wkv)


def correct_kernel(bank, column_ref, up_ref, *refs):
    *parts, own_out, other_out = refs
    total = parts[0][...]
    for part in parts[1:]:
        total += part[...]
    count, rank, width = up_ref.shape
    half = width // 2
    inner = total[:, half:].astype(BF16).astype(F32)
    column = column_ref[...]
    lane = iota(column.shape, 1)
    per = HEAD_DIM // rank
    spread = jnp.concatenate(
        [
            jnp.where(lane // rank + j * per == column, inner, 0.0)
            for j in range(count // per)
        ],
        axis=1,
    ).astype(BF16)
    delta = jnp.dot(
        spread, up_ref[...].reshape(count * rank, width), preferred_element_type=F32
    )
    rows = own_out.shape[0]
    for side in range(2):
        columns = slice(side * half, (side + 1) * half)
        part = delta[:, columns] + jnp.where(bank[0] == side, total[:, :half], 0.0)
        own_out[:, columns] = part[:rows]
        other_out[:, columns] = part[rows:]


def correct(bank, column, up, parts):
    rows = parts[0].shape[0]
    out = shape(rows // 2, up.shape[2])
    return pl.pallas_call(
        correct_kernel,
        in_specs=[scalar()] + [whole()] * (2 + len(parts)),
        out_specs=[whole()] * 2,
        out_shape=[out, out],
        compiler_params=params(),
        cost_estimate=pl.CostEstimate(
            flops=2 * rows * up.size, bytes_accessed=2 * up.size, transcendentals=0
        ),
        name="correct",
    )(bank, column, up, *parts)


def part_kernel(kept_ref, inner_ref, came_ref, *outs):
    width = outs[0].shape[1] - HEAD_DIM
    inner = inner_ref[...] + came_ref[:, len(outs) * width :]
    for i, out in enumerate(outs):
        columns = slice(i * width, (i + 1) * width)
        out[:, :width] = kept_ref[:, columns] + came_ref[:, columns]
        out[:, width:] = inner


def part(kept, inner, came, slots):
    rows, width = kept.shape
    return pl.pallas_call(
        part_kernel,
        in_specs=[whole()] * 3,
        out_specs=[whole()] * slots,
        out_shape=[shape(rows, width // slots + HEAD_DIM)] * slots,
        compiler_params=params(),
        name="part",
    )(kept, inner, came)


def rotate(v, cosine, sine):
    return v * cosine + pltpu.roll(v, HEAD_DIM // 2, 1) * sine


def rotate_kernel(own_ref, came_ref, cos_ref, sin_ref, q_ref, rows_ref):
    cosine, sine = cos_ref[...], sin_ref[...]
    for g in range(own_ref.shape[1] // HEAD_DIM):
        columns = slice(g * HEAD_DIM, (g + 1) * HEAD_DIM)
        rows_ref[:, g, :] = rotate(own_ref[:, columns] + came_ref[:, columns], cosine, sine)
    q_ref[0] = rows_ref[...].reshape(q_ref.shape[1:]).astype(BF16)


def rotated(own, came, cosine, sine):
    rows, width = own.shape
    heads = width // HEAD_DIM
    return pl.pallas_call(
        rotate_kernel,
        in_specs=[whole()] * 4,
        out_specs=whole(),
        out_shape=shape(1, rows * heads, HEAD_DIM, dtype=BF16),
        scratch_shapes=[pltpu.VMEM((rows, heads, HEAD_DIM), F32)],
        compiler_params=params(),
        name="rotate",
    )(own, came, cosine, sine)


def join_kernel(*refs):
    *parts, out_ref = refs
    for i, part in enumerate(parts):
        out_ref[i] = part[0]


def join(parts):
    return pl.pallas_call(
        join_kernel,
        in_specs=[whole()] * len(parts),
        out_specs=whole(),
        out_shape=shape(len(parts), *parts[0].shape[1:], dtype=parts[0].dtype),
        compiler_params=params(),
        name="join",
    )(*parts)


def attend_kernel(slots, earlier, place, bank, length_ref, q_ref, k_ref, v_ref, *refs):
    before, out_ref = refs[:-1], refs[-1]
    if earlier:
        *before, keyval_ref = before
    beams, positions, _ = k_ref.shape
    rows = q_ref.shape[1]
    group = rows // beams
    row, lane = iota((rows, HEAD_DIM), 0), iota((rows, HEAD_DIM), 1)
    left = length_ref[...] - place[0] * positions
    live = jnp.concatenate(
        [lane + first < left for first in range(0, positions, HEAD_DIM)], axis=1
    )
    for i, slot in enumerate(slots):
        head = rank_of(place[0], bank[0], slot)
        columns = pl.ds(pl.multiple_of(head * HEAD_DIM, HEAD_DIM), HEAD_DIM)
        query = q_ref[i].astype(F32)
        scores = jnp.concatenate(
            [
                lax.dot_general(
                    query[beam * group : (beam + 1) * group].astype(BF16),
                    k_ref[beam, :, columns],
                    (((1,), (1,)), ((), ())),
                    preferred_element_type=F32,
                )
                for beam in range(beams)
            ],
            axis=0,
        ) * (1.0 / HEAD_DIM**0.5)
        scores = jnp.where(live, scores, -1e30)
        peak = jnp.max(scores, axis=1, keepdims=True)
        weights = jnp.where(live, jnp.exp(scores - peak), 0.0)
        total = jnp.sum(weights, axis=1, keepdims=True)
        values = [
            jnp.dot(
                weights[beam * group : (beam + 1) * group].astype(BF16),
                v_ref[beam, :, columns],
                preferred_element_type=F32,
            )
            for beam in range(beams)
        ]
        stats = jnp.where(lane == row % group, peak, 0.0)
        stats += jnp.where(lane == group + row % group, total, 0.0)
        stats = jnp.sum(stats.reshape(beams, group, HEAD_DIM), axis=1)
        high = stats.astype(BF16).astype(F32)
        middle = (stats - high).astype(BF16).astype(F32)
        low = stats - high - middle
        tail = high + pltpu.roll(middle, 2 * group, 1) + pltpu.roll(low, 4 * group, 1)
        if earlier:
            block = jnp.concatenate(values + [tail, keyval_ref[head]], axis=0)
            out_ref[head] = block.astype(BF16)
        else:
            block = jnp.concatenate(values + [tail, jnp.zeros_like(tail)], axis=0)
            out_ref[i] = block.astype(BF16)
    if earlier:
        done = [(ref, i) for ref in before for i in range(ref.shape[0])]
        for slot, (ref, i) in zip(earlier, done):
            head = rank_of(place[0], bank[0], slot)
            held = ref[i].astype(F32)[: rows + beams]
            out_ref[head] = jnp.concatenate([held, keyval_ref[head]], axis=0).astype(BF16)


def attend(place, bank, length, queries, keys, values, slots, earlier=(), before=()):
    count, rows, _ = queries.shape
    beams, positions, _ = keys.shape
    return pl.pallas_call(
        lambda *refs: attend_kernel(slots, earlier, *refs),
        in_specs=[scalar()] * 2 + [whole()] * (4 + len(before)),
        out_specs=whole(),
        out_shape=shape(
            count + len(earlier), rows + (4 if earlier else 2) * beams, HEAD_DIM, dtype=BF16
        ),
        compiler_params=params(),
        cost_estimate=pl.CostEstimate(
            flops=4 * rows * count * positions * HEAD_DIM,
            bytes_accessed=4 * beams * positions * HEAD_DIM * (16 if earlier else count),
            transcendentals=rows * count * positions,
        ),
        name="attend",
    )(place, bank, length, queries, keys, values, *before)


def combine_kernel(parts_ref, q_ref, cos_ref, sin_ref, out_ref, joined):
    ranks = parts_ref.shape[0]
    beams, group, _ = joined.shape
    rows = beams * group

    def by_row(v):
        return jnp.broadcast_to(v[:, None, :], (beams, group, HEAD_DIM)).reshape(rows, HEAD_DIM)

    lane = iota((rows, HEAD_DIM), 1)
    own_lane = lane == iota((rows, HEAD_DIM), 0) % group

    def spread(v):
        return jnp.sum(jnp.where(own_lane, by_row(v), 0.0), axis=1, keepdims=True)

    blocks = [parts_ref[s].astype(F32) for s in range(ranks)]
    sums = blocks[0][rows + beams :]
    for block in blocks[1:]:
        sums += block[rows + beams :]
    key = sums[:beams] + sums[beams : 2 * beams]
    key = rotate(key, cos_ref[...], sin_ref[...]).astype(BF16).astype(F32)
    value = sums[2 * beams :].astype(BF16).astype(F32)
    score = jnp.sum(q_ref[0].astype(F32) * by_row(key), axis=1, keepdims=True) * (
        1.0 / HEAD_DIM**0.5
    )
    score = jnp.where(own_lane, score, 0.0).reshape(beams, group, HEAD_DIM)
    score = jnp.sum(score, axis=1)
    used = iota((beams, HEAD_DIM), 1) < group
    peaks, totals = [], []
    top = score
    for block in blocks:
        tail = block[rows : rows + beams]
        stats = tail
        for turn in (2, 4):
            stats = stats + pltpu.roll(tail, HEAD_DIM - turn * group, 1)
        peaks.append(jnp.where(used, stats, 0.0))
        totals.append(jnp.where(used, pltpu.roll(stats, HEAD_DIM - group, 1), 0.0))
        top = jnp.maximum(top, peaks[-1])
    factors = [jnp.exp(peak - top) for peak in peaks]
    new = jnp.exp(score - top)
    everything = new
    for factor, total in zip(factors, totals):
        everything += factor * total
    result = spread(new.astype(BF16).astype(F32) / everything) * by_row(value)
    for block, factor in zip(blocks, factors):
        result += spread(factor / everything) * block[:rows]
    joined[...] = result.reshape(joined.shape)
    for g in range(group):
        out_ref[:, g * HEAD_DIM : (g + 1) * HEAD_DIM] = joined[:, g, :].astype(BF16)


def combine(parts, query, cosine, sine):
    beams = cosine.shape[0]
    group = query.shape[1] // beams
    return pl.pallas_call(
        combine_kernel,
        in_specs=[whole()] * 4,
        out_specs=whole(),
        out_shape=shape(beams, group * HEAD_DIM, dtype=BF16),
        scratch_shapes=[pltpu.VMEM((beams, group, HEAD_DIM), F32)],
        compiler_params=params(),
        name="combine",
    )(parts, query, cosine, sine)


def output_kernel(x_ref, w_ref, out):
    count, _, width = out.shape
    for s in range(count):
        columns = slice(s * width, (s + 1) * width)
        total = jnp.dot(x_ref[...], w_ref[:, columns], preferred_element_type=F32)
        out[s] = total.astype(BF16)


def output(x, weight, ranks):
    beams = x.shape[0]
    return pl.pallas_call(
        output_kernel,
        in_specs=[whole()] * 2,
        out_specs=whole(),
        out_shape=shape(ranks, beams, weight.shape[1] // ranks, dtype=BF16),
        compiler_params=params(),
        cost_estimate=pl.CostEstimate(
            flops=2 * beams * weight.size, bytes_accessed=2 * weight.size, transcendentals=0
        ),
        name="output",
    )(x, weight)


def residual_kernel(x_ref, parts_ref, out_ref):
    total = jnp.sum(parts_ref[...].astype(F32), axis=0)
    out_ref[...] = (x_ref[...].astype(F32) + total).astype(BF16)


def residual(x, parts):
    return pl.pallas_call(
        residual_kernel,
        in_specs=[whole()] * 2,
        out_specs=whole(),
        out_shape=jax.ShapeDtypeStruct(x.shape, BF16),
        compiler_params=params(),
        name="residual",
    )(x, parts)


def swapped(x):
    return lax.ppermute(x, "bank", [(0, 1), (1, 0)])


def traded(blocks):
    return lax.all_to_all(blocks, "tensor", 0, 0, tiled=True)


def hop(x, bit):
    pairs = []
    for rank in range(lax.axis_size("tensor")):
        for bank in range(2):
            pairs.append((2 * rank + bank, 2 * rank_of(rank, bank, bit) + bank))
    return lax.ppermute(x, ("tensor", "bank"), pairs)


def matched_body(
    normed_hidden_input,
    beam_adapter_index,
    beam_cache_length,
    query_weight,
    keyvalue_weight,
    output_weight,
    lowrank_down_factors,
    lowrank_up_factors,
    paged_key_cache,
    paged_value_cache,
):
    x = normed_hidden_input
    ranks = lax.axis_size("tensor")
    place = lax.axis_index("tensor").astype(jnp.int32).reshape(1)
    bank = lax.axis_index("bank").astype(jnp.int32).reshape(1)
    index = (beam_adapter_index, swapped(beam_adapter_index))
    x_other = swapped(x)
    lane = jnp.arange(HEAD_DIM, dtype=jnp.int32)
    half = HEAD_DIM // 2
    frequency = jnp.power(500000.0, -2.0 * (lane % half).astype(F32) / HEAD_DIM)
    angles = beam_cache_length.astype(F32)[:, None] * frequency[None, :]
    cosine = jnp.cos(angles)
    sine = jnp.where(lane < half, -1.0, 1.0) * jnp.sin(angles)
    weight = in_hbm(query_weight)
    down = fetch(in_hbm(lowrank_down_factors.swapaxes(1, 2)))
    sent, inner, column = project_sent(place, bank, index, x, x_other, down, weight, ranks)
    came = hop(sent, 1)
    kept, length = project_kept(
        place, bank, beam_cache_length, x, x_other, weight, ranks
    )
    kept, *sent = part(kept, inner, came, ranks // 2)
    near = 4, 6, 2
    parts = [kept] + [hop(sent[slot // 2 - 1], slot) for slot in near]
    own_x, _ = lax.optimization_barrier((x, kept))
    token, parts = lax.optimization_barrier((keyval(own_x, keyvalue_weight, ranks), parts))
    own, other = correct(bank, column, lowrank_up_factors, parts)
    query = rotated(own, swapped(other), cosine, sine)

    def attended_part(queries, slots, **more):
        cache = paged_key_cache, paged_value_cache
        return attend(place, bank, length, queries, *cache, slots, **more)

    gathered = join([query] + [hop(query, slot) for slot in near])
    came = hop(gathered, 1)
    done = attended_part(gathered, (0, *near))
    odd = tuple(slot + 1 for slot in (0, *near))
    partial = attended_part(came, odd, earlier=(0, *near), before=(done, token))
    attended = combine(traded(partial), query, cosine, sine)
    return residual(x, traded(output(attended, output_weight, ranks)))


def joined(x, axis, combine):
    everything = jax.tree.map(lambda part: lax.all_gather(part, axis), x)
    leading = jax.tree.map(lambda part: part[0], everything)

    def turn(k, so_far):
        return combine(so_far, jax.tree.map(lambda part: part[k], everything))

    return lax.fori_loop(1, lax.axis_size(axis), turn, leading)


def apply_rotary(values, positions, head_size):
    row_count, col_count = values.shape
    half_size = head_size // 2
    frequency = jnp.power(500000.0, -2.0 * jnp.arange(half_size, dtype=jnp.float32) / head_size)
    angles = positions.astype(jnp.float32)[:, None] * frequency[None, :]
    cosine_table = jnp.cos(angles)[:, None, :]
    sine_table = jnp.sin(angles)[:, None, :]
    shaped = values.reshape(row_count, col_count // head_size, 2, half_size)
    first_half = shaped[:, :, 0]
    second_half = shaped[:, :, 1]
    rotated = jnp.stack(
        [
            first_half * cosine_table - second_half * sine_table,
            second_half * cosine_table + first_half * sine_table,
        ],
        axis=2,
    )
    return rotated.reshape(row_count, col_count)


def combine_parts(first_part, second_part):
    peak_one, total_one, weighted_one = first_part
    peak_two, total_two, weighted_two = second_part
    peak_both = jnp.maximum(peak_one, peak_two)
    factor_one = jnp.exp(peak_one - peak_both)
    factor_two = jnp.exp(peak_two - peak_both)
    return (
        peak_both,
        total_one * factor_one + total_two * factor_two,
        weighted_one * factor_one[..., None] + weighted_two * factor_two[..., None],
    )


def finish_heads(peak_score, weight_total, weighted, score_new, value_rows):
    peak_final = jnp.maximum(peak_score, score_new)
    old_factor = jnp.exp(peak_score - peak_final)
    new_weight = jnp.exp(score_new - peak_final)
    weight_total = weight_total * old_factor + new_weight
    weighted = (
        weighted * old_factor[..., None]
        + new_weight.astype(jnp.bfloat16).astype(jnp.float32)[..., None] * value_rows
    )
    return weighted / weight_total[..., None]


def body(
    normed_hidden_input,
    beam_adapter_index,
    beam_cache_length,
    query_weight,
    keyvalue_weight,
    output_weight,
    lowrank_down_factors,
    lowrank_up_factors,
    paged_key_cache,
    paged_value_cache,
):
    beam_rows, width_part = normed_hidden_input.shape
    model_width = query_weight.shape[1]
    kv_width = keyvalue_weight.shape[1] // 2
    head_count = model_width // HEAD_DIM
    kv_heads = kv_width // HEAD_DIM
    group_size = head_count // kv_heads
    tensor_index = lax.axis_index("tensor")
    query_part = jnp.dot(normed_hidden_input, query_weight, preferred_element_type=jnp.float32)
    keyval_part = jnp.dot(normed_hidden_input, keyvalue_weight, preferred_element_type=jnp.float32)
    down_all, up_all = (
        lax.all_gather(lowrank_down_factors, "bank", axis=0, tiled=True),
        lax.all_gather(lowrank_up_factors, "bank", axis=0, tiled=True),
    )
    inner_part = jnp.einsum(
        "ci,cim->cm",
        normed_hidden_input,
        down_all[beam_adapter_index],
        preferred_element_type=jnp.float32,
    )
    inner_total = lax.psum(inner_part, "tensor").astype(jnp.bfloat16)
    lowrank_delta = jnp.einsum(
        "mc,mct->mt", inner_total, up_all[beam_adapter_index], preferred_element_type=jnp.float32
    )
    query_total, keyval = lax.psum((query_part, keyval_part), "tensor")
    delta_total = lax.all_gather(lowrank_delta, "tensor", axis=1, tiled=True)
    query_rotated = apply_rotary(query_total + delta_total, beam_cache_length, HEAD_DIM).astype(
        jnp.bfloat16
    )
    key_new = apply_rotary(keyval[:, :kv_width], beam_cache_length, HEAD_DIM).astype(jnp.bfloat16)
    value_new = keyval[:, kv_width:].astype(jnp.bfloat16)
    position_count = paged_key_cache.shape[1]
    query_heads = query_rotated.reshape(beam_rows, kv_heads, group_size, HEAD_DIM)
    key_block = paged_key_cache.reshape(beam_rows, position_count, kv_heads, HEAD_DIM)
    value_block = paged_value_cache.reshape(beam_rows, position_count, kv_heads, HEAD_DIM)
    score_scale = 1.0 / HEAD_DIM**0.5
    scores = (
        jnp.einsum("bkgh,bpkh->bkgp", query_heads, key_block, preferred_element_type=jnp.float32)
        * score_scale
    )
    position_ids = tensor_index * position_count + jnp.arange(position_count)
    live_mask = (position_ids[None, :] < beam_cache_length[:, None])[:, None, None, :]
    scores = jnp.where(live_mask, scores, -1e30)
    peak_score = jnp.max(scores, axis=-1)
    weights = jnp.where(live_mask, jnp.exp(scores - peak_score[..., None]), 0.0)
    weight_total = jnp.sum(weights, axis=-1)
    weighted = jnp.einsum(
        "bkgp,bpkh->bkgh",
        weights.astype(jnp.bfloat16),
        value_block,
        preferred_element_type=jnp.float32,
    )
    peak_score, weight_total, weighted = joined(
        (peak_score, weight_total, weighted), "tensor", combine_parts
    )
    score_new = (
        jnp.einsum(
            "bkgh,bkh->bkg",
            query_heads,
            key_new.reshape(beam_rows, kv_heads, HEAD_DIM),
            preferred_element_type=jnp.float32,
        )
        * score_scale
    )
    value_rows = value_new.reshape(beam_rows, kv_heads, HEAD_DIM).astype(jnp.float32)[:, :, None, :]
    attended = (
        finish_heads(peak_score, weight_total, weighted, score_new, value_rows)
        .reshape(beam_rows, model_width)
        .astype(jnp.bfloat16)
    )
    attended_cols = lax.dynamic_slice_in_dim(attended, tensor_index * width_part, width_part, 1)
    mixed_cols = lax.psum_scatter(
        lax.dot_general(
            output_weight,
            attended_cols,
            (((0,), (1,)), ((), ())),
            preferred_element_type=jnp.float32,
        ),
        "tensor",
        scatter_dimension=0,
        tiled=True,
    )
    return (normed_hidden_input.astype(jnp.float32) + mixed_cols.T).astype(jnp.bfloat16)


def solution(mesh):
    matched = mesh.shape["tensor"] == 8 and mesh.shape["bank"] == 2
    return jax.shard_map(
        matched_body if matched else body,
        mesh=mesh,
        in_specs=(
            P(("groups", "bank"), "tensor"),
            P(("groups", "bank")),
            P(("groups", "bank")),
            P("tensor", None),
            P("tensor", None),
            P("tensor", None),
            P("bank", "tensor", None),
            P("bank", None, "tensor"),
            P(("groups", "bank"), "tensor", None),
            P(("groups", "bank"), "tensor", None),
        ),
        out_specs=P(("groups", "bank"), "tensor"),
        check_vma=False,
    )
```

```python
import jax
import jax.numpy as jnp
from jax import lax
from jax.experimental import pallas as pl
from jax.experimental.pallas import tpu as pltpu
from jax.sharding import PartitionSpec as P

HEAD_DIM = 128
F32 = jnp.float32
BF16 = jnp.bfloat16
CHUNKS = 1
MIB = 1024 * 1024


def whole():
    return pl.BlockSpec(memory_space=pltpu.VMEM)


def big():
    return pl.BlockSpec(memory_space=pltpu.HBM)


def scalar():
    return pl.BlockSpec(memory_space=pltpu.SMEM)


def in_hbm(array):
    return pltpu.with_memory_space_constraint(array, pltpu.HBM)


def shape(*dims, dtype=F32):
    return jax.ShapeDtypeStruct(dims, dtype)


def iota(dims, axis):
    return lax.broadcasted_iota(jnp.int32, dims, axis)


def params(mib=4):
    return pltpu.CompilerParams(vmem_limit_bytes=mib * MIB)


def exchanged(slot):
    return slot & ~3 | (slot & 1) << 1 | slot >> 1 & 1


def rank_of(place, bank, slot):
    return place ^ (slot + bank * (exchanged(slot) - slot))


def adapter_column(refs, bank, count):
    columns = []
    for ref in refs:
        rows = ref.shape[1]
        index = jnp.broadcast_to(ref[...].astype(F32), (rows, rows))
        diagonal = iota((rows, rows), 0) == iota((rows, rows), 1)
        columns.append(jnp.sum(jnp.where(diagonal, index, 0.0), axis=1, keepdims=True))
    column = jnp.concatenate(columns, axis=0).astype(jnp.int32) - bank * count
    return jnp.broadcast_to(column, (column.shape[0], HEAD_DIM))


def start_slots(parity, place, bank, w_ref, w_buf, sems):
    count, depth, width = w_buf.shape
    part = depth // CHUNKS
    copies = []
    for c in range(CHUNKS):
        rows = pl.ds(c * part, part)
        copies.append([])
        for s in range(count):
            target = rank_of(place[0], bank[0], 2 * s + parity)
            columns = pl.ds(pl.multiple_of((2 * target + bank[0]) * width, width), width)
            copy = pltpu.make_async_copy(
                w_ref.at[rows, columns], w_buf.at[s, rows], sems.at[s, c]
            )
            copy.start()
            copies[-1].append(copy)
    return copies


def slot_products(x, copies, w_buf, out):
    count, depth, width = w_buf.shape
    part = depth // CHUNKS
    for c, chunk in enumerate(copies):
        rows = slice(c * part, (c + 1) * part)
        for s, copy in enumerate(chunk):
            copy.wait()
            columns = slice(s * width, (s + 1) * width)
            product = jnp.dot(x[:, rows], w_buf[s, rows], preferred_element_type=F32)
            out[:, columns] = product if c == 0 else out[:, columns] + product


def wait_all(copies):
    for copy in copies:
        copy.wait()


def start_parts(source, target, sems):
    part = source.shape[0] // sems.shape[0]
    copies = []
    for c in range(sems.shape[0]):
        rows = pl.ds(c * part, part)
        copies.append(pltpu.make_async_copy(source.at[rows], target.at[rows], sems.at[c]))
        copies[-1].start()
    return copies


def fetch_kernel(ref, out, sems):
    wait_all(start_parts(ref, out, sems))


def fetch(array):
    return pl.pallas_call(
        fetch_kernel,
        in_specs=[big()],
        out_specs=whole(),
        out_shape=jax.ShapeDtypeStruct(array.shape, array.dtype),
        scratch_shapes=[pltpu.SemaphoreType.DMA((2,))],
        compiler_params=params(),
        cost_estimate=pl.CostEstimate(
            flops=0, bytes_accessed=2 * array.size, transcendentals=0
        ),
        name="fetch",
    )(array)


def slot_scratch(wq, ranks):
    half, depth = ranks // 2, wq.shape[0]
    return [
        pltpu.VMEM((half, depth, wq.shape[1] // ranks // 2), BF16),
        pltpu.SemaphoreType.DMA((half, CHUNKS)),
    ]


def beam_rows(x_ref, other_ref):
    rows = [x_ref[...].astype(F32), other_ref[...].astype(F32)]
    return jnp.concatenate(rows, axis=0).astype(BF16)


def project_sent_kernel(
    place, bank, own_ref, came_ref, x_ref, other_ref, down_ref, w_ref, *refs
):
    out, inner, column_out, w_buf, sems = refs
    copies = start_slots(1, place, bank, w_ref, w_buf, sems)
    x = beam_rows(x_ref, other_ref)
    adapters, rank, depth = down_ref.shape
    every = lax.dot_general(
        x,
        down_ref[...].reshape(adapters * rank, depth),
        (((1,), (1,)), ((), ())),
        preferred_element_type=F32,
    )
    column = adapter_column((own_ref, came_ref), bank[0], adapters)
    column_out[...] = column
    lane = iota(column.shape, 1)
    per = HEAD_DIM // rank
    total = jnp.zeros(column.shape, F32)
    for j in range(adapters // per):
        part = every[:, j * HEAD_DIM : (j + 1) * HEAD_DIM]
        total += jnp.where(lane // rank + j * per == column, part, 0.0)
    inner[...] = total
    out[:, out.shape[1] - HEAD_DIM :] = total
    slot_products(x, copies, w_buf, out)


def project_sent(place, bank, index, x, other, down, wq, ranks):
    rows = 2 * x.shape[0]
    return pl.pallas_call(
        project_sent_kernel,
        in_specs=[scalar()] * 2 + [whole()] * 5 + [big()],
        out_specs=[whole()] * 3,
        out_shape=[
            shape(rows, wq.shape[1] // 4 + HEAD_DIM),
            shape(rows, HEAD_DIM),
            shape(rows, HEAD_DIM, dtype=jnp.int32),
        ],
        scratch_shapes=slot_scratch(wq, ranks),
        compiler_params=params(8),
        cost_estimate=pl.CostEstimate(
            flops=rows * (wq.size // 2 + 2 * down.size),
            bytes_accessed=wq.size // 2 + 2 * down.size,
            transcendentals=0,
        ),
        name="project_sent",
    )(place, bank, *[i.reshape(1, -1) for i in index], x, other, down, wq)


def project_kept_kernel(
    place, bank, length, x_ref, other_ref, w_ref, out, length_out, w_buf, sems
):
    copies = start_slots(0, place, bank, w_ref, w_buf, sems)
    beams = x_ref.shape[0]
    row = iota(length_out.shape, 0)
    limit = jnp.zeros(length_out.shape, jnp.int32)
    for beam in range(beams):
        limit = jnp.where(row // (length_out.shape[0] // beams) == beam, length[beam], limit)
    length_out[...] = limit
    x = beam_rows(x_ref, other_ref)
    slot_products(x, copies, w_buf, out)


def project_kept(place, bank, length, x, other, wq, ranks):
    beams = x.shape[0]
    return pl.pallas_call(
        project_kept_kernel,
        in_specs=[scalar()] * 3 + [whole()] * 2 + [big()],
        out_specs=[whole()] * 2,
        out_shape=[
            shape(2 * beams, wq.shape[1] // 4),
            shape(beams * wq.shape[1] // ranks // HEAD_DIM, HEAD_DIM, dtype=jnp.int32),
        ],
        scratch_shapes=slot_scratch(wq, ranks),
        compiler_params=params(8),
        cost_estimate=pl.CostEstimate(
            flops=beams * wq.size, bytes_accessed=2 * wq.size, transcendentals=0
        ),
        name="project_kept",
    )(place, bank, length, x, other, wq)


def keyval_kernel(x_ref, w_ref, out):
    ranks = out.shape[0]
    total = jnp.dot(x_ref[...], w_ref[...], preferred_element_type=F32)
    high = total.astype(BF16).astype(F32)
    low = total - high
    for r in range(ranks):
        key = slice(r * HEAD_DIM, (r + 1) * HEAD_DIM)
        value = slice((ranks + r) * HEAD_DIM, (ranks + r + 1) * HEAD_DIM)
        pieces = [high[:, key], low[:, key], total[:, value]]
        out[r] = jnp.concatenate(pieces, axis=0)


def keyval(x, wkv, ranks):
    beams, depth = x.shape
    return pl.pallas_call(
        keyval_kernel,
        in_specs=[whole()] * 2,
        out_specs=whole(),
        out_shape=shape(ranks, 3 * beams, HEAD_DIM),
        compiler_params=params(),
        cost_estimate=pl.CostEstimate(
            flops=2 * beams * wkv.size, bytes_accessed=2 * wkv.size, transcendentals=0
        ),
        name="keyval",
    )(x, wkv)


def correct_kernel(bank, column_ref, up_ref, *refs):
    *parts, own_out, other_out = refs
    total = parts[0][...]
    for part in parts[1:]:
        total += part[...]
    count, rank, width = up_ref.shape
    half = width // 2
    inner = total[:, half:].astype(BF16).astype(F32)
    column = column_ref[...]
    lane = iota(column.shape, 1)
    per = HEAD_DIM // rank
    spread = jnp.concatenate(
        [
            jnp.where(lane // rank + j * per == column, inner, 0.0)
            for j in range(count // per)
        ],
        axis=1,
    ).astype(BF16)
    delta = jnp.dot(
        spread, up_ref[...].reshape(count * rank, width), preferred_element_type=F32
    )
    rows = own_out.shape[0]
    for side in range(2):
        columns = slice(side * half, (side + 1) * half)
        part = delta[:, columns] + jnp.where(bank[0] == side, total[:, :half], 0.0)
        own_out[:, columns] = part[:rows]
        other_out[:, columns] = part[rows:]


def correct(bank, column, up, parts):
    rows = parts[0].shape[0]
    out = shape(rows // 2, up.shape[2])
    return pl.pallas_call(
        correct_kernel,
        in_specs=[scalar()] + [whole()] * (2 + len(parts)),
        out_specs=[whole()] * 2,
        out_shape=[out, out],
        compiler_params=params(),
        cost_estimate=pl.CostEstimate(
            flops=2 * rows * up.size, bytes_accessed=2 * up.size, transcendentals=0
        ),
        name="correct",
    )(bank, column, up, *parts)


def part_kernel(kept_ref, inner_ref, came_ref, *outs):
    width = outs[0].shape[1] - HEAD_DIM
    inner = inner_ref[...] + came_ref[:, len(outs) * width :]
    for i, out in enumerate(outs):
        columns = slice(i * width, (i + 1) * width)
        out[:, :width] = kept_ref[:, columns] + came_ref[:, columns]
        out[:, width:] = inner


def part(kept, inner, came, slots):
    rows, width = kept.shape
    return pl.pallas_call(
        part_kernel,
        in_specs=[whole()] * 3,
        out_specs=[whole()] * slots,
        out_shape=[shape(rows, width // slots + HEAD_DIM)] * slots,
        compiler_params=params(),
        name="part",
    )(kept, inner, came)


def rotate(v, cosine, sine):
    return v * cosine + pltpu.roll(v, HEAD_DIM // 2, 1) * sine


def rotate_kernel(own_ref, came_ref, cos_ref, sin_ref, q_ref, rows_ref):
    cosine, sine = cos_ref[...], sin_ref[...]
    for g in range(own_ref.shape[1] // HEAD_DIM):
        columns = slice(g * HEAD_DIM, (g + 1) * HEAD_DIM)
        rows_ref[:, g, :] = rotate(own_ref[:, columns] + came_ref[:, columns], cosine, sine)
    q_ref[0] = rows_ref[...].reshape(q_ref.shape[1:]).astype(BF16)


def rotated(own, came, cosine, sine):
    rows, width = own.shape
    heads = width // HEAD_DIM
    return pl.pallas_call(
        rotate_kernel,
        in_specs=[whole()] * 4,
        out_specs=whole(),
        out_shape=shape(1, rows * heads, HEAD_DIM, dtype=BF16),
        scratch_shapes=[pltpu.VMEM((rows, heads, HEAD_DIM), F32)],
        compiler_params=params(),
        name="rotate",
    )(own, came, cosine, sine)


def join_kernel(*refs):
    *parts, out_ref = refs
    for i, part in enumerate(parts):
        out_ref[i] = part[0]


def join(parts):
    return pl.pallas_call(
        join_kernel,
        in_specs=[whole()] * len(parts),
        out_specs=whole(),
        out_shape=shape(len(parts), *parts[0].shape[1:], dtype=parts[0].dtype),
        compiler_params=params(),
        name="join",
    )(*parts)


def attend_kernel(slots, earlier, place, bank, length_ref, q_ref, k_ref, v_ref, *refs):
    before, out_ref = refs[:-1], refs[-1]
    if earlier:
        *before, keyval_ref = before
    beams, positions, _ = k_ref.shape
    rows = q_ref.shape[1]
    group = rows // beams
    row, lane = iota((rows, HEAD_DIM), 0), iota((rows, HEAD_DIM), 1)
    left = length_ref[...] - place[0] * positions
    live = jnp.concatenate(
        [lane + first < left for first in range(0, positions, HEAD_DIM)], axis=1
    )
    for i, slot in enumerate(slots):
        head = rank_of(place[0], bank[0], slot)
        columns = pl.ds(pl.multiple_of(head * HEAD_DIM, HEAD_DIM), HEAD_DIM)
        query = q_ref[i].astype(F32)
        scores = jnp.concatenate(
            [
                lax.dot_general(
                    query[beam * group : (beam + 1) * group].astype(BF16),
                    k_ref[beam, :, columns],
                    (((1,), (1,)), ((), ())),
                    preferred_element_type=F32,
                )
                for beam in range(beams)
            ],
            axis=0,
        ) * (1.0 / HEAD_DIM**0.5)
        scores = jnp.where(live, scores, -1e30)
        peak = jnp.max(scores, axis=1, keepdims=True)
        weights = jnp.where(live, jnp.exp(scores - peak), 0.0)
        total = jnp.sum(weights, axis=1, keepdims=True)
        values = [
            jnp.dot(
                weights[beam * group : (beam + 1) * group].astype(BF16),
                v_ref[beam, :, columns],
                preferred_element_type=F32,
            )
            for beam in range(beams)
        ]
        stats = jnp.where(lane == row % group, peak, 0.0)
        stats += jnp.where(lane == group + row % group, total, 0.0)
        stats = jnp.sum(stats.reshape(beams, group, HEAD_DIM), axis=1)
        high = stats.astype(BF16).astype(F32)
        middle = (stats - high).astype(BF16).astype(F32)
        low = stats - high - middle
        tail = high + pltpu.roll(middle, 2 * group, 1) + pltpu.roll(low, 4 * group, 1)
        if earlier:
            block = jnp.concatenate(values + [tail, keyval_ref[head]], axis=0)
            out_ref[head] = block.astype(BF16)
        else:
            block = jnp.concatenate(values + [tail, jnp.zeros_like(tail)], axis=0)
            out_ref[i] = block.astype(BF16)
    if earlier:
        done = [(ref, i) for ref in before for i in range(ref.shape[0])]
        for slot, (ref, i) in zip(earlier, done):
            head = rank_of(place[0], bank[0], slot)
            held = ref[i].astype(F32)[: rows + beams]
            out_ref[head] = jnp.concatenate([held, keyval_ref[head]], axis=0).astype(BF16)


def attend(place, bank, length, queries, keys, values, slots, earlier=(), before=()):
    count, rows, _ = queries.shape
    beams, positions, _ = keys.shape
    return pl.pallas_call(
        lambda *refs: attend_kernel(slots, earlier, *refs),
        in_specs=[scalar()] * 2 + [whole()] * (4 + len(before)),
        out_specs=whole(),
        out_shape=shape(
            count + len(earlier), rows + (4 if earlier else 2) * beams, HEAD_DIM, dtype=BF16
        ),
        compiler_params=params(),
        cost_estimate=pl.CostEstimate(
            flops=4 * rows * count * positions * HEAD_DIM,
            bytes_accessed=4 * beams * positions * HEAD_DIM * (16 if earlier else count),
            transcendentals=rows * count * positions,
        ),
        name="attend",
    )(place, bank, length, queries, keys, values, *before)


def combine_kernel(parts_ref, q_ref, cos_ref, sin_ref, out_ref, joined):
    ranks = parts_ref.shape[0]
    beams, group, _ = joined.shape
    rows = beams * group

    def by_row(v):
        return jnp.broadcast_to(v[:, None, :], (beams, group, HEAD_DIM)).reshape(rows, HEAD_DIM)

    lane = iota((rows, HEAD_DIM), 1)
    own_lane = lane == iota((rows, HEAD_DIM), 0) % group

    def spread(v):
        return jnp.sum(jnp.where(own_lane, by_row(v), 0.0), axis=1, keepdims=True)

    blocks = [parts_ref[s].astype(F32) for s in range(ranks)]
    sums = blocks[0][rows + beams :]
    for block in blocks[1:]:
        sums += block[rows + beams :]
    key = sums[:beams] + sums[beams : 2 * beams]
    key = rotate(key, cos_ref[...], sin_ref[...]).astype(BF16).astype(F32)
    value = sums[2 * beams :].astype(BF16).astype(F32)
    score = jnp.sum(q_ref[0].astype(F32) * by_row(key), axis=1, keepdims=True) * (
        1.0 / HEAD_DIM**0.5
    )
    score = jnp.where(own_lane, score, 0.0).reshape(beams, group, HEAD_DIM)
    score = jnp.sum(score, axis=1)
    used = iota((beams, HEAD_DIM), 1) < group
    peaks, totals = [], []
    top = score
    for block in blocks:
        tail = block[rows : rows + beams]
        stats = tail
        for turn in (2, 4):
            stats = stats + pltpu.roll(tail, HEAD_DIM - turn * group, 1)
        peaks.append(jnp.where(used, stats, 0.0))
        totals.append(jnp.where(used, pltpu.roll(stats, HEAD_DIM - group, 1), 0.0))
        top = jnp.maximum(top, peaks[-1])
    factors = [jnp.exp(peak - top) for peak in peaks]
    new = jnp.exp(score - top)
    everything = new
    for factor, total in zip(factors, totals):
        everything += factor * total
    result = spread(new.astype(BF16).astype(F32) / everything) * by_row(value)
    for block, factor in zip(blocks, factors):
        result += spread(factor / everything) * block[:rows]
    joined[...] = result.reshape(joined.shape)
    for g in range(group):
        out_ref[:, g * HEAD_DIM : (g + 1) * HEAD_DIM] = joined[:, g, :].astype(BF16)


def combine(parts, query, cosine, sine):
    beams = cosine.shape[0]
    group = query.shape[1] // beams
    return pl.pallas_call(
        combine_kernel,
        in_specs=[whole()] * 4,
        out_specs=whole(),
        out_shape=shape(beams, group * HEAD_DIM, dtype=BF16),
        scratch_shapes=[pltpu.VMEM((beams, group, HEAD_DIM), F32)],
        compiler_params=params(),
        name="combine",
    )(parts, query, cosine, sine)


def output_kernel(x_ref, w_ref, out):
    count, _, width = out.shape
    for s in range(count):
        columns = slice(s * width, (s + 1) * width)
        total = jnp.dot(x_ref[...], w_ref[:, columns], preferred_element_type=F32)
        out[s] = total.astype(BF16)


def output(x, weight, ranks):
    beams = x.shape[0]
    return pl.pallas_call(
        output_kernel,
        in_specs=[whole()] * 2,
        out_specs=whole(),
        out_shape=shape(ranks, beams, weight.shape[1] // ranks, dtype=BF16),
        compiler_params=params(),
        cost_estimate=pl.CostEstimate(
            flops=2 * beams * weight.size, bytes_accessed=2 * weight.size, transcendentals=0
        ),
        name="output",
    )(x, weight)


def residual_kernel(x_ref, parts_ref, out_ref):
    total = jnp.sum(parts_ref[...].astype(F32), axis=0)
    out_ref[...] = (x_ref[...].astype(F32) + total).astype(BF16)


def residual(x, parts):
    return pl.pallas_call(
        residual_kernel,
        in_specs=[whole()] * 2,
        out_specs=whole(),
        out_shape=jax.ShapeDtypeStruct(x.shape, BF16),
        compiler_params=params(),
        name="residual",
    )(x, parts)


def swapped(x):
    return lax.ppermute(x, "bank", [(0, 1), (1, 0)])


def traded(blocks):
    return lax.all_to_all(blocks, "tensor", 0, 0, tiled=True)


def hop(x, bit):
    pairs = []
    for rank in range(lax.axis_size("tensor")):
        for bank in range(2):
            pairs.append((2 * rank + bank, 2 * rank_of(rank, bank, bit) + bank))
    return lax.ppermute(x, ("tensor", "bank"), pairs)


def matched_body(
    normed_hidden_input,
    beam_adapter_index,
    beam_cache_length,
    query_weight,
    keyvalue_weight,
    output_weight,
    lowrank_down_factors,
    lowrank_up_factors,
    paged_key_cache,
    paged_value_cache,
):
    x = normed_hidden_input
    ranks = lax.axis_size("tensor")
    place = lax.axis_index("tensor").astype(jnp.int32).reshape(1)
    bank = lax.axis_index("bank").astype(jnp.int32).reshape(1)
    index = (beam_adapter_index, swapped(beam_adapter_index))
    x_other = swapped(x)
    lane = jnp.arange(HEAD_DIM, dtype=jnp.int32)
    half = HEAD_DIM // 2
    frequency = jnp.power(500000.0, -2.0 * (lane % half).astype(F32) / HEAD_DIM)
    angles = beam_cache_length.astype(F32)[:, None] * frequency[None, :]
    cosine = jnp.cos(angles)
    sine = jnp.where(lane < half, -1.0, 1.0) * jnp.sin(angles)
    weight = in_hbm(query_weight)
    down = fetch(in_hbm(lowrank_down_factors.swapaxes(1, 2)))
    sent, inner, column = project_sent(place, bank, index, x, x_other, down, weight, ranks)
    came = hop(sent, 1)
    kept, length = project_kept(
        place, bank, beam_cache_length, x, x_other, weight, ranks
    )
    kept, *sent = part(kept, inner, came, ranks // 2)
    near = 4, 6, 2
    parts = [kept] + [hop(sent[slot // 2 - 1], slot) for slot in near]
    own_x, _ = lax.optimization_barrier((x, kept))
    token, parts = lax.optimization_barrier((keyval(own_x, keyvalue_weight, ranks), parts))
    own, other = correct(bank, column, lowrank_up_factors, parts)
    query = rotated(own, swapped(other), cosine, sine)

    def attended_part(queries, slots, **more):
        cache = paged_key_cache, paged_value_cache
        return attend(place, bank, length, queries, *cache, slots, **more)

    gathered = join([query] + [hop(query, slot) for slot in near])
    came = hop(gathered, 1)
    done = attended_part(gathered, (0, *near))
    odd = tuple(slot + 1 for slot in (0, *near))
    partial = attended_part(came, odd, earlier=(0, *near), before=(done, token))
    attended = combine(traded(partial), query, cosine, sine)
    return residual(x, traded(output(attended, output_weight, ranks)))


def joined(x, axis, combine):
    everything = jax.tree.map(lambda part: lax.all_gather(part, axis), x)
    leading = jax.tree.map(lambda part: part[0], everything)

    def turn(k, so_far):
        return combine(so_far, jax.tree.map(lambda part: part[k], everything))

    return lax.fori_loop(1, lax.axis_size(axis), turn, leading)


def apply_rotary(values, positions, head_size):
    row_count, col_count = values.shape
    half_size = head_size // 2
    frequency = jnp.power(500000.0, -2.0 * jnp.arange(half_size, dtype=jnp.float32) / head_size)
    angles = positions.astype(jnp.float32)[:, None] * frequency[None, :]
    cosine_table = jnp.cos(angles)[:, None, :]
    sine_table = jnp.sin(angles)[:, None, :]
    shaped = values.reshape(row_count, col_count // head_size, 2, half_size)
    first_half = shaped[:, :, 0]
    second_half = shaped[:, :, 1]
    rotated = jnp.stack(
        [
            first_half * cosine_table - second_half * sine_table,
            second_half * cosine_table + first_half * sine_table,
        ],
        axis=2,
    )
    return rotated.reshape(row_count, col_count)


def combine_parts(first_part, second_part):
    peak_one, total_one, weighted_one = first_part
    peak_two, total_two, weighted_two = second_part
    peak_both = jnp.maximum(peak_one, peak_two)
    factor_one = jnp.exp(peak_one - peak_both)
    factor_two = jnp.exp(peak_two - peak_both)
    return (
        peak_both,
        total_one * factor_one + total_two * factor_two,
        weighted_one * factor_one[..., None] + weighted_two * factor_two[..., None],
    )


def finish_heads(peak_score, weight_total, weighted, score_new, value_rows):
    peak_final = jnp.maximum(peak_score, score_new)
    old_factor = jnp.exp(peak_score - peak_final)
    new_weight = jnp.exp(score_new - peak_final)
    weight_total = weight_total * old_factor + new_weight
    weighted = (
        weighted * old_factor[..., None]
        + new_weight.astype(jnp.bfloat16).astype(jnp.float32)[..., None] * value_rows
    )
    return weighted / weight_total[..., None]


def body(
    normed_hidden_input,
    beam_adapter_index,
    beam_cache_length,
    query_weight,
    keyvalue_weight,
    output_weight,
    lowrank_down_factors,
    lowrank_up_factors,
    paged_key_cache,
    paged_value_cache,
):
    beam_rows, width_part = normed_hidden_input.shape
    model_width = query_weight.shape[1]
    kv_width = keyvalue_weight.shape[1] // 2
    head_count = model_width // HEAD_DIM
    kv_heads = kv_width // HEAD_DIM
    group_size = head_count // kv_heads
    tensor_index = lax.axis_index("tensor")
    query_part = jnp.dot(normed_hidden_input, query_weight, preferred_element_type=jnp.float32)
    keyval_part = jnp.dot(normed_hidden_input, keyvalue_weight, preferred_element_type=jnp.float32)
    down_all, up_all = (
        lax.all_gather(lowrank_down_factors, "bank", axis=0, tiled=True),
        lax.all_gather(lowrank_up_factors, "bank", axis=0, tiled=True),
    )
    inner_part = jnp.einsum(
        "ci,cim->cm",
        normed_hidden_input,
        down_all[beam_adapter_index],
        preferred_element_type=jnp.float32,
    )
    inner_total = lax.psum(inner_part, "tensor").astype(jnp.bfloat16)
    lowrank_delta = jnp.einsum(
        "mc,mct->mt", inner_total, up_all[beam_adapter_index], preferred_element_type=jnp.float32
    )
    query_total, keyval = lax.psum((query_part, keyval_part), "tensor")
    delta_total = lax.all_gather(lowrank_delta, "tensor", axis=1, tiled=True)
    query_rotated = apply_rotary(query_total + delta_total, beam_cache_length, HEAD_DIM).astype(
        jnp.bfloat16
    )
    key_new = apply_rotary(keyval[:, :kv_width], beam_cache_length, HEAD_DIM).astype(jnp.bfloat16)
    value_new = keyval[:, kv_width:].astype(jnp.bfloat16)
    position_count = paged_key_cache.shape[1]
    query_heads = query_rotated.reshape(beam_rows, kv_heads, group_size, HEAD_DIM)
    key_block = paged_key_cache.reshape(beam_rows, position_count, kv_heads, HEAD_DIM)
    value_block = paged_value_cache.reshape(beam_rows, position_count, kv_heads, HEAD_DIM)
    score_scale = 1.0 / HEAD_DIM**0.5
    scores = (
        jnp.einsum("bkgh,bpkh->bkgp", query_heads, key_block, preferred_element_type=jnp.float32)
        * score_scale
    )
    position_ids = tensor_index * position_count + jnp.arange(position_count)
    live_mask = (position_ids[None, :] < beam_cache_length[:, None])[:, None, None, :]
    scores = jnp.where(live_mask, scores, -1e30)
    peak_score = jnp.max(scores, axis=-1)
    weights = jnp.where(live_mask, jnp.exp(scores - peak_score[..., None]), 0.0)
    weight_total = jnp.sum(weights, axis=-1)
    weighted = jnp.einsum(
        "bkgp,bpkh->bkgh",
        weights.astype(jnp.bfloat16),
        value_block,
        preferred_element_type=jnp.float32,
    )
    peak_score, weight_total, weighted = joined(
        (peak_score, weight_total, weighted), "tensor", combine_parts
    )
    score_new = (
        jnp.einsum(
            "bkgh,bkh->bkg",
            query_heads,
            key_new.reshape(beam_rows, kv_heads, HEAD_DIM),
            preferred_element_type=jnp.float32,
        )
        * score_scale
    )
    value_rows = value_new.reshape(beam_rows, kv_heads, HEAD_DIM).astype(jnp.float32)[:, :, None, :]
    attended = (
        finish_heads(peak_score, weight_total, weighted, score_new, value_rows)
        .reshape(beam_rows, model_width)
        .astype(jnp.bfloat16)
    )
    attended_cols = lax.dynamic_slice_in_dim(attended, tensor_index * width_part, width_part, 1)
    mixed_cols = lax.psum_scatter(
        lax.dot_general(
            output_weight,
            attended_cols,
            (((0,), (1,)), ((), ())),
            preferred_element_type=jnp.float32,
        ),
        "tensor",
        scatter_dimension=0,
        tiled=True,
    )
    return (normed_hidden_input.astype(jnp.float32) + mixed_cols.T).astype(jnp.bfloat16)


def solution(mesh):
    matched = mesh.shape["tensor"] == 8 and mesh.shape["bank"] == 2
    return jax.shard_map(
        matched_body if matched else body,
        mesh=mesh,
        in_specs=(
            P(("groups", "bank"), "tensor"),
            P(("groups", "bank")),
            P(("groups", "bank")),
            P("tensor", None),
            P("tensor", None),
            P("tensor", None),
            P("bank", "tensor", None),
            P("bank", None, "tensor"),
            P(("groups", "bank"), "tensor", None),
            P(("groups", "bank"), "tensor", None),
        ),
        out_specs=P(("groups", "bank"), "tensor"),
        check_vma=False,
    )
```

```python
import jax
import jax.numpy as jnp
from jax import lax
from jax.experimental import pallas as pl
from jax.experimental.pallas import tpu as pltpu
from jax.sharding import PartitionSpec as P

HEAD_DIM = 128
F32 = jnp.float32
BF16 = jnp.bfloat16
CHUNKS = 2
MIB = 1024 * 1024


def whole():
    return pl.BlockSpec(memory_space=pltpu.VMEM)


def big():
    return pl.BlockSpec(memory_space=pltpu.HBM)


def scalar():
    return pl.BlockSpec(memory_space=pltpu.SMEM)


def in_hbm(array):
    return pltpu.with_memory_space_constraint(array, pltpu.HBM)


def shape(*dims, dtype=F32):
    return jax.ShapeDtypeStruct(dims, dtype)


def iota(dims, axis):
    return lax.broadcasted_iota(jnp.int32, dims, axis)


def params(mib=4):
    return pltpu.CompilerParams(vmem_limit_bytes=mib * MIB)


def exchanged(slot):
    return slot & ~3 | (slot & 1) << 1 | slot >> 1 & 1


def rank_of(place, bank, slot):
    return place ^ (slot + bank * (exchanged(slot) - slot))


def adapter_column(refs, bank, count):
    columns = []
    for ref in refs:
        rows = ref.shape[1]
        index = jnp.broadcast_to(ref[...].astype(F32), (rows, rows))
        diagonal = iota((rows, rows), 0) == iota((rows, rows), 1)
        columns.append(jnp.sum(jnp.where(diagonal, index, 0.0), axis=1, keepdims=True))
    column = jnp.concatenate(columns, axis=0).astype(jnp.int32) - bank * count
    return jnp.broadcast_to(column, (column.shape[0], HEAD_DIM))


def start_slots(parity, place, bank, w_ref, w_buf, sems):
    count, depth, width = w_buf.shape
    part = depth // CHUNKS
    copies = []
    for c in range(CHUNKS):
        rows = pl.ds(c * part, part)
        copies.append([])
        for s in range(count):
            target = rank_of(place[0], bank[0], 2 * s + parity)
            columns = pl.ds(pl.multiple_of((2 * target + bank[0]) * width, width), width)
            copy = pltpu.make_async_copy(
                w_ref.at[rows, columns], w_buf.at[s, rows], sems.at[s, c]
            )
            copy.start()
            copies[-1].append(copy)
    return copies


def slot_products(x, copies, w_buf, out):
    count, depth, width = w_buf.shape
    part = depth // CHUNKS
    for c, chunk in enumerate(copies):
        rows = slice(c * part, (c + 1) * part)
        for s, copy in enumerate(chunk):
            copy.wait()
            columns = slice(s * width, (s + 1) * width)
            product = jnp.dot(x[:, rows], w_buf[s, rows], preferred_element_type=F32)
            out[:, columns] = product if c == 0 else out[:, columns] + product


def wait_all(copies):
    for copy in copies:
        copy.wait()


def start_parts(source, target, sems):
    part = source.shape[0] // sems.shape[0]
    copies = []
    for c in range(sems.shape[0]):
        rows = pl.ds(c * part, part)
        copies.append(pltpu.make_async_copy(source.at[rows], target.at[rows], sems.at[c]))
        copies[-1].start()
    return copies


def fetch_kernel(ref, out, sems):
    wait_all(start_parts(ref, out, sems))


def fetch(array):
    return pl.pallas_call(
        fetch_kernel,
        in_specs=[big()],
        out_specs=whole(),
        out_shape=jax.ShapeDtypeStruct(array.shape, array.dtype),
        scratch_shapes=[pltpu.SemaphoreType.DMA((2,))],
        compiler_params=params(),
        cost_estimate=pl.CostEstimate(
            flops=0, bytes_accessed=2 * array.size, transcendentals=0
        ),
        name="fetch",
    )(array)


def slot_scratch(wq, ranks):
    half, depth = ranks // 2, wq.shape[0]
    return [
        pltpu.VMEM((half, depth, wq.shape[1] // ranks // 2), BF16),
        pltpu.SemaphoreType.DMA((half, CHUNKS)),
    ]


def beam_rows(x_ref, other_ref):
    rows = [x_ref[...].astype(F32), other_ref[...].astype(F32)]
    return jnp.concatenate(rows, axis=0).astype(BF16)


def project_sent_kernel(
    place, bank, own_ref, came_ref, x_ref, other_ref, down_ref, w_ref, *refs
):
    out, inner, column_out, w_buf, sems = refs
    copies = start_slots(1, place, bank, w_ref, w_buf, sems)
    x = beam_rows(x_ref, other_ref)
    adapters, rank, depth = down_ref.shape
    every = lax.dot_general(
        x,
        down_ref[...].reshape(adapters * rank, depth),
        (((1,), (1,)), ((), ())),
        preferred_element_type=F32,
    )
    column = adapter_column((own_ref, came_ref), bank[0], adapters)
    column_out[...] = column
    lane = iota(column.shape, 1)
    per = HEAD_DIM // rank
    total = jnp.zeros(column.shape, F32)
    for j in range(adapters // per):
        part = every[:, j * HEAD_DIM : (j + 1) * HEAD_DIM]
        total += jnp.where(lane // rank + j * per == column, part, 0.0)
    inner[...] = total
    out[:, out.shape[1] - HEAD_DIM :] = total
    slot_products(x, copies, w_buf, out)


def project_sent(place, bank, index, x, other, down, wq, ranks):
    rows = 2 * x.shape[0]
    return pl.pallas_call(
        project_sent_kernel,
        in_specs=[scalar()] * 2 + [whole()] * 5 + [big()],
        out_specs=[whole()] * 3,
        out_shape=[
            shape(rows, wq.shape[1] // 4 + HEAD_DIM),
            shape(rows, HEAD_DIM),
            shape(rows, HEAD_DIM, dtype=jnp.int32),
        ],
        scratch_shapes=slot_scratch(wq, ranks),
        compiler_params=params(8),
        cost_estimate=pl.CostEstimate(
            flops=rows * (wq.size // 2 + 2 * down.size),
            bytes_accessed=wq.size // 2 + 2 * down.size,
            transcendentals=0,
        ),
        name="project_sent",
    )(place, bank, *[i.reshape(1, -1) for i in index], x, other, down, wq)


def project_kept_kernel(
    place, bank, length, x_ref, other_ref, w_ref, out, length_out, w_buf, sems
):
    copies = start_slots(0, place, bank, w_ref, w_buf, sems)
    beams = x_ref.shape[0]
    row = iota(length_out.shape, 0)
    limit = jnp.zeros(length_out.shape, jnp.int32)
    for beam in range(beams):
        limit = jnp.where(row // (length_out.shape[0] // beams) == beam, length[beam], limit)
    length_out[...] = limit
    x = beam_rows(x_ref, other_ref)
    slot_products(x, copies, w_buf, out)


def project_kept(place, bank, length, x, other, wq, ranks):
    beams = x.shape[0]
    return pl.pallas_call(
        project_kept_kernel,
        in_specs=[scalar()] * 3 + [whole()] * 2 + [big()],
        out_specs=[whole()] * 2,
        out_shape=[
            shape(2 * beams, wq.shape[1] // 4),
            shape(beams * wq.shape[1] // ranks // HEAD_DIM, HEAD_DIM, dtype=jnp.int32),
        ],
        scratch_shapes=slot_scratch(wq, ranks),
        compiler_params=params(8),
        cost_estimate=pl.CostEstimate(
            flops=beams * wq.size, bytes_accessed=2 * wq.size, transcendentals=0
        ),
        name="project_kept",
    )(place, bank, length, x, other, wq)


def keyval_kernel(x_ref, w_ref, out):
    ranks = out.shape[0]
    total = jnp.dot(x_ref[...], w_ref[...], preferred_element_type=F32)
    high = total.astype(BF16).astype(F32)
    low = total - high
    for r in range(ranks):
        key = slice(r * HEAD_DIM, (r + 1) * HEAD_DIM)
        value = slice((ranks + r) * HEAD_DIM, (ranks + r + 1) * HEAD_DIM)
        pieces = [high[:, key], low[:, key], total[:, value]]
        out[r] = jnp.concatenate(pieces, axis=0)


def keyval(x, wkv, ranks):
    beams, depth = x.shape
    return pl.pallas_call(
        keyval_kernel,
        in_specs=[whole()] * 2,
        out_specs=whole(),
        out_shape=shape(ranks, 3 * beams, HEAD_DIM),
        compiler_params=params(),
        cost_estimate=pl.CostEstimate(
            flops=2 * beams * wkv.size, bytes_accessed=2 * wkv.size, transcendentals=0
        ),
        name="keyval",
    )(x, wkv)


def correct_kernel(bank, column_ref, up_ref, *refs):
    *parts, own_out, other_out = refs
    total = parts[0][...]
    for part in parts[1:]:
        total += part[...]
    count, rank, width = up_ref.shape
    half = width // 2
    inner = total[:, half:].astype(BF16).astype(F32)
    column = column_ref[...]
    lane = iota(column.shape, 1)
    per = HEAD_DIM // rank
    spread = jnp.concatenate(
        [
            jnp.where(lane // rank + j * per == column, inner, 0.0)
            for j in range(count // per)
        ],
        axis=1,
    ).astype(BF16)
    delta = jnp.dot(
        spread, up_ref[...].reshape(count * rank, width), preferred_element_type=F32
    )
    rows = own_out.shape[0]
    for side in range(2):
        columns = slice(side * half, (side + 1) * half)
        part = delta[:, columns] + jnp.where(bank[0] == side, total[:, :half], 0.0)
        own_out[:, columns] = part[:rows]
        other_out[:, columns] = part[rows:]


def correct(bank, column, up, parts):
    rows = parts[0].shape[0]
    out = shape(rows // 2, up.shape[2])
    return pl.pallas_call(
        correct_kernel,
        in_specs=[scalar()] + [whole()] * (2 + len(parts)),
        out_specs=[whole()] * 2,
        out_shape=[out, out],
        compiler_params=params(),
        cost_estimate=pl.CostEstimate(
            flops=2 * rows * up.size, bytes_accessed=2 * up.size, transcendentals=0
        ),
        name="correct",
    )(bank, column, up, *parts)


def part_kernel(kept_ref, inner_ref, came_ref, *outs):
    width = outs[0].shape[1] - HEAD_DIM
    inner = inner_ref[...] + came_ref[:, len(outs) * width :]
    for i, out in enumerate(outs):
        columns = slice(i * width, (i + 1) * width)
        out[:, :width] = kept_ref[:, columns] + came_ref[:, columns]
        out[:, width:] = inner


def part(kept, inner, came, slots):
    rows, width = kept.shape
    return pl.pallas_call(
        part_kernel,
        in_specs=[whole()] * 3,
        out_specs=[whole()] * slots,
        out_shape=[shape(rows, width // slots + HEAD_DIM)] * slots,
        compiler_params=params(),
        name="part",
    )(kept, inner, came)


def rotate(v, cosine, sine):
    return v * cosine + pltpu.roll(v, HEAD_DIM // 2, 1) * sine


def rotate_kernel(own_ref, came_ref, cos_ref, sin_ref, q_ref, rows_ref):
    cosine, sine = cos_ref[...], sin_ref[...]
    for g in range(own_ref.shape[1] // HEAD_DIM):
        columns = slice(g * HEAD_DIM, (g + 1) * HEAD_DIM)
        rows_ref[:, g, :] = rotate(own_ref[:, columns] + came_ref[:, columns], cosine, sine)
    q_ref[0] = rows_ref[...].reshape(q_ref.shape[1:]).astype(BF16)


def rotated(own, came, cosine, sine):
    rows, width = own.shape
    heads = width // HEAD_DIM
    return pl.pallas_call(
        rotate_kernel,
        in_specs=[whole()] * 4,
        out_specs=whole(),
        out_shape=shape(1, rows * heads, HEAD_DIM, dtype=BF16),
        scratch_shapes=[pltpu.VMEM((rows, heads, HEAD_DIM), F32)],
        compiler_params=params(),
        name="rotate",
    )(own, came, cosine, sine)


def join_kernel(*refs):
    *parts, out_ref = refs
    for i, part in enumerate(parts):
        out_ref[i] = part[0]


def join(parts):
    return pl.pallas_call(
        join_kernel,
        in_specs=[whole()] * len(parts),
        out_specs=whole(),
        out_shape=shape(len(parts), *parts[0].shape[1:], dtype=parts[0].dtype),
        compiler_params=params(),
        name="join",
    )(*parts)


def attend_kernel(slots, earlier, place, bank, length_ref, q_ref, k_ref, v_ref, *refs):
    before, out_ref = refs[:-1], refs[-1]
    if earlier:
        *before, keyval_ref = before
    beams, positions, _ = k_ref.shape
    rows = q_ref.shape[1]
    group = rows // beams
    row, lane = iota((rows, HEAD_DIM), 0), iota((rows, HEAD_DIM), 1)
    left = length_ref[...] - place[0] * positions
    live = jnp.concatenate(
        [lane + first < left for first in range(0, positions, HEAD_DIM)], axis=1
    )
    for i, slot in enumerate(slots):
        head = rank_of(place[0], bank[0], slot)
        columns = pl.ds(pl.multiple_of(head * HEAD_DIM, HEAD_DIM), HEAD_DIM)
        query = q_ref[i].astype(F32)
        scores = jnp.concatenate(
            [
                lax.dot_general(
                    query[beam * group : (beam + 1) * group].astype(BF16),
                    k_ref[beam, :, columns],
                    (((1,), (1,)), ((), ())),
                    preferred_element_type=F32,
                )
                for beam in range(beams)
            ],
            axis=0,
        ) * (1.0 / HEAD_DIM**0.5)
        scores = jnp.where(live, scores, -1e30)
        peak = jnp.max(scores, axis=1, keepdims=True)
        weights = jnp.where(live, jnp.exp(scores - peak), 0.0)
        total = jnp.sum(weights, axis=1, keepdims=True)
        values = [
            jnp.dot(
                weights[beam * group : (beam + 1) * group].astype(BF16),
                v_ref[beam, :, columns],
                preferred_element_type=F32,
            )
            for beam in range(beams)
        ]
        stats = jnp.where(lane == row % group, peak, 0.0)
        stats += jnp.where(lane == group + row % group, total, 0.0)
        stats = jnp.sum(stats.reshape(beams, group, HEAD_DIM), axis=1)
        high = stats.astype(BF16).astype(F32)
        middle = (stats - high).astype(BF16).astype(F32)
        low = stats - high - middle
        tail = high + pltpu.roll(middle, 2 * group, 1) + pltpu.roll(low, 4 * group, 1)
        if earlier:
            block = jnp.concatenate(values + [tail, keyval_ref[head]], axis=0)
            out_ref[head] = block.astype(BF16)
        else:
            block = jnp.concatenate(values + [tail, jnp.zeros_like(tail)], axis=0)
            out_ref[i] = block.astype(BF16)
    if earlier:
        done = [(ref, i) for ref in before for i in range(ref.shape[0])]
        for slot, (ref, i) in zip(earlier, done):
            head = rank_of(place[0], bank[0], slot)
            held = ref[i].astype(F32)[: rows + beams]
            out_ref[head] = jnp.concatenate([held, keyval_ref[head]], axis=0).astype(BF16)


def attend(place, bank, length, queries, keys, values, slots, earlier=(), before=()):
    count, rows, _ = queries.shape
    beams, positions, _ = keys.shape
    return pl.pallas_call(
        lambda *refs: attend_kernel(slots, earlier, *refs),
        in_specs=[scalar()] * 2 + [whole()] * (4 + len(before)),
        out_specs=whole(),
        out_shape=shape(
            count + len(earlier), rows + (4 if earlier else 2) * beams, HEAD_DIM, dtype=BF16
        ),
        compiler_params=params(),
        cost_estimate=pl.CostEstimate(
            flops=4 * rows * count * positions * HEAD_DIM,
            bytes_accessed=4 * beams * positions * HEAD_DIM * (16 if earlier else count),
            transcendentals=rows * count * positions,
        ),
        name="attend",
    )(place, bank, length, queries, keys, values, *before)


def combine_kernel(parts_ref, q_ref, cos_ref, sin_ref, out_ref, joined):
    ranks = parts_ref.shape[0]
    beams, group, _ = joined.shape
    rows = beams * group

    def by_row(v):
        return jnp.broadcast_to(v[:, None, :], (beams, group, HEAD_DIM)).reshape(rows, HEAD_DIM)

    lane = iota((rows, HEAD_DIM), 1)
    own_lane = lane == iota((rows, HEAD_DIM), 0) % group

    def spread(v):
        return jnp.sum(jnp.where(own_lane, by_row(v), 0.0), axis=1, keepdims=True)

    blocks = [parts_ref[s].astype(F32) for s in range(ranks)]
    sums = blocks[0][rows + beams :]
    for block in blocks[1:]:
        sums += block[rows + beams :]
    key = sums[:beams] + sums[beams : 2 * beams]
    key = rotate(key, cos_ref[...], sin_ref[...]).astype(BF16).astype(F32)
    value = sums[2 * beams :].astype(BF16).astype(F32)
    score = jnp.sum(q_ref[0].astype(F32) * by_row(key), axis=1, keepdims=True) * (
        1.0 / HEAD_DIM**0.5
    )
    score = jnp.where(own_lane, score, 0.0).reshape(beams, group, HEAD_DIM)
    score = jnp.sum(score, axis=1)
    used = iota((beams, HEAD_DIM), 1) < group
    peaks, totals = [], []
    top = score
    for block in blocks:
        tail = block[rows : rows + beams]
        stats = tail
        for turn in (2, 4):
            stats = stats + pltpu.roll(tail, HEAD_DIM - turn * group, 1)
        peaks.append(jnp.where(used, stats, 0.0))
        totals.append(jnp.where(used, pltpu.roll(stats, HEAD_DIM - group, 1), 0.0))
        top = jnp.maximum(top, peaks[-1])
    factors = [jnp.exp(peak - top) for peak in peaks]
    new = jnp.exp(score - top)
    everything = new
    for factor, total in zip(factors, totals):
        everything += factor * total
    result = spread(new.astype(BF16).astype(F32) / everything) * by_row(value)
    for block, factor in zip(blocks, factors):
        result += spread(factor / everything) * block[:rows]
    joined[...] = result.reshape(joined.shape)
    for g in range(group):
        out_ref[:, g * HEAD_DIM : (g + 1) * HEAD_DIM] = joined[:, g, :].astype(BF16)


def output_kernel(parts_ref, q_ref, cos_ref, sin_ref, w_ref, out, joined, attended):
    combine_kernel(parts_ref, q_ref, cos_ref, sin_ref, attended, joined)
    count, _, width = out.shape
    for s in range(count):
        columns = slice(s * width, (s + 1) * width)
        total = jnp.dot(attended[...], w_ref[:, columns], preferred_element_type=F32)
        out[s] = total.astype(BF16)


def output(parts, query, cosine, sine, weight, ranks):
    beams = cosine.shape[0]
    group = query.shape[1] // beams
    return pl.pallas_call(
        output_kernel,
        in_specs=[whole()] * 5,
        out_specs=whole(),
        out_shape=shape(ranks, beams, weight.shape[1] // ranks, dtype=BF16),
        scratch_shapes=[
            pltpu.VMEM((beams, group, HEAD_DIM), F32),
            pltpu.VMEM((beams, group * HEAD_DIM), BF16),
        ],
        compiler_params=params(),
        cost_estimate=pl.CostEstimate(
            flops=2 * beams * weight.size, bytes_accessed=2 * weight.size, transcendentals=0
        ),
        name="output",
    )(parts, query, cosine, sine, weight)


def residual_kernel(x_ref, parts_ref, out_ref):
    total = jnp.sum(parts_ref[...].astype(F32), axis=0)
    out_ref[...] = (x_ref[...].astype(F32) + total).astype(BF16)


def residual(x, parts):
    return pl.pallas_call(
        residual_kernel,
        in_specs=[whole()] * 2,
        out_specs=whole(),
        out_shape=jax.ShapeDtypeStruct(x.shape, BF16),
        compiler_params=params(),
        name="residual",
    )(x, parts)


def swapped(x):
    return lax.ppermute(x, "bank", [(0, 1), (1, 0)])


def traded(blocks):
    return lax.all_to_all(blocks, "tensor", 0, 0, tiled=True)


def hop(x, bit):
    pairs = []
    for rank in range(lax.axis_size("tensor")):
        for bank in range(2):
            pairs.append((2 * rank + bank, 2 * rank_of(rank, bank, bit) + bank))
    return lax.ppermute(x, ("tensor", "bank"), pairs)


def matched_body(
    normed_hidden_input,
    beam_adapter_index,
    beam_cache_length,
    query_weight,
    keyvalue_weight,
    output_weight,
    lowrank_down_factors,
    lowrank_up_factors,
    paged_key_cache,
    paged_value_cache,
):
    x = normed_hidden_input
    ranks = lax.axis_size("tensor")
    place = lax.axis_index("tensor").astype(jnp.int32).reshape(1)
    bank = lax.axis_index("bank").astype(jnp.int32).reshape(1)
    index = (beam_adapter_index, swapped(beam_adapter_index))
    x_other = swapped(x)
    lane = jnp.arange(HEAD_DIM, dtype=jnp.int32)
    half = HEAD_DIM // 2
    frequency = jnp.power(500000.0, -2.0 * (lane % half).astype(F32) / HEAD_DIM)
    angles = beam_cache_length.astype(F32)[:, None] * frequency[None, :]
    cosine = jnp.cos(angles)
    sine = jnp.where(lane < half, -1.0, 1.0) * jnp.sin(angles)
    weight = in_hbm(query_weight)
    down = fetch(in_hbm(lowrank_down_factors.swapaxes(1, 2)))
    sent, inner, column = project_sent(place, bank, index, x, x_other, down, weight, ranks)
    came = hop(sent, 1)
    kept, length = project_kept(
        place, bank, beam_cache_length, x, x_other, weight, ranks
    )
    kept, *sent = part(kept, inner, came, ranks // 2)
    near = 4, 6, 2
    parts = [kept] + [hop(sent[slot // 2 - 1], slot) for slot in near]
    own_x, _ = lax.optimization_barrier((x, kept))
    token, parts = lax.optimization_barrier((keyval(own_x, keyvalue_weight, ranks), parts))
    own, other = correct(bank, column, lowrank_up_factors, parts)
    query = rotated(own, swapped(other), cosine, sine)

    def attended_part(queries, slots, **more):
        cache = paged_key_cache, paged_value_cache
        return attend(place, bank, length, queries, *cache, slots, **more)

    gathered = join([query] + [hop(query, slot) for slot in near])
    came = hop(gathered, 1)
    done = attended_part(gathered, (0, *near))
    odd = tuple(slot + 1 for slot in (0, *near))
    partial = attended_part(came, odd, earlier=(0, *near), before=(done, token))
    mixed = output(traded(partial), query, cosine, sine, output_weight, ranks)
    return residual(x, traded(mixed))


def joined(x, axis, combine):
    everything = jax.tree.map(lambda part: lax.all_gather(part, axis), x)
    leading = jax.tree.map(lambda part: part[0], everything)

    def turn(k, so_far):
        return combine(so_far, jax.tree.map(lambda part: part[k], everything))

    return lax.fori_loop(1, lax.axis_size(axis), turn, leading)


def apply_rotary(values, positions, head_size):
    row_count, col_count = values.shape
    half_size = head_size // 2
    frequency = jnp.power(500000.0, -2.0 * jnp.arange(half_size, dtype=jnp.float32) / head_size)
    angles = positions.astype(jnp.float32)[:, None] * frequency[None, :]
    cosine_table = jnp.cos(angles)[:, None, :]
    sine_table = jnp.sin(angles)[:, None, :]
    shaped = values.reshape(row_count, col_count // head_size, 2, half_size)
    first_half = shaped[:, :, 0]
    second_half = shaped[:, :, 1]
    rotated = jnp.stack(
        [
            first_half * cosine_table - second_half * sine_table,
            second_half * cosine_table + first_half * sine_table,
        ],
        axis=2,
    )
    return rotated.reshape(row_count, col_count)


def combine_parts(first_part, second_part):
    peak_one, total_one, weighted_one = first_part
    peak_two, total_two, weighted_two = second_part
    peak_both = jnp.maximum(peak_one, peak_two)
    factor_one = jnp.exp(peak_one - peak_both)
    factor_two = jnp.exp(peak_two - peak_both)
    return (
        peak_both,
        total_one * factor_one + total_two * factor_two,
        weighted_one * factor_one[..., None] + weighted_two * factor_two[..., None],
    )


def finish_heads(peak_score, weight_total, weighted, score_new, value_rows):
    peak_final = jnp.maximum(peak_score, score_new)
    old_factor = jnp.exp(peak_score - peak_final)
    new_weight = jnp.exp(score_new - peak_final)
    weight_total = weight_total * old_factor + new_weight
    weighted = (
        weighted * old_factor[..., None]
        + new_weight.astype(jnp.bfloat16).astype(jnp.float32)[..., None] * value_rows
    )
    return weighted / weight_total[..., None]


def body(
    normed_hidden_input,
    beam_adapter_index,
    beam_cache_length,
    query_weight,
    keyvalue_weight,
    output_weight,
    lowrank_down_factors,
    lowrank_up_factors,
    paged_key_cache,
    paged_value_cache,
):
    beam_rows, width_part = normed_hidden_input.shape
    model_width = query_weight.shape[1]
    kv_width = keyvalue_weight.shape[1] // 2
    head_count = model_width // HEAD_DIM
    kv_heads = kv_width // HEAD_DIM
    group_size = head_count // kv_heads
    tensor_index = lax.axis_index("tensor")
    query_part = jnp.dot(normed_hidden_input, query_weight, preferred_element_type=jnp.float32)
    keyval_part = jnp.dot(normed_hidden_input, keyvalue_weight, preferred_element_type=jnp.float32)
    down_all, up_all = (
        lax.all_gather(lowrank_down_factors, "bank", axis=0, tiled=True),
        lax.all_gather(lowrank_up_factors, "bank", axis=0, tiled=True),
    )
    inner_part = jnp.einsum(
        "ci,cim->cm",
        normed_hidden_input,
        down_all[beam_adapter_index],
        preferred_element_type=jnp.float32,
    )
    inner_total = lax.psum(inner_part, "tensor").astype(jnp.bfloat16)
    lowrank_delta = jnp.einsum(
        "mc,mct->mt", inner_total, up_all[beam_adapter_index], preferred_element_type=jnp.float32
    )
    query_total, keyval = lax.psum((query_part, keyval_part), "tensor")
    delta_total = lax.all_gather(lowrank_delta, "tensor", axis=1, tiled=True)
    query_rotated = apply_rotary(query_total + delta_total, beam_cache_length, HEAD_DIM).astype(
        jnp.bfloat16
    )
    key_new = apply_rotary(keyval[:, :kv_width], beam_cache_length, HEAD_DIM).astype(jnp.bfloat16)
    value_new = keyval[:, kv_width:].astype(jnp.bfloat16)
    position_count = paged_key_cache.shape[1]
    query_heads = query_rotated.reshape(beam_rows, kv_heads, group_size, HEAD_DIM)
    key_block = paged_key_cache.reshape(beam_rows, position_count, kv_heads, HEAD_DIM)
    value_block = paged_value_cache.reshape(beam_rows, position_count, kv_heads, HEAD_DIM)
    score_scale = 1.0 / HEAD_DIM**0.5
    scores = (
        jnp.einsum("bkgh,bpkh->bkgp", query_heads, key_block, preferred_element_type=jnp.float32)
        * score_scale
    )
    position_ids = tensor_index * position_count + jnp.arange(position_count)
    live_mask = (position_ids[None, :] < beam_cache_length[:, None])[:, None, None, :]
    scores = jnp.where(live_mask, scores, -1e30)
    peak_score = jnp.max(scores, axis=-1)
    weights = jnp.where(live_mask, jnp.exp(scores - peak_score[..., None]), 0.0)
    weight_total = jnp.sum(weights, axis=-1)
    weighted = jnp.einsum(
        "bkgp,bpkh->bkgh",
        weights.astype(jnp.bfloat16),
        value_block,
        preferred_element_type=jnp.float32,
    )
    peak_score, weight_total, weighted = joined(
        (peak_score, weight_total, weighted), "tensor", combine_parts
    )
    score_new = (
        jnp.einsum(
            "bkgh,bkh->bkg",
            query_heads,
            key_new.reshape(beam_rows, kv_heads, HEAD_DIM),
            preferred_element_type=jnp.float32,
        )
        * score_scale
    )
    value_rows = value_new.reshape(beam_rows, kv_heads, HEAD_DIM).astype(jnp.float32)[:, :, None, :]
    attended = (
        finish_heads(peak_score, weight_total, weighted, score_new, value_rows)
        .reshape(beam_rows, model_width)
        .astype(jnp.bfloat16)
    )
    attended_cols = lax.dynamic_slice_in_dim(attended, tensor_index * width_part, width_part, 1)
    mixed_cols = lax.psum_scatter(
        lax.dot_general(
            output_weight,
            attended_cols,
            (((0,), (1,)), ((), ())),
            preferred_element_type=jnp.float32,
        ),
        "tensor",
        scatter_dimension=0,
        tiled=True,
    )
    return (normed_hidden_input.astype(jnp.float32) + mixed_cols.T).astype(jnp.bfloat16)


def solution(mesh):
    matched = mesh.shape["tensor"] == 8 and mesh.shape["bank"] == 2
    return jax.shard_map(
        matched_body if matched else body,
        mesh=mesh,
        in_specs=(
            P(("groups", "bank"), "tensor"),
            P(("groups", "bank")),
            P(("groups", "bank")),
            P("tensor", None),
            P("tensor", None),
            P("tensor", None),
            P("bank", "tensor", None),
            P("bank", None, "tensor"),
            P(("groups", "bank"), "tensor", None),
            P(("groups", "bank"), "tensor", None),
        ),
        out_specs=P(("groups", "bank"), "tensor"),
        check_vma=False,
    )
```

```python
import jax
import jax.numpy as jnp
from jax import lax
from jax.experimental import pallas as pl
from jax.experimental.pallas import tpu as pltpu
from jax.sharding import PartitionSpec as P

HEAD_DIM = 128
F32 = jnp.float32
BF16 = jnp.bfloat16
CHUNKS = 4
MIB = 1024 * 1024


def whole():
    return pl.BlockSpec(memory_space=pltpu.VMEM)


def big():
    return pl.BlockSpec(memory_space=pltpu.HBM)


def scalar():
    return pl.BlockSpec(memory_space=pltpu.SMEM)


def in_hbm(array):
    return pltpu.with_memory_space_constraint(array, pltpu.HBM)


def shape(*dims, dtype=F32):
    return jax.ShapeDtypeStruct(dims, dtype)


def iota(dims, axis):
    return lax.broadcasted_iota(jnp.int32, dims, axis)


def params(mib=4):
    return pltpu.CompilerParams(vmem_limit_bytes=mib * MIB)


def exchanged(slot):
    return slot & ~3 | (slot & 1) << 1 | slot >> 1 & 1


def rank_of(place, bank, slot):
    return place ^ (slot + bank * (exchanged(slot) - slot))


def adapter_column(refs, bank, count):
    columns = []
    for ref in refs:
        rows = ref.shape[1]
        index = jnp.broadcast_to(ref[...].astype(F32), (rows, rows))
        diagonal = iota((rows, rows), 0) == iota((rows, rows), 1)
        columns.append(jnp.sum(jnp.where(diagonal, index, 0.0), axis=1, keepdims=True))
    column = jnp.concatenate(columns, axis=0).astype(jnp.int32) - bank * count
    return jnp.broadcast_to(column, (column.shape[0], HEAD_DIM))


def start_slots(parity, place, bank, w_ref, w_buf, sems):
    count, depth, width = w_buf.shape
    part = depth // CHUNKS
    copies = []
    for c in range(CHUNKS):
        rows = pl.ds(c * part, part)
        copies.append([])
        for s in range(count):
            target = rank_of(place[0], bank[0], 2 * s + parity)
            columns = pl.ds(pl.multiple_of((2 * target + bank[0]) * width, width), width)
            copy = pltpu.make_async_copy(
                w_ref.at[rows, columns], w_buf.at[s, rows], sems.at[s, c]
            )
            copy.start()
            copies[-1].append(copy)
    return copies


def slot_products(x, copies, w_buf, out):
    count, depth, width = w_buf.shape
    part = depth // CHUNKS
    for c, chunk in enumerate(copies):
        rows = slice(c * part, (c + 1) * part)
        for s, copy in enumerate(chunk):
            copy.wait()
            columns = slice(s * width, (s + 1) * width)
            product = jnp.dot(x[:, rows], w_buf[s, rows], preferred_element_type=F32)
            out[:, columns] = product if c == 0 else out[:, columns] + product


def wait_all(copies):
    for copy in copies:
        copy.wait()


def start_parts(source, target, sems):
    part = source.shape[0] // sems.shape[0]
    copies = []
    for c in range(sems.shape[0]):
        rows = pl.ds(c * part, part)
        copies.append(pltpu.make_async_copy(source.at[rows], target.at[rows], sems.at[c]))
        copies[-1].start()
    return copies


def fetch_kernel(ref, out, sems):
    wait_all(start_parts(ref, out, sems))


def fetch(array):
    return pl.pallas_call(
        fetch_kernel,
        in_specs=[big()],
        out_specs=whole(),
        out_shape=jax.ShapeDtypeStruct(array.shape, array.dtype),
        scratch_shapes=[pltpu.SemaphoreType.DMA((2,))],
        compiler_params=params(),
        cost_estimate=pl.CostEstimate(
            flops=0, bytes_accessed=2 * array.size, transcendentals=0
        ),
        name="fetch",
    )(array)


def slot_scratch(wq, ranks):
    half, depth = ranks // 2, wq.shape[0]
    return [
        pltpu.VMEM((half, depth, wq.shape[1] // ranks // 2), BF16),
        pltpu.SemaphoreType.DMA((half, CHUNKS)),
    ]


def beam_rows(x_ref, other_ref):
    rows = [x_ref[...].astype(F32), other_ref[...].astype(F32)]
    return jnp.concatenate(rows, axis=0).astype(BF16)


def project_sent_kernel(
    place, bank, own_ref, came_ref, x_ref, other_ref, down_ref, w_ref, *refs
):
    out, inner, column_out, w_buf, sems = refs
    copies = start_slots(1, place, bank, w_ref, w_buf, sems)
    x = beam_rows(x_ref, other_ref)
    adapters, rank, depth = down_ref.shape
    every = lax.dot_general(
        x,
        down_ref[...].reshape(adapters * rank, depth),
        (((1,), (1,)), ((), ())),
        preferred_element_type=F32,
    )
    column = adapter_column((own_ref, came_ref), bank[0], adapters)
    column_out[...] = column
    lane = iota(column.shape, 1)
    per = HEAD_DIM // rank
    total = jnp.zeros(column.shape, F32)
    for j in range(adapters // per):
        part = every[:, j * HEAD_DIM : (j + 1) * HEAD_DIM]
        total += jnp.where(lane // rank + j * per == column, part, 0.0)
    inner[...] = total
    out[:, out.shape[1] - HEAD_DIM :] = total
    slot_products(x, copies, w_buf, out)


def project_sent(place, bank, index, x, other, down, wq, ranks):
    rows = 2 * x.shape[0]
    return pl.pallas_call(
        project_sent_kernel,
        in_specs=[scalar()] * 2 + [whole()] * 5 + [big()],
        out_specs=[whole()] * 3,
        out_shape=[
            shape(rows, wq.shape[1] // 4 + HEAD_DIM),
            shape(rows, HEAD_DIM),
            shape(rows, HEAD_DIM, dtype=jnp.int32),
        ],
        scratch_shapes=slot_scratch(wq, ranks),
        compiler_params=params(8),
        cost_estimate=pl.CostEstimate(
            flops=rows * (wq.size // 2 + 2 * down.size),
            bytes_accessed=wq.size // 2 + 2 * down.size,
            transcendentals=0,
        ),
        name="project_sent",
    )(place, bank, *[i.reshape(1, -1) for i in index], x, other, down, wq)


def project_kept_kernel(
    place, bank, length, x_ref, other_ref, w_ref, out, length_out, w_buf, sems
):
    copies = start_slots(0, place, bank, w_ref, w_buf, sems)
    beams = x_ref.shape[0]
    row = iota(length_out.shape, 0)
    limit = jnp.zeros(length_out.shape, jnp.int32)
    for beam in range(beams):
        limit = jnp.where(row // (length_out.shape[0] // beams) == beam, length[beam], limit)
    length_out[...] = limit
    x = beam_rows(x_ref, other_ref)
    slot_products(x, copies, w_buf, out)


def project_kept(place, bank, length, x, other, wq, ranks):
    beams = x.shape[0]
    return pl.pallas_call(
        project_kept_kernel,
        in_specs=[scalar()] * 3 + [whole()] * 2 + [big()],
        out_specs=[whole()] * 2,
        out_shape=[
            shape(2 * beams, wq.shape[1] // 4),
            shape(beams * wq.shape[1] // ranks // HEAD_DIM, HEAD_DIM, dtype=jnp.int32),
        ],
        scratch_shapes=slot_scratch(wq, ranks),
        compiler_params=params(8),
        cost_estimate=pl.CostEstimate(
            flops=beams * wq.size, bytes_accessed=2 * wq.size, transcendentals=0
        ),
        name="project_kept",
    )(place, bank, length, x, other, wq)


def keyval_kernel(x_ref, w_ref, out):
    ranks = out.shape[0]
    total = jnp.dot(x_ref[...], w_ref[...], preferred_element_type=F32)
    high = total.astype(BF16).astype(F32)
    low = total - high
    for r in range(ranks):
        key = slice(r * HEAD_DIM, (r + 1) * HEAD_DIM)
        value = slice((ranks + r) * HEAD_DIM, (ranks + r + 1) * HEAD_DIM)
        pieces = [high[:, key], low[:, key], total[:, value]]
        out[r] = jnp.concatenate(pieces, axis=0)


def keyval(x, wkv, ranks):
    beams, depth = x.shape
    return pl.pallas_call(
        keyval_kernel,
        in_specs=[whole()] * 2,
        out_specs=whole(),
        out_shape=shape(ranks, 3 * beams, HEAD_DIM),
        compiler_params=params(),
        cost_estimate=pl.CostEstimate(
            flops=2 * beams * wkv.size, bytes_accessed=2 * wkv.size, transcendentals=0
        ),
        name="keyval",
    )(x, wkv)


def correct_kernel(bank, column_ref, up_ref, *refs):
    *parts, own_out, other_out = refs
    total = parts[0][...]
    for part in parts[1:]:
        total += part[...]
    count, rank, width = up_ref.shape
    half = width // 2
    inner = total[:, half:].astype(BF16).astype(F32)
    column = column_ref[...]
    lane = iota(column.shape, 1)
    per = HEAD_DIM // rank
    spread = jnp.concatenate(
        [
            jnp.where(lane // rank + j * per == column, inner, 0.0)
            for j in range(count // per)
        ],
        axis=1,
    ).astype(BF16)
    delta = jnp.dot(
        spread, up_ref[...].reshape(count * rank, width), preferred_element_type=F32
    )
    rows = own_out.shape[0]
    for side in range(2):
        columns = slice(side * half, (side + 1) * half)
        part = delta[:, columns] + jnp.where(bank[0] == side, total[:, :half], 0.0)
        own_out[:, columns] = part[:rows]
        other_out[:, columns] = part[rows:]


def correct(bank, column, up, parts):
    rows = parts[0].shape[0]
    out = shape(rows // 2, up.shape[2])
    return pl.pallas_call(
        correct_kernel,
        in_specs=[scalar()] + [whole()] * (2 + len(parts)),
        out_specs=[whole()] * 2,
        out_shape=[out, out],
        compiler_params=params(),
        cost_estimate=pl.CostEstimate(
            flops=2 * rows * up.size, bytes_accessed=2 * up.size, transcendentals=0
        ),
        name="correct",
    )(bank, column, up, *parts)


def part_kernel(kept_ref, inner_ref, came_ref, *outs):
    width = outs[0].shape[1] - HEAD_DIM
    inner = inner_ref[...] + came_ref[:, len(outs) * width :]
    for i, out in enumerate(outs):
        columns = slice(i * width, (i + 1) * width)
        out[:, :width] = kept_ref[:, columns] + came_ref[:, columns]
        out[:, width:] = inner


def part(kept, inner, came, slots):
    rows, width = kept.shape
    return pl.pallas_call(
        part_kernel,
        in_specs=[whole()] * 3,
        out_specs=[whole()] * slots,
        out_shape=[shape(rows, width // slots + HEAD_DIM)] * slots,
        compiler_params=params(),
        name="part",
    )(kept, inner, came)


def rotate(v, cosine, sine):
    return v * cosine + pltpu.roll(v, HEAD_DIM // 2, 1) * sine


def rotate_kernel(own_ref, came_ref, cos_ref, sin_ref, q_ref, rows_ref):
    cosine, sine = cos_ref[...], sin_ref[...]
    for g in range(own_ref.shape[1] // HEAD_DIM):
        columns = slice(g * HEAD_DIM, (g + 1) * HEAD_DIM)
        rows_ref[:, g, :] = rotate(own_ref[:, columns] + came_ref[:, columns], cosine, sine)
    q_ref[0] = rows_ref[...].reshape(q_ref.shape[1:]).astype(BF16)


def rotated(own, came, cosine, sine):
    rows, width = own.shape
    heads = width // HEAD_DIM
    return pl.pallas_call(
        rotate_kernel,
        in_specs=[whole()] * 4,
        out_specs=whole(),
        out_shape=shape(1, rows * heads, HEAD_DIM, dtype=BF16),
        scratch_shapes=[pltpu.VMEM((rows, heads, HEAD_DIM), F32)],
        compiler_params=params(),
        name="rotate",
    )(own, came, cosine, sine)


def join_kernel(*refs):
    *parts, out_ref = refs
    for i, part in enumerate(parts):
        out_ref[i] = part[0]


def join(parts):
    return pl.pallas_call(
        join_kernel,
        in_specs=[whole()] * len(parts),
        out_specs=whole(),
        out_shape=shape(len(parts), *parts[0].shape[1:], dtype=parts[0].dtype),
        compiler_params=params(),
        name="join",
    )(*parts)


def attend_kernel(slots, earlier, place, bank, length_ref, q_ref, k_ref, v_ref, *refs):
    before, out_ref = refs[:-1], refs[-1]
    if earlier:
        *before, keyval_ref = before
    beams, positions, _ = k_ref.shape
    rows = q_ref.shape[1]
    group = rows // beams
    row, lane = iota((rows, HEAD_DIM), 0), iota((rows, HEAD_DIM), 1)
    left = length_ref[...] - place[0] * positions
    live = jnp.concatenate(
        [lane + first < left for first in range(0, positions, HEAD_DIM)], axis=1
    )
    for i, slot in enumerate(slots):
        head = rank_of(place[0], bank[0], slot)
        columns = pl.ds(pl.multiple_of(head * HEAD_DIM, HEAD_DIM), HEAD_DIM)
        query = q_ref[i].astype(F32)
        scores = jnp.concatenate(
            [
                lax.dot_general(
                    query[beam * group : (beam + 1) * group].astype(BF16),
                    k_ref[beam, :, columns],
                    (((1,), (1,)), ((), ())),
                    preferred_element_type=F32,
                )
                for beam in range(beams)
            ],
            axis=0,
        ) * (1.0 / HEAD_DIM**0.5)
        scores = jnp.where(live, scores, -1e30)
        peak = jnp.max(scores, axis=1, keepdims=True)
        weights = jnp.where(live, jnp.exp(scores - peak), 0.0)
        total = jnp.sum(weights, axis=1, keepdims=True)
        values = [
            jnp.dot(
                weights[beam * group : (beam + 1) * group].astype(BF16),
                v_ref[beam, :, columns],
                preferred_element_type=F32,
            )
            for beam in range(beams)
        ]
        stats = jnp.where(lane == row % group, peak, 0.0)
        stats += jnp.where(lane == group + row % group, total, 0.0)
        stats = jnp.sum(stats.reshape(beams, group, HEAD_DIM), axis=1)
        high = stats.astype(BF16).astype(F32)
        middle = (stats - high).astype(BF16).astype(F32)
        low = stats - high - middle
        tail = high + pltpu.roll(middle, 2 * group, 1) + pltpu.roll(low, 4 * group, 1)
        if earlier:
            block = jnp.concatenate(values + [tail, keyval_ref[head]], axis=0)
            out_ref[head] = block.astype(BF16)
        else:
            block = jnp.concatenate(values + [tail, jnp.zeros_like(tail)], axis=0)
            out_ref[i] = block.astype(BF16)
    if earlier:
        done = [(ref, i) for ref in before for i in range(ref.shape[0])]
        for slot, (ref, i) in zip(earlier, done):
            head = rank_of(place[0], bank[0], slot)
            held = ref[i].astype(F32)[: rows + beams]
            out_ref[head] = jnp.concatenate([held, keyval_ref[head]], axis=0).astype(BF16)


def attend(place, bank, length, queries, keys, values, slots, earlier=(), before=()):
    count, rows, _ = queries.shape
    beams, positions, _ = keys.shape
    return pl.pallas_call(
        lambda *refs: attend_kernel(slots, earlier, *refs),
        in_specs=[scalar()] * 2 + [whole()] * (4 + len(before)),
        out_specs=whole(),
        out_shape=shape(
            count + len(earlier), rows + (4 if earlier else 2) * beams, HEAD_DIM, dtype=BF16
        ),
        compiler_params=params(),
        cost_estimate=pl.CostEstimate(
            flops=4 * rows * count * positions * HEAD_DIM,
            bytes_accessed=4 * beams * positions * HEAD_DIM * (16 if earlier else count),
            transcendentals=rows * count * positions,
        ),
        name="attend",
    )(place, bank, length, queries, keys, values, *before)


def combine_kernel(parts_ref, q_ref, cos_ref, sin_ref, out_ref, joined):
    ranks = parts_ref.shape[0]
    beams, group, _ = joined.shape
    rows = beams * group

    def by_row(v):
        return jnp.broadcast_to(v[:, None, :], (beams, group, HEAD_DIM)).reshape(rows, HEAD_DIM)

    lane = iota((rows, HEAD_DIM), 1)
    own_lane = lane == iota((rows, HEAD_DIM), 0) % group

    def spread(v):
        return jnp.sum(jnp.where(own_lane, by_row(v), 0.0), axis=1, keepdims=True)

    blocks = [parts_ref[s].astype(F32) for s in range(ranks)]
    sums = blocks[0][rows + beams :]
    for block in blocks[1:]:
        sums += block[rows + beams :]
    key = sums[:beams] + sums[beams : 2 * beams]
    key = rotate(key, cos_ref[...], sin_ref[...]).astype(BF16).astype(F32)
    value = sums[2 * beams :].astype(BF16).astype(F32)
    score = jnp.sum(q_ref[0].astype(F32) * by_row(key), axis=1, keepdims=True) * (
        1.0 / HEAD_DIM**0.5
    )
    score = jnp.where(own_lane, score, 0.0).reshape(beams, group, HEAD_DIM)
    score = jnp.sum(score, axis=1)
    used = iota((beams, HEAD_DIM), 1) < group
    peaks, totals = [], []
    top = score
    for block in blocks:
        tail = block[rows : rows + beams]
        stats = tail
        for turn in (2, 4):
            stats = stats + pltpu.roll(tail, HEAD_DIM - turn * group, 1)
        peaks.append(jnp.where(used, stats, 0.0))
        totals.append(jnp.where(used, pltpu.roll(stats, HEAD_DIM - group, 1), 0.0))
        top = jnp.maximum(top, peaks[-1])
    factors = [jnp.exp(peak - top) for peak in peaks]
    new = jnp.exp(score - top)
    everything = new
    for factor, total in zip(factors, totals):
        everything += factor * total
    result = spread(new.astype(BF16).astype(F32) / everything) * by_row(value)
    for block, factor in zip(blocks, factors):
        result += spread(factor / everything) * block[:rows]
    joined[...] = result.reshape(joined.shape)
    for g in range(group):
        out_ref[:, g * HEAD_DIM : (g + 1) * HEAD_DIM] = joined[:, g, :].astype(BF16)


def output_kernel(parts_ref, q_ref, cos_ref, sin_ref, w_ref, out, joined, attended):
    combine_kernel(parts_ref, q_ref, cos_ref, sin_ref, attended, joined)
    count, _, width = out.shape
    for s in range(count):
        columns = slice(s * width, (s + 1) * width)
        total = jnp.dot(attended[...], w_ref[:, columns], preferred_element_type=F32)
        out[s] = total.astype(BF16)


def output(parts, query, cosine, sine, weight, ranks):
    beams = cosine.shape[0]
    group = query.shape[1] // beams
    return pl.pallas_call(
        output_kernel,
        in_specs=[whole()] * 5,
        out_specs=whole(),
        out_shape=shape(ranks, beams, weight.shape[1] // ranks, dtype=BF16),
        scratch_shapes=[
            pltpu.VMEM((beams, group, HEAD_DIM), F32),
            pltpu.VMEM((beams, group * HEAD_DIM), BF16),
        ],
        compiler_params=params(),
        cost_estimate=pl.CostEstimate(
            flops=2 * beams * weight.size, bytes_accessed=2 * weight.size, transcendentals=0
        ),
        name="output",
    )(parts, query, cosine, sine, weight)


def residual_kernel(x_ref, parts_ref, out_ref):
    total = jnp.sum(parts_ref[...].astype(F32), axis=0)
    out_ref[...] = (x_ref[...].astype(F32) + total).astype(BF16)


def residual(x, parts):
    return pl.pallas_call(
        residual_kernel,
        in_specs=[whole()] * 2,
        out_specs=whole(),
        out_shape=jax.ShapeDtypeStruct(x.shape, BF16),
        compiler_params=params(),
        name="residual",
    )(x, parts)


def swapped(x):
    return lax.ppermute(x, "bank", [(0, 1), (1, 0)])


def traded(blocks):
    return lax.all_to_all(blocks, "tensor", 0, 0, tiled=True)


def hop(x, bit):
    pairs = []
    for rank in range(lax.axis_size("tensor")):
        for bank in range(2):
            pairs.append((2 * rank + bank, 2 * rank_of(rank, bank, bit) + bank))
    return lax.ppermute(x, ("tensor", "bank"), pairs)


def matched_body(
    normed_hidden_input,
    beam_adapter_index,
    beam_cache_length,
    query_weight,
    keyvalue_weight,
    output_weight,
    lowrank_down_factors,
    lowrank_up_factors,
    paged_key_cache,
    paged_value_cache,
):
    x = normed_hidden_input
    ranks = lax.axis_size("tensor")
    place = lax.axis_index("tensor").astype(jnp.int32).reshape(1)
    bank = lax.axis_index("bank").astype(jnp.int32).reshape(1)
    index = (beam_adapter_index, swapped(beam_adapter_index))
    x_other = swapped(x)
    lane = jnp.arange(HEAD_DIM, dtype=jnp.int32)
    half = HEAD_DIM // 2
    frequency = jnp.power(500000.0, -2.0 * (lane % half).astype(F32) / HEAD_DIM)
    angles = beam_cache_length.astype(F32)[:, None] * frequency[None, :]
    cosine = jnp.cos(angles)
    sine = jnp.where(lane < half, -1.0, 1.0) * jnp.sin(angles)
    weight = in_hbm(query_weight)
    down = fetch(in_hbm(lowrank_down_factors.swapaxes(1, 2)))
    sent, inner, column = project_sent(place, bank, index, x, x_other, down, weight, ranks)
    came = hop(sent, 1)
    kept, length = project_kept(
        place, bank, beam_cache_length, x, x_other, weight, ranks
    )
    kept, *sent = part(kept, inner, came, ranks // 2)
    near = 4, 6, 2
    parts = [kept] + [hop(sent[slot // 2 - 1], slot) for slot in near]
    own_x, _ = lax.optimization_barrier((x, kept))
    token, parts = lax.optimization_barrier((keyval(own_x, keyvalue_weight, ranks), parts))
    own, other = correct(bank, column, lowrank_up_factors, parts)
    query = rotated(own, swapped(other), cosine, sine)

    def attended_part(queries, slots, **more):
        cache = paged_key_cache, paged_value_cache
        return attend(place, bank, length, queries, *cache, slots, **more)

    gathered = join([query] + [hop(query, slot) for slot in near])
    came = hop(gathered, 1)
    done = attended_part(gathered, (0, *near))
    odd = tuple(slot + 1 for slot in (0, *near))
    partial = attended_part(came, odd, earlier=(0, *near), before=(done, token))
    mixed = output(traded(partial), query, cosine, sine, output_weight, ranks)
    return residual(x, traded(mixed))


def joined(x, axis, combine):
    everything = jax.tree.map(lambda part: lax.all_gather(part, axis), x)
    leading = jax.tree.map(lambda part: part[0], everything)

    def turn(k, so_far):
        return combine(so_far, jax.tree.map(lambda part: part[k], everything))

    return lax.fori_loop(1, lax.axis_size(axis), turn, leading)


def apply_rotary(values, positions, head_size):
    row_count, col_count = values.shape
    half_size = head_size // 2
    frequency = jnp.power(500000.0, -2.0 * jnp.arange(half_size, dtype=jnp.float32) / head_size)
    angles = positions.astype(jnp.float32)[:, None] * frequency[None, :]
    cosine_table = jnp.cos(angles)[:, None, :]
    sine_table = jnp.sin(angles)[:, None, :]
    shaped = values.reshape(row_count, col_count // head_size, 2, half_size)
    first_half = shaped[:, :, 0]
    second_half = shaped[:, :, 1]
    rotated = jnp.stack(
        [
            first_half * cosine_table - second_half * sine_table,
            second_half * cosine_table + first_half * sine_table,
        ],
        axis=2,
    )
    return rotated.reshape(row_count, col_count)


def combine_parts(first_part, second_part):
    peak_one, total_one, weighted_one = first_part
    peak_two, total_two, weighted_two = second_part
    peak_both = jnp.maximum(peak_one, peak_two)
    factor_one = jnp.exp(peak_one - peak_both)
    factor_two = jnp.exp(peak_two - peak_both)
    return (
        peak_both,
        total_one * factor_one + total_two * factor_two,
        weighted_one * factor_one[..., None] + weighted_two * factor_two[..., None],
    )


def finish_heads(peak_score, weight_total, weighted, score_new, value_rows):
    peak_final = jnp.maximum(peak_score, score_new)
    old_factor = jnp.exp(peak_score - peak_final)
    new_weight = jnp.exp(score_new - peak_final)
    weight_total = weight_total * old_factor + new_weight
    weighted = (
        weighted * old_factor[..., None]
        + new_weight.astype(jnp.bfloat16).astype(jnp.float32)[..., None] * value_rows
    )
    return weighted / weight_total[..., None]


def body(
    normed_hidden_input,
    beam_adapter_index,
    beam_cache_length,
    query_weight,
    keyvalue_weight,
    output_weight,
    lowrank_down_factors,
    lowrank_up_factors,
    paged_key_cache,
    paged_value_cache,
):
    beam_rows, width_part = normed_hidden_input.shape
    model_width = query_weight.shape[1]
    kv_width = keyvalue_weight.shape[1] // 2
    head_count = model_width // HEAD_DIM
    kv_heads = kv_width // HEAD_DIM
    group_size = head_count // kv_heads
    tensor_index = lax.axis_index("tensor")
    query_part = jnp.dot(normed_hidden_input, query_weight, preferred_element_type=jnp.float32)
    keyval_part = jnp.dot(normed_hidden_input, keyvalue_weight, preferred_element_type=jnp.float32)
    down_all, up_all = (
        lax.all_gather(lowrank_down_factors, "bank", axis=0, tiled=True),
        lax.all_gather(lowrank_up_factors, "bank", axis=0, tiled=True),
    )
    inner_part = jnp.einsum(
        "ci,cim->cm",
        normed_hidden_input,
        down_all[beam_adapter_index],
        preferred_element_type=jnp.float32,
    )
    inner_total = lax.psum(inner_part, "tensor").astype(jnp.bfloat16)
    lowrank_delta = jnp.einsum(
        "mc,mct->mt", inner_total, up_all[beam_adapter_index], preferred_element_type=jnp.float32
    )
    query_total, keyval = lax.psum((query_part, keyval_part), "tensor")
    delta_total = lax.all_gather(lowrank_delta, "tensor", axis=1, tiled=True)
    query_rotated = apply_rotary(query_total + delta_total, beam_cache_length, HEAD_DIM).astype(
        jnp.bfloat16
    )
    key_new = apply_rotary(keyval[:, :kv_width], beam_cache_length, HEAD_DIM).astype(jnp.bfloat16)
    value_new = keyval[:, kv_width:].astype(jnp.bfloat16)
    position_count = paged_key_cache.shape[1]
    query_heads = query_rotated.reshape(beam_rows, kv_heads, group_size, HEAD_DIM)
    key_block = paged_key_cache.reshape(beam_rows, position_count, kv_heads, HEAD_DIM)
    value_block = paged_value_cache.reshape(beam_rows, position_count, kv_heads, HEAD_DIM)
    score_scale = 1.0 / HEAD_DIM**0.5
    scores = (
        jnp.einsum("bkgh,bpkh->bkgp", query_heads, key_block, preferred_element_type=jnp.float32)
        * score_scale
    )
    position_ids = tensor_index * position_count + jnp.arange(position_count)
    live_mask = (position_ids[None, :] < beam_cache_length[:, None])[:, None, None, :]
    scores = jnp.where(live_mask, scores, -1e30)
    peak_score = jnp.max(scores, axis=-1)
    weights = jnp.where(live_mask, jnp.exp(scores - peak_score[..., None]), 0.0)
    weight_total = jnp.sum(weights, axis=-1)
    weighted = jnp.einsum(
        "bkgp,bpkh->bkgh",
        weights.astype(jnp.bfloat16),
        value_block,
        preferred_element_type=jnp.float32,
    )
    peak_score, weight_total, weighted = joined(
        (peak_score, weight_total, weighted), "tensor", combine_parts
    )
    score_new = (
        jnp.einsum(
            "bkgh,bkh->bkg",
            query_heads,
            key_new.reshape(beam_rows, kv_heads, HEAD_DIM),
            preferred_element_type=jnp.float32,
        )
        * score_scale
    )
    value_rows = value_new.reshape(beam_rows, kv_heads, HEAD_DIM).astype(jnp.float32)[:, :, None, :]
    attended = (
        finish_heads(peak_score, weight_total, weighted, score_new, value_rows)
        .reshape(beam_rows, model_width)
        .astype(jnp.bfloat16)
    )
    attended_cols = lax.dynamic_slice_in_dim(attended, tensor_index * width_part, width_part, 1)
    mixed_cols = lax.psum_scatter(
        lax.dot_general(
            output_weight,
            attended_cols,
            (((0,), (1,)), ((), ())),
            preferred_element_type=jnp.float32,
        ),
        "tensor",
        scatter_dimension=0,
        tiled=True,
    )
    return (normed_hidden_input.astype(jnp.float32) + mixed_cols.T).astype(jnp.bfloat16)


def solution(mesh):
    matched = mesh.shape["tensor"] == 8 and mesh.shape["bank"] == 2
    return jax.shard_map(
        matched_body if matched else body,
        mesh=mesh,
        in_specs=(
            P(("groups", "bank"), "tensor"),
            P(("groups", "bank")),
            P(("groups", "bank")),
            P("tensor", None),
            P("tensor", None),
            P("tensor", None),
            P("bank", "tensor", None),
            P("bank", None, "tensor"),
            P(("groups", "bank"), "tensor", None),
            P(("groups", "bank"), "tensor", None),
        ),
        out_specs=P(("groups", "bank"), "tensor"),
        check_vma=False,
    )
```
